32 devices in a mesh: row: 8 (over z, x), col: 4 (over y, core).
Axes of the slice: x: 2, y: 2, z: 4, core: 2. Of those that a mesh axis runs over, the one named last changes fastest.
Arguments:
- right_side: float32 [32, 512, 256], P('row', 'col'), may hold values from -12 to 12
- permeability: bfloat16 [32, 512, 256], P('row', 'col'), may hold values from 0.25 to 4
- lift_weight: float32 [16, 3], replicated, may hold values from -3 to 3
- spectral_weight: float32 [2, 32, 16, 16, 512], P(None, 'row', None, None, 'col'), may hold values from -3 to 3
- mix_weight: float32 [16, 17], replicated, may hold values from -3 to 3
- proj_weight: float32 [17], replicated, may hold values from -3 to 3
Outputs:
- solution: float32 [32, 512, 256], P('row', 'col')
- residual: float32 [32, 512, 256], P('row', 'col')
- kept: float32 [2, 32, 512, 256], P(None, 'row', 'col')
The draws below stay inside these ranges and needn't reach their ends.
All inputs are finite; a program needn't handle non-finite values.
Results may differ from the reference program's by a relative error of at most 0.0007.
Values may be sent and summed in bfloat16 or wider, within the bound.
No kernel may reach another device: no remote copies, remote signals or barrier semaphores. Data moves between devices by JAX's collectives and lax.ppermute only.
A program may use at most 128 MiB of HBM per device.

```python
import math
import jax
import jax.numpy as jnp
from jax import lax

NZ = 256
CHANNELS = 16
KX = 16
KY = 32
KZ = 32
ITERS = 2
NX = 32
NY = 512


def draw_right_side(key, part):
    first_frac = lax.broadcasted_iota(jnp.float32, (NX, NY, NZ), 0) / NX
    second_frac = lax.broadcasted_iota(jnp.float32, (NX, NY, NZ), 1) / NY
    ramp = 0.6 + 0.8 * first_frac + 0.6 * second_frac
    noise = jnp.clip(jax.random.normal(key, (NX, NY, NZ), jnp.float32), -6.0, 6.0)
    return noise * ramp


def steps_of(key, dims, shards, least, largest):
    factor_of = 1.0
    for dim, shards_of in shards:
        draws = jax.random.uniform(jax.random.fold_in(jax.random.fold_in(key, 6), dim), (shards_of,), jnp.float32, least / len(shards), largest / len(shards))
        factor_of = factor_of * jnp.repeat(jnp.exp(draws), dims[dim] // shards_of).reshape((-1,) + (1,) * (len(dims) - 1 - dim))
    return factor_of


def centred(rng, dims, scale, bound, shards=(), kind=jnp.bfloat16):
    drawn = jax.random.normal(rng, dims, jnp.float32) * scale
    if len(shards) > 0:
        drawn = steps_of(rng, dims, shards, -0.22, 0.18) * drawn
    return jnp.clip(drawn, min=-bound, max=bound).astype(kind)


def setup_inputs(seed: int = 0) -> dict:
    streams_of = jax.random.split(jax.random.key(seed), 7)
    return {
        "right_side": draw_right_side(jax.random.fold_in(streams_of[6], 71), 0),
        "permeability": jnp.clip(jnp.exp(math.log(4.0) - 2.7725887 * jax.random.uniform(streams_of[1], (NX, NY, NZ), jnp.float32) ** steps_of(streams_of[1], (NX, NY, NZ), ((0, 8), (1, 4)), -0.2, 0.2)), 0.25, 4.0).astype(jnp.bfloat16),
        "lift_weight": centred(streams_of[2], (CHANNELS, 3), 0.8, 3.0, (), jnp.float32),
        "spectral_weight": centred(streams_of[3], (2, KZ, CHANNELS, CHANNELS, KX * KY), 0.25, 3.0, ((1, 8), (4, 4)), jnp.float32),
        "mix_weight": centred(streams_of[4], (CHANNELS, CHANNELS + 1), 0.25, 3.0, (), jnp.float32),
        "proj_weight": centred(streams_of[5], (CHANNELS + 1,), 0.35, 3.0, (), jnp.float32),
    }


HIGHEST = lax.Precision.HIGHEST

def einsum_high(form, left, right):
    return jnp.einsum(form, left, right, precision=HIGHEST)

def harmonic(first, second):
    return 2.0 * first * second / (first + second)

def wave_table(freqs, places, length):
    turns = freqs[None, :] * places[:, None] % length
    angle = turns.astype(jnp.float32) * (2.0 * jnp.pi / length)
    return (jnp.cos(angle), jnp.sin(angle))

def signed_freqs(count):
    return jnp.arange(count, dtype=jnp.int32) - count // 2

def apply_operator(field, faces):
    first, second, third = faces
    padded = jnp.pad(field, 1)
    total = first[:-1] * (field - padded[:-2, 1:-1, 1:-1])
    total = total + first[1:] * (field - padded[2:, 1:-1, 1:-1])
    total = total + second[:, :-1] * (field - padded[1:-1, :-2, 1:-1])
    total = total + second[:, 1:] * (field - padded[1:-1, 2:, 1:-1])
    total = total + third[:, :, :-1] * (field - padded[1:-1, 1:-1, :-2])
    total = total + third[:, :, 1:] * (field - padded[1:-1, 1:-1, 2:])
    return total

def precondition(res, squares_total, log_perm, lift_weight, spectral_weight, mix_weight, proj_weight, tables):
    cosine_rows, sine_rows, cosine_cols, sine_cols, cosine_deep, sine_deep = tables
    cells = NX * NY * NZ
    scale = jnp.sqrt(squares_total / cells + 1e-06)
    scaled = res / scale

    def lifted(channel):
        return jax.nn.gelu(lift_weight[channel, 0] * scaled + lift_weight[channel, 1] * log_perm + lift_weight[channel, 2])
    real_list = []
    imag_list = []
    for channel in range(CHANNELS):
        values = lifted(channel)
        deep_real = einsum_high('xyz,zk->xyk', values, cosine_deep)
        deep_imag = -einsum_high('xyz,zk->xyk', values, sine_deep)
        first_real = einsum_high('xyk,xf->fyk', deep_real, cosine_rows) + einsum_high('xyk,xf->fyk', deep_imag, sine_rows)
        first_imag = einsum_high('xyk,xf->fyk', deep_imag, cosine_rows) - einsum_high('xyk,xf->fyk', deep_real, sine_rows)
        second_real = einsum_high('fyk,yg->fgk', first_real, cosine_cols) + einsum_high('fyk,yg->fgk', first_imag, sine_cols)
        second_imag = einsum_high('fyk,yg->fgk', first_imag, cosine_cols) - einsum_high('fyk,yg->fgk', first_real, sine_cols)
        real_list.append(second_real)
        imag_list.append(second_imag)
    spec_real = jnp.stack(real_list)
    spec_imag = jnp.stack(imag_list)
    table = spectral_weight.reshape(2, KZ, CHANNELS, CHANNELS, KX, KY)
    mixed_real = einsum_high('cfgk,kcofg->ofgk', spec_real, table[0]) - einsum_high('cfgk,kcofg->ofgk', spec_imag, table[1])
    mixed_imag = einsum_high('cfgk,kcofg->ofgk', spec_imag, table[0]) + einsum_high('cfgk,kcofg->ofgk', spec_real, table[1])
    output = jnp.zeros_like(res)
    for target in range(CHANNELS):
        back_real = einsum_high('fgk,yg->fyk', mixed_real[target], cosine_cols) - einsum_high('fgk,yg->fyk', mixed_imag[target], sine_cols)
        back_imag = einsum_high('fgk,yg->fyk', mixed_imag[target], cosine_cols) + einsum_high('fgk,yg->fyk', mixed_real[target], sine_cols)
        whole_real = einsum_high('fyk,xf->xyk', back_real, cosine_rows) - einsum_high('fyk,xf->xyk', back_imag, sine_rows)
        whole_imag = einsum_high('fyk,xf->xyk', back_imag, cosine_rows) + einsum_high('fyk,xf->xyk', back_real, sine_rows)
        spatial = (einsum_high('xyk,zk->xyz', whole_real, cosine_deep) - einsum_high('xyk,zk->xyz', whole_imag, sine_deep)) / cells
        point = mix_weight[target, CHANNELS] + jnp.zeros_like(res)
        for channel in range(CHANNELS):
            point = point + mix_weight[target, channel] * lifted(channel)
        output = output + proj_weight[target] * jax.nn.gelu(spatial + point)
    return scale * (output + proj_weight[CHANNELS])

def reference(right_side, permeability, lift_weight, spectral_weight, mix_weight, proj_weight):
    conductance = permeability.astype(jnp.float32)
    log_perm = jnp.log(conductance)
    edged = jnp.pad(conductance, 1, mode='edge')
    faces = (harmonic(edged[:-1, 1:-1, 1:-1], edged[1:, 1:-1, 1:-1]), harmonic(edged[1:-1, :-1, 1:-1], edged[1:-1, 1:, 1:-1]), harmonic(edged[1:-1, 1:-1, :-1], edged[1:-1, 1:-1, 1:]))
    cosine_rows, sine_rows = wave_table(signed_freqs(KX), jnp.arange(NX, dtype=jnp.int32), NX)
    cosine_cols, sine_cols = wave_table(signed_freqs(KY), jnp.arange(NY, dtype=jnp.int32), NY)
    cosine_deep, sine_deep = wave_table(jnp.arange(KZ, dtype=jnp.int32), jnp.arange(NZ, dtype=jnp.int32), NZ)
    tables = (cosine_rows, sine_rows, cosine_cols, sine_cols, cosine_deep, sine_deep)

    def precond(res):
        return precondition(res, jnp.sum(res * res), log_perm, lift_weight, spectral_weight, mix_weight, proj_weight, tables)
    solution = jnp.zeros_like(right_side)
    residual = right_side
    update = precond(residual)
    kept = [update]
    direction = update
    for step in range(ITERS):
        image = apply_operator(direction, faces)
        curvature = jnp.sum(direction * image)
        alpha = jnp.sum(residual * direction) / curvature
        solution = solution + alpha * direction
        residual = residual - alpha * image
        if step + 1 < ITERS:
            update = precond(residual)
            kept.append(update)
            beta = jnp.sum(update * image) / curvature
            direction = update - beta * direction
    return (solution, residual, jnp.stack(kept))
```

```python
import functools

import jax
import jax.numpy as jnp
import ml_dtypes
import numpy as np
from jax import lax
from jax.experimental import pallas as pl
from jax.experimental.pallas import tpu as pltpu
from jax.sharding import PartitionSpec as P

CHANNELS = 16
KX = 16
KY = 32
KZ = 32
ITERS = 2


HIGHEST = lax.Precision.HIGHEST


def with_halo(block, sides, width):
    for axis, dim in sides:
        count = lax.axis_size(axis)
        forward = [(i, i + 1) for i in range(count - 1)]
        backward = [(target, source) for source, target in forward]
        low = lax.ppermute(
            lax.slice_in_dim(block, block.shape[dim] - width, None, axis=dim), axis, forward
        )
        high = lax.ppermute(lax.slice_in_dim(block, 0, width, axis=dim), axis, backward)
        block = jnp.concatenate([low, block, high], axis=dim)
    return block


def einsum_high(form, left, right):
    return jnp.einsum(form, left, right, precision=HIGHEST)


def harmonic(first, second):
    return 2.0 * first * second / (first + second)


def wave_table(freqs, places, length):
    turns = freqs[None, :] * places[:, None] % length
    angle = turns.astype(jnp.float32) * (2.0 * jnp.pi / length)
    return (jnp.cos(angle), jnp.sin(angle))


def signed_freqs(count):
    return jnp.arange(count, dtype=jnp.int32) - count // 2


def face_arrays(permeability):
    padded = with_halo(permeability, (("row", 0), ("col", 1)), 1).astype(jnp.float32)
    own = permeability.astype(jnp.float32)
    edged = jnp.pad(own, ((1, 1), (1, 1), (0, 0)), mode="edge")
    padded = jnp.where(padded > 0.0, padded, edged)
    first = harmonic(padded[:-1, 1:-1], padded[1:, 1:-1])
    second = harmonic(padded[1:-1, :-1], padded[1:-1, 1:])
    deep = jnp.pad(own, ((0, 0), (0, 0), (1, 1)), mode="edge")
    third = harmonic(deep[:, :, :-1], deep[:, :, 1:])
    return ((first, second, third), jnp.log(own))


def apply_operator(field, faces):
    first, second, third = faces
    padded = with_halo(field, (("row", 0), ("col", 1)), 1)
    padded = jnp.pad(padded, ((0, 0), (0, 0), (1, 1)))
    total = first[:-1] * (field - padded[:-2, 1:-1, 1:-1])
    total = total + first[1:] * (field - padded[2:, 1:-1, 1:-1])
    total = total + second[:, :-1] * (field - padded[1:-1, :-2, 1:-1])
    total = total + second[:, 1:] * (field - padded[1:-1, 2:, 1:-1])
    total = total + third[:, :, :-1] * (field - padded[1:-1, 1:-1, :-2])
    total = total + third[:, :, 1:] * (field - padded[1:-1, 1:-1, 2:])
    return total


def global_squares(field):
    return lax.psum(jnp.sum(field * field), ("row", "col"))


def mix_modes(real_in, imag_in, spectral_weight, deep_count, freq_count):
    block = spectral_weight.reshape(2, deep_count, CHANNELS, CHANNELS, freq_count, KY)
    real_out = einsum_high("kcfg,kcofg->kofg", real_in, block[0]) - einsum_high(
        "kcfg,kcofg->kofg", imag_in, block[1]
    )
    imag_out = einsum_high("kcfg,kcofg->kofg", imag_in, block[0]) + einsum_high(
        "kcfg,kcofg->kofg", real_in, block[1]
    )
    return (real_out, imag_out)


def spectral_transpose(real_part, imag_part, spectral_weight, grid):
    rows, cols, n_row, n_col, row_id, col_id = grid
    full_rows = rows * n_row
    full_cols = cols * n_col
    cosine_rows, sine_rows = wave_table(
        signed_freqs(KX), jnp.arange(full_rows, dtype=jnp.int32), full_rows
    )
    cosine_cols, sine_cols = wave_table(
        signed_freqs(KY), jnp.arange(full_cols, dtype=jnp.int32), full_cols
    )
    real_part, imag_part = (
        lax.all_to_all(real_part, "row", split_axis=0, concat_axis=1, tiled=True),
        lax.all_to_all(imag_part, "row", split_axis=0, concat_axis=1, tiled=True),
    )
    first_real = einsum_high("qxy,xf->qfy", real_part, cosine_rows) + einsum_high(
        "qxy,xf->qfy", imag_part, sine_rows
    )
    first_imag = einsum_high("qxy,xf->qfy", imag_part, cosine_rows) - einsum_high(
        "qxy,xf->qfy", real_part, sine_rows
    )
    first_real, first_imag = (
        lax.all_to_all(first_real, "col", split_axis=1, concat_axis=2, tiled=True),
        lax.all_to_all(first_imag, "col", split_axis=1, concat_axis=2, tiled=True),
    )
    second_real = einsum_high("qfy,yg->qfg", first_real, cosine_cols) + einsum_high(
        "qfy,yg->qfg", first_imag, sine_cols
    )
    second_imag = einsum_high("qfy,yg->qfg", first_imag, cosine_cols) - einsum_high(
        "qfy,yg->qfg", first_real, sine_cols
    )
    deep_count = KZ // n_row
    freq_count = KX // n_col
    shape_in = (deep_count, CHANNELS, freq_count, KY)
    mixed_real, mixed_imag = mix_modes(
        second_real.reshape(shape_in),
        second_imag.reshape(shape_in),
        spectral_weight,
        deep_count,
        freq_count,
    )
    shape_out = (deep_count * CHANNELS, freq_count, KY)
    mixed_real = mixed_real.reshape(shape_out)
    mixed_imag = mixed_imag.reshape(shape_out)
    back_real = einsum_high("qfg,yg->qfy", mixed_real, cosine_cols) - einsum_high(
        "qfg,yg->qfy", mixed_imag, sine_cols
    )
    back_imag = einsum_high("qfg,yg->qfy", mixed_imag, cosine_cols) + einsum_high(
        "qfg,yg->qfy", mixed_real, sine_cols
    )
    back_real, back_imag = (
        lax.all_to_all(back_real, "col", split_axis=2, concat_axis=1, tiled=True),
        lax.all_to_all(back_imag, "col", split_axis=2, concat_axis=1, tiled=True),
    )
    out_real = einsum_high("qfy,xf->qxy", back_real, cosine_rows) - einsum_high(
        "qfy,xf->qxy", back_imag, sine_rows
    )
    out_imag = einsum_high("qfy,xf->qxy", back_imag, cosine_rows) + einsum_high(
        "qfy,xf->qxy", back_real, sine_rows
    )
    out_real, out_imag = (
        lax.all_to_all(out_real, "row", split_axis=1, concat_axis=0, tiled=True),
        lax.all_to_all(out_imag, "row", split_axis=1, concat_axis=0, tiled=True),
    )
    return (out_real, out_imag)


def precondition(residual, squares_total, log_perm, weights, grid, cells):
    lift_weight, spectral_weight, mix_weight, proj_weight = weights
    rows, cols, depth = residual.shape
    scale = jnp.sqrt(squares_total / cells + 1e-06)
    scaled = residual / scale
    lifted = jax.nn.gelu(
        lift_weight[:, 0, None, None, None] * scaled[None]
        + lift_weight[:, 1, None, None, None] * log_perm[None]
        + lift_weight[:, 2, None, None, None]
    )
    cosine_deep, sine_deep = wave_table(
        jnp.arange(KZ, dtype=jnp.int32), jnp.arange(depth, dtype=jnp.int32), depth
    )
    real_part = einsum_high("cxyz,zk->kcxy", lifted, cosine_deep).reshape(KZ * CHANNELS, rows, cols)
    imag_part = -einsum_high("cxyz,zk->kcxy", lifted, sine_deep).reshape(KZ * CHANNELS, rows, cols)
    out_real, out_imag = spectral_transpose(real_part, imag_part, spectral_weight, grid)
    out_real = out_real.reshape(KZ, CHANNELS, rows, cols)
    out_imag = out_imag.reshape(KZ, CHANNELS, rows, cols)
    spatial = (
        einsum_high("kcxy,zk->cxyz", out_real, cosine_deep)
        - einsum_high("kcxy,zk->cxyz", out_imag, sine_deep)
    ) / cells
    point = (
        einsum_high("oc,cxyz->oxyz", mix_weight[:, :CHANNELS], lifted)
        + mix_weight[:, CHANNELS, None, None, None]
    )
    hidden = jax.nn.gelu(spatial + point)
    return scale * (
        einsum_high("o,oxyz->xyz", proj_weight[:CHANNELS], hidden) + proj_weight[CHANNELS]
    )


def local(right_side, permeability, lift_weight, spectral_weight, mix_weight, proj_weight):
    rows, cols, depth = right_side.shape
    n_row = lax.axis_size("row")
    n_col = lax.axis_size("col")
    grid = (rows, cols, n_row, n_col, lax.axis_index("row"), lax.axis_index("col"))
    cells = float(rows * n_row * cols * n_col * depth)
    faces, log_perm = face_arrays(permeability)
    weights = (lift_weight, spectral_weight, mix_weight, proj_weight)

    def precond(residual, squares_total):
        return precondition(residual, squares_total, log_perm, weights, grid, cells)

    solution = jnp.zeros_like(right_side)
    residual = right_side
    kept = []
    update = precond(residual, global_squares(residual))
    kept.append(update)
    direction = update
    for step in range(ITERS):
        image = apply_operator(direction, faces)
        curvature, along = lax.psum(
            (jnp.sum(direction * image), jnp.sum(residual * direction)), ("row", "col")
        )
        alpha = along / curvature
        solution = solution + alpha * direction
        residual = residual - alpha * image
        if step + 1 < ITERS:
            update = precond(residual, global_squares(residual))
            kept.append(update)
            beta = lax.psum(jnp.sum(update * image), ("row", "col")) / curvature
            direction = update - beta * direction
    return (solution, residual, jnp.stack(kept))


LANES = 128
SUBLANES = 8
BOTH = ("row", "col")
F32 = jnp.float32
BF16 = jnp.bfloat16


def split_table(table):
    high = table.astype(ml_dtypes.bfloat16)
    low = (table - high.astype(np.float64)).astype(ml_dtypes.bfloat16)
    return high, low


def split(value):
    high = value.astype(BF16)
    return high, (value - high.astype(F32)).astype(BF16)


def split_three(value):
    high = value.astype(BF16).astype(F32)
    rest = value - high
    middle = rest.astype(BF16).astype(F32)
    return high, middle, rest - middle


def matmul(left, right):
    return jnp.dot(left, right, preferred_element_type=F32)


def matmul_nt(left, right):
    return lax.dot_general(left, right, (((1,), (1,)), ((), ())), preferred_element_type=F32)


def angles(freqs, places, length):
    turns = np.multiply.outer(freqs, places) % length
    return turns * (2.0 * np.pi / length)


def deep_order(n_row):
    count = KZ // n_row
    order = [
        (part, row * count + place)
        for row in range(n_row)
        for part in range(2)
        for place in range(count)
    ]
    return np.array(order)


def deep_tables(n_row, depth):
    order = deep_order(n_row)
    angle = angles(order[:, 1], np.arange(depth), depth)
    wave = np.where(order[:, :1] == 0, np.cos(angle), -np.sin(angle))
    high, low = split_table(wave)
    return np.concatenate([high, low], 0), np.concatenate([high.T, high.T, high.T, low.T], 1)


def column_tables(n_col, cols):
    freqs = np.arange(KY) - KY // 2
    forward = []
    back = []
    for place in range(n_col):
        angle = angles(freqs, place * cols + np.arange(cols), n_col * cols)
        both = np.concatenate([np.cos(angle), np.sin(angle)], 1)
        high, low = split_table(both)
        forward.append(np.concatenate([high, low], 0))
        both = np.concatenate([np.cos(angle), np.sin(angle)], 0)
        high, low = split_table(both)
        back.append(
            np.concatenate(
                [
                    np.concatenate([high, low], 1),
                    np.concatenate([high, low], 1),
                    np.concatenate([high, np.zeros_like(low)], 1),
                ],
                0,
            )
        )
    return np.stack(forward), np.stack(back)


def gelu(value):
    inner = value * (0.7978845608028654 + 0.035677408136300125 * (value * value))
    return (0.5 * value) * (1.0 + jnp.tanh(inner))


def call(body, outs, in_specs, out_specs, grid=(), scratch=(), flops=0, moved=0, alias=None, limit=8, near=()):
    single = not isinstance(outs, tuple)
    outs = (outs,) if single else outs
    out_specs = (out_specs,) if single else out_specs
    run = pl.pallas_call(
        body,
        out_shape=tuple(
            pltpu.HBM(out.shape, out.dtype) if out.size > 2**16 else out for out in outs
        ),
        grid=grid,
        in_specs=in_specs,
        out_specs=out_specs,
        scratch_shapes=list(scratch),
        input_output_aliases=alias or {},
        compiler_params=pltpu.CompilerParams(vmem_limit_bytes=limit * 1024 * 1024),
        cost_estimate=pl.CostEstimate(
            flops=int(flops), bytes_accessed=int(moved), transcendentals=0
        ),
    )

    def wrapped(*args):
        held = [
            arg
            if place in near or spec.memory_space == pltpu.SMEM
            else pltpu.with_memory_space_constraint(arg, pltpu.HBM)
            for place, (arg, spec) in enumerate(zip(args, in_specs))
        ]
        found = run(*held)
        return found[0] if single else found

    return wrapped


def whole(memory=pltpu.VMEM):
    return pl.BlockSpec(memory_space=memory)


def shape(*dims):
    return jax.ShapeDtypeStruct(dims, F32)


def lane_sums(value):
    folded = jnp.sum(value.reshape(-1, SUBLANES, value.shape[-1]), axis=0)
    folded = sum(
        folded[:, start : start + LANES] for start in range(0, folded.shape[1], LANES)
    )
    return jnp.sum(folded, axis=0, keepdims=True)


def spread(rows, ref):
    rows = rows + [jnp.zeros_like(rows[0])] * (SUBLANES - len(rows))
    ref[...] = jnp.broadcast_to(jnp.concatenate(rows, 0)[None], ref.shape)


def gathered(ref, row):
    total = jnp.sum(ref[...], axis=0)
    return jnp.sum(total[row : row + 1], axis=1, keepdims=True)


def squares_body(field_ref, perm_ref, out_ref, low_ref, high_ref, left_ref, right_ref):
    total = field_ref[0] * field_ref[0]
    for place in range(1, field_ref.shape[0]):
        total = total + field_ref[place] * field_ref[place]
    spread([lane_sums(total)], out_ref)
    rows, cols, _ = perm_ref.shape
    low_ref[...] = perm_ref[0]
    high_ref[...] = perm_ref[rows - 1]
    for place in range(rows):
        plane = perm_ref[place].astype(F32)
        left_ref[place : place + 1, :] = plane[:1]
        right_ref[place : place + 1, :] = plane[cols - 1 :]


def weight_body(weight_ref, out_ref):
    groups, freq, channels, fine, _ = out_ref.shape
    parts, deep, _, outs, modes = weight_ref.shape
    for channel in range(channels):
        block = weight_ref[:, :, channel].reshape(parts * deep * outs, modes)
        block = block.T.reshape(freq, groups, fine, parts * deep * outs)
        for group in range(groups):
            out_ref[group, :, channel] = block[:, group]


def turn_body(weight_ref, out_ref):
    out_ref[...] = pltpu.roll(weight_ref[...], LANES // 2, 1)


def harmonic_faces(perm_ref, low_ref, high_ref, left_ref, right_ref, first_ref, sec_lo, sec_hi, thi_lo, thi_hi):
    rows, cols, depth = perm_ref.shape
    planes = [perm_ref[place].astype(F32) for place in range(rows)]
    line = lax.broadcasted_iota(jnp.int32, (cols, depth), 0)
    deep = lax.broadcasted_iota(jnp.int32, (cols, depth), 1)
    before = low_ref[...].astype(F32)
    after = high_ref[...].astype(F32)
    around = [jnp.where(before > 0.0, before, planes[0])] + planes
    around = around + [jnp.where(after > 0.0, after, planes[-1])]
    for place in range(rows + 1):
        first_ref[place] = harmonic(around[place], around[place + 1])
    for place in range(rows):
        own = planes[place]
        left = left_ref[place : place + 1]
        right = right_ref[place : place + 1]
        left = jnp.where(left > 0.0, left, own[:1])
        right = jnp.where(right > 0.0, right, own[cols - 1 :])
        lower = jnp.where(line == 0, left, pltpu.roll(own, 1, 0))
        upper = jnp.where(line == cols - 1, right, pltpu.roll(own, cols - 1, 0))
        sec_lo[place] = harmonic(own, lower)
        sec_hi[place] = harmonic(own, upper)
        lower = jnp.where(deep == 0, own, pltpu.roll(own, 1, 1))
        upper = jnp.where(deep == depth - 1, own, pltpu.roll(own, depth - 1, 1))
        thi_lo[place] = harmonic(own, lower)
        thi_hi[place] = harmonic(own, upper)


def scale_of(total, cells):
    return jnp.sqrt(total / cells + 1e-06)


def lift_channel(weight_ref, channel, scaled, log_perm):
    return gelu(
        weight_ref[0, channel] * scaled
        + (weight_ref[1, channel] * log_perm + weight_ref[2, channel])
    )


def transform(lift_ref, deep_ref, col_ref, scaled, log_perm, spectra_ref, zt_ref):
    half = 2 * KZ
    cols = scaled.shape[1]
    for channel in range(0, CHANNELS, 2):
        lifted = jnp.concatenate(
            [lift_channel(lift_ref, channel + j, scaled, log_perm) for j in range(2)], 1
        )
        high, low = split(lifted)
        part = matmul(deep_ref[...], high)
        part = part[:half] + part[half:] + matmul(deep_ref[:half], low)
        for j in range(2):
            zt_ref[pl.ds(channel + j, half, stride=CHANNELS), :] = part[:, j * cols : (j + 1) * cols]
    groups = half * CHANNELS // LANES
    waves = zt_ref[...].reshape(groups, 2, LANES // 2, cols)
    turned = jnp.concatenate([waves[:, 1:], -waves[:, :1]], 1)
    waves = jnp.concatenate(
        [waves.reshape(groups * LANES, cols), turned.reshape(groups * LANES, cols)], 1
    )
    high, low = split(waves)
    table = col_ref[lax.axis_index("col")]
    part = matmul_nt(table, high)
    part = part[:KY] + part[KY:] + matmul_nt(table[:KY], low)
    n_col = KY // SUBLANES
    for row in range(groups):
        for col in range(n_col):
            spectra_ref[row * n_col + col, 0] = part[
                col * SUBLANES : (col + 1) * SUBLANES, row * LANES : (row + 1) * LANES
            ]


def lift_first_body(cells, lift_ref, sums_ref, res_ref, perm_ref, deep_ref, col_ref, spectra_ref, zt_ref):
    scale = scale_of(gathered(sums_ref, 0), cells)
    scaled = (res_ref[0] / scale).T
    log_perm = jnp.log(perm_ref[0].astype(F32)).T
    transform(lift_ref, deep_ref, col_ref, scaled, log_perm, spectra_ref, zt_ref)


def next_scalars(first_ref, sums_ref):
    curvature = gathered(sums_ref, 0)
    alpha = gathered(sums_ref, 1) / curvature
    total = gathered(first_ref, 0) + alpha * (
        alpha * gathered(sums_ref, 2) - 2.0 * gathered(sums_ref, 3)
    )
    return curvature, alpha, jnp.maximum(total, 0.0)


def lift_next_body(cells, lift_ref, first_ref, sums_ref, res_ref, image_ref, perm_ref, deep_ref, col_ref, spectra_ref, next_ref, zt_ref):
    _, alpha, total = next_scalars(first_ref, sums_ref)
    scale = scale_of(total, cells)
    residual = res_ref[0] - alpha * image_ref[0]
    next_ref[0] = residual
    scaled = (residual / scale).T
    log_perm = jnp.log(perm_ref[0].astype(F32)).T
    transform(lift_ref, deep_ref, col_ref, scaled, log_perm, spectra_ref, zt_ref)


def point_body(scale_of_refs, lift_ref, mix_ref, *refs):
    *scalar_refs, res_ref, perm_ref, _, _, point_ref, scaled_ref, log_ref, lifted_ref = refs
    scaled_ref[...] = (res_ref[0] / scale_of_refs(*scalar_refs)).T
    log_ref[...] = jnp.log(perm_ref[0].astype(F32)).T
    size = lifted_ref.shape[1]
    group = 4

    def step(index, carry):
        lines = pl.ds(pl.multiple_of(index * size, size), size)
        scaled = scaled_ref[lines, :]
        log_perm = log_ref[lines, :]
        for channel in range(CHANNELS):
            lifted_ref[channel] = lift_channel(lift_ref, channel, scaled, log_perm)
        for first in range(0, CHANNELS, group):
            sums = [mix_ref[first + j, CHANNELS] for j in range(group)]
            for channel in range(CHANNELS):
                lifted = lifted_ref[channel]
                sums = [
                    total + mix_ref[first + j, channel] * lifted for j, total in enumerate(sums)
                ]
            for j, total in enumerate(sums):
                point_ref[0, first + j, lines, :] = total
        return carry

    lax.fori_loop(0, scaled_ref.shape[0] // size, step, 0)


def modes_body(cells, n_row, n_col, recv_ref, weight_ref, other_ref, _, out_ref, field_ref, turned_ref, spec_ref, odd_ref):
    rows = recv_ref.shape[1]
    places = n_row * rows
    tile = (SUBLANES, LANES)
    lane = lax.broadcasted_iota(jnp.int32, tile, 1)
    first = lane < LANES // 2
    sign = jnp.where(first, 1.0, -1.0).astype(F32)
    base = lane - lane % CHANNELS

    def turn(value):
        return pltpu.roll(value, LANES // 2, 1) * sign

    for row in range(n_row):
        for place in range(rows):
            value = recv_ref[row * n_col, place]
            for col in range(1, n_col):
                value = value + recv_ref[row * n_col + col, place]
            field_ref[row * rows + place] = value
            turned_ref[row * rows + place] = turn(value)
    angle = 2.0 * np.pi / places
    half = KX // 2

    def weigh(coefs, ref):
        total = None
        for place, coef in enumerate(coefs):
            coef = float(coef)
            if abs(coef) < 1e-12:
                continue
            term = ref[place]
            if coef == -1.0:
                term = -term
            elif coef != 1.0:
                term = coef * term
            total = term if total is None else total + term
        return jnp.zeros(tile, F32) if total is None else total

    for freq in range(half + 1):
        turns = freq * np.arange(places) % places
        even = weigh(np.cos(angle * turns), field_ref)
        odd = weigh(np.sin(angle * turns), turned_ref)
        if freq < half:
            spec_ref[half + freq] = even + odd
        if freq > 0:
            spec_ref[half - freq] = even - odd

    def mix(freq, carry):
        value = spec_ref[freq]
        same = [None, None]
        cross = [None, None]
        for channel in range(CHANNELS):
            wide = jnp.take_along_axis(value, base + channel, axis=1)
            for sums, ref in ((same, weight_ref), (cross, other_ref)):
                term = ref[freq, channel] * wide
                kept = sums[channel % 2]
                sums[channel % 2] = term if kept is None else kept + term
        same = same[0] + same[1]
        cross = cross[0] + cross[1]
        total = jnp.where(
            first,
            same - pltpu.roll(same, LANES // 2, 1),
            cross + pltpu.roll(cross, LANES // 2, 1),
        )
        field_ref[freq] = total
        turned_ref[freq] = -turn(total)
        return carry

    lax.fori_loop(0, KX, mix, 0)
    gain = 1.0 / cells
    evens = [field_ref[half] * gain]
    odds = [None]
    for freq in range(1, half):
        evens.append((field_ref[half + freq] + field_ref[half - freq]) * gain)
        odds.append((turned_ref[half + freq] - turned_ref[half - freq]) * gain)
    evens.append(field_ref[0] * gain)
    odds.append(-turned_ref[0] * gain)
    for freq in range(half + 1):
        spec_ref[freq] = evens[freq]
        if freq > 0:
            odd_ref[freq] = odds[freq]

    def store(place, value):
        for col in range(n_col):
            out_ref[(place // rows) * n_col + col, place % rows] = value

    for place in range(places // 2 + 1):
        turns = place * np.arange(half + 1) % places
        even = weigh(np.cos(angle * turns), spec_ref)
        odd = weigh(np.sin(angle * turns), odd_ref)
        store(place, even + odd)
        if 0 < place < places // 2:
            store(places - place, even - odd)


def back_transform(recv_ref, point_ref, proj_ref, col_ref, deep_ref, wave_ref, scale):
    groups = 2 * KZ * CHANNELS // LANES
    n_col = KY // SUBLANES
    cols = col_ref.shape[2] // 2
    lane = lax.broadcasted_iota(jnp.int32, (KY, LANES), 1)
    sign = jnp.where(lane < LANES // 2, -1.0, 1.0).astype(F32)
    half = 2 * KZ
    pieces = []
    for row in range(groups):
        value = recv_ref[row * n_col : (row + 1) * n_col, 0].reshape(KY, LANES)
        turned = pltpu.roll(value, LANES // 2, 1) * sign
        both = jnp.concatenate([value, turned], 0)
        pieces.append(jnp.concatenate(split_three(both), 0).T.astype(BF16))
    part = matmul(jnp.concatenate(pieces, 0), col_ref[lax.axis_index("col")])
    wave_ref[...] = part[:, :cols] + part[:, cols:]
    total = None
    for out in range(0, CHANNELS, 2):
        waves = jnp.concatenate(
            [wave_ref[pl.ds(out + j, half, stride=CHANNELS), :] for j in range(2)], 1
        )
        high, middle, low = (part.astype(BF16) for part in split_three(waves))
        spatial = matmul(deep_ref[...], jnp.concatenate([high, middle, low, high], 0))
        for j in range(2):
            hidden = gelu(spatial[:, j * cols : (j + 1) * cols] + point_ref[0, out + j])
            term = proj_ref[out + j] * hidden
            total = term if total is None else total + term
    return (scale * (total + proj_ref[CHANNELS])).T


def put_edges(update, low_ref, high_ref, left_ref, right_ref):
    step = pl.program_id(0)
    left_ref[pl.ds(step, 1), :] = update[:1]
    right_ref[pl.ds(step, 1), :] = update[update.shape[0] - 1 :]

    @pl.when(step == 0)
    def _():
        low_ref[...] = update

    @pl.when(step == pl.num_programs(0) - 1)
    def _():
        high_ref[...] = update


def back_first_body(cells, proj_ref, sums_ref, recv_ref, point_ref, col_ref, deep_ref, kept_ref, *refs):
    *edges, wave_ref = refs
    scale = scale_of(gathered(sums_ref, 0), cells)
    update = back_transform(
        recv_ref, point_ref, proj_ref, col_ref, deep_ref, wave_ref, scale
    )
    kept_ref[0, 0] = update
    put_edges(update, *edges)


def back_next_body(cells, proj_ref, first_ref, sums_ref, recv_ref, point_ref, col_ref, deep_ref, image_ref, _, kept_ref, out_ref, *refs):
    *edges, wave_ref, acc_ref = refs
    _, _, total = next_scalars(first_ref, sums_ref)
    update = back_transform(
        recv_ref, point_ref, proj_ref, col_ref, deep_ref, wave_ref, scale_of(total, cells)
    )
    kept_ref[0, 0] = update
    put_edges(update, *edges)
    line = lane_sums(update * image_ref[0])
    step = pl.program_id(0)

    @pl.when(step == 0)
    def _():
        acc_ref[...] = jnp.zeros_like(acc_ref)

    acc_ref[0:1] += line

    @pl.when(step == pl.num_programs(0) - 1)
    def _():
        spread([acc_ref[0:1]], out_ref)


def stencil(own, before, after, left, right, faces):
    first_lo, first_hi, sec_lo, sec_hi, thi_lo, thi_hi = (ref[0] for ref in faces)
    cols, depth = own.shape
    line = lax.broadcasted_iota(jnp.int32, (cols, depth), 0)
    deep = lax.broadcasted_iota(jnp.int32, (cols, depth), 1)
    total = first_lo * (own - before)
    total = total + first_hi * (own - after)
    other = jnp.where(line == 0, left, pltpu.roll(own, 1, 0))
    total = total + sec_lo * (own - other)
    other = jnp.where(line == cols - 1, right, pltpu.roll(own, cols - 1, 0))
    total = total + sec_hi * (own - other)
    other = jnp.where(deep == 0, 0.0, pltpu.roll(own, 1, 1))
    total = total + thi_lo * (own - other)
    other = jnp.where(deep == depth - 1, 0.0, pltpu.roll(own, depth - 1, 1))
    return total + thi_hi * (own - other)


def add_sums(terms, out_ref, acc_ref):
    step = pl.program_id(0)

    @pl.when(step == 0)
    def _():
        acc_ref[...] = jnp.zeros_like(acc_ref)

    for j, term in enumerate(terms):
        acc_ref[j : j + 1] += lane_sums(term)

    @pl.when(step == pl.num_programs(0) - 1)
    def _():
        spread([acc_ref[j : j + 1] for j in range(len(terms))], out_ref)


def around(ref, index, low, high):
    step = pl.program_id(0)
    last = pl.num_programs(0) - 1
    before = jnp.where(step == 0, low, ref[index, jnp.maximum(step - 1, 0)])
    after = jnp.where(step == last, high, ref[index, jnp.minimum(step + 1, last)])
    return ref[index, step], before, after


def operator_first_body(kept_ref, low_ref, high_ref, left_ref, right_ref, res_ref, *refs):
    *faces, image_ref, out_ref, acc_ref = refs
    line = pl.ds(pl.program_id(0), 1)
    own, before, after = around(kept_ref, 0, low_ref[...], high_ref[...])
    image = stencil(own, before, after, left_ref[line, :], right_ref[line, :], faces)
    residual = res_ref[0]
    image_ref[0] = image
    add_sums((own * image, residual * own, image * image, residual * image), out_ref, acc_ref)


def operator_next_body(first_ref, beta_ref, kept_ref, low_ref, high_ref, left_ref, right_ref, old_low, old_high, old_left, old_right, res_ref, *refs):
    *faces, way_ref, image_ref, out_ref, acc_ref = refs
    line = pl.ds(pl.program_id(0), 1)
    beta = gathered(beta_ref, 0) / gathered(first_ref, 0)
    fields = zip(
        around(kept_ref, 1, low_ref[...], high_ref[...]),
        around(kept_ref, 0, old_low[...], old_high[...]),
    )
    own, before, after = (new - beta * old for new, old in fields)
    left = left_ref[line, :] - beta * old_left[line, :]
    right = right_ref[line, :] - beta * old_right[line, :]
    image = stencil(own, before, after, left, right, faces)
    way_ref[0] = own
    image_ref[0] = image
    add_sums((own * image, res_ref[0] * own), out_ref, acc_ref)


def last_body(first_ref, sums_ref, old_ref, way_ref, res_ref, image_ref, sol_ref, out_ref):
    alpha = gathered(first_ref, 1) / gathered(first_ref, 0)
    later = gathered(sums_ref, 1) / gathered(sums_ref, 0)
    sol_ref[0] = alpha * old_ref[0, 0] + later * way_ref[0]
    out_ref[0] = res_ref[0] - later * image_ref[0]


def exchange(blocks):
    return lax.all_to_all(blocks, BOTH, split_axis=0, concat_axis=0, tiled=True)


def neighbours(low, high, left, right):
    found = []
    for axis, first, last in (("row", low, high), ("col", left, right)):
        forward = [(i, i + 1) for i in range(lax.axis_size(axis) - 1)]
        backward = [(target, source) for source, target in forward]
        found.append(lax.ppermute(last, axis, forward))
        found.append(lax.ppermute(first, axis, backward))
    return found


def tiled_local(right_side, permeability, lift_weight, spectral_weight, mix_weight, proj_weight):
    rows, cols, depth = right_side.shape
    n_row = lax.axis_size("row")
    n_col = lax.axis_size("col")
    count = n_row * n_col
    cells = float(rows * n_row * cols * n_col * depth)
    freq = KX // n_col
    deep_forward, deep_back = (jnp.asarray(t) for t in deep_tables(n_row, depth))
    col_forward, col_back = (jnp.asarray(t) for t in column_tables(n_col, cols))
    lift_weight = lift_weight.T
    field = shape(rows, cols, depth)
    field_bytes = 4 * rows * cols * depth
    partial = shape(count, SUBLANES, LANES)
    spectra = shape(count, rows, SUBLANES, LANES)
    spectra_bytes = 4 * count * rows * SUBLANES * LANES
    smem = whole(pltpu.SMEM)
    vmem = whole()
    plane = pl.BlockSpec((1, cols, depth), lambda i: (i, 0, 0))
    spectra_block = pl.BlockSpec((count, 1, SUBLANES, LANES), lambda i: (0, i, 0, 0))
    point_block = pl.BlockSpec((1, CHANNELS, depth, cols), lambda i: (i, 0, 0, 0))
    kept_shape = shape(ITERS, rows, cols, depth)
    lift_flops = 2.0e9
    back_flops = 2.0e9

    edge_shapes = (shape(cols, depth),) * 2 + (shape(rows, depth),) * 2
    thin = jax.ShapeDtypeStruct((cols, depth), permeability.dtype)
    squares, *edges = call(
        squares_body,
        (partial, thin, thin) + edge_shapes[2:],
        [vmem, vmem],
        (vmem,) * 5,
        moved=field_bytes,
    )(right_side, permeability)
    squares = exchange(squares)

    weights = call(
        weight_body,
        shape(n_col, freq, CHANNELS, SUBLANES, LANES),
        [vmem],
        vmem,
        moved=8 * spectral_weight.size,
    )(spectral_weight)
    weights = lax.all_to_all(weights, "col", split_axis=0, concat_axis=0, tiled=True)
    weights = weights.reshape(KX * CHANNELS * SUBLANES, LANES)
    others = call(
        turn_body,
        shape(*weights.shape),
        [vmem],
        vmem,
        moved=8 * weights.size,
    )(weights)
    weights, others = (
        array.reshape(KX, CHANNELS, SUBLANES, LANES) for array in (weights, others)
    )

    first, *faces = call(
        harmonic_faces,
        (shape(rows + 1, cols, depth),) + (field,) * 4,
        [vmem] * 5,
        (vmem,) * 5,
        moved=6 * field_bytes,
        near=(1, 2, 3, 4),
    )(permeability, *neighbours(*edges))
    faces = [first, first] + faces
    next_plane = pl.BlockSpec((1, cols, depth), lambda i: (i + 1, 0, 0))
    face_specs = [plane, next_plane] + [plane] * 4
    acc_scratch = pltpu.VMEM((SUBLANES, LANES), F32)

    zt_scratch = pltpu.VMEM((2 * KZ * CHANNELS, cols), F32)

    anywhere = whole(pl.ANY)

    def points(scale_of_refs, scalars, residual, part, before, after):
        first = part * rows // 2
        moved_plane = pl.BlockSpec((1, cols, depth), lambda i: (first + i, 0, 0))
        count_in = 4 + len(scalars)
        return call(
            functools.partial(point_body, scale_of_refs),
            shape(rows, CHANNELS, depth, cols),
            [smem, smem]
            + [vmem] * len(scalars)
            + [moved_plane, moved_plane, anywhere, anywhere],
            pl.BlockSpec((1, CHANNELS, depth, cols), lambda i: (first + i, 0, 0, 0)),
            grid=(rows // 2,),
            scratch=[
                pltpu.VMEM((depth, cols), F32),
                pltpu.VMEM((depth, cols), F32),
                pltpu.VMEM((CHANNELS, 4 * SUBLANES, cols), F32),
            ],
            flops=2.5e9,
            moved=9 * field_bytes,
            alias={count_in: 0} if part else None,
            limit=12,
        )(lift_weight, mix_weight, *scalars, residual, permeability, before, after)

    def modes(received, before):
        places = rows * n_row
        tiles = lambda size: pltpu.VMEM((size, SUBLANES, LANES), F32)
        return call(
            functools.partial(modes_body, cells, n_row, n_col),
            spectra,
            [vmem, vmem, vmem, anywhere],
            vmem,
            scratch=[tiles(places), tiles(places), tiles(KX), tiles(KX)],
            moved=2 * spectra_bytes + 8 * weights.size,
            near=(0,),
        )(received, weights, others, before)

    def mixed_modes(blocks, scale_of_refs, scalars, residual):
        received = exchange(blocks)
        point = points(scale_of_refs, scalars, residual, 0, right_side, right_side)
        blocks = modes(received, point)
        received = exchange(blocks)
        point = points(scale_of_refs, scalars, residual, 1, point, blocks)
        return received, point

    blocks = call(
        functools.partial(lift_first_body, cells),
        spectra,
        [smem, vmem, plane, plane, vmem, vmem],
        spectra_block,
        grid=(rows,),
        scratch=[zt_scratch],
        flops=lift_flops,
        moved=2 * field_bytes + spectra_bytes,
    )(lift_weight, squares, right_side, permeability, deep_forward, col_forward)
    received, point = mixed_modes(
        blocks,
        lambda sums_ref: scale_of(gathered(sums_ref, 0), cells),
        (squares,),
        right_side,
    )
    kept, *edges = call(
        functools.partial(back_first_body, cells),
        (kept_shape,) + edge_shapes,
        [smem, vmem, spectra_block, point_block, vmem, vmem],
        (pl.BlockSpec((1, 1, cols, depth), lambda i: (0, i, 0, 0)),) + (vmem,) * 4,
        grid=(rows,),
        scratch=[zt_scratch],
        limit=12,
        flops=back_flops,
        moved=18 * field_bytes,
    )(proj_weight, squares, received, point, col_back, deep_back)

    old_halo = neighbours(*edges)
    args = (kept, *old_halo, right_side, *faces)
    image, sums = call(
        operator_first_body,
        (field, partial),
        [vmem] * 5 + [plane] + face_specs,
        (plane, vmem),
        grid=(rows,),
        scratch=[acc_scratch],
        moved=9 * field_bytes,
        near=(1, 2, 3, 4),
    )(*args)
    sums = exchange(sums)

    blocks, residual = call(
        functools.partial(lift_next_body, cells),
        (spectra, field),
        [smem, vmem, vmem, plane, plane, plane, vmem, vmem],
        (spectra_block, plane),
        grid=(rows,),
        scratch=[zt_scratch],
        flops=lift_flops,
        moved=4 * field_bytes + spectra_bytes,
    )(lift_weight, squares, sums, right_side, image, permeability, deep_forward, col_forward)
    received, point = mixed_modes(
        blocks,
        lambda first_ref, sums_ref: scale_of(next_scalars(first_ref, sums_ref)[2], cells),
        (squares, sums),
        residual,
    )
    kept, beta, *edges = call(
        functools.partial(back_next_body, cells),
        (kept_shape, partial) + edge_shapes,
        [smem, vmem, vmem, spectra_block, point_block, vmem, vmem, plane, whole(pl.ANY)],
        (pl.BlockSpec((1, 1, cols, depth), lambda i: (1, i, 0, 0)),) + (vmem,) * 5,
        grid=(rows,),
        limit=12,
        scratch=[zt_scratch, acc_scratch],
        flops=back_flops,
        moved=19 * field_bytes,
        alias={8: 0},
    )(proj_weight, squares, sums, received, point, col_back, deep_back, image, kept)

    beta = exchange(beta)
    halo = neighbours(*edges)
    args = (sums, beta, kept, *halo, *old_halo, residual, *faces)
    way, image, later = call(
        operator_next_body,
        (field, field, partial),
        [vmem] * 11 + [plane] + face_specs,
        (plane, plane, vmem),
        grid=(rows,),
        scratch=[acc_scratch],
        near=(0, 1, 3, 4, 5, 6, 7, 8, 9, 10),
        moved=11 * field_bytes,
    )(*args)
    later = exchange(later)
    answer, residual = call(
        last_body,
        (field, field),
        [vmem, vmem, pl.BlockSpec((1, 1, cols, depth), lambda i: (0, i, 0, 0)), plane, plane, plane],
        (plane, plane),
        grid=(rows,),
        moved=6 * field_bytes,
    )(sums, later, kept, way, residual, image)
    return (answer, residual, kept)


def fits_tiles(mesh, block):
    rows, cols, depth = block
    n_row, n_col = mesh.shape["row"], mesh.shape["col"]
    return (
        ITERS == 2
        and KZ == n_row * (LANES // (2 * CHANNELS))
        and KY == n_col * SUBLANES
        and KX % n_col == 0
        and cols == LANES
        and depth % LANES == 0
        and rows * n_row >= KX
    )


def solution(mesh):
    placed = (
        P("row", "col", None),
        P("row", "col", None),
        P(),
        P(None, "row", None, None, "col"),
        P(),
        P(),
    )

    def run(right_side, *others):
        rows, cols, depth = right_side.shape
        block = (rows // mesh.shape["row"], cols // mesh.shape["col"], depth)
        return jax.shard_map(
            tiled_local if fits_tiles(mesh, block) else local,
            mesh=mesh,
            in_specs=placed,
            out_specs=(P("row", "col", None), P("row", "col", None), P(None, "row", "col", None)),
            check_vma=False,
        )(right_side, *others)

    return run
```

```python
import functools

import jax
import jax.numpy as jnp
import ml_dtypes
import numpy as np
from jax import lax
from jax.experimental import pallas as pl
from jax.experimental.pallas import tpu as pltpu
from jax.sharding import PartitionSpec as P

CHANNELS = 16
KX = 16
KY = 32
KZ = 32
ITERS = 2


HIGHEST = lax.Precision.HIGHEST


def with_halo(block, sides, width):
    for axis, dim in sides:
        count = lax.axis_size(axis)
        forward = [(i, i + 1) for i in range(count - 1)]
        backward = [(target, source) for source, target in forward]
        low = lax.ppermute(
            lax.slice_in_dim(block, block.shape[dim] - width, None, axis=dim), axis, forward
        )
        high = lax.ppermute(lax.slice_in_dim(block, 0, width, axis=dim), axis, backward)
        block = jnp.concatenate([low, block, high], axis=dim)
    return block


def einsum_high(form, left, right):
    return jnp.einsum(form, left, right, precision=HIGHEST)


def harmonic(first, second):
    return 2.0 * first * second / (first + second)


def wave_table(freqs, places, length):
    turns = freqs[None, :] * places[:, None] % length
    angle = turns.astype(jnp.float32) * (2.0 * jnp.pi / length)
    return (jnp.cos(angle), jnp.sin(angle))


def signed_freqs(count):
    return jnp.arange(count, dtype=jnp.int32) - count // 2


def face_arrays(permeability):
    padded = with_halo(permeability, (("row", 0), ("col", 1)), 1).astype(jnp.float32)
    own = permeability.astype(jnp.float32)
    edged = jnp.pad(own, ((1, 1), (1, 1), (0, 0)), mode="edge")
    padded = jnp.where(padded > 0.0, padded, edged)
    first = harmonic(padded[:-1, 1:-1], padded[1:, 1:-1])
    second = harmonic(padded[1:-1, :-1], padded[1:-1, 1:])
    deep = jnp.pad(own, ((0, 0), (0, 0), (1, 1)), mode="edge")
    third = harmonic(deep[:, :, :-1], deep[:, :, 1:])
    return ((first, second, third), jnp.log(own))


def apply_operator(field, faces):
    first, second, third = faces
    padded = with_halo(field, (("row", 0), ("col", 1)), 1)
    padded = jnp.pad(padded, ((0, 0), (0, 0), (1, 1)))
    total = first[:-1] * (field - padded[:-2, 1:-1, 1:-1])
    total = total + first[1:] * (field - padded[2:, 1:-1, 1:-1])
    total = total + second[:, :-1] * (field - padded[1:-1, :-2, 1:-1])
    total = total + second[:, 1:] * (field - padded[1:-1, 2:, 1:-1])
    total = total + third[:, :, :-1] * (field - padded[1:-1, 1:-1, :-2])
    total = total + third[:, :, 1:] * (field - padded[1:-1, 1:-1, 2:])
    return total


def global_squares(field):
    return lax.psum(jnp.sum(field * field), ("row", "col"))


def mix_modes(real_in, imag_in, spectral_weight, deep_count, freq_count):
    block = spectral_weight.reshape(2, deep_count, CHANNELS, CHANNELS, freq_count, KY)
    real_out = einsum_high("kcfg,kcofg->kofg", real_in, block[0]) - einsum_high(
        "kcfg,kcofg->kofg", imag_in, block[1]
    )
    imag_out = einsum_high("kcfg,kcofg->kofg", imag_in, block[0]) + einsum_high(
        "kcfg,kcofg->kofg", real_in, block[1]
    )
    return (real_out, imag_out)


def spectral_transpose(real_part, imag_part, spectral_weight, grid):
    rows, cols, n_row, n_col, row_id, col_id = grid
    full_rows = rows * n_row
    full_cols = cols * n_col
    cosine_rows, sine_rows = wave_table(
        signed_freqs(KX), jnp.arange(full_rows, dtype=jnp.int32), full_rows
    )
    cosine_cols, sine_cols = wave_table(
        signed_freqs(KY), jnp.arange(full_cols, dtype=jnp.int32), full_cols
    )
    real_part, imag_part = (
        lax.all_to_all(real_part, "row", split_axis=0, concat_axis=1, tiled=True),
        lax.all_to_all(imag_part, "row", split_axis=0, concat_axis=1, tiled=True),
    )
    first_real = einsum_high("qxy,xf->qfy", real_part, cosine_rows) + einsum_high(
        "qxy,xf->qfy", imag_part, sine_rows
    )
    first_imag = einsum_high("qxy,xf->qfy", imag_part, cosine_rows) - einsum_high(
        "qxy,xf->qfy", real_part, sine_rows
    )
    first_real, first_imag = (
        lax.all_to_all(first_real, "col", split_axis=1, concat_axis=2, tiled=True),
        lax.all_to_all(first_imag, "col", split_axis=1, concat_axis=2, tiled=True),
    )
    second_real = einsum_high("qfy,yg->qfg", first_real, cosine_cols) + einsum_high(
        "qfy,yg->qfg", first_imag, sine_cols
    )
    second_imag = einsum_high("qfy,yg->qfg", first_imag, cosine_cols) - einsum_high(
        "qfy,yg->qfg", first_real, sine_cols
    )
    deep_count = KZ // n_row
    freq_count = KX // n_col
    shape_in = (deep_count, CHANNELS, freq_count, KY)
    mixed_real, mixed_imag = mix_modes(
        second_real.reshape(shape_in),
        second_imag.reshape(shape_in),
        spectral_weight,
        deep_count,
        freq_count,
    )
    shape_out = (deep_count * CHANNELS, freq_count, KY)
    mixed_real = mixed_real.reshape(shape_out)
    mixed_imag = mixed_imag.reshape(shape_out)
    back_real = einsum_high("qfg,yg->qfy", mixed_real, cosine_cols) - einsum_high(
        "qfg,yg->qfy", mixed_imag, sine_cols
    )
    back_imag = einsum_high("qfg,yg->qfy", mixed_imag, cosine_cols) + einsum_high(
        "qfg,yg->qfy", mixed_real, sine_cols
    )
    back_real, back_imag = (
        lax.all_to_all(back_real, "col", split_axis=2, concat_axis=1, tiled=True),
        lax.all_to_all(back_imag, "col", split_axis=2, concat_axis=1, tiled=True),
    )
    out_real = einsum_high("qfy,xf->qxy", back_real, cosine_rows) - einsum_high(
        "qfy,xf->qxy", back_imag, sine_rows
    )
    out_imag = einsum_high("qfy,xf->qxy", back_imag, cosine_rows) + einsum_high(
        "qfy,xf->qxy", back_real, sine_rows
    )
    out_real, out_imag = (
        lax.all_to_all(out_real, "row", split_axis=1, concat_axis=0, tiled=True),
        lax.all_to_all(out_imag, "row", split_axis=1, concat_axis=0, tiled=True),
    )
    return (out_real, out_imag)


def precondition(residual, squares_total, log_perm, weights, grid, cells):
    lift_weight, spectral_weight, mix_weight, proj_weight = weights
    rows, cols, depth = residual.shape
    scale = jnp.sqrt(squares_total / cells + 1e-06)
    scaled = residual / scale
    lifted = jax.nn.gelu(
        lift_weight[:, 0, None, None, None] * scaled[None]
        + lift_weight[:, 1, None, None, None] * log_perm[None]
        + lift_weight[:, 2, None, None, None]
    )
    cosine_deep, sine_deep = wave_table(
        jnp.arange(KZ, dtype=jnp.int32), jnp.arange(depth, dtype=jnp.int32), depth
    )
    real_part = einsum_high("cxyz,zk->kcxy", lifted, cosine_deep).reshape(KZ * CHANNELS, rows, cols)
    imag_part = -einsum_high("cxyz,zk->kcxy", lifted, sine_deep).reshape(KZ * CHANNELS, rows, cols)
    out_real, out_imag = spectral_transpose(real_part, imag_part, spectral_weight, grid)
    out_real = out_real.reshape(KZ, CHANNELS, rows, cols)
    out_imag = out_imag.reshape(KZ, CHANNELS, rows, cols)
    spatial = (
        einsum_high("kcxy,zk->cxyz", out_real, cosine_deep)
        - einsum_high("kcxy,zk->cxyz", out_imag, sine_deep)
    ) / cells
    point = (
        einsum_high("oc,cxyz->oxyz", mix_weight[:, :CHANNELS], lifted)
        + mix_weight[:, CHANNELS, None, None, None]
    )
    hidden = jax.nn.gelu(spatial + point)
    return scale * (
        einsum_high("o,oxyz->xyz", proj_weight[:CHANNELS], hidden) + proj_weight[CHANNELS]
    )


def local(right_side, permeability, lift_weight, spectral_weight, mix_weight, proj_weight):
    rows, cols, depth = right_side.shape
    n_row = lax.axis_size("row")
    n_col = lax.axis_size("col")
    grid = (rows, cols, n_row, n_col, lax.axis_index("row"), lax.axis_index("col"))
    cells = float(rows * n_row * cols * n_col * depth)
    faces, log_perm = face_arrays(permeability)
    weights = (lift_weight, spectral_weight, mix_weight, proj_weight)

    def precond(residual, squares_total):
        return precondition(residual, squares_total, log_perm, weights, grid, cells)

    solution = jnp.zeros_like(right_side)
    residual = right_side
    kept = []
    update = precond(residual, global_squares(residual))
    kept.append(update)
    direction = update
    for step in range(ITERS):
        image = apply_operator(direction, faces)
        curvature, along = lax.psum(
            (jnp.sum(direction * image), jnp.sum(residual * direction)), ("row", "col")
        )
        alpha = along / curvature
        solution = solution + alpha * direction
        residual = residual - alpha * image
        if step + 1 < ITERS:
            update = precond(residual, global_squares(residual))
            kept.append(update)
            beta = lax.psum(jnp.sum(update * image), ("row", "col")) / curvature
            direction = update - beta * direction
    return (solution, residual, jnp.stack(kept))


LANES = 128
SUBLANES = 8
BOTH = ("row", "col")
F32 = jnp.float32
BF16 = jnp.bfloat16


def split_table(table):
    high = table.astype(ml_dtypes.bfloat16)
    low = (table - high.astype(np.float64)).astype(ml_dtypes.bfloat16)
    return high, low


def split(value):
    high = value.astype(BF16)
    return high, (value - high.astype(F32)).astype(BF16)


def split_three(value):
    high = value.astype(BF16).astype(F32)
    rest = value - high
    middle = rest.astype(BF16).astype(F32)
    return high, middle, rest - middle


def matmul(left, right):
    return jnp.dot(left, right, preferred_element_type=F32)


def matmul_nt(left, right):
    return lax.dot_general(left, right, (((1,), (1,)), ((), ())), preferred_element_type=F32)


def angles(freqs, places, length):
    turns = np.multiply.outer(freqs, places) % length
    return turns * (2.0 * np.pi / length)


def deep_order(n_row):
    count = KZ // n_row
    order = [
        (part, row * count + place)
        for row in range(n_row)
        for part in range(2)
        for place in range(count)
    ]
    return np.array(order)


def deep_tables(n_row, depth):
    order = deep_order(n_row)
    angle = angles(order[:, 1], np.arange(depth), depth)
    wave = np.where(order[:, :1] == 0, np.cos(angle), -np.sin(angle))
    high, low = split_table(wave)
    return np.concatenate([high, low], 0), np.concatenate([high.T, high.T, high.T, low.T], 1)


def column_tables(n_col, cols):
    freqs = np.arange(KY) - KY // 2
    forward = []
    back = []
    for place in range(n_col):
        angle = angles(freqs, place * cols + np.arange(cols), n_col * cols)
        both = np.concatenate([np.cos(angle), np.sin(angle)], 1)
        high, low = split_table(both)
        forward.append(np.concatenate([high, low], 0))
        both = np.concatenate([np.cos(angle), np.sin(angle)], 0)
        high, low = split_table(both)
        back.append(
            np.concatenate(
                [
                    np.concatenate([high, low], 1),
                    np.concatenate([high, low], 1),
                    np.concatenate([high, np.zeros_like(low)], 1),
                ],
                0,
            )
        )
    return np.stack(forward), np.stack(back)


def gelu(value):
    inner = value * (0.7978845608028654 + 0.035677408136300125 * (value * value))
    return (0.5 * value) * (1.0 + jnp.tanh(inner))


def call(body, outs, in_specs, out_specs, grid=(), scratch=(), flops=0, moved=0, alias=None, limit=8, near=(), loose=False):
    single = not isinstance(outs, tuple)
    outs = (outs,) if single else outs
    out_specs = (out_specs,) if single else out_specs
    run = pl.pallas_call(
        body,
        out_shape=tuple(
            out if loose or out.size <= 2**16 else pltpu.HBM(out.shape, out.dtype) for out in outs
        ),
        grid=grid,
        in_specs=in_specs,
        out_specs=out_specs,
        scratch_shapes=list(scratch),
        input_output_aliases=alias or {},
        compiler_params=pltpu.CompilerParams(vmem_limit_bytes=limit * 1024 * 1024),
        cost_estimate=pl.CostEstimate(
            flops=int(flops), bytes_accessed=int(moved), transcendentals=0
        ),
    )

    def wrapped(*args):
        held = [
            arg
            if place in near or spec.memory_space == pltpu.SMEM
            else pltpu.with_memory_space_constraint(arg, pltpu.HBM)
            for place, (arg, spec) in enumerate(zip(args, in_specs))
        ]
        found = run(*held)
        return found[0] if single else found

    return wrapped


def whole(memory=pltpu.VMEM):
    return pl.BlockSpec(memory_space=memory)


def shape(*dims):
    return jax.ShapeDtypeStruct(dims, F32)


def lane_sums(value):
    folded = jnp.sum(value.reshape(-1, SUBLANES, value.shape[-1]), axis=0)
    folded = sum(
        folded[:, start : start + LANES] for start in range(0, folded.shape[1], LANES)
    )
    return jnp.sum(folded, axis=0, keepdims=True)


def spread(rows, ref):
    rows = rows + [jnp.zeros_like(rows[0])] * (SUBLANES - len(rows))
    ref[...] = jnp.broadcast_to(jnp.concatenate(rows, 0)[None], ref.shape)


def gathered(ref, row):
    total = jnp.sum(ref[...], axis=0)
    return jnp.sum(total[row : row + 1], axis=1, keepdims=True)


def squares_body(field_ref, perm_ref, out_ref, low_ref, high_ref, left_ref, right_ref):
    total = field_ref[0] * field_ref[0]
    for place in range(1, field_ref.shape[0]):
        total = total + field_ref[place] * field_ref[place]
    spread([lane_sums(total)], out_ref)
    rows, cols, _ = perm_ref.shape
    low_ref[...] = perm_ref[0]
    high_ref[...] = perm_ref[rows - 1]
    for place in range(rows):
        plane = perm_ref[place].astype(F32)
        left_ref[place : place + 1, :] = plane[:1]
        right_ref[place : place + 1, :] = plane[cols - 1 :]


def weight_body(weight_ref, out_ref):
    groups, freq, channels, fine, _ = out_ref.shape
    parts, deep, _, outs, modes = weight_ref.shape
    for channel in range(channels):
        block = weight_ref[:, :, channel].reshape(parts * deep * outs, modes)
        block = block.T.reshape(freq, groups, fine, parts * deep * outs)
        for group in range(groups):
            out_ref[group, :, channel] = block[:, group]


def prepare_body(weight_ref, perm_ref, low_ref, high_ref, left_ref, right_ref, other_ref, first_ref, sec_lo, sec_hi, thi_lo, thi_hi):
    other_ref[...] = pltpu.roll(weight_ref[...], LANES // 2, 1)
    rows, cols, depth = perm_ref.shape
    planes = [perm_ref[place].astype(F32) for place in range(rows)]
    line = lax.broadcasted_iota(jnp.int32, (cols, depth), 0)
    deep = lax.broadcasted_iota(jnp.int32, (cols, depth), 1)
    before = low_ref[...].astype(F32)
    after = high_ref[...].astype(F32)
    around = [jnp.where(before > 0.0, before, planes[0])] + planes
    around = around + [jnp.where(after > 0.0, after, planes[-1])]
    for place in range(rows + 1):
        first_ref[place] = harmonic(around[place], around[place + 1])
    for place in range(rows):
        own = planes[place]
        left = left_ref[place : place + 1]
        right = right_ref[place : place + 1]
        left = jnp.where(left > 0.0, left, own[:1])
        right = jnp.where(right > 0.0, right, own[cols - 1 :])
        lower = jnp.where(line == 0, left, pltpu.roll(own, 1, 0))
        upper = jnp.where(line == cols - 1, right, pltpu.roll(own, cols - 1, 0))
        sec_lo[place] = harmonic(own, lower)
        sec_hi[place] = harmonic(own, upper)
        lower = jnp.where(deep == 0, own, pltpu.roll(own, 1, 1))
        upper = jnp.where(deep == depth - 1, own, pltpu.roll(own, depth - 1, 1))
        thi_lo[place] = harmonic(own, lower)
        thi_hi[place] = harmonic(own, upper)


def scale_of(total, cells):
    return jnp.sqrt(total / cells + 1e-06)


def lift_channel(weight_ref, channel, scaled, log_perm):
    return gelu(
        weight_ref[0, channel] * scaled
        + (weight_ref[1, channel] * log_perm + weight_ref[2, channel])
    )


def transform(lift_ref, deep_ref, col_ref, scaled, log_perm, spectra_ref, lifted_ref, zt_ref):
    half = 2 * KZ
    cols = scaled.shape[1]
    for channel in range(0, CHANNELS, 2):
        pair = [lift_channel(lift_ref, channel + j, scaled, log_perm) for j in range(2)]
        for j in range(2):
            lifted_ref[0, channel + j] = pair[j]
        high, low = split(jnp.concatenate(pair, 1))
        part = matmul(deep_ref[...], high)
        part = part[:half] + part[half:] + matmul(deep_ref[:half], low)
        for j in range(2):
            zt_ref[pl.ds(channel + j, half, stride=CHANNELS), :] = part[:, j * cols : (j + 1) * cols]
    groups = half * CHANNELS // LANES
    waves = zt_ref[...].reshape(groups, 2, LANES // 2, cols)
    turned = jnp.concatenate([waves[:, 1:], -waves[:, :1]], 1)
    waves = jnp.concatenate(
        [waves.reshape(groups * LANES, cols), turned.reshape(groups * LANES, cols)], 1
    )
    high, low = split(waves)
    table = col_ref[lax.axis_index("col")]
    part = matmul_nt(table, high)
    part = part[:KY] + part[KY:] + matmul_nt(table[:KY], low)
    n_col = KY // SUBLANES
    for row in range(groups):
        for col in range(n_col):
            spectra_ref[row * n_col + col, 0] = part[
                col * SUBLANES : (col + 1) * SUBLANES, row * LANES : (row + 1) * LANES
            ]


def lift_first_body(cells, lift_ref, sums_ref, res_ref, perm_ref, deep_ref, col_ref, spectra_ref, lifted_ref, zt_ref):
    scale = scale_of(gathered(sums_ref, 0), cells)
    scaled = (res_ref[0] / scale).T
    log_perm = jnp.log(perm_ref[0].astype(F32)).T
    transform(lift_ref, deep_ref, col_ref, scaled, log_perm, spectra_ref, lifted_ref, zt_ref)


def next_scalars(first_ref, sums_ref):
    curvature = gathered(sums_ref, 0)
    alpha = gathered(sums_ref, 1) / curvature
    total = gathered(first_ref, 0) + alpha * (
        alpha * gathered(sums_ref, 2) - 2.0 * gathered(sums_ref, 3)
    )
    return curvature, alpha, jnp.maximum(total, 0.0)


def lift_next_body(cells, lift_ref, first_ref, sums_ref, res_ref, image_ref, perm_ref, deep_ref, col_ref, spectra_ref, lifted_ref, next_ref, zt_ref):
    _, alpha, total = next_scalars(first_ref, sums_ref)
    scale = scale_of(total, cells)
    residual = res_ref[0] - alpha * image_ref[0]
    next_ref[0] = residual
    scaled = (residual / scale).T
    log_perm = jnp.log(perm_ref[0].astype(F32)).T
    transform(lift_ref, deep_ref, col_ref, scaled, log_perm, spectra_ref, lifted_ref, zt_ref)


def point_body(mix_ref, lifted_ref, _, __, point_ref):
    size = 4 * SUBLANES
    group = 4

    def step(index, carry):
        lines = pl.ds(pl.multiple_of(index * size, size), size)
        for first in range(0, CHANNELS, group):
            sums = [mix_ref[first + j, CHANNELS] for j in range(group)]
            for channel in range(CHANNELS):
                lifted = lifted_ref[0, channel, lines, :]
                sums = [
                    total + mix_ref[first + j, channel] * lifted for j, total in enumerate(sums)
                ]
            for j, total in enumerate(sums):
                point_ref[0, first + j, lines, :] = total
        return carry

    lax.fori_loop(0, lifted_ref.shape[2] // size, step, 0)


def modes_body(cells, n_row, n_col, recv_ref, weight_ref, other_ref, _, __, out_ref, field_ref, turned_ref, spec_ref, odd_ref):
    rows = recv_ref.shape[1]
    places = n_row * rows
    tile = (SUBLANES, LANES)
    lane = lax.broadcasted_iota(jnp.int32, tile, 1)
    first = lane < LANES // 2
    sign = jnp.where(first, 1.0, -1.0).astype(F32)
    base = lane - lane % CHANNELS

    def turn(value):
        return pltpu.roll(value, LANES // 2, 1) * sign

    for row in range(n_row):
        for place in range(rows):
            value = recv_ref[row * n_col, place]
            for col in range(1, n_col):
                value = value + recv_ref[row * n_col + col, place]
            field_ref[row * rows + place] = value
    angle = 2.0 * np.pi / places
    half = KX // 2

    def weigh(coefs, ref):
        total = None
        for place, coef in enumerate(coefs):
            coef = float(coef)
            if abs(coef) < 1e-12:
                continue
            term = ref[place]
            if coef == -1.0:
                term = -term
            elif coef != 1.0:
                term = coef * term
            total = term if total is None else total + term
        return jnp.zeros(tile, F32) if total is None else total

    middle = places // 2
    for place in range(1, middle):
        value, mirror = field_ref[place], field_ref[places - place]
        field_ref[place] = value + mirror
        turned_ref[place] = turn(value - mirror)
    for freq in range(half + 1):
        turns = freq * np.arange(middle + 1) % places
        even = weigh(np.cos(angle * turns), field_ref)
        odd = weigh(np.concatenate([[0.0], np.sin(angle * turns[1:middle])]), turned_ref)
        if freq < half:
            spec_ref[half + freq] = even + odd
        if freq > 0:
            spec_ref[half - freq] = even - odd

    def mix(freq, carry):
        value = spec_ref[freq]
        same = [None, None]
        cross = [None, None]
        for channel in range(CHANNELS):
            wide = jnp.take_along_axis(value, base + channel, axis=1)
            for sums, ref in ((same, weight_ref), (cross, other_ref)):
                term = ref[freq, channel] * wide
                kept = sums[channel % 2]
                sums[channel % 2] = term if kept is None else kept + term
        same = same[0] + same[1]
        cross = cross[0] + cross[1]
        total = jnp.where(
            first,
            same - pltpu.roll(same, LANES // 2, 1),
            cross + pltpu.roll(cross, LANES // 2, 1),
        )
        field_ref[freq] = total
        turned_ref[freq] = -turn(total)
        return carry

    lax.fori_loop(0, KX, mix, 0)
    gain = 1.0 / cells
    evens = [field_ref[half] * gain]
    odds = [None]
    for freq in range(1, half):
        evens.append((field_ref[half + freq] + field_ref[half - freq]) * gain)
        odds.append((turned_ref[half + freq] - turned_ref[half - freq]) * gain)
    evens.append(field_ref[0] * gain)
    odds.append(-turned_ref[0] * gain)
    for freq in range(half + 1):
        spec_ref[freq] = evens[freq]
        if freq > 0:
            odd_ref[freq] = odds[freq]

    def store(place, value):
        for col in range(n_col):
            out_ref[(place // rows) * n_col + col, place % rows] = value

    for place in range(places // 2 + 1):
        turns = place * np.arange(half + 1) % places
        even = weigh(np.cos(angle * turns), spec_ref)
        odd = weigh(np.sin(angle * turns), odd_ref)
        store(place, even + odd)
        if 0 < place < places // 2:
            store(places - place, even - odd)


def back_transform(recv_ref, point_ref, proj_ref, col_ref, deep_ref, wave_ref, scale):
    groups = 2 * KZ * CHANNELS // LANES
    n_col = KY // SUBLANES
    cols = col_ref.shape[2] // 2
    lane = lax.broadcasted_iota(jnp.int32, (KY, LANES), 1)
    sign = jnp.where(lane < LANES // 2, -1.0, 1.0).astype(F32)
    half = 2 * KZ
    pieces = []
    for row in range(groups):
        value = recv_ref[row * n_col : (row + 1) * n_col, 0].reshape(KY, LANES)
        turned = pltpu.roll(value, LANES // 2, 1) * sign
        both = jnp.concatenate([value, turned], 0)
        pieces.append(jnp.concatenate(split_three(both), 0).T.astype(BF16))
    part = matmul(jnp.concatenate(pieces, 0), col_ref[lax.axis_index("col")])
    wave_ref[...] = part[:, :cols] + part[:, cols:]
    total = None
    for out in range(0, CHANNELS, 2):
        waves = jnp.concatenate(
            [wave_ref[pl.ds(out + j, half, stride=CHANNELS), :] for j in range(2)], 1
        )
        high, middle, low = (part.astype(BF16) for part in split_three(waves))
        spatial = matmul(deep_ref[...], jnp.concatenate([high, middle, low, high], 0))
        for j in range(2):
            hidden = gelu(spatial[:, j * cols : (j + 1) * cols] + point_ref[0, out + j])
            term = proj_ref[out + j] * hidden
            total = term if total is None else total + term
    return (scale * (total + proj_ref[CHANNELS])).T


def put_edges(update, low_ref, high_ref, left_ref, right_ref):
    step = pl.program_id(0)
    left_ref[pl.ds(step, 1), :] = update[:1]
    right_ref[pl.ds(step, 1), :] = update[update.shape[0] - 1 :]

    @pl.when(step == 0)
    def _():
        low_ref[...] = update

    @pl.when(step == pl.num_programs(0) - 1)
    def _():
        high_ref[...] = update


def back_first_body(cells, proj_ref, sums_ref, recv_ref, point_ref, col_ref, deep_ref, kept_ref, *refs):
    *edges, wave_ref = refs
    scale = scale_of(gathered(sums_ref, 0), cells)
    update = back_transform(
        recv_ref, point_ref, proj_ref, col_ref, deep_ref, wave_ref, scale
    )
    kept_ref[0, 0] = update
    put_edges(update, *edges)


def back_next_body(cells, proj_ref, first_ref, sums_ref, recv_ref, point_ref, col_ref, deep_ref, image_ref, _, kept_ref, out_ref, *refs):
    *edges, wave_ref, acc_ref = refs
    _, _, total = next_scalars(first_ref, sums_ref)
    update = back_transform(
        recv_ref, point_ref, proj_ref, col_ref, deep_ref, wave_ref, scale_of(total, cells)
    )
    kept_ref[0, 0] = update
    put_edges(update, *edges)
    line = lane_sums(update * image_ref[0])
    step = pl.program_id(0)

    @pl.when(step == 0)
    def _():
        acc_ref[...] = jnp.zeros_like(acc_ref)

    acc_ref[0:1] += line

    @pl.when(step == pl.num_programs(0) - 1)
    def _():
        spread([acc_ref[0:1]], out_ref)


def stencil(own, before, after, left, right, faces):
    first_lo, first_hi, sec_lo, sec_hi, thi_lo, thi_hi = (ref[0] for ref in faces)
    cols, depth = own.shape
    line = lax.broadcasted_iota(jnp.int32, (cols, depth), 0)
    deep = lax.broadcasted_iota(jnp.int32, (cols, depth), 1)
    total = first_lo * (own - before)
    total = total + first_hi * (own - after)
    other = jnp.where(line == 0, left, pltpu.roll(own, 1, 0))
    total = total + sec_lo * (own - other)
    other = jnp.where(line == cols - 1, right, pltpu.roll(own, cols - 1, 0))
    total = total + sec_hi * (own - other)
    other = jnp.where(deep == 0, 0.0, pltpu.roll(own, 1, 1))
    total = total + thi_lo * (own - other)
    other = jnp.where(deep == depth - 1, 0.0, pltpu.roll(own, depth - 1, 1))
    return total + thi_hi * (own - other)


def add_sums(terms, out_ref, acc_ref):
    step = pl.program_id(0)

    @pl.when(step == 0)
    def _():
        acc_ref[...] = jnp.zeros_like(acc_ref)

    for j, term in enumerate(terms):
        acc_ref[j : j + 1] += lane_sums(term)

    @pl.when(step == pl.num_programs(0) - 1)
    def _():
        spread([acc_ref[j : j + 1] for j in range(len(terms))], out_ref)


def around(ref, index, low, high):
    step = pl.program_id(0)
    last = pl.num_programs(0) - 1
    before = jnp.where(step == 0, low, ref[index, jnp.maximum(step - 1, 0)])
    after = jnp.where(step == last, high, ref[index, jnp.minimum(step + 1, last)])
    return ref[index, step], before, after


def operator_first_body(kept_ref, low_ref, high_ref, left_ref, right_ref, res_ref, *refs):
    *faces, image_ref, out_ref, acc_ref = refs
    line = pl.ds(pl.program_id(0), 1)
    own, before, after = around(kept_ref, 0, low_ref[...], high_ref[...])
    image = stencil(own, before, after, left_ref[line, :], right_ref[line, :], faces)
    residual = res_ref[0]
    image_ref[0] = image
    add_sums((own * image, residual * own, image * image, residual * image), out_ref, acc_ref)


def operator_next_body(first_ref, beta_ref, kept_ref, low_ref, high_ref, left_ref, right_ref, old_low, old_high, old_left, old_right, res_ref, *refs):
    *faces, way_ref, image_ref, out_ref, acc_ref = refs
    line = pl.ds(pl.program_id(0), 1)
    beta = gathered(beta_ref, 0) / gathered(first_ref, 0)
    fields = zip(
        around(kept_ref, 1, low_ref[...], high_ref[...]),
        around(kept_ref, 0, old_low[...], old_high[...]),
    )
    own, before, after = (new - beta * old for new, old in fields)
    left = left_ref[line, :] - beta * old_left[line, :]
    right = right_ref[line, :] - beta * old_right[line, :]
    image = stencil(own, before, after, left, right, faces)
    way_ref[0] = own
    image_ref[0] = image
    add_sums((own * image, res_ref[0] * own), out_ref, acc_ref)


def last_body(first_ref, sums_ref, old_ref, way_ref, res_ref, image_ref, sol_ref, out_ref):
    alpha = gathered(first_ref, 1) / gathered(first_ref, 0)
    later = gathered(sums_ref, 1) / gathered(sums_ref, 0)
    sol_ref[0] = alpha * old_ref[0, 0] + later * way_ref[0]
    out_ref[0] = res_ref[0] - later * image_ref[0]


def exchange(blocks):
    return lax.all_to_all(blocks, BOTH, split_axis=0, concat_axis=0, tiled=True)


def total_body(in_ref, out_ref):
    out_ref[...] = jnp.broadcast_to(jnp.sum(in_ref[...], axis=0)[None], out_ref.shape)


def add_up(partial):
    found = lax.all_to_all(partial, "row", split_axis=0, concat_axis=0, tiled=True)
    found = call(
        total_body,
        shape(lax.axis_size("col"), SUBLANES, LANES),
        [whole()],
        whole(),
        near=(0,),
    )(found)
    return lax.all_to_all(found, "col", split_axis=0, concat_axis=0, tiled=True)


def neighbours(low, high, left, right):
    found = []
    for axis, first, last in (("row", low, high), ("col", left, right)):
        forward = [(i, i + 1) for i in range(lax.axis_size(axis) - 1)]
        backward = [(target, source) for source, target in forward]
        found.append(lax.ppermute(last, axis, forward))
        found.append(lax.ppermute(first, axis, backward))
    return found


def tiled_local(right_side, permeability, lift_weight, spectral_weight, mix_weight, proj_weight):
    rows, cols, depth = right_side.shape
    n_row = lax.axis_size("row")
    n_col = lax.axis_size("col")
    count = n_row * n_col
    cells = float(rows * n_row * cols * n_col * depth)
    freq = KX // n_col
    deep_forward, deep_back = (jnp.asarray(t) for t in deep_tables(n_row, depth))
    col_forward, col_back = (jnp.asarray(t) for t in column_tables(n_col, cols))
    lift_weight = lift_weight.T
    field = shape(rows, cols, depth)
    field_bytes = 4 * rows * cols * depth
    partial = shape(n_row, SUBLANES, LANES)
    channels = shape(rows, CHANNELS, depth, cols)
    spectra = shape(count, rows, SUBLANES, LANES)
    spectra_bytes = 4 * count * rows * SUBLANES * LANES
    smem = whole(pltpu.SMEM)
    vmem = whole()
    plane = pl.BlockSpec((1, cols, depth), lambda i: (i, 0, 0))
    spectra_block = pl.BlockSpec((count, 1, SUBLANES, LANES), lambda i: (0, i, 0, 0))
    point_block = pl.BlockSpec((1, CHANNELS, depth, cols), lambda i: (i, 0, 0, 0))
    kept_shape = shape(ITERS, rows, cols, depth)
    lift_flops = 2.0e9
    back_flops = 2.0e9

    edge_shapes = (shape(cols, depth),) * 2 + (shape(rows, depth),) * 2
    thin = jax.ShapeDtypeStruct((cols, depth), permeability.dtype)
    squares, *edges = call(
        squares_body,
        (partial, thin, thin) + edge_shapes[2:],
        [vmem, vmem],
        (vmem,) * 5,
        moved=field_bytes,
    )(right_side, permeability)
    squares = add_up(squares)

    weights = call(
        weight_body,
        shape(n_col, freq, CHANNELS, SUBLANES, LANES),
        [vmem],
        vmem,
        moved=8 * spectral_weight.size,
    )(spectral_weight)
    weights = lax.all_to_all(weights, "col", split_axis=0, concat_axis=0, tiled=True)
    weights = weights.reshape(KX * CHANNELS * SUBLANES, LANES)
    others, first, *faces = call(
        prepare_body,
        (shape(*weights.shape), shape(rows + 1, cols, depth)) + (field,) * 4,
        [vmem] * 6,
        (vmem,) * 6,
        moved=10 * field_bytes,
        near=(0, 2, 3, 4, 5),
        limit=12,
    )(weights, permeability, *neighbours(*edges))
    weights, others = (
        array.reshape(KX, CHANNELS, SUBLANES, LANES) for array in (weights, others)
    )
    faces = [first, first] + faces
    next_plane = pl.BlockSpec((1, cols, depth), lambda i: (i + 1, 0, 0))
    face_specs = [plane, next_plane] + [plane] * 4
    acc_scratch = pltpu.VMEM((SUBLANES, LANES), F32)

    zt_scratch = pltpu.VMEM((2 * KZ * CHANNELS, cols), F32)

    anywhere = whole(pl.ANY)

    def points(lifted, part, before, after):
        first = part * rows // 2
        half_block = pl.BlockSpec((1, CHANNELS, depth, cols), lambda i: (first + i, 0, 0, 0))
        return call(
            point_body,
            channels,
            [smem, half_block, anywhere, anywhere],
            half_block,
            grid=(rows // 2,),
            flops=2.5e9,
            moved=16 * field_bytes,
            alias={2: 0} if part else None,
            limit=12,
        )(mix_weight, lifted, before, after)

    def modes(received, before):
        places = rows * n_row
        tiles = lambda size: pltpu.VMEM((size, SUBLANES, LANES), F32)
        return call(
            functools.partial(modes_body, cells, n_row, n_col),
            spectra,
            [vmem, vmem, vmem, anywhere, anywhere],
            vmem,
            scratch=[tiles(places), tiles(places), tiles(KX), tiles(KX)],
            moved=2 * spectra_bytes + 8 * weights.size,
            near=(0,),
        )(received, weights, others, before, faces[0])

    def mixed_modes(blocks, lifted):
        received = exchange(blocks)
        point = points(lifted, 0, right_side, right_side)
        blocks = modes(received, point)
        received = exchange(blocks)
        point = points(lifted, 1, point, blocks)
        return received, point

    blocks, lifted = call(
        functools.partial(lift_first_body, cells),
        (spectra, channels),
        [smem, vmem, plane, plane, vmem, vmem],
        (spectra_block, point_block),
        limit=16,
        grid=(rows,),
        scratch=[zt_scratch],
        flops=lift_flops,
        moved=2 * field_bytes + spectra_bytes,
    )(lift_weight, squares, right_side, permeability, deep_forward, col_forward)
    received, point = mixed_modes(blocks, lifted)
    kept, *edges = call(
        functools.partial(back_first_body, cells),
        (kept_shape,) + edge_shapes,
        [smem, vmem, spectra_block, point_block, vmem, vmem],
        (pl.BlockSpec((1, 1, cols, depth), lambda i: (0, i, 0, 0)),) + (vmem,) * 4,
        grid=(rows,),
        scratch=[zt_scratch],
        limit=12,
        flops=back_flops,
        moved=18 * field_bytes,
    )(proj_weight, squares, received, point, col_back, deep_back)

    old_halo = neighbours(*edges)
    args = (kept, *old_halo, right_side, *faces)
    image, sums = call(
        operator_first_body,
        (field, partial),
        [vmem] * 5 + [plane] + face_specs,
        (plane, vmem),
        grid=(rows,),
        scratch=[acc_scratch],
        moved=9 * field_bytes,
        near=range(12),
        loose=True,
    )(*args)
    sums = add_up(sums)

    blocks, lifted, residual = call(
        functools.partial(lift_next_body, cells),
        (spectra, channels, field),
        [smem, vmem, vmem, plane, plane, plane, vmem, vmem],
        (spectra_block, point_block, plane),
        limit=16,
        near=(4,),
        grid=(rows,),
        scratch=[zt_scratch],
        flops=lift_flops,
        moved=4 * field_bytes + spectra_bytes,
    )(lift_weight, squares, sums, right_side, image, permeability, deep_forward, col_forward)
    received, point = mixed_modes(blocks, lifted)
    kept, beta, *edges = call(
        functools.partial(back_next_body, cells),
        (kept_shape, partial) + edge_shapes,
        [smem, vmem, vmem, spectra_block, point_block, vmem, vmem, plane, whole(pl.ANY)],
        (pl.BlockSpec((1, 1, cols, depth), lambda i: (1, i, 0, 0)),) + (vmem,) * 5,
        grid=(rows,),
        limit=12,
        scratch=[zt_scratch, acc_scratch],
        flops=back_flops,
        moved=19 * field_bytes,
        alias={8: 0},
    )(proj_weight, squares, sums, received, point, col_back, deep_back, image, kept)

    beta = add_up(beta)
    halo = neighbours(*edges)
    args = (sums, beta, kept, *halo, *old_halo, residual, *faces)
    way, image, later = call(
        operator_next_body,
        (field, field, partial),
        [vmem] * 11 + [plane] + face_specs,
        (plane, plane, vmem),
        grid=(rows,),
        scratch=[acc_scratch],
        near=range(18),
        loose=True,
        moved=11 * field_bytes,
    )(*args)
    later = add_up(later)
    answer, residual = call(
        last_body,
        (field, field),
        [vmem, vmem, pl.BlockSpec((1, 1, cols, depth), lambda i: (0, i, 0, 0)), plane, plane, plane],
        (plane, plane),
        grid=(rows,),
        moved=6 * field_bytes,
        near=range(6),
        loose=True,
    )(sums, later, kept, way, residual, image)
    return (answer, residual, kept)


def fits_tiles(mesh, block):
    rows, cols, depth = block
    n_row, n_col = mesh.shape["row"], mesh.shape["col"]
    return (
        ITERS == 2
        and KZ == n_row * (LANES // (2 * CHANNELS))
        and KY == n_col * SUBLANES
        and KX % n_col == 0
        and cols == LANES
        and depth % LANES == 0
        and rows * n_row >= KX
    )


def solution(mesh):
    placed = (
        P("row", "col", None),
        P("row", "col", None),
        P(),
        P(None, "row", None, None, "col"),
        P(),
        P(),
    )

    def run(right_side, *others):
        rows, cols, depth = right_side.shape
        block = (rows // mesh.shape["row"], cols // mesh.shape["col"], depth)
        return jax.shard_map(
            tiled_local if fits_tiles(mesh, block) else local,
            mesh=mesh,
            in_specs=placed,
            out_specs=(P("row", "col", None), P("row", "col", None), P(None, "row", "col", None)),
            check_vma=False,
        )(right_side, *others)

    return run
```

```python
import functools

import jax
import jax.numpy as jnp
import ml_dtypes
import numpy as np
from jax import lax
from jax.experimental import pallas as pl
from jax.experimental.pallas import tpu as pltpu
from jax.sharding import PartitionSpec as P

CHANNELS = 16
KX = 16
KY = 32
KZ = 32
ITERS = 2


HIGHEST = lax.Precision.HIGHEST


def with_halo(block, sides, width):
    for axis, dim in sides:
        count = lax.axis_size(axis)
        forward = [(i, i + 1) for i in range(count - 1)]
        backward = [(target, source) for source, target in forward]
        low = lax.ppermute(
            lax.slice_in_dim(block, block.shape[dim] - width, None, axis=dim), axis, forward
        )
        high = lax.ppermute(lax.slice_in_dim(block, 0, width, axis=dim), axis, backward)
        block = jnp.concatenate([low, block, high], axis=dim)
    return block


def einsum_high(form, left, right):
    return jnp.einsum(form, left, right, precision=HIGHEST)


def harmonic(first, second):
    return 2.0 * first * second / (first + second)


def wave_table(freqs, places, length):
    turns = freqs[None, :] * places[:, None] % length
    angle = turns.astype(jnp.float32) * (2.0 * jnp.pi / length)
    return (jnp.cos(angle), jnp.sin(angle))


def signed_freqs(count):
    return jnp.arange(count, dtype=jnp.int32) - count // 2


def face_arrays(permeability):
    padded = with_halo(permeability, (("row", 0), ("col", 1)), 1).astype(jnp.float32)
    own = permeability.astype(jnp.float32)
    edged = jnp.pad(own, ((1, 1), (1, 1), (0, 0)), mode="edge")
    padded = jnp.where(padded > 0.0, padded, edged)
    first = harmonic(padded[:-1, 1:-1], padded[1:, 1:-1])
    second = harmonic(padded[1:-1, :-1], padded[1:-1, 1:])
    deep = jnp.pad(own, ((0, 0), (0, 0), (1, 1)), mode="edge")
    third = harmonic(deep[:, :, :-1], deep[:, :, 1:])
    return ((first, second, third), jnp.log(own))


def apply_operator(field, faces):
    first, second, third = faces
    padded = with_halo(field, (("row", 0), ("col", 1)), 1)
    padded = jnp.pad(padded, ((0, 0), (0, 0), (1, 1)))
    total = first[:-1] * (field - padded[:-2, 1:-1, 1:-1])
    total = total + first[1:] * (field - padded[2:, 1:-1, 1:-1])
    total = total + second[:, :-1] * (field - padded[1:-1, :-2, 1:-1])
    total = total + second[:, 1:] * (field - padded[1:-1, 2:, 1:-1])
    total = total + third[:, :, :-1] * (field - padded[1:-1, 1:-1, :-2])
    total = total + third[:, :, 1:] * (field - padded[1:-1, 1:-1, 2:])
    return total


def global_squares(field):
    return lax.psum(jnp.sum(field * field), ("row", "col"))


def mix_modes(real_in, imag_in, spectral_weight, deep_count, freq_count):
    block = spectral_weight.reshape(2, deep_count, CHANNELS, CHANNELS, freq_count, KY)
    real_out = einsum_high("kcfg,kcofg->kofg", real_in, block[0]) - einsum_high(
        "kcfg,kcofg->kofg", imag_in, block[1]
    )
    imag_out = einsum_high("kcfg,kcofg->kofg", imag_in, block[0]) + einsum_high(
        "kcfg,kcofg->kofg", real_in, block[1]
    )
    return (real_out, imag_out)


def spectral_transpose(real_part, imag_part, spectral_weight, grid):
    rows, cols, n_row, n_col, row_id, col_id = grid
    full_rows = rows * n_row
    full_cols = cols * n_col
    cosine_rows, sine_rows = wave_table(
        signed_freqs(KX), jnp.arange(full_rows, dtype=jnp.int32), full_rows
    )
    cosine_cols, sine_cols = wave_table(
        signed_freqs(KY), jnp.arange(full_cols, dtype=jnp.int32), full_cols
    )
    real_part, imag_part = (
        lax.all_to_all(real_part, "row", split_axis=0, concat_axis=1, tiled=True),
        lax.all_to_all(imag_part, "row", split_axis=0, concat_axis=1, tiled=True),
    )
    first_real = einsum_high("qxy,xf->qfy", real_part, cosine_rows) + einsum_high(
        "qxy,xf->qfy", imag_part, sine_rows
    )
    first_imag = einsum_high("qxy,xf->qfy", imag_part, cosine_rows) - einsum_high(
        "qxy,xf->qfy", real_part, sine_rows
    )
    first_real, first_imag = (
        lax.all_to_all(first_real, "col", split_axis=1, concat_axis=2, tiled=True),
        lax.all_to_all(first_imag, "col", split_axis=1, concat_axis=2, tiled=True),
    )
    second_real = einsum_high("qfy,yg->qfg", first_real, cosine_cols) + einsum_high(
        "qfy,yg->qfg", first_imag, sine_cols
    )
    second_imag = einsum_high("qfy,yg->qfg", first_imag, cosine_cols) - einsum_high(
        "qfy,yg->qfg", first_real, sine_cols
    )
    deep_count = KZ // n_row
    freq_count = KX // n_col
    shape_in = (deep_count, CHANNELS, freq_count, KY)
    mixed_real, mixed_imag = mix_modes(
        second_real.reshape(shape_in),
        second_imag.reshape(shape_in),
        spectral_weight,
        deep_count,
        freq_count,
    )
    shape_out = (deep_count * CHANNELS, freq_count, KY)
    mixed_real = mixed_real.reshape(shape_out)
    mixed_imag = mixed_imag.reshape(shape_out)
    back_real = einsum_high("qfg,yg->qfy", mixed_real, cosine_cols) - einsum_high(
        "qfg,yg->qfy", mixed_imag, sine_cols
    )
    back_imag = einsum_high("qfg,yg->qfy", mixed_imag, cosine_cols) + einsum_high(
        "qfg,yg->qfy", mixed_real, sine_cols
    )
    back_real, back_imag = (
        lax.all_to_all(back_real, "col", split_axis=2, concat_axis=1, tiled=True),
        lax.all_to_all(back_imag, "col", split_axis=2, concat_axis=1, tiled=True),
    )
    out_real = einsum_high("qfy,xf->qxy", back_real, cosine_rows) - einsum_high(
        "qfy,xf->qxy", back_imag, sine_rows
    )
    out_imag = einsum_high("qfy,xf->qxy", back_imag, cosine_rows) + einsum_high(
        "qfy,xf->qxy", back_real, sine_rows
    )
    out_real, out_imag = (
        lax.all_to_all(out_real, "row", split_axis=1, concat_axis=0, tiled=True),
        lax.all_to_all(out_imag, "row", split_axis=1, concat_axis=0, tiled=True),
    )
    return (out_real, out_imag)


def precondition(residual, squares_total, log_perm, weights, grid, cells):
    lift_weight, spectral_weight, mix_weight, proj_weight = weights
    rows, cols, depth = residual.shape
    scale = jnp.sqrt(squares_total / cells + 1e-06)
    scaled = residual / scale
    lifted = jax.nn.gelu(
        lift_weight[:, 0, None, None, None] * scaled[None]
        + lift_weight[:, 1, None, None, None] * log_perm[None]
        + lift_weight[:, 2, None, None, None]
    )
    cosine_deep, sine_deep = wave_table(
        jnp.arange(KZ, dtype=jnp.int32), jnp.arange(depth, dtype=jnp.int32), depth
    )
    real_part = einsum_high("cxyz,zk->kcxy", lifted, cosine_deep).reshape(KZ * CHANNELS, rows, cols)
    imag_part = -einsum_high("cxyz,zk->kcxy", lifted, sine_deep).reshape(KZ * CHANNELS, rows, cols)
    out_real, out_imag = spectral_transpose(real_part, imag_part, spectral_weight, grid)
    out_real = out_real.reshape(KZ, CHANNELS, rows, cols)
    out_imag = out_imag.reshape(KZ, CHANNELS, rows, cols)
    spatial = (
        einsum_high("kcxy,zk->cxyz", out_real, cosine_deep)
        - einsum_high("kcxy,zk->cxyz", out_imag, sine_deep)
    ) / cells
    point = (
        einsum_high("oc,cxyz->oxyz", mix_weight[:, :CHANNELS], lifted)
        + mix_weight[:, CHANNELS, None, None, None]
    )
    hidden = jax.nn.gelu(spatial + point)
    return scale * (
        einsum_high("o,oxyz->xyz", proj_weight[:CHANNELS], hidden) + proj_weight[CHANNELS]
    )


def local(right_side, permeability, lift_weight, spectral_weight, mix_weight, proj_weight):
    rows, cols, depth = right_side.shape
    n_row = lax.axis_size("row")
    n_col = lax.axis_size("col")
    grid = (rows, cols, n_row, n_col, lax.axis_index("row"), lax.axis_index("col"))
    cells = float(rows * n_row * cols * n_col * depth)
    faces, log_perm = face_arrays(permeability)
    weights = (lift_weight, spectral_weight, mix_weight, proj_weight)

    def precond(residual, squares_total):
        return precondition(residual, squares_total, log_perm, weights, grid, cells)

    solution = jnp.zeros_like(right_side)
    residual = right_side
    kept = []
    update = precond(residual, global_squares(residual))
    kept.append(update)
    direction = update
    for step in range(ITERS):
        image = apply_operator(direction, faces)
        curvature, along = lax.psum(
            (jnp.sum(direction * image), jnp.sum(residual * direction)), ("row", "col")
        )
        alpha = along / curvature
        solution = solution + alpha * direction
        residual = residual - alpha * image
        if step + 1 < ITERS:
            update = precond(residual, global_squares(residual))
            kept.append(update)
            beta = lax.psum(jnp.sum(update * image), ("row", "col")) / curvature
            direction = update - beta * direction
    return (solution, residual, jnp.stack(kept))


LANES = 128
SUBLANES = 8
BOTH = ("row", "col")
F32 = jnp.float32
BF16 = jnp.bfloat16


def split_table(table):
    high = table.astype(ml_dtypes.bfloat16)
    low = (table - high.astype(np.float64)).astype(ml_dtypes.bfloat16)
    return high, low


def split(value):
    high = value.astype(BF16)
    return high, (value - high.astype(F32)).astype(BF16)


def split_three(value):
    high = value.astype(BF16).astype(F32)
    rest = value - high
    middle = rest.astype(BF16).astype(F32)
    return high, middle, rest - middle


def matmul(left, right):
    return jnp.dot(left, right, preferred_element_type=F32)


def matmul_nt(left, right):
    return lax.dot_general(left, right, (((1,), (1,)), ((), ())), preferred_element_type=F32)


def angles(freqs, places, length):
    turns = np.multiply.outer(freqs, places) % length
    return turns * (2.0 * np.pi / length)


def deep_order(n_row):
    count = KZ // n_row
    order = [
        (part, row * count + place)
        for row in range(n_row)
        for part in range(2)
        for place in range(count)
    ]
    return np.array(order)


def deep_tables(n_row, depth):
    order = deep_order(n_row)
    angle = angles(order[:, 1], np.arange(depth), depth)
    wave = np.where(order[:, :1] == 0, np.cos(angle), -np.sin(angle))
    high, low = split_table(wave)
    return np.concatenate([high, low], 0), np.concatenate([high.T, high.T, high.T, low.T], 1)


def column_tables(n_col, cols):
    freqs = np.arange(KY) - KY // 2
    forward = []
    back = []
    for place in range(n_col):
        angle = angles(freqs, place * cols + np.arange(cols), n_col * cols)
        both = np.concatenate([np.cos(angle), np.sin(angle)], 1)
        high, low = split_table(both)
        forward.append(np.concatenate([high, low], 0))
        both = np.concatenate([np.cos(angle), np.sin(angle)], 0)
        high, low = split_table(both)
        back.append(
            np.concatenate(
                [
                    np.concatenate([high, low], 1),
                    np.concatenate([high, low], 1),
                    np.concatenate([high, np.zeros_like(low)], 1),
                ],
                0,
            )
        )
    return np.stack(forward), np.stack(back)


def gelu(value):
    inner = value * (0.7978845608028654 + 0.035677408136300125 * (value * value))
    return (0.5 * value) * (1.0 + jnp.tanh(inner))


def call(body, outs, in_specs, out_specs, grid=(), scratch=(), flops=0, moved=0, alias=None, limit=8, near=(), loose=False):
    single = not isinstance(outs, tuple)
    outs = (outs,) if single else outs
    out_specs = (out_specs,) if single else out_specs
    run = pl.pallas_call(
        body,
        out_shape=tuple(
            out if loose or out.size <= 2**16 else pltpu.HBM(out.shape, out.dtype) for out in outs
        ),
        grid=grid,
        in_specs=in_specs,
        out_specs=out_specs,
        scratch_shapes=list(scratch),
        input_output_aliases=alias or {},
        compiler_params=pltpu.CompilerParams(vmem_limit_bytes=limit * 1024 * 1024),
        cost_estimate=pl.CostEstimate(
            flops=int(flops), bytes_accessed=int(moved), transcendentals=0
        ),
    )

    def wrapped(*args):
        held = [
            arg
            if place in near or spec.memory_space == pltpu.SMEM
            else pltpu.with_memory_space_constraint(arg, pltpu.HBM)
            for place, (arg, spec) in enumerate(zip(args, in_specs))
        ]
        found = run(*held)
        return found[0] if single else found

    return wrapped


def whole(memory=pltpu.VMEM):
    return pl.BlockSpec(memory_space=memory)


def shape(*dims):
    return jax.ShapeDtypeStruct(dims, F32)


def lane_sums(value):
    folded = jnp.sum(value.reshape(-1, SUBLANES, value.shape[-1]), axis=0)
    folded = sum(
        folded[:, start : start + LANES] for start in range(0, folded.shape[1], LANES)
    )
    return jnp.sum(folded, axis=0, keepdims=True)


def spread(rows, ref):
    rows = rows + [jnp.zeros_like(rows[0])] * (SUBLANES - len(rows))
    ref[...] = jnp.broadcast_to(jnp.concatenate(rows, 0)[None], ref.shape)


def gathered(ref, row):
    total = jnp.sum(ref[...], axis=0)
    return jnp.sum(total[row : row + 1], axis=1, keepdims=True)


def squares_body(field_ref, out_ref):
    total = field_ref[0] * field_ref[0]
    for place in range(1, field_ref.shape[0]):
        total = total + field_ref[place] * field_ref[place]
    spread([lane_sums(total)], out_ref)


def weight_body(weight_ref, *refs):
    *out_refs, hold_ref = refs
    groups, freq, channels, fine, _ = hold_ref.shape
    parts, deep, _, outs, modes = weight_ref.shape
    for channel in range(channels):
        block = weight_ref[:, :, channel].reshape(parts * deep * outs, modes)
        block = block.T.reshape(freq, groups, fine, parts * deep * outs)
        for group in range(groups):
            hold_ref[group, :, channel] = block[:, group]
    place = lax.axis_index("col")
    for shift, out_ref in enumerate(out_refs):
        out_ref[...] = hold_ref[lax.rem(place + shift, groups)]


def scale_of(total, cells):
    return jnp.sqrt(total / cells + 1e-06)


def lift_channel(weight_ref, channel, scaled, log_perm):
    return gelu(
        weight_ref[0, channel] * scaled
        + (weight_ref[1, channel] * log_perm + weight_ref[2, channel])
    )


def transform(lift_ref, deep_ref, col_ref, scaled, log_perm, spectra_ref, lifted_ref, zt_ref):
    half = 2 * KZ
    cols = scaled.shape[1]
    for channel in range(0, CHANNELS, 2):
        pair = [lift_channel(lift_ref, channel + j, scaled, log_perm) for j in range(2)]
        for j in range(2):
            lifted_ref[0, channel + j] = pair[j]
        high, low = split(jnp.concatenate(pair, 1))
        part = matmul(deep_ref[...], high)
        part = part[:half] + part[half:] + matmul(deep_ref[:half], low)
        for j in range(2):
            zt_ref[pl.ds(channel + j, half, stride=CHANNELS), :] = part[:, j * cols : (j + 1) * cols]
    groups = half * CHANNELS // LANES
    waves = zt_ref[...].reshape(groups, 2, LANES // 2, cols)
    turned = jnp.concatenate([waves[:, 1:], -waves[:, :1]], 1)
    waves = jnp.concatenate(
        [waves.reshape(groups * LANES, cols), turned.reshape(groups * LANES, cols)], 1
    )
    high, low = split(waves)
    table = col_ref[lax.axis_index("col")]
    part = matmul_nt(table, high)
    part = part[:KY] + part[KY:] + matmul_nt(table[:KY], low)
    n_col = KY // SUBLANES
    for row in range(groups):
        for col in range(n_col):
            spectra_ref[row * n_col + col, 0] = part[
                col * SUBLANES : (col + 1) * SUBLANES, row * LANES : (row + 1) * LANES
            ]


def lift_first_body(cells, lift_ref, sums_ref, res_ref, perm_ref, deep_ref, col_ref, _, spectra_ref, lifted_ref, zt_ref):
    scale = scale_of(gathered(sums_ref, 0), cells)
    scaled = (res_ref[0] / scale).T
    log_perm = jnp.log(perm_ref[0].astype(F32)).T
    transform(lift_ref, deep_ref, col_ref, scaled, log_perm, spectra_ref, lifted_ref, zt_ref)


def next_scalars(first_ref, sums_ref):
    curvature = gathered(sums_ref, 0)
    alpha = gathered(sums_ref, 1) / curvature
    total = gathered(first_ref, 0) + alpha * (
        alpha * gathered(sums_ref, 2) - 2.0 * gathered(sums_ref, 3)
    )
    return curvature, alpha, jnp.maximum(total, 0.0)


def lift_next_body(cells, lift_ref, first_ref, sums_ref, res_ref, image_ref, perm_ref, deep_ref, col_ref, spectra_ref, lifted_ref, next_ref, zt_ref):
    _, alpha, total = next_scalars(first_ref, sums_ref)
    scale = scale_of(total, cells)
    residual = res_ref[0] - alpha * image_ref[0]
    next_ref[0] = residual
    scaled = (residual / scale).T
    log_perm = jnp.log(perm_ref[0].astype(F32)).T
    transform(lift_ref, deep_ref, col_ref, scaled, log_perm, spectra_ref, lifted_ref, zt_ref)


def point_body(mix_ref, lifted_ref, _, __, point_ref):
    size = 4 * SUBLANES
    group = 4

    def step(index, carry):
        lines = pl.ds(pl.multiple_of(index * size, size), size)
        for first in range(0, CHANNELS, group):
            sums = [mix_ref[first + j, CHANNELS] for j in range(group)]
            for channel in range(CHANNELS):
                lifted = lifted_ref[0, channel, lines, :]
                sums = [
                    total + mix_ref[first + j, channel] * lifted for j, total in enumerate(sums)
                ]
            for j, total in enumerate(sums):
                point_ref[0, first + j, lines, :] = total
        return carry

    lax.fori_loop(0, lifted_ref.shape[2] // size, step, 0)


def modes_body(cells, n_row, n_col, recv_ref, *refs):
    sources = refs[:n_col]
    _, out_ref, weight_ref, sems, field_ref, turned_ref, spec_ref, odd_ref = refs[n_col:]
    own = lax.axis_index("col")
    copies = [
        pltpu.make_async_copy(
            source, weight_ref.at[lax.rem(own + n_col - shift, n_col)], sems.at[shift]
        )
        for shift, source in enumerate(sources)
    ]
    for copy in copies:
        copy.start()
    rows = recv_ref.shape[1]
    places = n_row * rows
    tile = (SUBLANES, LANES)
    lane = lax.broadcasted_iota(jnp.int32, tile, 1)
    first = lane < LANES // 2
    sign = jnp.where(first, 1.0, -1.0).astype(F32)
    base = lane - lane % CHANNELS

    def turn(value):
        return pltpu.roll(value, LANES // 2, 1) * sign

    for row in range(n_row):
        for place in range(rows):
            value = recv_ref[row * n_col, place]
            for col in range(1, n_col):
                value = value + recv_ref[row * n_col + col, place]
            field_ref[row * rows + place] = value
    angle = 2.0 * np.pi / places
    half = KX // 2

    def weigh(coefs, ref):
        total = None
        for place, coef in enumerate(coefs):
            coef = float(coef)
            if abs(coef) < 1e-12:
                continue
            term = ref[place]
            if coef == -1.0:
                term = -term
            elif coef != 1.0:
                term = coef * term
            total = term if total is None else total + term
        return jnp.zeros(tile, F32) if total is None else total

    middle = places // 2
    for place in range(1, middle):
        value, mirror = field_ref[place], field_ref[places - place]
        field_ref[place] = value + mirror
        turned_ref[place] = turn(value - mirror)
    for freq in range(half + 1):
        turns = freq * np.arange(middle + 1) % places
        even = weigh(np.cos(angle * turns), field_ref)
        odd = weigh(np.concatenate([[0.0], np.sin(angle * turns[1:middle])]), turned_ref)
        if freq < half:
            spec_ref[half + freq] = even + odd
        if freq > 0:
            spec_ref[half - freq] = even - odd

    for copy in copies:
        copy.wait()
    share = KX // n_col
    for freq in range(KX):
        value = spec_ref[freq]
        same = [None, None]
        cross = [None, None]
        for channel in range(CHANNELS):
            wide = jnp.take_along_axis(value, base + channel, axis=1)
            weight = weight_ref[freq // share, freq % share, channel]
            for sums, factor in ((same, weight), (cross, pltpu.roll(weight, LANES // 2, 1))):
                term = factor * wide
                kept = sums[channel % 2]
                sums[channel % 2] = term if kept is None else kept + term
        same = same[0] + same[1]
        cross = cross[0] + cross[1]
        total = jnp.where(
            first,
            same - pltpu.roll(same, LANES // 2, 1),
            cross + pltpu.roll(cross, LANES // 2, 1),
        )
        field_ref[freq] = total
        turned_ref[freq] = -turn(total)
    gain = 1.0 / cells
    evens = [field_ref[half] * gain]
    odds = [None]
    for freq in range(1, half):
        evens.append((field_ref[half + freq] + field_ref[half - freq]) * gain)
        odds.append((turned_ref[half + freq] - turned_ref[half - freq]) * gain)
    evens.append(field_ref[0] * gain)
    odds.append(-turned_ref[0] * gain)
    for freq in range(half + 1):
        spec_ref[freq] = evens[freq]
        if freq > 0:
            odd_ref[freq] = odds[freq]

    def store(place, value):
        for col in range(n_col):
            out_ref[(place // rows) * n_col + col, place % rows] = value

    for place in range(places // 2 + 1):
        turns = place * np.arange(half + 1) % places
        even = weigh(np.cos(angle * turns), spec_ref)
        odd = weigh(np.sin(angle * turns), odd_ref)
        store(place, even + odd)
        if 0 < place < places // 2:
            store(places - place, even - odd)


def back_transform(recv_ref, point_ref, proj_ref, col_ref, deep_ref, wave_ref, scale):
    groups = 2 * KZ * CHANNELS // LANES
    n_col = KY // SUBLANES
    cols = col_ref.shape[2] // 2
    lane = lax.broadcasted_iota(jnp.int32, (KY, LANES), 1)
    sign = jnp.where(lane < LANES // 2, -1.0, 1.0).astype(F32)
    half = 2 * KZ
    pieces = []
    for row in range(groups):
        value = recv_ref[row * n_col : (row + 1) * n_col, 0].reshape(KY, LANES)
        turned = pltpu.roll(value, LANES // 2, 1) * sign
        both = jnp.concatenate([value, turned], 0)
        pieces.append(jnp.concatenate(split_three(both), 0).T.astype(BF16))
    part = matmul(jnp.concatenate(pieces, 0), col_ref[lax.axis_index("col")])
    wave_ref[...] = part[:, :cols] + part[:, cols:]
    total = None
    for out in range(0, CHANNELS, 2):
        waves = jnp.concatenate(
            [wave_ref[pl.ds(out + j, half, stride=CHANNELS), :] for j in range(2)], 1
        )
        high, middle, low = (part.astype(BF16) for part in split_three(waves))
        spatial = matmul(deep_ref[...], jnp.concatenate([high, middle, low, high], 0))
        for j in range(2):
            hidden = gelu(spatial[:, j * cols : (j + 1) * cols] + point_ref[0, out + j])
            term = proj_ref[out + j] * hidden
            total = term if total is None else total + term
    return (scale * (total + proj_ref[CHANNELS])).T


def put_edges(update, low_ref, high_ref, left_ref, right_ref, first=0):
    step = pl.program_id(0)
    cols = update.shape[0]
    line = pl.ds(step + first * pl.num_programs(0), 1)
    left_ref[line, :] = update[:1]
    right_ref[line, :] = update[cols - 1 :]

    @pl.when(step == 0)
    def _():
        low_ref[first * cols : (first + 1) * cols] = update

    @pl.when(step == pl.num_programs(0) - 1)
    def _():
        high_ref[first * cols : (first + 1) * cols] = update


def back_first_body(cells, proj_ref, sums_ref, recv_ref, point_ref, col_ref, deep_ref, perm_ref, kept_ref, *refs):
    *edges, wave_ref = refs
    scale = scale_of(gathered(sums_ref, 0), cells)
    update = back_transform(
        recv_ref, point_ref, proj_ref, col_ref, deep_ref, wave_ref, scale
    )
    kept_ref[0, 0] = update
    put_edges(update, *edges)
    put_edges(perm_ref[0].astype(F32), *edges, first=1)


def back_next_body(cells, proj_ref, first_ref, sums_ref, recv_ref, point_ref, col_ref, deep_ref, image_ref, _, kept_ref, out_ref, *refs):
    *edges, wave_ref, acc_ref = refs
    _, _, total = next_scalars(first_ref, sums_ref)
    update = back_transform(
        recv_ref, point_ref, proj_ref, col_ref, deep_ref, wave_ref, scale_of(total, cells)
    )
    kept_ref[0, 0] = update
    put_edges(update, *edges)
    line = lane_sums(update * image_ref[0])
    step = pl.program_id(0)

    @pl.when(step == 0)
    def _():
        acc_ref[...] = jnp.zeros_like(acc_ref)

    acc_ref[0:1] += line

    @pl.when(step == pl.num_programs(0) - 1)
    def _():
        spread([acc_ref[0:1]], out_ref)


def stencil(fields, perms):
    own, before, after, left, right = fields
    cols, depth = own.shape
    line = lax.broadcasted_iota(jnp.int32, (cols, depth), 0)
    deep = lax.broadcasted_iota(jnp.int32, (cols, depth), 1)

    def sides(array, before, after, left, right, first, last):
        return (
            before,
            after,
            jnp.where(line == 0, left, pltpu.roll(array, 1, 0)),
            jnp.where(line == cols - 1, right, pltpu.roll(array, cols - 1, 0)),
            jnp.where(deep == 0, first, pltpu.roll(array, 1, 1)),
            jnp.where(deep == depth - 1, last, pltpu.roll(array, depth - 1, 1)),
        )

    perm, *others = perms
    others = [
        jnp.where(other > 0.0, other, edge)
        for other, edge in zip(others, (perm, perm, perm[:1], perm[cols - 1 :]))
    ]
    total = None
    for other, conductance in zip(
        sides(own, before, after, left, right, 0.0, 0.0), sides(perm, *others, perm, perm)
    ):
        term = harmonic(perm, conductance) * (own - other)
        total = term if total is None else total + term
    return total


def add_sums(terms, out_ref, acc_ref):
    step = pl.program_id(0)

    @pl.when(step == 0)
    def _():
        acc_ref[...] = jnp.zeros_like(acc_ref)

    for j, term in enumerate(terms):
        acc_ref[j : j + 1] += lane_sums(term)

    @pl.when(step == pl.num_programs(0) - 1)
    def _():
        spread([acc_ref[j : j + 1] for j in range(len(terms))], out_ref)


def around(ref, index, halo, part):
    low_ref, high_ref, left_ref, right_ref = halo
    step = pl.program_id(0)
    last = pl.num_programs(0) - 1
    cols = ref.shape[-2]
    planes = slice(part * cols, (part + 1) * cols)
    line = pl.ds(step + part * pl.num_programs(0), 1)

    def plane(place):
        return ref[index + (place,)].astype(F32)

    def outside(axis, edge, value):
        return jnp.where(lax.axis_index(axis) == edge, 0.0, value)

    low = outside("row", 0, low_ref[planes])
    high = outside("row", lax.axis_size("row") - 1, high_ref[planes])
    left = outside("col", 0, left_ref[line, :])
    right = outside("col", lax.axis_size("col") - 1, right_ref[line, :])
    before = jnp.where(step == 0, low, plane(jnp.maximum(step - 1, 0)))
    after = jnp.where(step == last, high, plane(jnp.minimum(step + 1, last)))
    return plane(step), before, after, left, right


def operator_first_body(kept_ref, perm_ref, *refs):
    halo = refs[:4]
    res_ref, image_ref, out_ref, acc_ref = refs[4:]
    fields = around(kept_ref, (0,), halo, 0)
    image = stencil(fields, around(perm_ref, (), halo, 1))
    own = fields[0]
    residual = res_ref[0]
    image_ref[0] = image
    add_sums((own * image, residual * own, image * image, residual * image), out_ref, acc_ref)


def operator_next_body(first_ref, beta_ref, kept_ref, perm_ref, *refs):
    halo, old = refs[:4], refs[4:8]
    res_ref, way_ref, image_ref, out_ref, acc_ref = refs[8:]
    beta = gathered(beta_ref, 0) / gathered(first_ref, 0)
    fields = [
        new - beta * other
        for new, other in zip(around(kept_ref, (1,), halo, 0), around(kept_ref, (0,), old, 0))
    ]
    image = stencil(fields, around(perm_ref, (), old, 1))
    own = fields[0]
    way_ref[0] = own
    image_ref[0] = image
    add_sums((own * image, res_ref[0] * own), out_ref, acc_ref)


def last_body(first_ref, sums_ref, old_ref, way_ref, res_ref, image_ref, sol_ref, out_ref):
    alpha = gathered(first_ref, 1) / gathered(first_ref, 0)
    later = gathered(sums_ref, 1) / gathered(sums_ref, 0)
    sol_ref[0] = alpha * old_ref[0, 0] + later * way_ref[0]
    out_ref[0] = res_ref[0] - later * image_ref[0]


def exchange(blocks):
    return lax.all_to_all(blocks, BOTH, split_axis=0, concat_axis=0, tiled=True)


def add_up(partial):
    return exchange(partial)


def neighbours(low, high, left, right):
    found = []
    for axis, first, last in (("row", low, high), ("col", left, right)):
        count = lax.axis_size(axis)
        forward = [(i, (i + 1) % count) for i in range(count)]
        backward = [(target, source) for source, target in forward]
        found.append(lax.ppermute(last, axis, forward))
        found.append(lax.ppermute(first, axis, backward))
    return found


def tiled_local(right_side, permeability, lift_weight, spectral_weight, mix_weight, proj_weight):
    rows, cols, depth = right_side.shape
    n_row = lax.axis_size("row")
    n_col = lax.axis_size("col")
    count = n_row * n_col
    cells = float(rows * n_row * cols * n_col * depth)
    freq = KX // n_col
    deep_forward, deep_back = (jnp.asarray(t) for t in deep_tables(n_row, depth))
    col_forward, col_back = (jnp.asarray(t) for t in column_tables(n_col, cols))
    lift_weight = lift_weight.T
    field = shape(rows, cols, depth)
    field_bytes = 4 * rows * cols * depth
    partial = shape(count, SUBLANES, LANES)
    channels = shape(rows, CHANNELS, depth, cols)
    spectra = shape(count, rows, SUBLANES, LANES)
    spectra_bytes = 4 * count * rows * SUBLANES * LANES
    smem = whole(pltpu.SMEM)
    vmem = whole()
    plane = pl.BlockSpec((1, cols, depth), lambda i: (i, 0, 0))
    spectra_block = pl.BlockSpec((count, 1, SUBLANES, LANES), lambda i: (0, i, 0, 0))
    point_block = pl.BlockSpec((1, CHANNELS, depth, cols), lambda i: (i, 0, 0, 0))
    kept_shape = shape(ITERS, rows, cols, depth)
    lift_flops = 2.0e9
    back_flops = 2.0e9

    squares = call(squares_body, partial, [vmem], vmem, moved=field_bytes)(right_side)
    squares = add_up(squares)

    weight_shape = (freq, CHANNELS, SUBLANES, LANES)
    own, *weights = call(
        weight_body,
        (shape(*weight_shape),) * n_col,
        [vmem],
        (vmem,) * n_col,
        scratch=[pltpu.VMEM((n_col,) + weight_shape, F32)],
        moved=8 * spectral_weight.size,
    )(spectral_weight)
    weights = [own] + [
        lax.ppermute(part, "col", [(i, (i + shift + 1) % n_col) for i in range(n_col)])
        for shift, part in enumerate(weights)
    ]
    edge_shapes = (shape(cols, depth),) * 2 + (shape(rows, depth),) * 2
    both_shapes = (shape(2 * cols, depth),) * 2 + (shape(2 * rows, depth),) * 2
    acc_scratch = pltpu.VMEM((SUBLANES, LANES), F32)
    zt_scratch = pltpu.VMEM((2 * KZ * CHANNELS, cols), F32)

    anywhere = whole(pl.ANY)

    def points(lifted, part, before, after):
        first = part * rows // 2
        half_block = pl.BlockSpec((1, CHANNELS, depth, cols), lambda i: (first + i, 0, 0, 0))
        return call(
            point_body,
            channels,
            [smem, half_block, anywhere, anywhere],
            half_block,
            grid=(rows // 2,),
            flops=2.5e9,
            moved=16 * field_bytes,
            alias={2: 0} if part else None,
            limit=12,
        )(mix_weight, lifted, before, after)

    def modes(received, before):
        places = rows * n_row
        tiles = lambda size: pltpu.VMEM((size, SUBLANES, LANES), F32)
        return call(
            functools.partial(modes_body, cells, n_row, n_col),
            spectra,
            [vmem] + [anywhere] * (n_col + 1),
            vmem,
            scratch=[
                pltpu.VMEM((n_col,) + weight_shape, F32),
                pltpu.SemaphoreType.DMA((n_col,)),
                tiles(places),
                tiles(places),
                tiles(KX),
                tiles(KX),
            ],
            moved=2 * spectra_bytes + 4 * spectral_weight.size,
            near=(0,),
        )(received, *weights, before)

    def mixed_modes(blocks, lifted):
        received = exchange(blocks)
        point = points(lifted, 0, right_side, right_side)
        blocks = modes(received, point)
        received = exchange(blocks)
        point = points(lifted, 1, point, blocks)
        return received, point

    blocks, lifted = call(
        functools.partial(lift_first_body, cells),
        (spectra, channels),
        [smem, vmem, plane, plane, vmem, vmem, anywhere],
        (spectra_block, point_block),
        limit=16,
        grid=(rows,),
        scratch=[zt_scratch],
        flops=lift_flops,
        moved=2 * field_bytes + spectra_bytes,
    )(lift_weight, squares, right_side, permeability, deep_forward, col_forward, weights[0])
    received, point = mixed_modes(blocks, lifted)
    kept, *edges = call(
        functools.partial(back_first_body, cells),
        (kept_shape,) + both_shapes,
        [smem, vmem, spectra_block, point_block, vmem, vmem, plane],
        (pl.BlockSpec((1, 1, cols, depth), lambda i: (0, i, 0, 0)),) + (vmem,) * 4,
        grid=(rows,),
        scratch=[zt_scratch],
        limit=12,
        flops=back_flops,
        moved=18 * field_bytes,
    )(proj_weight, squares, received, point, col_back, deep_back, permeability)

    old_halo = neighbours(*edges)
    args = (kept, permeability, *old_halo, right_side)
    image, sums = call(
        operator_first_body,
        (field, partial),
        [vmem] * 6 + [plane],
        (plane, vmem),
        grid=(rows,),
        scratch=[acc_scratch],
        moved=9 * field_bytes,
        near=range(7),
        loose=True,
    )(*args)
    sums = add_up(sums)

    blocks, lifted, residual = call(
        functools.partial(lift_next_body, cells),
        (spectra, channels, field),
        [smem, vmem, vmem, plane, plane, plane, vmem, vmem],
        (spectra_block, point_block, plane),
        limit=16,
        near=(4,),
        grid=(rows,),
        scratch=[zt_scratch],
        flops=lift_flops,
        moved=4 * field_bytes + spectra_bytes,
    )(lift_weight, squares, sums, right_side, image, permeability, deep_forward, col_forward)
    received, point = mixed_modes(blocks, lifted)
    kept, beta, *edges = call(
        functools.partial(back_next_body, cells),
        (kept_shape, partial) + edge_shapes,
        [smem, vmem, vmem, spectra_block, point_block, vmem, vmem, plane, whole(pl.ANY)],
        (pl.BlockSpec((1, 1, cols, depth), lambda i: (1, i, 0, 0)),) + (vmem,) * 5,
        grid=(rows,),
        limit=12,
        scratch=[zt_scratch, acc_scratch],
        flops=back_flops,
        moved=19 * field_bytes,
        alias={8: 0},
    )(proj_weight, squares, sums, received, point, col_back, deep_back, image, kept)

    beta = add_up(beta)
    halo = neighbours(*edges)
    args = (sums, beta, kept, permeability, *halo, *old_halo, residual)
    way, image, later = call(
        operator_next_body,
        (field, field, partial),
        [vmem] * 12 + [plane],
        (plane, plane, vmem),
        grid=(rows,),
        scratch=[acc_scratch],
        near=range(13),
        loose=True,
        moved=11 * field_bytes,
    )(*args)
    later = add_up(later)
    answer, residual = call(
        last_body,
        (field, field),
        [vmem, vmem, pl.BlockSpec((1, 1, cols, depth), lambda i: (0, i, 0, 0)), plane, plane, plane],
        (plane, plane),
        grid=(rows,),
        moved=6 * field_bytes,
        near=range(6),
        loose=True,
    )(sums, later, kept, way, residual, image)
    return (answer, residual, kept)


def fits_tiles(mesh, block):
    rows, cols, depth = block
    n_row, n_col = mesh.shape["row"], mesh.shape["col"]
    return (
        ITERS == 2
        and KZ == n_row * (LANES // (2 * CHANNELS))
        and KY == n_col * SUBLANES
        and KX % n_col == 0
        and cols == LANES
        and depth % LANES == 0
        and rows * n_row >= KX
    )


def solution(mesh):
    placed = (
        P("row", "col", None),
        P("row", "col", None),
        P(),
        P(None, "row", None, None, "col"),
        P(),
        P(),
    )

    def run(right_side, *others):
        rows, cols, depth = right_side.shape
        block = (rows // mesh.shape["row"], cols // mesh.shape["col"], depth)
        return jax.shard_map(
            tiled_local if fits_tiles(mesh, block) else local,
            mesh=mesh,
            in_specs=placed,
            out_specs=(P("row", "col", None), P("row", "col", None), P(None, "row", "col", None)),
            check_vma=False,
        )(right_side, *others)

    return run
```

```python
import functools
import math

import jax
import jax.numpy as jnp
import ml_dtypes
import numpy as np
from jax import lax
from jax.experimental import pallas as pl
from jax.experimental.pallas import tpu as pltpu
from jax.sharding import PartitionSpec as P

CHANNELS = 16
KX = 16
KY = 32
KZ = 32
ITERS = 2


HIGHEST = lax.Precision.HIGHEST


def with_halo(block, sides, width):
    for axis, dim in sides:
        count = lax.axis_size(axis)
        forward = [(i, i + 1) for i in range(count - 1)]
        backward = [(target, source) for source, target in forward]
        low = lax.ppermute(
            lax.slice_in_dim(block, block.shape[dim] - width, None, axis=dim), axis, forward
        )
        high = lax.ppermute(lax.slice_in_dim(block, 0, width, axis=dim), axis, backward)
        block = jnp.concatenate([low, block, high], axis=dim)
    return block


def einsum_high(form, left, right):
    return jnp.einsum(form, left, right, precision=HIGHEST)


def harmonic(first, second):
    return 2.0 * first * second / (first + second)


def wave_table(freqs, places, length):
    turns = freqs[None, :] * places[:, None] % length
    angle = turns.astype(jnp.float32) * (2.0 * jnp.pi / length)
    return (jnp.cos(angle), jnp.sin(angle))


def signed_freqs(count):
    return jnp.arange(count, dtype=jnp.int32) - count // 2


def face_arrays(permeability):
    padded = with_halo(permeability, (("row", 0), ("col", 1)), 1).astype(jnp.float32)
    own = permeability.astype(jnp.float32)
    edged = jnp.pad(own, ((1, 1), (1, 1), (0, 0)), mode="edge")
    padded = jnp.where(padded > 0.0, padded, edged)
    first = harmonic(padded[:-1, 1:-1], padded[1:, 1:-1])
    second = harmonic(padded[1:-1, :-1], padded[1:-1, 1:])
    deep = jnp.pad(own, ((0, 0), (0, 0), (1, 1)), mode="edge")
    third = harmonic(deep[:, :, :-1], deep[:, :, 1:])
    return ((first, second, third), jnp.log(own))


def apply_operator(field, faces):
    first, second, third = faces
    padded = with_halo(field, (("row", 0), ("col", 1)), 1)
    padded = jnp.pad(padded, ((0, 0), (0, 0), (1, 1)))
    total = first[:-1] * (field - padded[:-2, 1:-1, 1:-1])
    total = total + first[1:] * (field - padded[2:, 1:-1, 1:-1])
    total = total + second[:, :-1] * (field - padded[1:-1, :-2, 1:-1])
    total = total + second[:, 1:] * (field - padded[1:-1, 2:, 1:-1])
    total = total + third[:, :, :-1] * (field - padded[1:-1, 1:-1, :-2])
    total = total + third[:, :, 1:] * (field - padded[1:-1, 1:-1, 2:])
    return total


def global_squares(field):
    return lax.psum(jnp.sum(field * field), ("row", "col"))


def mix_modes(real_in, imag_in, spectral_weight, deep_count, freq_count):
    block = spectral_weight.reshape(2, deep_count, CHANNELS, CHANNELS, freq_count, KY)
    real_out = einsum_high("kcfg,kcofg->kofg", real_in, block[0]) - einsum_high(
        "kcfg,kcofg->kofg", imag_in, block[1]
    )
    imag_out = einsum_high("kcfg,kcofg->kofg", imag_in, block[0]) + einsum_high(
        "kcfg,kcofg->kofg", real_in, block[1]
    )
    return (real_out, imag_out)


def spectral_transpose(real_part, imag_part, spectral_weight, grid):
    rows, cols, n_row, n_col, row_id, col_id = grid
    full_rows = rows * n_row
    full_cols = cols * n_col
    cosine_rows, sine_rows = wave_table(
        signed_freqs(KX), jnp.arange(full_rows, dtype=jnp.int32), full_rows
    )
    cosine_cols, sine_cols = wave_table(
        signed_freqs(KY), jnp.arange(full_cols, dtype=jnp.int32), full_cols
    )
    real_part, imag_part = (
        lax.all_to_all(real_part, "row", split_axis=0, concat_axis=1, tiled=True),
        lax.all_to_all(imag_part, "row", split_axis=0, concat_axis=1, tiled=True),
    )
    first_real = einsum_high("qxy,xf->qfy", real_part, cosine_rows) + einsum_high(
        "qxy,xf->qfy", imag_part, sine_rows
    )
    first_imag = einsum_high("qxy,xf->qfy", imag_part, cosine_rows) - einsum_high(
        "qxy,xf->qfy", real_part, sine_rows
    )
    first_real, first_imag = (
        lax.all_to_all(first_real, "col", split_axis=1, concat_axis=2, tiled=True),
        lax.all_to_all(first_imag, "col", split_axis=1, concat_axis=2, tiled=True),
    )
    second_real = einsum_high("qfy,yg->qfg", first_real, cosine_cols) + einsum_high(
        "qfy,yg->qfg", first_imag, sine_cols
    )
    second_imag = einsum_high("qfy,yg->qfg", first_imag, cosine_cols) - einsum_high(
        "qfy,yg->qfg", first_real, sine_cols
    )
    deep_count = KZ // n_row
    freq_count = KX // n_col
    shape_in = (deep_count, CHANNELS, freq_count, KY)
    mixed_real, mixed_imag = mix_modes(
        second_real.reshape(shape_in),
        second_imag.reshape(shape_in),
        spectral_weight,
        deep_count,
        freq_count,
    )
    shape_out = (deep_count * CHANNELS, freq_count, KY)
    mixed_real = mixed_real.reshape(shape_out)
    mixed_imag = mixed_imag.reshape(shape_out)
    back_real = einsum_high("qfg,yg->qfy", mixed_real, cosine_cols) - einsum_high(
        "qfg,yg->qfy", mixed_imag, sine_cols
    )
    back_imag = einsum_high("qfg,yg->qfy", mixed_imag, cosine_cols) + einsum_high(
        "qfg,yg->qfy", mixed_real, sine_cols
    )
    back_real, back_imag = (
        lax.all_to_all(back_real, "col", split_axis=2, concat_axis=1, tiled=True),
        lax.all_to_all(back_imag, "col", split_axis=2, concat_axis=1, tiled=True),
    )
    out_real = einsum_high("qfy,xf->qxy", back_real, cosine_rows) - einsum_high(
        "qfy,xf->qxy", back_imag, sine_rows
    )
    out_imag = einsum_high("qfy,xf->qxy", back_imag, cosine_rows) + einsum_high(
        "qfy,xf->qxy", back_real, sine_rows
    )
    out_real, out_imag = (
        lax.all_to_all(out_real, "row", split_axis=1, concat_axis=0, tiled=True),
        lax.all_to_all(out_imag, "row", split_axis=1, concat_axis=0, tiled=True),
    )
    return (out_real, out_imag)


def precondition(residual, squares_total, log_perm, weights, grid, cells):
    lift_weight, spectral_weight, mix_weight, proj_weight = weights
    rows, cols, depth = residual.shape
    scale = jnp.sqrt(squares_total / cells + 1e-06)
    scaled = residual / scale
    lifted = jax.nn.gelu(
        lift_weight[:, 0, None, None, None] * scaled[None]
        + lift_weight[:, 1, None, None, None] * log_perm[None]
        + lift_weight[:, 2, None, None, None]
    )
    cosine_deep, sine_deep = wave_table(
        jnp.arange(KZ, dtype=jnp.int32), jnp.arange(depth, dtype=jnp.int32), depth
    )
    real_part = einsum_high("cxyz,zk->kcxy", lifted, cosine_deep).reshape(KZ * CHANNELS, rows, cols)
    imag_part = -einsum_high("cxyz,zk->kcxy", lifted, sine_deep).reshape(KZ * CHANNELS, rows, cols)
    out_real, out_imag = spectral_transpose(real_part, imag_part, spectral_weight, grid)
    out_real = out_real.reshape(KZ, CHANNELS, rows, cols)
    out_imag = out_imag.reshape(KZ, CHANNELS, rows, cols)
    spatial = (
        einsum_high("kcxy,zk->cxyz", out_real, cosine_deep)
        - einsum_high("kcxy,zk->cxyz", out_imag, sine_deep)
    ) / cells
    point = (
        einsum_high("oc,cxyz->oxyz", mix_weight[:, :CHANNELS], lifted)
        + mix_weight[:, CHANNELS, None, None, None]
    )
    hidden = jax.nn.gelu(spatial + point)
    return scale * (
        einsum_high("o,oxyz->xyz", proj_weight[:CHANNELS], hidden) + proj_weight[CHANNELS]
    )


def local(right_side, permeability, lift_weight, spectral_weight, mix_weight, proj_weight):
    rows, cols, depth = right_side.shape
    n_row = lax.axis_size("row")
    n_col = lax.axis_size("col")
    grid = (rows, cols, n_row, n_col, lax.axis_index("row"), lax.axis_index("col"))
    cells = float(rows * n_row * cols * n_col * depth)
    faces, log_perm = face_arrays(permeability)
    weights = (lift_weight, spectral_weight, mix_weight, proj_weight)

    def precond(residual, squares_total):
        return precondition(residual, squares_total, log_perm, weights, grid, cells)

    solution = jnp.zeros_like(right_side)
    residual = right_side
    kept = []
    update = precond(residual, global_squares(residual))
    kept.append(update)
    direction = update
    for step in range(ITERS):
        image = apply_operator(direction, faces)
        curvature, along = lax.psum(
            (jnp.sum(direction * image), jnp.sum(residual * direction)), ("row", "col")
        )
        alpha = along / curvature
        solution = solution + alpha * direction
        residual = residual - alpha * image
        if step + 1 < ITERS:
            update = precond(residual, global_squares(residual))
            kept.append(update)
            beta = lax.psum(jnp.sum(update * image), ("row", "col")) / curvature
            direction = update - beta * direction
    return (solution, residual, jnp.stack(kept))


LANES = 128
SUBLANES = 8
BOTH = ("row", "col")
F32 = jnp.float32
BF16 = jnp.bfloat16


def split_table(table):
    high = table.astype(ml_dtypes.bfloat16)
    low = (table - high.astype(np.float64)).astype(ml_dtypes.bfloat16)
    return high, low


def split(value):
    high = value.astype(BF16)
    return high, (value - high.astype(F32)).astype(BF16)


def split_three(value):
    high = value.astype(BF16).astype(F32)
    rest = value - high
    middle = rest.astype(BF16).astype(F32)
    return high, middle, rest - middle


def matmul(left, right):
    return jnp.dot(left, right, preferred_element_type=F32)


def matmul_nt(left, right):
    return lax.dot_general(left, right, (((1,), (1,)), ((), ())), preferred_element_type=F32)


def angles(freqs, places, length):
    turns = np.multiply.outer(freqs, places) % length
    return turns * (2.0 * np.pi / length)


def deep_order(n_row):
    count = KZ // n_row
    order = [
        (part, row * count + place)
        for row in range(n_row)
        for part in range(2)
        for place in range(count)
    ]
    return np.array(order)


def deep_tables(n_row, depth):
    order = deep_order(n_row)
    angle = angles(order[:, 1], np.arange(depth), depth)
    wave = np.where(order[:, :1] == 0, np.cos(angle), -np.sin(angle))
    high, low = split_table(wave)
    return np.concatenate([high, low], 0), np.concatenate([high.T, high.T, high.T, low.T], 1)


def column_tables(n_col, cols):
    freqs = np.arange(KY) - KY // 2
    forward = []
    back = []
    for place in range(n_col):
        angle = angles(freqs, place * cols + np.arange(cols), n_col * cols)
        both = np.concatenate([np.cos(angle), np.sin(angle)], 0)
        high, low = split_table(both)
        forward.append(
            np.concatenate(
                [
                    np.concatenate([high, high], 1),
                    np.concatenate([low, np.zeros_like(low)], 1),
                ],
                0,
            )
        )
        both = np.concatenate([np.cos(angle), np.sin(angle)], 0)
        high, low = split_table(both)
        back.append(
            np.concatenate(
                [
                    np.concatenate([high, low], 1),
                    np.concatenate([high, low], 1),
                    np.concatenate([high, np.zeros_like(low)], 1),
                ],
                0,
            )
        )
    return np.stack(forward), np.stack(back)


GAIN = (math.sqrt(2.0 / math.pi) * 0.044715) ** (1.0 / 3.0)
LINEAR = math.sqrt(2.0 / math.pi) / GAIN


def scaled_gelu(value):
    return value + value * jnp.tanh(value * (value * value + LINEAR))


def call(body, outs, in_specs, out_specs, grid=(), scratch=(), flops=0, moved=0, alias=None, limit=8, near=(), loose=False):
    single = not isinstance(outs, tuple)
    outs = (outs,) if single else outs
    out_specs = (out_specs,) if single else out_specs
    run = pl.pallas_call(
        body,
        out_shape=tuple(
            out if loose or out.size <= 2**16 else pltpu.HBM(out.shape, out.dtype) for out in outs
        ),
        grid=grid,
        in_specs=in_specs,
        out_specs=out_specs,
        scratch_shapes=list(scratch),
        input_output_aliases=alias or {},
        compiler_params=pltpu.CompilerParams(vmem_limit_bytes=limit * 1024 * 1024),
        cost_estimate=pl.CostEstimate(
            flops=int(flops), bytes_accessed=int(moved), transcendentals=0
        ),
    )

    def wrapped(*args):
        held = [
            arg
            if place in near or spec.memory_space == pltpu.SMEM
            else pltpu.with_memory_space_constraint(arg, pltpu.HBM)
            for place, (arg, spec) in enumerate(zip(args, in_specs))
        ]
        found = run(*held)
        return found[0] if single else found

    return wrapped


def whole(memory=pltpu.VMEM):
    return pl.BlockSpec(memory_space=memory)


def shape(*dims):
    return jax.ShapeDtypeStruct(dims, F32)


def lane_sums(value):
    folded = jnp.sum(value.reshape(-1, SUBLANES, value.shape[-1]), axis=0)
    folded = sum(
        folded[:, start : start + LANES] for start in range(0, folded.shape[1], LANES)
    )
    return jnp.sum(folded, axis=0, keepdims=True)


def spread(rows, ref):
    rows = rows + [jnp.zeros_like(rows[0])] * (SUBLANES - len(rows))
    ref[...] = jnp.broadcast_to(jnp.concatenate(rows, 0)[None], ref.shape)


def gathered(ref, row):
    total = jnp.sum(ref[...], axis=0)
    return jnp.sum(total[row : row + 1], axis=1, keepdims=True)


def squares_body(field_ref, perm_ref, _, out_ref, low_ref, high_ref, left_ref, right_ref):
    total = field_ref[0] * field_ref[0]
    for place in range(1, field_ref.shape[0]):
        total = total + field_ref[place] * field_ref[place]
    spread([lane_sums(total)], out_ref)
    rows, cols, _ = perm_ref.shape
    low_ref[...] = perm_ref[0].astype(F32)
    high_ref[...] = perm_ref[rows - 1].astype(F32)
    for place in range(rows):
        plane = perm_ref[place].astype(F32)
        left_ref[place : place + 1, :] = plane[:1]
        right_ref[place : place + 1, :] = plane[cols - 1 :]


def weight_body(weight_ref, *refs):
    *out_refs, hold_ref = refs
    groups, freq, channels, fine, _ = hold_ref.shape
    parts, deep, _, outs, modes = weight_ref.shape
    for channel in range(channels):
        block = weight_ref[:, :, channel].reshape(parts * deep * outs, modes)
        block = block.T.reshape(freq, groups, fine, parts * deep * outs)
        for group in range(groups):
            hold_ref[group, :, channel] = block[:, group]
    place = lax.axis_index("col")
    for shift, out_ref in enumerate(out_refs):
        out_ref[...] = hold_ref[lax.rem(place + shift, groups)]


def scale_of(total, cells):
    return jnp.sqrt(total / cells + 1e-06)


def lift_channel(weight_ref, channel, scaled, log_perm):
    return scaled_gelu(
        weight_ref[0, channel] * scaled
        + (weight_ref[1, channel] * log_perm + weight_ref[2, channel])
    )


def transform(lift_ref, deep_ref, col_ref, scaled, log_perm, spectra_ref, lifted_ref, zt_ref):
    half = 2 * KZ
    cols = scaled.shape[1]
    for channel in range(0, CHANNELS, 2):
        pair = [lift_channel(lift_ref, channel + j, scaled, log_perm) for j in range(2)]
        for j in range(2):
            lifted_ref[0, channel + j] = pair[j]
        high, low = split(jnp.concatenate(pair, 1))
        part = matmul(deep_ref[...], high)
        part = part[:half] + part[half:] + matmul(deep_ref[:half], low)
        for j in range(2):
            zt_ref[pl.ds(channel + j, half, stride=CHANNELS), :] = part[:, j * cols : (j + 1) * cols]
    groups = half * CHANNELS // LANES
    part = matmul_nt(col_ref[lax.axis_index("col")], jnp.concatenate(split(zt_ref[...]), 1))
    part = part[: 2 * KY] + part[2 * KY :]
    lane = lax.broadcasted_iota(jnp.int32, (KY, LANES), 1)
    sign = jnp.where(lane < LANES // 2, 1.0, -1.0).astype(F32)
    n_col = KY // SUBLANES
    for row in range(groups):
        lanes = slice(row * LANES, (row + 1) * LANES)
        block = part[:KY, lanes] + pltpu.roll(part[KY:, lanes], LANES // 2, 1) * sign
        for col in range(n_col):
            spectra_ref[row * n_col + col, 0] = block[col * SUBLANES : (col + 1) * SUBLANES]


def lift_first_body(cells, lift_ref, sums_ref, res_ref, perm_ref, deep_ref, col_ref, *refs):
    spectra_ref, lifted_ref, zt_ref = refs[-3:]
    scale = scale_of(gathered(sums_ref, 0), cells)
    scaled = (res_ref[0] / scale).T
    log_perm = jnp.log(perm_ref[0].astype(F32)).T
    transform(lift_ref, deep_ref, col_ref, scaled, log_perm, spectra_ref, lifted_ref, zt_ref)


def next_scalars(first_ref, sums_ref):
    curvature = gathered(sums_ref, 0)
    alpha = gathered(sums_ref, 1) / curvature
    total = gathered(first_ref, 0) + alpha * (
        alpha * gathered(sums_ref, 2) - 2.0 * gathered(sums_ref, 3)
    )
    return curvature, alpha, jnp.maximum(total, 0.0)


def lift_next_body(cells, lift_ref, first_ref, sums_ref, res_ref, image_ref, perm_ref, deep_ref, col_ref, spectra_ref, lifted_ref, next_ref, zt_ref):
    _, alpha, total = next_scalars(first_ref, sums_ref)
    scale = scale_of(total, cells)
    residual = res_ref[0] - alpha * image_ref[0]
    next_ref[0] = residual
    scaled = (residual / scale).T
    log_perm = jnp.log(perm_ref[0].astype(F32)).T
    transform(lift_ref, deep_ref, col_ref, scaled, log_perm, spectra_ref, lifted_ref, zt_ref)


def point_body(mix_ref, lifted_ref, _, __, point_ref):
    size = 4 * SUBLANES
    group = 4

    def step(index, carry):
        lines = pl.ds(pl.multiple_of(index * size, size), size)
        for first in range(0, CHANNELS, group):
            sums = [mix_ref[first + j, CHANNELS] for j in range(group)]
            for channel in range(CHANNELS):
                lifted = lifted_ref[0, channel, lines, :]
                sums = [
                    total + mix_ref[first + j, channel] * lifted for j, total in enumerate(sums)
                ]
            for j, total in enumerate(sums):
                point_ref[0, first + j, lines, :] = total
        return carry

    lax.fori_loop(0, lifted_ref.shape[2] // size, step, 0)


def modes_body(cells, n_row, n_col, recv_ref, *refs):
    sources = refs[:n_col]
    _, out_ref, weight_ref, sems, field_ref, turned_ref, spec_ref, odd_ref = refs[n_col:]
    own = lax.axis_index("col")
    copies = [
        pltpu.make_async_copy(
            source, weight_ref.at[lax.rem(own + n_col - shift, n_col)], sems.at[shift]
        )
        for shift, source in enumerate(sources)
    ]
    for copy in copies:
        copy.start()
    rows = recv_ref.shape[1]
    places = n_row * rows
    tile = (SUBLANES, LANES)
    lane = lax.broadcasted_iota(jnp.int32, tile, 1)
    first = lane < LANES // 2
    sign = jnp.where(first, 1.0, -1.0).astype(F32)
    base = lane - lane % CHANNELS

    def turn(value):
        return pltpu.roll(value, LANES // 2, 1) * sign

    for row in range(n_row):
        for place in range(rows):
            value = recv_ref[row * n_col, place]
            for col in range(1, n_col):
                value = value + recv_ref[row * n_col + col, place]
            field_ref[row * rows + place] = value
    angle = 2.0 * np.pi / places
    half = KX // 2

    def weigh(coefs, ref):
        total = None
        for place, coef in enumerate(coefs):
            coef = float(coef)
            if abs(coef) < 1e-12:
                continue
            term = ref[place]
            if coef == -1.0:
                term = -term
            elif coef != 1.0:
                term = coef * term
            total = term if total is None else total + term
        return jnp.zeros(tile, F32) if total is None else total

    middle = places // 2
    for place in range(1, middle):
        value, mirror = field_ref[place], field_ref[places - place]
        field_ref[place] = value + mirror
        turned_ref[place] = turn(value - mirror)
    for freq in range(half + 1):
        turns = freq * np.arange(middle + 1) % places
        even = weigh(np.cos(angle * turns), field_ref)
        odd = weigh(np.concatenate([[0.0], np.sin(angle * turns[1:middle])]), turned_ref)
        if freq < half:
            spec_ref[half + freq] = even + odd
        if freq > 0:
            spec_ref[half - freq] = even - odd

    for copy in copies:
        copy.wait()
    share = KX // n_col
    for freq in range(KX):
        value = spec_ref[freq]
        same = [None, None]
        cross = [None, None]
        for channel in range(CHANNELS):
            wide = jnp.take_along_axis(value, base + channel, axis=1)
            weight = weight_ref[freq // share, freq % share, channel]
            for sums, factor in ((same, weight), (cross, pltpu.roll(weight, LANES // 2, 1))):
                term = factor * wide
                kept = sums[channel % 2]
                sums[channel % 2] = term if kept is None else kept + term
        same = same[0] + same[1]
        cross = cross[0] + cross[1]
        total = jnp.where(
            first,
            same - pltpu.roll(same, LANES // 2, 1),
            cross + pltpu.roll(cross, LANES // 2, 1),
        )
        field_ref[freq] = total
        turned_ref[freq] = -turn(total)
    gain = 0.5 / cells
    evens = [field_ref[half] * gain]
    odds = [None]
    for freq in range(1, half):
        evens.append((field_ref[half + freq] + field_ref[half - freq]) * gain)
        odds.append((turned_ref[half + freq] - turned_ref[half - freq]) * gain)
    evens.append(field_ref[0] * gain)
    odds.append(-turned_ref[0] * gain)
    for freq in range(half + 1):
        spec_ref[freq] = evens[freq]
        if freq > 0:
            odd_ref[freq] = odds[freq]

    def store(place, value):
        for col in range(n_col):
            out_ref[(place // rows) * n_col + col, place % rows] = value

    for place in range(places // 2 + 1):
        turns = place * np.arange(half + 1) % places
        even = weigh(np.cos(angle * turns), spec_ref)
        odd = weigh(np.sin(angle * turns), odd_ref)
        store(place, even + odd)
        if 0 < place < places // 2:
            store(places - place, even - odd)


def back_transform(recv_ref, point_ref, proj_ref, col_ref, deep_ref, wave_ref, scale):
    groups = 2 * KZ * CHANNELS // LANES
    n_col = KY // SUBLANES
    cols = col_ref.shape[2] // 2
    lane = lax.broadcasted_iota(jnp.int32, (KY, LANES), 1)
    sign = jnp.where(lane < LANES // 2, -1.0, 1.0).astype(F32)
    half = 2 * KZ
    pieces = []
    for row in range(groups):
        value = recv_ref[row * n_col : (row + 1) * n_col, 0].reshape(KY, LANES)
        turned = pltpu.roll(value, LANES // 2, 1) * sign
        both = jnp.concatenate([value, turned], 0)
        pieces.append(jnp.concatenate(split_three(both), 0).T.astype(BF16))
    part = matmul(jnp.concatenate(pieces, 0), col_ref[lax.axis_index("col")])
    wave_ref[...] = part[:, :cols] + part[:, cols:]
    total = None
    for out in range(0, CHANNELS, 2):
        waves = jnp.concatenate(
            [wave_ref[pl.ds(out + j, half, stride=CHANNELS), :] for j in range(2)], 1
        )
        high, middle, low = (part.astype(BF16) for part in split_three(waves))
        spatial = matmul(deep_ref[...], jnp.concatenate([high, middle, low, high], 0))
        for j in range(2):
            hidden = scaled_gelu(spatial[:, j * cols : (j + 1) * cols] + point_ref[0, out + j])
            term = proj_ref[out + j] * hidden
            total = term if total is None else total + term
    return (scale * (total + proj_ref[CHANNELS])).T


def put_edges(update, low_ref, high_ref, left_ref, right_ref):
    step = pl.program_id(0)
    left_ref[pl.ds(step, 1), :] = update[:1]
    right_ref[pl.ds(step, 1), :] = update[update.shape[0] - 1 :]

    @pl.when(step == 0)
    def _():
        low_ref[...] = update

    @pl.when(step == pl.num_programs(0) - 1)
    def _():
        high_ref[...] = update


def back_first_body(cells, proj_ref, sums_ref, recv_ref, point_ref, col_ref, deep_ref, *refs):
    kept_ref, *edges, wave_ref = refs[4:]
    scale = scale_of(gathered(sums_ref, 0), cells)
    update = back_transform(
        recv_ref, point_ref, proj_ref, col_ref, deep_ref, wave_ref, scale
    )
    kept_ref[0, 0] = update
    put_edges(update, *edges)


def back_next_body(cells, proj_ref, first_ref, sums_ref, recv_ref, point_ref, col_ref, deep_ref, image_ref, _, kept_ref, out_ref, *refs):
    *edges, wave_ref, acc_ref = refs
    _, _, total = next_scalars(first_ref, sums_ref)
    update = back_transform(
        recv_ref, point_ref, proj_ref, col_ref, deep_ref, wave_ref, scale_of(total, cells)
    )
    kept_ref[0, 0] = update
    put_edges(update, *edges)
    line = lane_sums(update * image_ref[0])
    step = pl.program_id(0)

    @pl.when(step == 0)
    def _():
        acc_ref[...] = jnp.zeros_like(acc_ref)

    acc_ref[0:1] += line

    @pl.when(step == pl.num_programs(0) - 1)
    def _():
        spread([acc_ref[0:1]], out_ref)


def stencil(fields, perms):
    own, before, after, left, right = fields
    cols, depth = own.shape
    line = lax.broadcasted_iota(jnp.int32, (cols, depth), 0)
    deep = lax.broadcasted_iota(jnp.int32, (cols, depth), 1)

    def sides(array, before, after, left, right, first, last):
        return (
            before,
            after,
            jnp.where(line == 0, left, pltpu.roll(array, 1, 0)),
            jnp.where(line == cols - 1, right, pltpu.roll(array, cols - 1, 0)),
            jnp.where(deep == 0, first, pltpu.roll(array, 1, 1)),
            jnp.where(deep == depth - 1, last, pltpu.roll(array, depth - 1, 1)),
        )

    perm, *others = perms
    others = [
        jnp.where(other > 0.0, other, edge)
        for other, edge in zip(others, (perm, perm, perm[:1], perm[cols - 1 :]))
    ]
    total = None
    for other, conductance in zip(
        sides(own, before, after, left, right, 0.0, 0.0), sides(perm, *others, perm, perm)
    ):
        term = harmonic(perm, conductance) * (own - other)
        total = term if total is None else total + term
    return total


def add_sums(terms, out_ref, acc_ref):
    step = pl.program_id(0)

    @pl.when(step == 0)
    def _():
        acc_ref[...] = jnp.zeros_like(acc_ref)

    for j, term in enumerate(terms):
        acc_ref[j : j + 1] += lane_sums(term)

    @pl.when(step == pl.num_programs(0) - 1)
    def _():
        spread([acc_ref[j : j + 1] for j in range(len(terms))], out_ref)


def around(ref, index, halo):
    low_ref, high_ref, left_ref, right_ref = halo
    step = pl.program_id(0)
    last = pl.num_programs(0) - 1
    line = pl.ds(step, 1)

    def plane(place):
        return ref[index + (place,)].astype(F32)

    def outside(axis, edge, value):
        return jnp.where(lax.axis_index(axis) == edge, 0.0, value)

    low = outside("row", 0, low_ref[...])
    high = outside("row", lax.axis_size("row") - 1, high_ref[...])
    left = outside("col", 0, left_ref[line, :])
    right = outside("col", lax.axis_size("col") - 1, right_ref[line, :])
    before = jnp.where(step == 0, low, plane(jnp.maximum(step - 1, 0)))
    after = jnp.where(step == last, high, plane(jnp.minimum(step + 1, last)))
    return plane(step), before, after, left, right


def operator_first_body(kept_ref, perm_ref, *refs):
    halo, perm_halo = refs[:4], refs[4:8]
    res_ref, image_ref, out_ref, acc_ref = refs[8:]
    fields = around(kept_ref, (0,), halo)
    image = stencil(fields, around(perm_ref, (), perm_halo))
    own = fields[0]
    residual = res_ref[0]
    image_ref[0] = image
    add_sums((own * image, residual * own, image * image, residual * image), out_ref, acc_ref)


def operator_next_body(first_ref, beta_ref, kept_ref, perm_ref, *refs):
    halo, old, perm_halo = refs[:4], refs[4:8], refs[8:12]
    res_ref, way_ref, image_ref, out_ref, acc_ref = refs[12:]
    beta = gathered(beta_ref, 0) / gathered(first_ref, 0)
    fields = [
        new - beta * other
        for new, other in zip(around(kept_ref, (1,), halo), around(kept_ref, (0,), old))
    ]
    image = stencil(fields, around(perm_ref, (), perm_halo))
    own = fields[0]
    way_ref[0] = own
    image_ref[0] = image
    add_sums((own * image, res_ref[0] * own), out_ref, acc_ref)


def last_body(first_ref, sums_ref, old_ref, way_ref, res_ref, image_ref, sol_ref, out_ref):
    alpha = gathered(first_ref, 1) / gathered(first_ref, 0)
    later = gathered(sums_ref, 1) / gathered(sums_ref, 0)
    sol_ref[0] = alpha * old_ref[0, 0] + later * way_ref[0]
    out_ref[0] = res_ref[0] - later * image_ref[0]


def exchange(blocks):
    return lax.all_to_all(blocks, BOTH, split_axis=0, concat_axis=0, tiled=True)


def add_up(partial):
    return exchange(partial)


def neighbours(low, high, left, right):
    found = []
    for axis, first, last in (("row", low, high), ("col", left, right)):
        count = lax.axis_size(axis)
        forward = [(i, (i + 1) % count) for i in range(count)]
        backward = [(target, source) for source, target in forward]
        found.append(lax.ppermute(last, axis, forward))
        found.append(lax.ppermute(first, axis, backward))
    return found


def tiled_local(right_side, permeability, lift_weight, spectral_weight, mix_weight, proj_weight):
    rows, cols, depth = right_side.shape
    n_row = lax.axis_size("row")
    n_col = lax.axis_size("col")
    count = n_row * n_col
    cells = float(rows * n_row * cols * n_col * depth)
    freq = KX // n_col
    deep_forward, deep_back = (jnp.asarray(t) for t in deep_tables(n_row, depth))
    col_forward, col_back = (jnp.asarray(t) for t in column_tables(n_col, cols))
    lift_weight = GAIN * lift_weight.T
    mix_weight = jnp.where(jnp.arange(CHANNELS + 1) < CHANNELS, 0.5, GAIN) * mix_weight
    proj_weight = jnp.where(jnp.arange(CHANNELS + 1) < CHANNELS, 0.5 / GAIN, 1.0) * proj_weight
    field = shape(rows, cols, depth)
    field_bytes = 4 * rows * cols * depth
    partial = shape(count, SUBLANES, LANES)
    channels = shape(rows, CHANNELS, depth, cols)
    spectra = shape(count, rows, SUBLANES, LANES)
    spectra_bytes = 4 * count * rows * SUBLANES * LANES
    smem = whole(pltpu.SMEM)
    vmem = whole()
    anywhere = whole(pl.ANY)
    plane = pl.BlockSpec((1, cols, depth), lambda i: (i, 0, 0))
    spectra_block = pl.BlockSpec((count, 1, SUBLANES, LANES), lambda i: (0, i, 0, 0))
    point_block = pl.BlockSpec((1, CHANNELS, depth, cols), lambda i: (i, 0, 0, 0))
    kept_shape = shape(ITERS, rows, cols, depth)
    lift_flops = 2.0e9
    back_flops = 2.0e9

    weight_shape = (freq, CHANNELS, SUBLANES, LANES)
    own, *weights = call(
        weight_body,
        (shape(*weight_shape),) * n_col,
        [vmem],
        (vmem,) * n_col,
        scratch=[pltpu.VMEM((n_col,) + weight_shape, F32)],
        moved=8 * spectral_weight.size,
    )(spectral_weight)
    weights = [own] + [
        lax.ppermute(part, "col", [(i, (i + shift + 1) % n_col) for i in range(n_col)])
        for shift, part in enumerate(weights)
    ]
    edge_shapes = (shape(cols, depth),) * 2 + (shape(rows, depth),) * 2
    squares, *perm_edges = call(
        squares_body,
        (partial,) + edge_shapes,
        [vmem, vmem, anywhere],
        (vmem,) * 5,
        moved=2 * field_bytes,
    )(right_side, permeability, own)
    squares = add_up(squares)
    perm_halo = neighbours(*perm_edges)
    acc_scratch = pltpu.VMEM((SUBLANES, LANES), F32)
    zt_scratch = pltpu.VMEM((2 * KZ * CHANNELS, cols), F32)

    def points(lifted, part, before, after):
        first = part * rows // 2
        half_block = pl.BlockSpec((1, CHANNELS, depth, cols), lambda i: (first + i, 0, 0, 0))
        return call(
            point_body,
            channels,
            [smem, half_block, anywhere, anywhere],
            half_block,
            grid=(rows // 2,),
            flops=2.5e9,
            moved=16 * field_bytes,
            alias={2: 0} if part else None,
            limit=12,
        )(mix_weight, lifted, before, after)

    def modes(received, before):
        places = rows * n_row
        tiles = lambda size: pltpu.VMEM((size, SUBLANES, LANES), F32)
        return call(
            functools.partial(modes_body, cells, n_row, n_col),
            spectra,
            [vmem] + [anywhere] * (n_col + 1),
            vmem,
            scratch=[
                pltpu.VMEM((n_col,) + weight_shape, F32),
                pltpu.SemaphoreType.DMA((n_col,)),
                tiles(places),
                tiles(places),
                tiles(KX),
                tiles(KX),
            ],
            moved=2 * spectra_bytes + 4 * spectral_weight.size,
            near=(0,),
        )(received, *weights, before)

    def mixed_modes(blocks, lifted):
        received = exchange(blocks)
        point = points(lifted, 0, right_side, right_side)
        blocks = modes(received, point)
        received = exchange(blocks)
        point = points(lifted, 1, point, blocks)
        return received, point

    blocks, lifted = call(
        functools.partial(lift_first_body, cells),
        (spectra, channels),
        [smem, vmem, plane, plane, vmem, vmem] + [anywhere] * n_col,
        (spectra_block, point_block),
        limit=16,
        grid=(rows,),
        scratch=[zt_scratch],
        flops=lift_flops,
        moved=2 * field_bytes + spectra_bytes,
    )(lift_weight, squares, right_side, permeability, deep_forward, col_forward, *weights)
    received, point = mixed_modes(blocks, lifted)
    kept, *edges = call(
        functools.partial(back_first_body, cells),
        (kept_shape,) + edge_shapes,
        [smem, vmem, spectra_block, point_block, vmem, vmem] + [anywhere] * 4,
        (pl.BlockSpec((1, 1, cols, depth), lambda i: (0, i, 0, 0)),) + (vmem,) * 4,
        grid=(rows,),
        scratch=[zt_scratch],
        limit=12,
        flops=back_flops,
        moved=18 * field_bytes,
    )(proj_weight, squares, received, point, col_back, deep_back, *perm_halo)

    old_halo = neighbours(*edges)
    kept_first = pl.BlockSpec((1, rows, cols, depth), lambda i: (0, 0, 0, 0))
    args = (kept, permeability, *old_halo, *perm_halo, right_side)
    image, sums = call(
        operator_first_body,
        (field, partial),
        [kept_first] + [vmem] * 9 + [plane],
        (plane, vmem),
        grid=(rows,),
        scratch=[acc_scratch],
        moved=9 * field_bytes,
        near=range(1, 11),
        loose=True,
    )(*args)
    sums = add_up(sums)

    blocks, lifted, residual = call(
        functools.partial(lift_next_body, cells),
        (spectra, channels, field),
        [smem, vmem, vmem, plane, plane, plane, vmem, vmem],
        (spectra_block, point_block, plane),
        limit=16,
        near=(4,),
        grid=(rows,),
        scratch=[zt_scratch],
        flops=lift_flops,
        moved=4 * field_bytes + spectra_bytes,
    )(lift_weight, squares, sums, right_side, image, permeability, deep_forward, col_forward)
    received, point = mixed_modes(blocks, lifted)
    kept, beta, *edges = call(
        functools.partial(back_next_body, cells),
        (kept_shape, partial) + edge_shapes,
        [smem, vmem, vmem, spectra_block, point_block, vmem, vmem, plane, whole(pl.ANY)],
        (pl.BlockSpec((1, 1, cols, depth), lambda i: (1, i, 0, 0)),) + (vmem,) * 5,
        grid=(rows,),
        limit=12,
        scratch=[zt_scratch, acc_scratch],
        flops=back_flops,
        moved=19 * field_bytes,
        alias={8: 0},
    )(proj_weight, squares, sums, received, point, col_back, deep_back, image, kept)

    beta = add_up(beta)
    halo = neighbours(*edges)
    args = (sums, beta, kept, permeability, *halo, *old_halo, *perm_halo, residual)
    way, image, later = call(
        operator_next_body,
        (field, field, partial),
        [vmem] * 16 + [plane],
        (plane, plane, vmem),
        grid=(rows,),
        scratch=[acc_scratch],
        near=(0, 1) + tuple(range(3, 17)),
        loose=True,
        moved=11 * field_bytes,
    )(*args)
    later = add_up(later)
    answer, residual = call(
        last_body,
        (field, field),
        [vmem, vmem, pl.BlockSpec((1, 1, cols, depth), lambda i: (0, i, 0, 0)), plane, plane, plane],
        (plane, plane),
        grid=(rows,),
        moved=6 * field_bytes,
        near=(0, 1, 3, 4, 5),
        loose=True,
    )(sums, later, kept, way, residual, image)
    return (answer, residual, kept)


def fits_tiles(mesh, block):
    rows, cols, depth = block
    n_row, n_col = mesh.shape["row"], mesh.shape["col"]
    return (
        ITERS == 2
        and KZ == n_row * (LANES // (2 * CHANNELS))
        and KY == n_col * SUBLANES
        and KX % n_col == 0
        and cols == LANES
        and depth % LANES == 0
        and rows * n_row >= KX
    )


def solution(mesh):
    placed = (
        P("row", "col", None),
        P("row", "col", None),
        P(),
        P(None, "row", None, None, "col"),
        P(),
        P(),
    )

    def run(right_side, *others):
        rows, cols, depth = right_side.shape
        block = (rows // mesh.shape["row"], cols // mesh.shape["col"], depth)
        return jax.shard_map(
            tiled_local if fits_tiles(mesh, block) else local,
            mesh=mesh,
            in_specs=placed,
            out_specs=(P("row", "col", None), P("row", "col", None), P(None, "row", "col", None)),
            check_vma=False,
        )(right_side, *others)

    return run
```

```python
import functools
import math

import jax
import jax.numpy as jnp
import ml_dtypes
import numpy as np
from jax import lax
from jax.experimental import pallas as pl
from jax.experimental.pallas import tpu as pltpu
from jax.sharding import PartitionSpec as P

CHANNELS = 16
KX = 16
KY = 32
KZ = 32
ITERS = 2


HIGHEST = lax.Precision.HIGHEST


def with_halo(block, sides, width):
    for axis, dim in sides:
        count = lax.axis_size(axis)
        forward = [(i, i + 1) for i in range(count - 1)]
        backward = [(target, source) for source, target in forward]
        low = lax.ppermute(
            lax.slice_in_dim(block, block.shape[dim] - width, None, axis=dim), axis, forward
        )
        high = lax.ppermute(lax.slice_in_dim(block, 0, width, axis=dim), axis, backward)
        block = jnp.concatenate([low, block, high], axis=dim)
    return block


def einsum_high(form, left, right):
    return jnp.einsum(form, left, right, precision=HIGHEST)


def harmonic(first, second):
    return 2.0 * first * second / (first + second)


def wave_table(freqs, places, length):
    turns = freqs[None, :] * places[:, None] % length
    angle = turns.astype(jnp.float32) * (2.0 * jnp.pi / length)
    return (jnp.cos(angle), jnp.sin(angle))


def signed_freqs(count):
    return jnp.arange(count, dtype=jnp.int32) - count // 2


def face_arrays(permeability):
    padded = with_halo(permeability, (("row", 0), ("col", 1)), 1).astype(jnp.float32)
    own = permeability.astype(jnp.float32)
    edged = jnp.pad(own, ((1, 1), (1, 1), (0, 0)), mode="edge")
    padded = jnp.where(padded > 0.0, padded, edged)
    first = harmonic(padded[:-1, 1:-1], padded[1:, 1:-1])
    second = harmonic(padded[1:-1, :-1], padded[1:-1, 1:])
    deep = jnp.pad(own, ((0, 0), (0, 0), (1, 1)), mode="edge")
    third = harmonic(deep[:, :, :-1], deep[:, :, 1:])
    return ((first, second, third), jnp.log(own))


def apply_operator(field, faces):
    first, second, third = faces
    padded = with_halo(field, (("row", 0), ("col", 1)), 1)
    padded = jnp.pad(padded, ((0, 0), (0, 0), (1, 1)))
    total = first[:-1] * (field - padded[:-2, 1:-1, 1:-1])
    total = total + first[1:] * (field - padded[2:, 1:-1, 1:-1])
    total = total + second[:, :-1] * (field - padded[1:-1, :-2, 1:-1])
    total = total + second[:, 1:] * (field - padded[1:-1, 2:, 1:-1])
    total = total + third[:, :, :-1] * (field - padded[1:-1, 1:-1, :-2])
    total = total + third[:, :, 1:] * (field - padded[1:-1, 1:-1, 2:])
    return total


def global_squares(field):
    return lax.psum(jnp.sum(field * field), ("row", "col"))


def mix_modes(real_in, imag_in, spectral_weight, deep_count, freq_count):
    block = spectral_weight.reshape(2, deep_count, CHANNELS, CHANNELS, freq_count, KY)
    real_out = einsum_high("kcfg,kcofg->kofg", real_in, block[0]) - einsum_high(
        "kcfg,kcofg->kofg", imag_in, block[1]
    )
    imag_out = einsum_high("kcfg,kcofg->kofg", imag_in, block[0]) + einsum_high(
        "kcfg,kcofg->kofg", real_in, block[1]
    )
    return (real_out, imag_out)


def spectral_transpose(real_part, imag_part, spectral_weight, grid):
    rows, cols, n_row, n_col, row_id, col_id = grid
    full_rows = rows * n_row
    full_cols = cols * n_col
    cosine_rows, sine_rows = wave_table(
        signed_freqs(KX), jnp.arange(full_rows, dtype=jnp.int32), full_rows
    )
    cosine_cols, sine_cols = wave_table(
        signed_freqs(KY), jnp.arange(full_cols, dtype=jnp.int32), full_cols
    )
    real_part, imag_part = (
        lax.all_to_all(real_part, "row", split_axis=0, concat_axis=1, tiled=True),
        lax.all_to_all(imag_part, "row", split_axis=0, concat_axis=1, tiled=True),
    )
    first_real = einsum_high("qxy,xf->qfy", real_part, cosine_rows) + einsum_high(
        "qxy,xf->qfy", imag_part, sine_rows
    )
    first_imag = einsum_high("qxy,xf->qfy", imag_part, cosine_rows) - einsum_high(
        "qxy,xf->qfy", real_part, sine_rows
    )
    first_real, first_imag = (
        lax.all_to_all(first_real, "col", split_axis=1, concat_axis=2, tiled=True),
        lax.all_to_all(first_imag, "col", split_axis=1, concat_axis=2, tiled=True),
    )
    second_real = einsum_high("qfy,yg->qfg", first_real, cosine_cols) + einsum_high(
        "qfy,yg->qfg", first_imag, sine_cols
    )
    second_imag = einsum_high("qfy,yg->qfg", first_imag, cosine_cols) - einsum_high(
        "qfy,yg->qfg", first_real, sine_cols
    )
    deep_count = KZ // n_row
    freq_count = KX // n_col
    shape_in = (deep_count, CHANNELS, freq_count, KY)
    mixed_real, mixed_imag = mix_modes(
        second_real.reshape(shape_in),
        second_imag.reshape(shape_in),
        spectral_weight,
        deep_count,
        freq_count,
    )
    shape_out = (deep_count * CHANNELS, freq_count, KY)
    mixed_real = mixed_real.reshape(shape_out)
    mixed_imag = mixed_imag.reshape(shape_out)
    back_real = einsum_high("qfg,yg->qfy", mixed_real, cosine_cols) - einsum_high(
        "qfg,yg->qfy", mixed_imag, sine_cols
    )
    back_imag = einsum_high("qfg,yg->qfy", mixed_imag, cosine_cols) + einsum_high(
        "qfg,yg->qfy", mixed_real, sine_cols
    )
    back_real, back_imag = (
        lax.all_to_all(back_real, "col", split_axis=2, concat_axis=1, tiled=True),
        lax.all_to_all(back_imag, "col", split_axis=2, concat_axis=1, tiled=True),
    )
    out_real = einsum_high("qfy,xf->qxy", back_real, cosine_rows) - einsum_high(
        "qfy,xf->qxy", back_imag, sine_rows
    )
    out_imag = einsum_high("qfy,xf->qxy", back_imag, cosine_rows) + einsum_high(
        "qfy,xf->qxy", back_real, sine_rows
    )
    out_real, out_imag = (
        lax.all_to_all(out_real, "row", split_axis=1, concat_axis=0, tiled=True),
        lax.all_to_all(out_imag, "row", split_axis=1, concat_axis=0, tiled=True),
    )
    return (out_real, out_imag)


def precondition(residual, squares_total, log_perm, weights, grid, cells):
    lift_weight, spectral_weight, mix_weight, proj_weight = weights
    rows, cols, depth = residual.shape
    scale = jnp.sqrt(squares_total / cells + 1e-06)
    scaled = residual / scale
    lifted = jax.nn.gelu(
        lift_weight[:, 0, None, None, None] * scaled[None]
        + lift_weight[:, 1, None, None, None] * log_perm[None]
        + lift_weight[:, 2, None, None, None]
    )
    cosine_deep, sine_deep = wave_table(
        jnp.arange(KZ, dtype=jnp.int32), jnp.arange(depth, dtype=jnp.int32), depth
    )
    real_part = einsum_high("cxyz,zk->kcxy", lifted, cosine_deep).reshape(KZ * CHANNELS, rows, cols)
    imag_part = -einsum_high("cxyz,zk->kcxy", lifted, sine_deep).reshape(KZ * CHANNELS, rows, cols)
    out_real, out_imag = spectral_transpose(real_part, imag_part, spectral_weight, grid)
    out_real = out_real.reshape(KZ, CHANNELS, rows, cols)
    out_imag = out_imag.reshape(KZ, CHANNELS, rows, cols)
    spatial = (
        einsum_high("kcxy,zk->cxyz", out_real, cosine_deep)
        - einsum_high("kcxy,zk->cxyz", out_imag, sine_deep)
    ) / cells
    point = (
        einsum_high("oc,cxyz->oxyz", mix_weight[:, :CHANNELS], lifted)
        + mix_weight[:, CHANNELS, None, None, None]
    )
    hidden = jax.nn.gelu(spatial + point)
    return scale * (
        einsum_high("o,oxyz->xyz", proj_weight[:CHANNELS], hidden) + proj_weight[CHANNELS]
    )


def local(right_side, permeability, lift_weight, spectral_weight, mix_weight, proj_weight):
    rows, cols, depth = right_side.shape
    n_row = lax.axis_size("row")
    n_col = lax.axis_size("col")
    grid = (rows, cols, n_row, n_col, lax.axis_index("row"), lax.axis_index("col"))
    cells = float(rows * n_row * cols * n_col * depth)
    faces, log_perm = face_arrays(permeability)
    weights = (lift_weight, spectral_weight, mix_weight, proj_weight)

    def precond(residual, squares_total):
        return precondition(residual, squares_total, log_perm, weights, grid, cells)

    solution = jnp.zeros_like(right_side)
    residual = right_side
    kept = []
    update = precond(residual, global_squares(residual))
    kept.append(update)
    direction = update
    for step in range(ITERS):
        image = apply_operator(direction, faces)
        curvature, along = lax.psum(
            (jnp.sum(direction * image), jnp.sum(residual * direction)), ("row", "col")
        )
        alpha = along / curvature
        solution = solution + alpha * direction
        residual = residual - alpha * image
        if step + 1 < ITERS:
            update = precond(residual, global_squares(residual))
            kept.append(update)
            beta = lax.psum(jnp.sum(update * image), ("row", "col")) / curvature
            direction = update - beta * direction
    return (solution, residual, jnp.stack(kept))


LANES = 128
SUBLANES = 8
BOTH = ("row", "col")
F32 = jnp.float32
BF16 = jnp.bfloat16


def split_table(table):
    high = table.astype(ml_dtypes.bfloat16)
    low = (table - high.astype(np.float64)).astype(ml_dtypes.bfloat16)
    return high, low


def split(value):
    high = value.astype(BF16)
    return high, (value - high.astype(F32)).astype(BF16)


def split_three(value):
    high = value.astype(BF16).astype(F32)
    rest = value - high
    middle = rest.astype(BF16).astype(F32)
    return high, middle, rest - middle


def matmul(left, right):
    return jnp.dot(left, right, preferred_element_type=F32)


def matmul_nt(left, right):
    return lax.dot_general(left, right, (((1,), (1,)), ((), ())), preferred_element_type=F32)


def angles(freqs, places, length):
    turns = np.multiply.outer(freqs, places) % length
    return turns * (2.0 * np.pi / length)


def deep_order(n_row):
    count = KZ // n_row
    order = [
        (part, row * count + place)
        for row in range(n_row)
        for part in range(2)
        for place in range(count)
    ]
    return np.array(order)


def deep_tables(n_row, depth):
    order = deep_order(n_row)
    angle = angles(order[:, 1], np.arange(depth), depth)
    wave = np.where(order[:, :1] == 0, np.cos(angle), -np.sin(angle))
    high, low = split_table(wave)
    return np.concatenate([high, low], 0), np.concatenate([high.T, high.T, high.T, low.T], 1)


def column_tables(n_col, cols):
    freqs = np.arange(KY) - KY // 2
    forward = []
    back = []
    for place in range(n_col):
        angle = angles(freqs, place * cols + np.arange(cols), n_col * cols)
        both = np.concatenate([np.cos(angle), np.sin(angle)], 0)
        high, low = split_table(both)
        forward.append(
            np.concatenate(
                [
                    np.concatenate([high, high], 1),
                    np.concatenate([low, np.zeros_like(low)], 1),
                ],
                0,
            )
        )
        both = np.concatenate([np.cos(angle), np.sin(angle)], 0)
        high, low = split_table(both)
        back.append(
            np.concatenate(
                [
                    np.concatenate([high, low], 1),
                    np.concatenate([high, low], 1),
                    np.concatenate([high, np.zeros_like(low)], 1),
                ],
                0,
            )
        )
    return np.stack(forward), np.stack(back)


GAIN = (math.sqrt(2.0 / math.pi) * 0.044715) ** (1.0 / 3.0)
LINEAR = math.sqrt(2.0 / math.pi) / GAIN


def scaled_gelu(value):
    return value + value * jnp.tanh(value * (value * value + LINEAR))


def call(body, outs, in_specs, out_specs, grid=(), scratch=(), flops=0, moved=0, alias=None, limit=8, near=(), loose=()):
    single = not isinstance(outs, tuple)
    outs = (outs,) if single else outs
    out_specs = (out_specs,) if single else out_specs
    run = pl.pallas_call(
        body,
        out_shape=tuple(
            out if place in loose or out.size <= 2**16 else pltpu.HBM(out.shape, out.dtype)
            for place, out in enumerate(outs)
        ),
        grid=grid,
        in_specs=in_specs,
        out_specs=out_specs,
        scratch_shapes=list(scratch),
        input_output_aliases=alias or {},
        compiler_params=pltpu.CompilerParams(vmem_limit_bytes=limit * 1024 * 1024),
        cost_estimate=pl.CostEstimate(
            flops=int(flops), bytes_accessed=int(moved), transcendentals=0
        ),
    )

    def wrapped(*args):
        held = [
            arg
            if place in near or spec.memory_space == pltpu.SMEM
            else pltpu.with_memory_space_constraint(arg, pltpu.HBM)
            for place, (arg, spec) in enumerate(zip(args, in_specs))
        ]
        found = run(*held)
        return found[0] if single else found

    return wrapped


def whole(memory=pltpu.VMEM):
    return pl.BlockSpec(memory_space=memory)


def shape(*dims):
    return jax.ShapeDtypeStruct(dims, F32)


def lane_sums(value):
    folded = jnp.sum(value.reshape(-1, SUBLANES, value.shape[-1]), axis=0)
    folded = sum(
        folded[:, start : start + LANES] for start in range(0, folded.shape[1], LANES)
    )
    return jnp.sum(folded, axis=0, keepdims=True)


def spread(rows, ref):
    rows = rows + [jnp.zeros_like(rows[0])] * (SUBLANES - len(rows))
    ref[...] = jnp.broadcast_to(jnp.concatenate(rows, 0)[None], ref.shape)


def gathered(ref, row):
    total = jnp.sum(ref[...], axis=0)
    return jnp.sum(total[row : row + 1], axis=1, keepdims=True)


def squares_body(field_ref, perm_ref, _, out_ref, low_ref, high_ref, left_ref, right_ref):
    total = field_ref[0] * field_ref[0]
    for place in range(1, field_ref.shape[0]):
        total = total + field_ref[place] * field_ref[place]
    spread([lane_sums(total)], out_ref)
    rows, cols, _ = perm_ref.shape
    low_ref[...] = perm_ref[0].astype(F32)
    high_ref[...] = perm_ref[rows - 1].astype(F32)
    for place in range(rows):
        plane = perm_ref[place].astype(F32)
        left_ref[place : place + 1, :] = plane[:1]
        right_ref[place : place + 1, :] = plane[cols - 1 :]


def weight_body(weight_ref, *refs):
    *out_refs, hold_ref = refs
    groups, freq, channels, fine, _ = hold_ref.shape
    parts, deep, _, outs, modes = weight_ref.shape
    for channel in range(channels):
        block = weight_ref[:, :, channel].reshape(parts * deep * outs, modes)
        block = block.T.reshape(freq, groups, fine, parts * deep * outs)
        for group in range(groups):
            hold_ref[group, :, channel] = block[:, group]
    place = lax.axis_index("col")
    for shift, out_ref in enumerate(out_refs):
        out_ref[...] = hold_ref[lax.rem(place + shift, groups)]


def scale_of(total, cells):
    return jnp.sqrt(total / cells + 1e-06)


def lift_channel(weight_ref, channel, scaled, log_perm):
    return scaled_gelu(
        weight_ref[0, channel] * scaled
        + (weight_ref[1, channel] * log_perm + weight_ref[2, channel])
    )


def transform(lift_ref, deep_ref, col_ref, scaled, log_perm, spectra_ref, lifted_ref, zt_ref):
    half = 2 * KZ
    cols = scaled.shape[1]
    for channel in range(0, CHANNELS, 2):
        pair = [lift_channel(lift_ref, channel + j, scaled, log_perm) for j in range(2)]
        for j in range(2):
            lifted_ref[0, channel + j] = pair[j]
        high, low = split(jnp.concatenate(pair, 1))
        part = matmul(deep_ref[...], high)
        part = part[:half] + part[half:] + matmul(deep_ref[:half], low)
        for j in range(2):
            zt_ref[pl.ds(channel + j, half, stride=CHANNELS), :] = part[:, j * cols : (j + 1) * cols]
    groups = half * CHANNELS // LANES
    part = matmul_nt(col_ref[lax.axis_index("col")], jnp.concatenate(split(zt_ref[...]), 1))
    part = part[: 2 * KY] + part[2 * KY :]
    lane = lax.broadcasted_iota(jnp.int32, (KY, LANES), 1)
    sign = jnp.where(lane < LANES // 2, 1.0, -1.0).astype(F32)
    n_col = KY // SUBLANES
    for row in range(groups):
        lanes = slice(row * LANES, (row + 1) * LANES)
        block = part[:KY, lanes] + pltpu.roll(part[KY:, lanes], LANES // 2, 1) * sign
        for col in range(n_col):
            spectra_ref[row * n_col + col, 0] = block[col * SUBLANES : (col + 1) * SUBLANES]


def lift_first_body(cells, lift_ref, sums_ref, res_ref, perm_ref, deep_ref, col_ref, *refs):
    spectra_ref, lifted_ref, zt_ref = refs[-3:]
    scale = scale_of(gathered(sums_ref, 0), cells)
    scaled = (res_ref[0] / scale).T
    log_perm = jnp.log(perm_ref[0].astype(F32)).T
    transform(lift_ref, deep_ref, col_ref, scaled, log_perm, spectra_ref, lifted_ref, zt_ref)


def next_scalars(first_ref, sums_ref):
    curvature = gathered(sums_ref, 0)
    alpha = gathered(sums_ref, 1) / curvature
    total = gathered(first_ref, 0) + alpha * (
        alpha * gathered(sums_ref, 2) - 2.0 * gathered(sums_ref, 3)
    )
    return curvature, alpha, jnp.maximum(total, 0.0)


def lift_next_body(cells, lift_ref, first_ref, sums_ref, res_ref, image_ref, perm_ref, deep_ref, col_ref, spectra_ref, lifted_ref, next_ref, zt_ref):
    _, alpha, total = next_scalars(first_ref, sums_ref)
    scale = scale_of(total, cells)
    residual = res_ref[0] - alpha * image_ref[0]
    next_ref[0] = residual
    scaled = (residual / scale).T
    log_perm = jnp.log(perm_ref[0].astype(F32)).T
    transform(lift_ref, deep_ref, col_ref, scaled, log_perm, spectra_ref, lifted_ref, zt_ref)


def point_body(mix_ref, lifted_ref, _, __, point_ref):
    size = 4 * SUBLANES
    group = 4

    def step(index, carry):
        lines = pl.ds(pl.multiple_of(index * size, size), size)
        for first in range(0, CHANNELS, group):
            sums = [mix_ref[first + j, CHANNELS] for j in range(group)]
            for channel in range(CHANNELS):
                lifted = lifted_ref[0, channel, lines, :]
                sums = [
                    total + mix_ref[first + j, channel] * lifted for j, total in enumerate(sums)
                ]
            for j, total in enumerate(sums):
                point_ref[0, first + j, lines, :] = total
        return carry

    lax.fori_loop(0, lifted_ref.shape[2] // size, step, 0)


def modes_body(cells, n_row, n_col, recv_ref, *refs):
    sources = refs[:n_col]
    _, out_ref, weight_ref, sems, field_ref, turned_ref, spec_ref, odd_ref = refs[n_col:]
    own = lax.axis_index("col")
    copies = [
        pltpu.make_async_copy(
            source, weight_ref.at[lax.rem(own + n_col - shift, n_col)], sems.at[shift]
        )
        for shift, source in enumerate(sources)
    ]
    for copy in copies:
        copy.start()
    rows = recv_ref.shape[1]
    places = n_row * rows
    tile = (SUBLANES, LANES)
    lane = lax.broadcasted_iota(jnp.int32, tile, 1)
    first = lane < LANES // 2
    sign = jnp.where(first, 1.0, -1.0).astype(F32)
    base = lane - lane % CHANNELS

    def turn(value):
        return pltpu.roll(value, LANES // 2, 1) * sign

    for row in range(n_row):
        for place in range(rows):
            value = recv_ref[row * n_col, place]
            for col in range(1, n_col):
                value = value + recv_ref[row * n_col + col, place]
            field_ref[row * rows + place] = value
    angle = 2.0 * np.pi / places
    half = KX // 2

    def weigh(coefs, ref):
        total = None
        for place, coef in enumerate(coefs):
            coef = float(coef)
            if abs(coef) < 1e-12:
                continue
            term = ref[place]
            if coef == -1.0:
                term = -term
            elif coef != 1.0:
                term = coef * term
            total = term if total is None else total + term
        return jnp.zeros(tile, F32) if total is None else total

    middle = places // 2
    for place in range(1, middle):
        value, mirror = field_ref[place], field_ref[places - place]
        field_ref[place] = value + mirror
        turned_ref[place] = turn(value - mirror)
    for freq in range(half + 1):
        turns = freq * np.arange(middle + 1) % places
        even = weigh(np.cos(angle * turns), field_ref)
        odd = weigh(np.concatenate([[0.0], np.sin(angle * turns[1:middle])]), turned_ref)
        if freq < half:
            spec_ref[half + freq] = even + odd
        if freq > 0:
            spec_ref[half - freq] = even - odd

    for copy in copies:
        copy.wait()
    share = KX // n_col
    for freq in range(KX):
        value = spec_ref[freq]
        same = [None, None]
        cross = [None, None]
        for channel in range(CHANNELS):
            wide = jnp.take_along_axis(value, base + channel, axis=1)
            weight = weight_ref[freq // share, freq % share, channel]
            for sums, factor in ((same, weight), (cross, pltpu.roll(weight, LANES // 2, 1))):
                term = factor * wide
                kept = sums[channel % 2]
                sums[channel % 2] = term if kept is None else kept + term
        same = same[0] + same[1]
        cross = cross[0] + cross[1]
        total = jnp.where(
            first,
            same - pltpu.roll(same, LANES // 2, 1),
            cross + pltpu.roll(cross, LANES // 2, 1),
        )
        field_ref[freq] = total
        turned_ref[freq] = -turn(total)
    gain = 0.5 / cells
    evens = [field_ref[half] * gain]
    odds = [None]
    for freq in range(1, half):
        evens.append((field_ref[half + freq] + field_ref[half - freq]) * gain)
        odds.append((turned_ref[half + freq] - turned_ref[half - freq]) * gain)
    evens.append(field_ref[0] * gain)
    odds.append(-turned_ref[0] * gain)
    for freq in range(half + 1):
        spec_ref[freq] = evens[freq]
        if freq > 0:
            odd_ref[freq] = odds[freq]

    def store(place, value):
        for col in range(n_col):
            out_ref[(place // rows) * n_col + col, place % rows] = value

    for place in range(places // 2 + 1):
        turns = place * np.arange(half + 1) % places
        even = weigh(np.cos(angle * turns), spec_ref)
        odd = weigh(np.sin(angle * turns), odd_ref)
        store(place, even + odd)
        if 0 < place < places // 2:
            store(places - place, even - odd)


def back_transform(recv_ref, point_ref, proj_ref, col_ref, deep_ref, wave_ref, scale):
    groups = 2 * KZ * CHANNELS // LANES
    n_col = KY // SUBLANES
    cols = col_ref.shape[2] // 2
    lane = lax.broadcasted_iota(jnp.int32, (KY, LANES), 1)
    sign = jnp.where(lane < LANES // 2, -1.0, 1.0).astype(F32)
    half = 2 * KZ
    pieces = []
    for row in range(groups):
        value = recv_ref[row * n_col : (row + 1) * n_col, 0].reshape(KY, LANES)
        turned = pltpu.roll(value, LANES // 2, 1) * sign
        both = jnp.concatenate([value, turned], 0)
        pieces.append(jnp.concatenate(split_three(both), 0).T.astype(BF16))
    part = matmul(jnp.concatenate(pieces, 0), col_ref[lax.axis_index("col")])
    wave_ref[...] = part[:, :cols] + part[:, cols:]
    total = None
    for out in range(0, CHANNELS, 2):
        waves = jnp.concatenate(
            [wave_ref[pl.ds(out + j, half, stride=CHANNELS), :] for j in range(2)], 1
        )
        high, middle, low = (part.astype(BF16) for part in split_three(waves))
        spatial = matmul(deep_ref[...], jnp.concatenate([high, middle, low, high], 0))
        for j in range(2):
            hidden = scaled_gelu(spatial[:, j * cols : (j + 1) * cols] + point_ref[0, out + j])
            term = proj_ref[out + j] * hidden
            total = term if total is None else total + term
    return (scale * (total + proj_ref[CHANNELS])).T


def put_edges(update, field_ref, low_ref, high_ref, left_ref, right_ref):
    step = pl.program_id(0)
    field_ref[0] = update
    left_ref[pl.ds(step, 1), :] = update[:1]
    right_ref[pl.ds(step, 1), :] = update[update.shape[0] - 1 :]

    @pl.when(step == 0)
    def _():
        low_ref[...] = update

    @pl.when(step == pl.num_programs(0) - 1)
    def _():
        high_ref[...] = update


def back_first_body(cells, proj_ref, sums_ref, recv_ref, point_ref, col_ref, deep_ref, *refs):
    kept_ref, *edges, wave_ref = refs[4:]
    scale = scale_of(gathered(sums_ref, 0), cells)
    update = back_transform(
        recv_ref, point_ref, proj_ref, col_ref, deep_ref, wave_ref, scale
    )
    kept_ref[0, 0] = update
    put_edges(update, *edges)


def back_next_body(cells, proj_ref, first_ref, sums_ref, recv_ref, point_ref, col_ref, deep_ref, _, kept_ref, *refs):
    *edges, wave_ref = refs
    _, _, total = next_scalars(first_ref, sums_ref)
    update = back_transform(
        recv_ref, point_ref, proj_ref, col_ref, deep_ref, wave_ref, scale_of(total, cells)
    )
    kept_ref[0, 0] = update
    put_edges(update, *edges)


def stencil(fields, perms):
    own, before, after, left, right = fields
    cols, depth = own.shape
    line = lax.broadcasted_iota(jnp.int32, (cols, depth), 0)
    deep = lax.broadcasted_iota(jnp.int32, (cols, depth), 1)

    def sides(array, before, after, left, right, first, last):
        return (
            before,
            after,
            jnp.where(line == 0, left, pltpu.roll(array, 1, 0)),
            jnp.where(line == cols - 1, right, pltpu.roll(array, cols - 1, 0)),
            jnp.where(deep == 0, first, pltpu.roll(array, 1, 1)),
            jnp.where(deep == depth - 1, last, pltpu.roll(array, depth - 1, 1)),
        )

    perm, *others = perms
    others = [
        jnp.where(other > 0.0, other, edge)
        for other, edge in zip(others, (perm, perm, perm[:1], perm[cols - 1 :]))
    ]
    total = None
    for other, conductance in zip(
        sides(own, before, after, left, right, 0.0, 0.0), sides(perm, *others, perm, perm)
    ):
        term = harmonic(perm, conductance) * (own - other)
        total = term if total is None else total + term
    return total


def add_sums(terms, out_ref, acc_ref):
    step = pl.program_id(0)

    @pl.when(step == 0)
    def _():
        acc_ref[...] = jnp.zeros_like(acc_ref)

    for j, term in enumerate(terms):
        acc_ref[j : j + 1] += lane_sums(term)

    @pl.when(step == pl.num_programs(0) - 1)
    def _():
        spread([acc_ref[j : j + 1] for j in range(len(terms))], out_ref)


def around(ref, index, halo):
    low_ref, high_ref, left_ref, right_ref = halo
    step = pl.program_id(0)
    last = pl.num_programs(0) - 1
    line = pl.ds(step, 1)

    def plane(place):
        return ref[index + (place,)].astype(F32)

    def outside(axis, edge, value):
        return jnp.where(lax.axis_index(axis) == edge, 0.0, value)

    low = outside("row", 0, low_ref[...])
    high = outside("row", lax.axis_size("row") - 1, high_ref[...])
    left = outside("col", 0, left_ref[line, :])
    right = outside("col", lax.axis_size("col") - 1, right_ref[line, :])
    before = jnp.where(step == 0, low, plane(jnp.maximum(step - 1, 0)))
    after = jnp.where(step == last, high, plane(jnp.minimum(step + 1, last)))
    return plane(step), before, after, left, right


def operator_first_body(field_ref, perm_ref, *refs):
    halo, perm_halo = refs[:4], refs[4:8]
    res_ref, image_ref, out_ref, acc_ref = refs[8:]
    fields = around(field_ref, (), halo)
    image = stencil(fields, around(perm_ref, (), perm_halo))
    own = fields[0]
    residual = res_ref[0]
    image_ref[0] = image
    add_sums((own * image, residual * own, image * image, residual * image), out_ref, acc_ref)


def operator_next_body(cells, first_ref, sums_ref, field_ref, old_ref, perm_ref, *refs):
    halo, old, perm_halo = refs[:4], refs[4:8], refs[8:12]
    res_ref, before_ref, way_ref, image_ref, out_ref, acc_ref = refs[12:]
    _, _, total = next_scalars(first_ref, sums_ref)
    factor = scale_of(total, cells) / scale_of(gathered(first_ref, 0), cells)
    old = around(old_ref, (), old)
    fields = [new - factor * other for new, other in zip(around(field_ref, (), halo), old)]
    image = stencil(fields, around(perm_ref, (), perm_halo))
    own = fields[0]
    residual = res_ref[0]
    way_ref[0] = own
    image_ref[0] = image
    add_sums((own * image, own * before_ref[0], residual * own, residual * old[0]), out_ref, acc_ref)


def last_body(sums_ref, later_ref, old_ref, way_ref, res_ref, before_ref, image_ref, sol_ref, out_ref):
    curvature = gathered(sums_ref, 0)
    alpha = gathered(sums_ref, 1) / curvature
    cross = gathered(later_ref, 1)
    delta = cross / curvature
    along = gathered(later_ref, 2) - delta * gathered(later_ref, 3)
    later = along / (gathered(later_ref, 0) - delta * cross)
    sol_ref[0] = alpha * old_ref[0] + later * (way_ref[0] - delta * old_ref[0])
    out_ref[0] = res_ref[0] - later * (image_ref[0] - delta * before_ref[0])


def exchange(blocks):
    return lax.all_to_all(blocks, BOTH, split_axis=0, concat_axis=0, tiled=True)


def add_up(partial):
    return exchange(partial)


def neighbours(low, high, left, right):
    found = []
    for axis, first, last in (("row", low, high), ("col", left, right)):
        count = lax.axis_size(axis)
        forward = [(i, (i + 1) % count) for i in range(count)]
        backward = [(target, source) for source, target in forward]
        found.append(lax.ppermute(last, axis, forward))
        found.append(lax.ppermute(first, axis, backward))
    return found


def tiled_local(right_side, permeability, lift_weight, spectral_weight, mix_weight, proj_weight):
    rows, cols, depth = right_side.shape
    n_row = lax.axis_size("row")
    n_col = lax.axis_size("col")
    count = n_row * n_col
    cells = float(rows * n_row * cols * n_col * depth)
    freq = KX // n_col
    deep_forward, deep_back = (jnp.asarray(t) for t in deep_tables(n_row, depth))
    col_forward, col_back = (jnp.asarray(t) for t in column_tables(n_col, cols))
    lift_weight = GAIN * lift_weight.T
    mix_weight = jnp.where(jnp.arange(CHANNELS + 1) < CHANNELS, 0.5, GAIN) * mix_weight
    proj_weight = jnp.where(jnp.arange(CHANNELS + 1) < CHANNELS, 0.5 / GAIN, 1.0) * proj_weight
    field = shape(rows, cols, depth)
    field_bytes = 4 * rows * cols * depth
    partial = shape(count, SUBLANES, LANES)
    channels = shape(rows, CHANNELS, depth, cols)
    spectra = shape(count, rows, SUBLANES, LANES)
    spectra_bytes = 4 * count * rows * SUBLANES * LANES
    smem = whole(pltpu.SMEM)
    vmem = whole()
    anywhere = whole(pl.ANY)
    plane = pl.BlockSpec((1, cols, depth), lambda i: (i, 0, 0))
    spectra_block = pl.BlockSpec((count, 1, SUBLANES, LANES), lambda i: (0, i, 0, 0))
    point_block = pl.BlockSpec((1, CHANNELS, depth, cols), lambda i: (i, 0, 0, 0))
    kept_shape = shape(ITERS, rows, cols, depth)
    lift_flops = 2.0e9
    back_flops = 2.0e9

    weight_shape = (freq, CHANNELS, SUBLANES, LANES)
    own, *weights = call(
        weight_body,
        (shape(*weight_shape),) * n_col,
        [vmem],
        (vmem,) * n_col,
        scratch=[pltpu.VMEM((n_col,) + weight_shape, F32)],
        moved=8 * spectral_weight.size,
    )(spectral_weight)
    weights = [own] + [
        lax.ppermute(part, "col", [(i, (i + shift + 1) % n_col) for i in range(n_col)])
        for shift, part in enumerate(weights)
    ]
    edge_shapes = (shape(cols, depth),) * 2 + (shape(rows, depth),) * 2
    squares, *perm_edges = call(
        squares_body,
        (partial,) + edge_shapes,
        [vmem, vmem, anywhere],
        (vmem,) * 5,
        moved=2 * field_bytes,
    )(right_side, permeability, own)
    squares = add_up(squares)
    perm_halo = neighbours(*perm_edges)
    acc_scratch = pltpu.VMEM((SUBLANES, LANES), F32)
    zt_scratch = pltpu.VMEM((2 * KZ * CHANNELS, cols), F32)

    def points(lifted, part, before, after):
        first = part * rows // 2
        half_block = pl.BlockSpec((1, CHANNELS, depth, cols), lambda i: (first + i, 0, 0, 0))
        return call(
            point_body,
            channels,
            [smem, half_block, anywhere, anywhere],
            half_block,
            grid=(rows // 2,),
            flops=2.5e9,
            moved=16 * field_bytes,
            alias={2: 0} if part else None,
            limit=12,
        )(mix_weight, lifted, before, after)

    def modes(received, before):
        places = rows * n_row
        tiles = lambda size: pltpu.VMEM((size, SUBLANES, LANES), F32)
        return call(
            functools.partial(modes_body, cells, n_row, n_col),
            spectra,
            [vmem] + [anywhere] * (n_col + 1),
            vmem,
            scratch=[
                pltpu.VMEM((n_col,) + weight_shape, F32),
                pltpu.SemaphoreType.DMA((n_col,)),
                tiles(places),
                tiles(places),
                tiles(KX),
                tiles(KX),
            ],
            moved=2 * spectra_bytes + 4 * spectral_weight.size,
            near=(0,),
        )(received, *weights, before)

    def mixed_modes(blocks, lifted):
        received = exchange(blocks)
        point = points(lifted, 0, right_side, right_side)
        blocks = modes(received, point)
        received = exchange(blocks)
        point = points(lifted, 1, point, blocks)
        return received, point

    blocks, lifted = call(
        functools.partial(lift_first_body, cells),
        (spectra, channels),
        [smem, vmem, plane, plane, vmem, vmem] + [anywhere] * n_col,
        (spectra_block, point_block),
        limit=16,
        grid=(rows,),
        scratch=[zt_scratch],
        flops=lift_flops,
        moved=2 * field_bytes + spectra_bytes,
    )(lift_weight, squares, right_side, permeability, deep_forward, col_forward, *weights)
    received, point = mixed_modes(blocks, lifted)
    kept, old, *edges = call(
        functools.partial(back_first_body, cells),
        (kept_shape, field) + edge_shapes,
        [smem, vmem, spectra_block, point_block, vmem, vmem] + [anywhere] * 4,
        (pl.BlockSpec((1, 1, cols, depth), lambda i: (0, i, 0, 0)), plane) + (vmem,) * 4,
        near=(2, 6, 7, 8, 9),
        loose=(1,),
        grid=(rows,),
        scratch=[zt_scratch],
        limit=12,
        flops=back_flops,
        moved=18 * field_bytes,
    )(proj_weight, squares, received, point, col_back, deep_back, *perm_halo)

    old_halo = neighbours(*edges)
    args = (old, permeability, *old_halo, *perm_halo, right_side)
    image, sums = call(
        operator_first_body,
        (field, partial),
        [vmem] * 10 + [plane],
        (plane, vmem),
        grid=(rows,),
        scratch=[acc_scratch],
        moved=9 * field_bytes,
        near=range(11),
        loose=range(3),
    )(*args)
    sums = add_up(sums)

    blocks, lifted, residual = call(
        functools.partial(lift_next_body, cells),
        (spectra, channels, field),
        [smem, vmem, vmem, plane, plane, plane, vmem, vmem],
        (spectra_block, point_block, plane),
        limit=16,
        near=(4,),
        grid=(rows,),
        scratch=[zt_scratch],
        flops=lift_flops,
        moved=4 * field_bytes + spectra_bytes,
    )(lift_weight, squares, sums, right_side, image, permeability, deep_forward, col_forward)
    received, point = mixed_modes(blocks, lifted)
    kept, update, *edges = call(
        functools.partial(back_next_body, cells),
        (kept_shape, field) + edge_shapes,
        [smem, vmem, vmem, spectra_block, point_block, vmem, vmem, anywhere],
        (pl.BlockSpec((1, 1, cols, depth), lambda i: (1, i, 0, 0)), plane) + (vmem,) * 4,
        near=(3,),
        loose=(1,),
        grid=(rows,),
        limit=12,
        scratch=[zt_scratch],
        flops=back_flops,
        moved=19 * field_bytes,
        alias={7: 0},
    )(proj_weight, squares, sums, received, point, col_back, deep_back, kept)

    halo = neighbours(*edges)
    args = (squares, sums, update, old, permeability, *halo, *old_halo, *perm_halo, residual, image)
    way, last_image, later = call(
        functools.partial(operator_next_body, cells),
        (field, field, partial),
        [vmem] * 17 + [plane] * 2,
        (plane, plane, vmem),
        grid=(rows,),
        scratch=[acc_scratch],
        near=range(19),
        loose=range(3),
        moved=11 * field_bytes,
    )(*args)
    later = add_up(later)
    answer, residual = call(
        last_body,
        (field, field),
        [vmem, vmem] + [plane] * 5,
        (plane, plane),
        grid=(rows,),
        moved=6 * field_bytes,
        near=range(7),
        loose=range(3),
    )(sums, later, old, way, residual, image, last_image)
    return (answer, residual, kept)


def fits_tiles(mesh, block):
    rows, cols, depth = block
    n_row, n_col = mesh.shape["row"], mesh.shape["col"]
    return (
        ITERS == 2
        and KZ == n_row * (LANES // (2 * CHANNELS))
        and KY == n_col * SUBLANES
        and KX % n_col == 0
        and cols == LANES
        and depth % LANES == 0
        and rows * n_row >= KX
    )


def solution(mesh):
    placed = (
        P("row", "col", None),
        P("row", "col", None),
        P(),
        P(None, "row", None, None, "col"),
        P(),
        P(),
    )

    def run(right_side, *others):
        rows, cols, depth = right_side.shape
        block = (rows // mesh.shape["row"], cols // mesh.shape["col"], depth)
        return jax.shard_map(
            tiled_local if fits_tiles(mesh, block) else local,
            mesh=mesh,
            in_specs=placed,
            out_specs=(P("row", "col", None), P("row", "col", None), P(None, "row", "col", None)),
            check_vma=False,
        )(right_side, *others)

    return run
```

```python
import functools
import math

import jax
import jax.numpy as jnp
import ml_dtypes
import numpy as np
from jax import lax
from jax.experimental import pallas as pl
from jax.experimental.pallas import tpu as pltpu
from jax.sharding import PartitionSpec as P

CHANNELS = 16
KX = 16
KY = 32
KZ = 32
ITERS = 2


HIGHEST = lax.Precision.HIGHEST


def with_halo(block, sides, width):
    for axis, dim in sides:
        count = lax.axis_size(axis)
        forward = [(i, i + 1) for i in range(count - 1)]
        backward = [(target, source) for source, target in forward]
        low = lax.ppermute(
            lax.slice_in_dim(block, block.shape[dim] - width, None, axis=dim), axis, forward
        )
        high = lax.ppermute(lax.slice_in_dim(block, 0, width, axis=dim), axis, backward)
        block = jnp.concatenate([low, block, high], axis=dim)
    return block


def einsum_high(form, left, right):
    return jnp.einsum(form, left, right, precision=HIGHEST)


def harmonic(first, second):
    return 2.0 * first * second / (first + second)


def wave_table(freqs, places, length):
    turns = freqs[None, :] * places[:, None] % length
    angle = turns.astype(jnp.float32) * (2.0 * jnp.pi / length)
    return (jnp.cos(angle), jnp.sin(angle))


def signed_freqs(count):
    return jnp.arange(count, dtype=jnp.int32) - count // 2


def face_arrays(permeability):
    padded = with_halo(permeability, (("row", 0), ("col", 1)), 1).astype(jnp.float32)
    own = permeability.astype(jnp.float32)
    edged = jnp.pad(own, ((1, 1), (1, 1), (0, 0)), mode="edge")
    padded = jnp.where(padded > 0.0, padded, edged)
    first = harmonic(padded[:-1, 1:-1], padded[1:, 1:-1])
    second = harmonic(padded[1:-1, :-1], padded[1:-1, 1:])
    deep = jnp.pad(own, ((0, 0), (0, 0), (1, 1)), mode="edge")
    third = harmonic(deep[:, :, :-1], deep[:, :, 1:])
    return ((first, second, third), jnp.log(own))


def apply_operator(field, faces):
    first, second, third = faces
    padded = with_halo(field, (("row", 0), ("col", 1)), 1)
    padded = jnp.pad(padded, ((0, 0), (0, 0), (1, 1)))
    total = first[:-1] * (field - padded[:-2, 1:-1, 1:-1])
    total = total + first[1:] * (field - padded[2:, 1:-1, 1:-1])
    total = total + second[:, :-1] * (field - padded[1:-1, :-2, 1:-1])
    total = total + second[:, 1:] * (field - padded[1:-1, 2:, 1:-1])
    total = total + third[:, :, :-1] * (field - padded[1:-1, 1:-1, :-2])
    total = total + third[:, :, 1:] * (field - padded[1:-1, 1:-1, 2:])
    return total


def global_squares(field):
    return lax.psum(jnp.sum(field * field), ("row", "col"))


def mix_modes(real_in, imag_in, spectral_weight, deep_count, freq_count):
    block = spectral_weight.reshape(2, deep_count, CHANNELS, CHANNELS, freq_count, KY)
    real_out = einsum_high("kcfg,kcofg->kofg", real_in, block[0]) - einsum_high(
        "kcfg,kcofg->kofg", imag_in, block[1]
    )
    imag_out = einsum_high("kcfg,kcofg->kofg", imag_in, block[0]) + einsum_high(
        "kcfg,kcofg->kofg", real_in, block[1]
    )
    return (real_out, imag_out)


def spectral_transpose(real_part, imag_part, spectral_weight, grid):
    rows, cols, n_row, n_col, row_id, col_id = grid
    full_rows = rows * n_row
    full_cols = cols * n_col
    cosine_rows, sine_rows = wave_table(
        signed_freqs(KX), jnp.arange(full_rows, dtype=jnp.int32), full_rows
    )
    cosine_cols, sine_cols = wave_table(
        signed_freqs(KY), jnp.arange(full_cols, dtype=jnp.int32), full_cols
    )
    real_part, imag_part = (
        lax.all_to_all(real_part, "row", split_axis=0, concat_axis=1, tiled=True),
        lax.all_to_all(imag_part, "row", split_axis=0, concat_axis=1, tiled=True),
    )
    first_real = einsum_high("qxy,xf->qfy", real_part, cosine_rows) + einsum_high(
        "qxy,xf->qfy", imag_part, sine_rows
    )
    first_imag = einsum_high("qxy,xf->qfy", imag_part, cosine_rows) - einsum_high(
        "qxy,xf->qfy", real_part, sine_rows
    )
    first_real, first_imag = (
        lax.all_to_all(first_real, "col", split_axis=1, concat_axis=2, tiled=True),
        lax.all_to_all(first_imag, "col", split_axis=1, concat_axis=2, tiled=True),
    )
    second_real = einsum_high("qfy,yg->qfg", first_real, cosine_cols) + einsum_high(
        "qfy,yg->qfg", first_imag, sine_cols
    )
    second_imag = einsum_high("qfy,yg->qfg", first_imag, cosine_cols) - einsum_high(
        "qfy,yg->qfg", first_real, sine_cols
    )
    deep_count = KZ // n_row
    freq_count = KX // n_col
    shape_in = (deep_count, CHANNELS, freq_count, KY)
    mixed_real, mixed_imag = mix_modes(
        second_real.reshape(shape_in),
        second_imag.reshape(shape_in),
        spectral_weight,
        deep_count,
        freq_count,
    )
    shape_out = (deep_count * CHANNELS, freq_count, KY)
    mixed_real = mixed_real.reshape(shape_out)
    mixed_imag = mixed_imag.reshape(shape_out)
    back_real = einsum_high("qfg,yg->qfy", mixed_real, cosine_cols) - einsum_high(
        "qfg,yg->qfy", mixed_imag, sine_cols
    )
    back_imag = einsum_high("qfg,yg->qfy", mixed_imag, cosine_cols) + einsum_high(
        "qfg,yg->qfy", mixed_real, sine_cols
    )
    back_real, back_imag = (
        lax.all_to_all(back_real, "col", split_axis=2, concat_axis=1, tiled=True),
        lax.all_to_all(back_imag, "col", split_axis=2, concat_axis=1, tiled=True),
    )
    out_real = einsum_high("qfy,xf->qxy", back_real, cosine_rows) - einsum_high(
        "qfy,xf->qxy", back_imag, sine_rows
    )
    out_imag = einsum_high("qfy,xf->qxy", back_imag, cosine_rows) + einsum_high(
        "qfy,xf->qxy", back_real, sine_rows
    )
    out_real, out_imag = (
        lax.all_to_all(out_real, "row", split_axis=1, concat_axis=0, tiled=True),
        lax.all_to_all(out_imag, "row", split_axis=1, concat_axis=0, tiled=True),
    )
    return (out_real, out_imag)


def precondition(residual, squares_total, log_perm, weights, grid, cells):
    lift_weight, spectral_weight, mix_weight, proj_weight = weights
    rows, cols, depth = residual.shape
    scale = jnp.sqrt(squares_total / cells + 1e-06)
    scaled = residual / scale
    lifted = jax.nn.gelu(
        lift_weight[:, 0, None, None, None] * scaled[None]
        + lift_weight[:, 1, None, None, None] * log_perm[None]
        + lift_weight[:, 2, None, None, None]
    )
    cosine_deep, sine_deep = wave_table(
        jnp.arange(KZ, dtype=jnp.int32), jnp.arange(depth, dtype=jnp.int32), depth
    )
    real_part = einsum_high("cxyz,zk->kcxy", lifted, cosine_deep).reshape(KZ * CHANNELS, rows, cols)
    imag_part = -einsum_high("cxyz,zk->kcxy", lifted, sine_deep).reshape(KZ * CHANNELS, rows, cols)
    out_real, out_imag = spectral_transpose(real_part, imag_part, spectral_weight, grid)
    out_real = out_real.reshape(KZ, CHANNELS, rows, cols)
    out_imag = out_imag.reshape(KZ, CHANNELS, rows, cols)
    spatial = (
        einsum_high("kcxy,zk->cxyz", out_real, cosine_deep)
        - einsum_high("kcxy,zk->cxyz", out_imag, sine_deep)
    ) / cells
    point = (
        einsum_high("oc,cxyz->oxyz", mix_weight[:, :CHANNELS], lifted)
        + mix_weight[:, CHANNELS, None, None, None]
    )
    hidden = jax.nn.gelu(spatial + point)
    return scale * (
        einsum_high("o,oxyz->xyz", proj_weight[:CHANNELS], hidden) + proj_weight[CHANNELS]
    )


def local(right_side, permeability, lift_weight, spectral_weight, mix_weight, proj_weight):
    rows, cols, depth = right_side.shape
    n_row = lax.axis_size("row")
    n_col = lax.axis_size("col")
    grid = (rows, cols, n_row, n_col, lax.axis_index("row"), lax.axis_index("col"))
    cells = float(rows * n_row * cols * n_col * depth)
    faces, log_perm = face_arrays(permeability)
    weights = (lift_weight, spectral_weight, mix_weight, proj_weight)

    def precond(residual, squares_total):
        return precondition(residual, squares_total, log_perm, weights, grid, cells)

    solution = jnp.zeros_like(right_side)
    residual = right_side
    kept = []
    update = precond(residual, global_squares(residual))
    kept.append(update)
    direction = update
    for step in range(ITERS):
        image = apply_operator(direction, faces)
        curvature, along = lax.psum(
            (jnp.sum(direction * image), jnp.sum(residual * direction)), ("row", "col")
        )
        alpha = along / curvature
        solution = solution + alpha * direction
        residual = residual - alpha * image
        if step + 1 < ITERS:
            update = precond(residual, global_squares(residual))
            kept.append(update)
            beta = lax.psum(jnp.sum(update * image), ("row", "col")) / curvature
            direction = update - beta * direction
    return (solution, residual, jnp.stack(kept))


LANES = 128
SUBLANES = 8
BOTH = ("row", "col")
CHUNK = 32
F32 = jnp.float32
BF16 = jnp.bfloat16


def split_table(table):
    high = table.astype(ml_dtypes.bfloat16)
    low = (table - high.astype(np.float64)).astype(ml_dtypes.bfloat16)
    return high, low


def split(value):
    high = value.astype(BF16)
    return high, (value - high.astype(F32)).astype(BF16)


def split_three(value):
    high = value.astype(BF16).astype(F32)
    rest = value - high
    middle = rest.astype(BF16).astype(F32)
    return high, middle, rest - middle


def matmul(left, right):
    return jnp.dot(left, right, preferred_element_type=F32)


def matmul_nt(left, right):
    return lax.dot_general(left, right, (((1,), (1,)), ((), ())), preferred_element_type=F32)


def angles(freqs, places, length):
    turns = np.multiply.outer(freqs, places) % length
    return turns * (2.0 * np.pi / length)


def deep_order(n_row):
    count = KZ // n_row
    order = [
        (part, row * count + place)
        for row in range(n_row)
        for part in range(2)
        for place in range(count)
    ]
    return np.array(order)


def deep_tables(n_row, depth):
    order = deep_order(n_row)
    angle = angles(order[:, 1], np.arange(depth), depth)
    wave = np.where(order[:, :1] == 0, np.cos(angle), -np.sin(angle))
    high, low = split_table(wave)
    return np.concatenate([high, low], 0), np.concatenate([high.T, high.T, high.T, low.T], 1)


def column_tables(n_col, cols):
    freqs = np.arange(KY) - KY // 2
    forward = []
    back = []
    for place in range(n_col):
        angle = angles(freqs, place * cols + np.arange(cols), n_col * cols)
        both = np.concatenate([np.cos(angle), np.sin(angle)], 0)
        high, low = split_table(both)
        forward.append(
            np.concatenate(
                [
                    np.concatenate([high, high], 1),
                    np.concatenate([low, np.zeros_like(low)], 1),
                ],
                0,
            )
        )
        both = np.concatenate([np.cos(angle), np.sin(angle)], 0)
        high, low = split_table(both)
        back.append(
            np.concatenate(
                [
                    np.concatenate([high, low], 1),
                    np.concatenate([high, low], 1),
                    np.concatenate([high, np.zeros_like(low)], 1),
                ],
                0,
            )
        )
    return np.stack(forward), np.stack(back)


GAIN = (math.sqrt(2.0 / math.pi) * 0.044715) ** (1.0 / 3.0)
LINEAR = math.sqrt(2.0 / math.pi) / GAIN


def scaled_gelu(value):
    return value + value * jnp.tanh(value * (value * value + LINEAR))


def call(body, outs, in_specs, out_specs, grid=(), scratch=(), flops=0, moved=0, alias=None, limit=8, near=(), loose=()):
    single = not isinstance(outs, tuple)
    outs = (outs,) if single else outs
    out_specs = (out_specs,) if single else out_specs
    run = pl.pallas_call(
        body,
        out_shape=tuple(
            out if place in loose or out.size <= 2**16 else pltpu.HBM(out.shape, out.dtype)
            for place, out in enumerate(outs)
        ),
        grid=grid,
        in_specs=in_specs,
        out_specs=out_specs,
        scratch_shapes=list(scratch),
        input_output_aliases=alias or {},
        compiler_params=pltpu.CompilerParams(vmem_limit_bytes=limit * 1024 * 1024),
        cost_estimate=pl.CostEstimate(
            flops=int(flops), bytes_accessed=int(moved), transcendentals=0
        ),
    )

    def wrapped(*args):
        held = [
            arg
            if place in near or spec.memory_space == pltpu.SMEM
            else pltpu.with_memory_space_constraint(arg, pltpu.HBM)
            for place, (arg, spec) in enumerate(zip(args, in_specs))
        ]
        found = run(*held)
        return found[0] if single else found

    return wrapped


def whole(memory=pltpu.VMEM):
    return pl.BlockSpec(memory_space=memory)


def shape(*dims):
    return jax.ShapeDtypeStruct(dims, F32)


def lane_sums(value):
    folded = jnp.sum(value.reshape(-1, SUBLANES, value.shape[-1]), axis=0)
    folded = sum(
        folded[:, start : start + LANES] for start in range(0, folded.shape[1], LANES)
    )
    return jnp.sum(folded, axis=0, keepdims=True)


def spread(rows, ref):
    rows = rows + [jnp.zeros_like(rows[0])] * (SUBLANES - len(rows))
    ref[...] = jnp.broadcast_to(jnp.concatenate(rows, 0)[None], ref.shape)


def gathered(ref, row):
    total = jnp.sum(ref[...], axis=0)
    return jnp.sum(total[row : row + 1], axis=1, keepdims=True)


def squares_body(field_ref, perm_ref, out_ref, low_ref, high_ref, left_ref, right_ref):
    total = field_ref[0] * field_ref[0]
    for place in range(1, field_ref.shape[0]):
        total = total + field_ref[place] * field_ref[place]
    spread([lane_sums(total)], out_ref)
    rows, cols, _ = perm_ref.shape
    low_ref[...] = perm_ref[0].astype(F32)
    high_ref[...] = perm_ref[rows - 1].astype(F32)
    for place in range(rows):
        plane = perm_ref[place].astype(F32)
        left_ref[place : place + 1, :] = plane[:1]
        right_ref[place : place + 1, :] = plane[cols - 1 :]


def weight_body(weight_ref, *refs):
    *out_refs, hold_ref = refs
    groups, freq, channels, fine, _ = hold_ref.shape
    parts, deep, _, outs, modes = weight_ref.shape
    for channel in range(channels):
        block = weight_ref[:, :, channel].reshape(parts * deep * outs, modes)
        block = block.T.reshape(freq, groups, fine, parts * deep * outs)
        for group in range(groups):
            hold_ref[group, :, channel] = block[:, group]
    place = lax.axis_index("col")
    for shift, out_ref in enumerate(out_refs):
        out_ref[...] = hold_ref[lax.rem(place + shift, groups)]


def scale_of(total, cells):
    return jnp.sqrt(total / cells + 1e-06)


def lift_channel(weight_ref, channel, scaled, log_perm):
    return scaled_gelu(
        weight_ref[0, channel] * scaled
        + (weight_ref[1, channel] * log_perm + weight_ref[2, channel])
    )


def transform(lift_ref, deep_ref, col_ref, scaled, log_perm, spectra_ref, lifted_ref, *refs):
    zt_ref, scaled_ref, log_ref, high_ref, low_ref = refs
    half = 2 * KZ
    depth, cols = scaled.shape
    scaled_ref[...] = scaled
    log_ref[...] = log_perm

    def lift(pair):
        for j in range(2):
            channel = 2 * pair + j
            for start in range(0, depth, CHUNK):
                lines = slice(start, start + CHUNK)
                lifted = lift_channel(lift_ref, channel, scaled_ref[lines], log_ref[lines])
                lifted_ref[0, channel, lines] = lifted
                high, low = split(lifted)
                high_ref[pair, lines, j * cols : (j + 1) * cols] = high
                low_ref[pair, lines, j * cols : (j + 1) * cols] = low

    lift(0)
    for pair in range(CHANNELS // 2):
        if pair + 1 < CHANNELS // 2:
            lift(pair + 1)
        channel = 2 * pair
        part = matmul(deep_ref[...], high_ref[pair])
        part = part[:half] + part[half:] + matmul(deep_ref[:half], low_ref[pair])
        for j in range(2):
            zt_ref[pl.ds(channel + j, half, stride=CHANNELS), :] = part[:, j * cols : (j + 1) * cols]
    groups = half * CHANNELS // LANES
    part = matmul_nt(col_ref[lax.axis_index("col")], jnp.concatenate(split(zt_ref[...]), 1))
    part = part[: 2 * KY] + part[2 * KY :]
    lane = lax.broadcasted_iota(jnp.int32, (KY, LANES), 1)
    sign = jnp.where(lane < LANES // 2, 1.0, -1.0).astype(F32)
    n_col = KY // SUBLANES
    for row in range(groups):
        lanes = slice(row * LANES, (row + 1) * LANES)
        block = part[:KY, lanes] + pltpu.roll(part[KY:, lanes], LANES // 2, 1) * sign
        for col in range(n_col):
            spectra_ref[row * n_col + col, 0] = block[col * SUBLANES : (col + 1) * SUBLANES]


def lift_first_body(cells, lift_ref, sums_ref, res_ref, perm_ref, deep_ref, col_ref, *refs):
    spectra_ref, lifted_ref, *scratch = refs
    scale = scale_of(gathered(sums_ref, 0), cells)
    scaled = (res_ref[0] / scale).T
    log_perm = jnp.log(perm_ref[0].astype(F32)).T
    transform(lift_ref, deep_ref, col_ref, scaled, log_perm, spectra_ref, lifted_ref, *scratch)


def next_scalars(first_ref, sums_ref):
    curvature = gathered(sums_ref, 0)
    alpha = gathered(sums_ref, 1) / curvature
    total = gathered(first_ref, 0) + alpha * (
        alpha * gathered(sums_ref, 2) - 2.0 * gathered(sums_ref, 3)
    )
    return curvature, alpha, jnp.maximum(total, 0.0)


def lift_next_body(cells, lift_ref, first_ref, sums_ref, res_ref, image_ref, perm_ref, deep_ref, col_ref, spectra_ref, lifted_ref, next_ref, *scratch):
    _, alpha, total = next_scalars(first_ref, sums_ref)
    scale = scale_of(total, cells)
    residual = res_ref[0] - alpha * image_ref[0]
    next_ref[0] = residual
    scaled = (residual / scale).T
    log_perm = jnp.log(perm_ref[0].astype(F32)).T
    transform(lift_ref, deep_ref, col_ref, scaled, log_perm, spectra_ref, lifted_ref, *scratch)


def point_body(mix_ref, lifted_ref, *refs):
    point_ref = refs[-1]
    size = 4 * SUBLANES
    group = 4

    def step(index, carry):
        lines = pl.ds(pl.multiple_of(index * size, size), size)
        for first in range(0, CHANNELS, group):
            sums = [mix_ref[first + j, CHANNELS] for j in range(group)]
            for channel in range(CHANNELS):
                lifted = lifted_ref[0, channel, lines, :]
                sums = [
                    total + mix_ref[first + j, channel] * lifted for j, total in enumerate(sums)
                ]
            for j, total in enumerate(sums):
                point_ref[0, first + j, lines, :] = total
        return carry

    lax.fori_loop(0, lifted_ref.shape[2] // size, step, 0)


def modes_body(cells, n_row, n_col, recv_ref, *refs):
    sources = refs[:n_col]
    _, out_ref, weight_ref, sems, field_ref, turned_ref, spec_ref, odd_ref = refs[n_col:]
    own = lax.axis_index("col")
    copies = [
        pltpu.make_async_copy(
            source, weight_ref.at[lax.rem(own + n_col - shift, n_col)], sems.at[shift]
        )
        for shift, source in enumerate(sources)
    ]
    for copy in copies:
        copy.start()
    rows = recv_ref.shape[1]
    places = n_row * rows
    tile = (SUBLANES, LANES)
    lane = lax.broadcasted_iota(jnp.int32, tile, 1)
    first = lane < LANES // 2
    sign = jnp.where(first, 1.0, -1.0).astype(F32)
    base = lane - lane % CHANNELS

    def turn(value):
        return pltpu.roll(value, LANES // 2, 1) * sign

    for row in range(n_row):
        for place in range(rows):
            value = recv_ref[row * n_col, place]
            for col in range(1, n_col):
                value = value + recv_ref[row * n_col + col, place]
            field_ref[row * rows + place] = value
    angle = 2.0 * np.pi / places
    half = KX // 2

    def weigh(coefs, ref):
        total = None
        for place, coef in enumerate(coefs):
            coef = float(coef)
            if abs(coef) < 1e-12:
                continue
            term = ref[place]
            if coef == -1.0:
                term = -term
            elif coef != 1.0:
                term = coef * term
            total = term if total is None else total + term
        return jnp.zeros(tile, F32) if total is None else total

    middle = places // 2
    for place in range(1, middle):
        value, mirror = field_ref[place], field_ref[places - place]
        field_ref[place] = value + mirror
        turned_ref[place] = turn(value - mirror)
    for freq in range(half + 1):
        turns = freq * np.arange(middle + 1) % places
        even = weigh(np.cos(angle * turns), field_ref)
        odd = weigh(np.concatenate([[0.0], np.sin(angle * turns[1:middle])]), turned_ref)
        if freq < half:
            spec_ref[half + freq] = even + odd
        if freq > 0:
            spec_ref[half - freq] = even - odd

    for copy in copies:
        copy.wait()
    share = KX // n_col
    for freq in range(KX):
        value = spec_ref[freq]
        same = [None, None]
        cross = [None, None]
        for channel in range(CHANNELS):
            wide = jnp.take_along_axis(value, base + channel, axis=1)
            weight = weight_ref[freq // share, freq % share, channel]
            for sums, factor in ((same, weight), (cross, pltpu.roll(weight, LANES // 2, 1))):
                term = factor * wide
                kept = sums[channel % 2]
                sums[channel % 2] = term if kept is None else kept + term
        same = same[0] + same[1]
        cross = cross[0] + cross[1]
        total = jnp.where(
            first,
            same - pltpu.roll(same, LANES // 2, 1),
            cross + pltpu.roll(cross, LANES // 2, 1),
        )
        field_ref[freq] = total
        turned_ref[freq] = -turn(total)
    gain = 0.5 / cells
    evens = [field_ref[half] * gain]
    odds = [None]
    for freq in range(1, half):
        evens.append((field_ref[half + freq] + field_ref[half - freq]) * gain)
        odds.append((turned_ref[half + freq] - turned_ref[half - freq]) * gain)
    evens.append(field_ref[0] * gain)
    odds.append(-turned_ref[0] * gain)
    for freq in range(half + 1):
        spec_ref[freq] = evens[freq]
        if freq > 0:
            odd_ref[freq] = odds[freq]

    def store(place, value):
        for col in range(n_col):
            out_ref[(place // rows) * n_col + col, place % rows] = value

    for place in range(places // 2 + 1):
        turns = place * np.arange(half + 1) % places
        even = weigh(np.cos(angle * turns), spec_ref)
        odd = weigh(np.sin(angle * turns), odd_ref)
        store(place, even + odd)
        if 0 < place < places // 2:
            store(places - place, even - odd)


def back_transform(recv_ref, point_ref, proj_ref, col_ref, deep_ref, wave_ref, total_ref, scale):
    groups = 2 * KZ * CHANNELS // LANES
    n_col = KY // SUBLANES
    cols = col_ref.shape[2] // 2
    lane = lax.broadcasted_iota(jnp.int32, (KY, LANES), 1)
    sign = jnp.where(lane < LANES // 2, -1.0, 1.0).astype(F32)
    half = 2 * KZ
    pieces = []
    for row in range(groups):
        value = recv_ref[row * n_col : (row + 1) * n_col, 0].reshape(KY, LANES)
        turned = pltpu.roll(value, LANES // 2, 1) * sign
        both = jnp.concatenate([value, turned], 0)
        pieces.append(jnp.concatenate(split_three(both), 0).T.astype(BF16))
    part = matmul(jnp.concatenate(pieces, 0), col_ref[lax.axis_index("col")])
    wave_ref[...] = part[:, :cols] + part[:, cols:]

    def waves(out):
        both = [wave_ref[pl.ds(out + j, half, stride=CHANNELS), :] for j in range(2)]
        high, middle, low = (
            part.astype(BF16) for part in split_three(jnp.concatenate(both, 1))
        )
        return jnp.concatenate([high, middle, low, high], 0)

    for out in range(0, CHANNELS, 2):
        spatial = matmul(deep_ref[...], waves(out))
        for start in range(0, spatial.shape[0], CHUNK):
            lines = slice(start, start + CHUNK)
            total = proj_ref[CHANNELS] if out == 0 else total_ref[lines]
            for j in range(2):
                value = spatial[lines, j * cols : (j + 1) * cols] + point_ref[0, out + j, lines]
                total = total + proj_ref[out + j] * scaled_gelu(value)
            total_ref[lines] = total
    return (scale * total_ref[...]).T


def put_edges(update, field_ref, low_ref, high_ref, left_ref, right_ref):
    step = pl.program_id(0)
    field_ref[0] = update
    left_ref[pl.ds(step, 1), :] = update[:1]
    right_ref[pl.ds(step, 1), :] = update[update.shape[0] - 1 :]

    @pl.when(step == 0)
    def _():
        low_ref[...] = update

    @pl.when(step == pl.num_programs(0) - 1)
    def _():
        high_ref[...] = update


def back_first_body(cells, proj_ref, sums_ref, recv_ref, point_ref, col_ref, deep_ref, *refs):
    kept_ref, *edges, wave_ref, total_ref = refs[4:]
    scale = scale_of(gathered(sums_ref, 0), cells)
    update = back_transform(
        recv_ref, point_ref, proj_ref, col_ref, deep_ref, wave_ref, total_ref, scale
    )
    kept_ref[0, 0] = update
    put_edges(update, *edges)


def back_next_body(cells, proj_ref, first_ref, sums_ref, recv_ref, point_ref, col_ref, deep_ref, _, kept_ref, *refs):
    *edges, wave_ref, total_ref = refs
    _, _, total = next_scalars(first_ref, sums_ref)
    update = back_transform(
        recv_ref, point_ref, proj_ref, col_ref, deep_ref, wave_ref, total_ref, scale_of(total, cells)
    )
    kept_ref[0, 0] = update
    put_edges(update, *edges)


def stencil(fields, perms):
    own, before, after, left, right = fields
    cols, depth = own.shape
    line = lax.broadcasted_iota(jnp.int32, (cols, depth), 0)
    deep = lax.broadcasted_iota(jnp.int32, (cols, depth), 1)

    def sides(array, before, after, left, right, first, last):
        return (
            before,
            after,
            jnp.where(line == 0, left, pltpu.roll(array, 1, 0)),
            jnp.where(line == cols - 1, right, pltpu.roll(array, cols - 1, 0)),
            jnp.where(deep == 0, first, pltpu.roll(array, 1, 1)),
            jnp.where(deep == depth - 1, last, pltpu.roll(array, depth - 1, 1)),
        )

    perm, *others = perms
    others = [
        jnp.where(other > 0.0, other, edge)
        for other, edge in zip(others, (perm, perm, perm[:1], perm[cols - 1 :]))
    ]
    total = None
    for other, conductance in zip(
        sides(own, before, after, left, right, 0.0, 0.0), sides(perm, *others, perm, perm)
    ):
        term = harmonic(perm, conductance) * (own - other)
        total = term if total is None else total + term
    return total


def add_sums(terms, out_ref, acc_ref):
    step = pl.program_id(0)

    @pl.when(step == 0)
    def _():
        acc_ref[...] = jnp.zeros_like(acc_ref)

    for j, term in enumerate(terms):
        acc_ref[j : j + 1] += lane_sums(term)

    @pl.when(step == pl.num_programs(0) - 1)
    def _():
        spread([acc_ref[j : j + 1] for j in range(len(terms))], out_ref)


def around(ref, index, halo):
    low_ref, high_ref, left_ref, right_ref = halo
    step = pl.program_id(0)
    last = pl.num_programs(0) - 1
    line = pl.ds(step, 1)

    def plane(place):
        return ref[index + (place,)].astype(F32)

    def outside(axis, edge, value):
        return jnp.where(lax.axis_index(axis) == edge, 0.0, value)

    low = outside("row", 0, low_ref[...])
    high = outside("row", lax.axis_size("row") - 1, high_ref[...])
    left = outside("col", 0, left_ref[line, :])
    right = outside("col", lax.axis_size("col") - 1, right_ref[line, :])
    before = jnp.where(step == 0, low, plane(jnp.maximum(step - 1, 0)))
    after = jnp.where(step == last, high, plane(jnp.minimum(step + 1, last)))
    return plane(step), before, after, left, right


def operator_first_body(field_ref, perm_ref, *refs):
    halo, perm_halo = refs[:4], refs[4:8]
    res_ref, image_ref, out_ref, acc_ref = refs[8:]
    fields = around(field_ref, (), halo)
    image = stencil(fields, around(perm_ref, (), perm_halo))
    own = fields[0]
    residual = res_ref[0]
    image_ref[0] = image
    add_sums((own * image, residual * own, image * image, residual * image), out_ref, acc_ref)


def operator_next_body(cells, first_ref, sums_ref, field_ref, old_ref, perm_ref, *refs):
    halo, old, perm_halo = refs[:4], refs[4:8], refs[8:12]
    res_ref, before_ref, way_ref, image_ref, out_ref, acc_ref = refs[12:]
    _, _, total = next_scalars(first_ref, sums_ref)
    factor = scale_of(total, cells) / scale_of(gathered(first_ref, 0), cells)
    old = around(old_ref, (), old)
    fields = [new - factor * other for new, other in zip(around(field_ref, (), halo), old)]
    image = stencil(fields, around(perm_ref, (), perm_halo))
    own = fields[0]
    residual = res_ref[0]
    way_ref[0] = own
    image_ref[0] = image
    add_sums((own * image, own * before_ref[0], residual * own, residual * old[0]), out_ref, acc_ref)


def last_body(sums_ref, later_ref, old_ref, way_ref, res_ref, before_ref, image_ref, sol_ref, out_ref):
    curvature = gathered(sums_ref, 0)
    alpha = gathered(sums_ref, 1) / curvature
    cross = gathered(later_ref, 1)
    delta = cross / curvature
    along = gathered(later_ref, 2) - delta * gathered(later_ref, 3)
    later = along / (gathered(later_ref, 0) - delta * cross)
    sol_ref[0] = alpha * old_ref[0] + later * (way_ref[0] - delta * old_ref[0])
    out_ref[0] = res_ref[0] - later * (image_ref[0] - delta * before_ref[0])


def exchange(blocks):
    return lax.all_to_all(blocks, BOTH, split_axis=0, concat_axis=0, tiled=True)


def add_up(partial):
    return exchange(partial)


def neighbours(low, high, left, right):
    found = []
    for axis, first, last in (("row", low, high), ("col", left, right)):
        count = lax.axis_size(axis)
        forward = [(i, (i + 1) % count) for i in range(count)]
        backward = [(target, source) for source, target in forward]
        found.append(lax.ppermute(last, axis, forward))
        found.append(lax.ppermute(first, axis, backward))
    return found


def tiled_local(right_side, permeability, lift_weight, spectral_weight, mix_weight, proj_weight):
    rows, cols, depth = right_side.shape
    n_row = lax.axis_size("row")
    n_col = lax.axis_size("col")
    count = n_row * n_col
    cells = float(rows * n_row * cols * n_col * depth)
    freq = KX // n_col
    deep_forward, deep_back = (jnp.asarray(t) for t in deep_tables(n_row, depth))
    col_forward, col_back = (jnp.asarray(t) for t in column_tables(n_col, cols))
    lift_weight = GAIN * lift_weight.T
    mix_weight = jnp.where(jnp.arange(CHANNELS + 1) < CHANNELS, 0.5, GAIN) * mix_weight
    proj_weight = jnp.where(jnp.arange(CHANNELS + 1) < CHANNELS, 0.5 / GAIN, 1.0) * proj_weight
    field = shape(rows, cols, depth)
    field_bytes = 4 * rows * cols * depth
    partial = shape(count, SUBLANES, LANES)
    channels = shape(rows, CHANNELS, depth, cols)
    spectra = shape(count, rows, SUBLANES, LANES)
    spectra_bytes = 4 * count * rows * SUBLANES * LANES
    smem = whole(pltpu.SMEM)
    vmem = whole()
    anywhere = whole(pl.ANY)
    plane = pl.BlockSpec((1, cols, depth), lambda i: (i, 0, 0))
    spectra_block = pl.BlockSpec((count, 1, SUBLANES, LANES), lambda i: (0, i, 0, 0))
    point_block = pl.BlockSpec((1, CHANNELS, depth, cols), lambda i: (i, 0, 0, 0))
    kept_shape = shape(ITERS, rows, cols, depth)
    lift_flops = 2.0e9
    back_flops = 2.0e9

    weight_shape = (freq, CHANNELS, SUBLANES, LANES)
    own, *weights = call(
        weight_body,
        (shape(*weight_shape),) * n_col,
        [vmem],
        (vmem,) * n_col,
        scratch=[pltpu.VMEM((n_col,) + weight_shape, F32)],
        moved=8 * spectral_weight.size,
    )(spectral_weight)
    weights = [own] + [
        lax.ppermute(part, "col", [(i, (i + shift + 1) % n_col) for i in range(n_col)])
        for shift, part in enumerate(weights)
    ]
    edge_shapes = (shape(cols, depth),) * 2 + (shape(rows, depth),) * 2
    squares, *perm_edges = call(
        squares_body,
        (partial,) + edge_shapes,
        [vmem, vmem],
        (vmem,) * 5,
        moved=2 * field_bytes,
    )(right_side, permeability)
    squares = add_up(squares)
    perm_halo = neighbours(*perm_edges)
    acc_scratch = pltpu.VMEM((SUBLANES, LANES), F32)
    plane_scratch = pltpu.VMEM((depth, cols), F32)
    part_scratch = pltpu.VMEM((CHANNELS // 2, depth, 2 * cols), BF16)
    zt_scratch = pltpu.VMEM((2 * KZ * CHANNELS, cols), F32)
    lift_scratch = [zt_scratch, plane_scratch, plane_scratch, part_scratch, part_scratch]

    def points(lifted, part, *others):
        first = part * rows // 2
        half_block = pl.BlockSpec((1, CHANNELS, depth, cols), lambda i: (first + i, 0, 0, 0))
        return call(
            point_body,
            channels,
            [smem, half_block] + [anywhere] * len(others),
            half_block,
            grid=(rows // 2,),
            flops=2.5e9,
            moved=16 * field_bytes,
            alias={2: 0} if part else None,
            limit=12,
            near=range(3, 2 + len(others)),
        )(mix_weight, lifted, *others)

    def modes(received, before):
        places = rows * n_row
        tiles = lambda size: pltpu.VMEM((size, SUBLANES, LANES), F32)
        return call(
            functools.partial(modes_body, cells, n_row, n_col),
            spectra,
            [vmem] + [anywhere] * (n_col + 1),
            vmem,
            scratch=[
                pltpu.VMEM((n_col,) + weight_shape, F32),
                pltpu.SemaphoreType.DMA((n_col,)),
                tiles(places),
                tiles(places),
                tiles(KX),
                tiles(KX),
            ],
            moved=2 * spectra_bytes + 4 * spectral_weight.size,
            near=(0,),
        )(received, *weights, before)

    def mixed_modes(blocks, lifted, others):
        received = exchange(blocks)
        point = points(lifted, 0, *others)
        blocks = modes(received, point)
        received = exchange(blocks)
        point = points(lifted, 1, point, blocks)
        return received, point

    blocks, lifted = call(
        functools.partial(lift_first_body, cells),
        (spectra, channels),
        [smem, vmem, plane, plane, vmem, vmem],
        (spectra_block, point_block),
        limit=16,
        grid=(rows,),
        scratch=lift_scratch,
        flops=lift_flops,
        moved=2 * field_bytes + spectra_bytes,
    )(lift_weight, squares, right_side, permeability, deep_forward, col_forward)
    received, point = mixed_modes(blocks, lifted, weights)
    kept, old, *edges = call(
        functools.partial(back_first_body, cells),
        (kept_shape, field) + edge_shapes,
        [smem, vmem, spectra_block, point_block, vmem, vmem] + [anywhere] * 4,
        (pl.BlockSpec((1, 1, cols, depth), lambda i: (0, i, 0, 0)), plane) + (vmem,) * 4,
        near=(2, 6, 7, 8, 9),
        loose=(1,),
        grid=(rows,),
        scratch=[zt_scratch, plane_scratch],
        limit=12,
        flops=back_flops,
        moved=18 * field_bytes,
    )(proj_weight, squares, received, point, col_back, deep_back, *perm_halo)

    old_halo = neighbours(*edges)
    args = (old, permeability, *old_halo, *perm_halo, right_side)
    image, sums = call(
        operator_first_body,
        (field, partial),
        [vmem] * 10 + [plane],
        (plane, vmem),
        grid=(rows,),
        scratch=[acc_scratch],
        moved=9 * field_bytes,
        near=range(11),
        loose=range(3),
    )(*args)
    sums = add_up(sums)

    blocks, lifted, residual = call(
        functools.partial(lift_next_body, cells),
        (spectra, channels, field),
        [smem, vmem, vmem, plane, plane, plane, vmem, vmem],
        (spectra_block, point_block, plane),
        limit=16,
        near=(4,),
        grid=(rows,),
        scratch=lift_scratch,
        flops=lift_flops,
        moved=4 * field_bytes + spectra_bytes,
    )(lift_weight, squares, sums, right_side, image, permeability, deep_forward, col_forward)
    received, point = mixed_modes(blocks, lifted, ())
    kept, update, *edges = call(
        functools.partial(back_next_body, cells),
        (kept_shape, field) + edge_shapes,
        [smem, vmem, vmem, spectra_block, point_block, vmem, vmem, anywhere],
        (pl.BlockSpec((1, 1, cols, depth), lambda i: (1, i, 0, 0)), plane) + (vmem,) * 4,
        near=(3,),
        loose=(1,),
        grid=(rows,),
        limit=12,
        scratch=[zt_scratch, plane_scratch],
        flops=back_flops,
        moved=19 * field_bytes,
        alias={7: 0},
    )(proj_weight, squares, sums, received, point, col_back, deep_back, kept)

    halo = neighbours(*edges)
    args = (squares, sums, update, old, permeability, *halo, *old_halo, *perm_halo, residual, image)
    way, last_image, later = call(
        functools.partial(operator_next_body, cells),
        (field, field, partial),
        [vmem] * 17 + [plane] * 2,
        (plane, plane, vmem),
        grid=(rows,),
        scratch=[acc_scratch],
        near=range(19),
        loose=range(3),
        moved=11 * field_bytes,
    )(*args)
    later = add_up(later)
    answer, residual = call(
        last_body,
        (field, field),
        [vmem, vmem] + [plane] * 5,
        (plane, plane),
        grid=(rows,),
        moved=6 * field_bytes,
        near=range(7),
        loose=range(3),
    )(sums, later, old, way, residual, image, last_image)
    return (answer, residual, kept)


def fits_tiles(mesh, block):
    rows, cols, depth = block
    n_row, n_col = mesh.shape["row"], mesh.shape["col"]
    return (
        ITERS == 2
        and KZ == n_row * (LANES // (2 * CHANNELS))
        and KY == n_col * SUBLANES
        and KX % n_col == 0
        and cols == LANES
        and depth % LANES == 0
        and rows * n_row >= KX
    )


def solution(mesh):
    placed = (
        P("row", "col", None),
        P("row", "col", None),
        P(),
        P(None, "row", None, None, "col"),
        P(),
        P(),
    )

    def run(right_side, *others):
        rows, cols, depth = right_side.shape
        block = (rows // mesh.shape["row"], cols // mesh.shape["col"], depth)
        return jax.shard_map(
            tiled_local if fits_tiles(mesh, block) else local,
            mesh=mesh,
            in_specs=placed,
            out_specs=(P("row", "col", None), P("row", "col", None), P(None, "row", "col", None)),
            check_vma=False,
        )(right_side, *others)

    return run
```

```python
import functools
import math

import jax
import jax.numpy as jnp
import ml_dtypes
import numpy as np
from jax import lax
from jax.experimental import pallas as pl
from jax.experimental.pallas import tpu as pltpu
from jax.sharding import PartitionSpec as P

CHANNELS = 16
KX = 16
KY = 32
KZ = 32
ITERS = 2


HIGHEST = lax.Precision.HIGHEST


def with_halo(block, sides, width):
    for axis, dim in sides:
        count = lax.axis_size(axis)
        forward = [(i, i + 1) for i in range(count - 1)]
        backward = [(target, source) for source, target in forward]
        low = lax.ppermute(
            lax.slice_in_dim(block, block.shape[dim] - width, None, axis=dim), axis, forward
        )
        high = lax.ppermute(lax.slice_in_dim(block, 0, width, axis=dim), axis, backward)
        block = jnp.concatenate([low, block, high], axis=dim)
    return block


def einsum_high(form, left, right):
    return jnp.einsum(form, left, right, precision=HIGHEST)


def harmonic(first, second):
    return 2.0 * first * second / (first + second)


def wave_table(freqs, places, length):
    turns = freqs[None, :] * places[:, None] % length
    angle = turns.astype(jnp.float32) * (2.0 * jnp.pi / length)
    return (jnp.cos(angle), jnp.sin(angle))


def signed_freqs(count):
    return jnp.arange(count, dtype=jnp.int32) - count // 2


def face_arrays(permeability):
    padded = with_halo(permeability, (("row", 0), ("col", 1)), 1).astype(jnp.float32)
    own = permeability.astype(jnp.float32)
    edged = jnp.pad(own, ((1, 1), (1, 1), (0, 0)), mode="edge")
    padded = jnp.where(padded > 0.0, padded, edged)
    first = harmonic(padded[:-1, 1:-1], padded[1:, 1:-1])
    second = harmonic(padded[1:-1, :-1], padded[1:-1, 1:])
    deep = jnp.pad(own, ((0, 0), (0, 0), (1, 1)), mode="edge")
    third = harmonic(deep[:, :, :-1], deep[:, :, 1:])
    return ((first, second, third), jnp.log(own))


def apply_operator(field, faces):
    first, second, third = faces
    padded = with_halo(field, (("row", 0), ("col", 1)), 1)
    padded = jnp.pad(padded, ((0, 0), (0, 0), (1, 1)))
    total = first[:-1] * (field - padded[:-2, 1:-1, 1:-1])
    total = total + first[1:] * (field - padded[2:, 1:-1, 1:-1])
    total = total + second[:, :-1] * (field - padded[1:-1, :-2, 1:-1])
    total = total + second[:, 1:] * (field - padded[1:-1, 2:, 1:-1])
    total = total + third[:, :, :-1] * (field - padded[1:-1, 1:-1, :-2])
    total = total + third[:, :, 1:] * (field - padded[1:-1, 1:-1, 2:])
    return total


def global_squares(field):
    return lax.psum(jnp.sum(field * field), ("row", "col"))


def mix_modes(real_in, imag_in, spectral_weight, deep_count, freq_count):
    block = spectral_weight.reshape(2, deep_count, CHANNELS, CHANNELS, freq_count, KY)
    real_out = einsum_high("kcfg,kcofg->kofg", real_in, block[0]) - einsum_high(
        "kcfg,kcofg->kofg", imag_in, block[1]
    )
    imag_out = einsum_high("kcfg,kcofg->kofg", imag_in, block[0]) + einsum_high(
        "kcfg,kcofg->kofg", real_in, block[1]
    )
    return (real_out, imag_out)


def spectral_transpose(real_part, imag_part, spectral_weight, grid):
    rows, cols, n_row, n_col, row_id, col_id = grid
    full_rows = rows * n_row
    full_cols = cols * n_col
    cosine_rows, sine_rows = wave_table(
        signed_freqs(KX), jnp.arange(full_rows, dtype=jnp.int32), full_rows
    )
    cosine_cols, sine_cols = wave_table(
        signed_freqs(KY), jnp.arange(full_cols, dtype=jnp.int32), full_cols
    )
    real_part, imag_part = (
        lax.all_to_all(real_part, "row", split_axis=0, concat_axis=1, tiled=True),
        lax.all_to_all(imag_part, "row", split_axis=0, concat_axis=1, tiled=True),
    )
    first_real = einsum_high("qxy,xf->qfy", real_part, cosine_rows) + einsum_high(
        "qxy,xf->qfy", imag_part, sine_rows
    )
    first_imag = einsum_high("qxy,xf->qfy", imag_part, cosine_rows) - einsum_high(
        "qxy,xf->qfy", real_part, sine_rows
    )
    first_real, first_imag = (
        lax.all_to_all(first_real, "col", split_axis=1, concat_axis=2, tiled=True),
        lax.all_to_all(first_imag, "col", split_axis=1, concat_axis=2, tiled=True),
    )
    second_real = einsum_high("qfy,yg->qfg", first_real, cosine_cols) + einsum_high(
        "qfy,yg->qfg", first_imag, sine_cols
    )
    second_imag = einsum_high("qfy,yg->qfg", first_imag, cosine_cols) - einsum_high(
        "qfy,yg->qfg", first_real, sine_cols
    )
    deep_count = KZ // n_row
    freq_count = KX // n_col
    shape_in = (deep_count, CHANNELS, freq_count, KY)
    mixed_real, mixed_imag = mix_modes(
        second_real.reshape(shape_in),
        second_imag.reshape(shape_in),
        spectral_weight,
        deep_count,
        freq_count,
    )
    shape_out = (deep_count * CHANNELS, freq_count, KY)
    mixed_real = mixed_real.reshape(shape_out)
    mixed_imag = mixed_imag.reshape(shape_out)
    back_real = einsum_high("qfg,yg->qfy", mixed_real, cosine_cols) - einsum_high(
        "qfg,yg->qfy", mixed_imag, sine_cols
    )
    back_imag = einsum_high("qfg,yg->qfy", mixed_imag, cosine_cols) + einsum_high(
        "qfg,yg->qfy", mixed_real, sine_cols
    )
    back_real, back_imag = (
        lax.all_to_all(back_real, "col", split_axis=2, concat_axis=1, tiled=True),
        lax.all_to_all(back_imag, "col", split_axis=2, concat_axis=1, tiled=True),
    )
    out_real = einsum_high("qfy,xf->qxy", back_real, cosine_rows) - einsum_high(
        "qfy,xf->qxy", back_imag, sine_rows
    )
    out_imag = einsum_high("qfy,xf->qxy", back_imag, cosine_rows) + einsum_high(
        "qfy,xf->qxy", back_real, sine_rows
    )
    out_real, out_imag = (
        lax.all_to_all(out_real, "row", split_axis=1, concat_axis=0, tiled=True),
        lax.all_to_all(out_imag, "row", split_axis=1, concat_axis=0, tiled=True),
    )
    return (out_real, out_imag)


def precondition(residual, squares_total, log_perm, weights, grid, cells):
    lift_weight, spectral_weight, mix_weight, proj_weight = weights
    rows, cols, depth = residual.shape
    scale = jnp.sqrt(squares_total / cells + 1e-06)
    scaled = residual / scale
    lifted = jax.nn.gelu(
        lift_weight[:, 0, None, None, None] * scaled[None]
        + lift_weight[:, 1, None, None, None] * log_perm[None]
        + lift_weight[:, 2, None, None, None]
    )
    cosine_deep, sine_deep = wave_table(
        jnp.arange(KZ, dtype=jnp.int32), jnp.arange(depth, dtype=jnp.int32), depth
    )
    real_part = einsum_high("cxyz,zk->kcxy", lifted, cosine_deep).reshape(KZ * CHANNELS, rows, cols)
    imag_part = -einsum_high("cxyz,zk->kcxy", lifted, sine_deep).reshape(KZ * CHANNELS, rows, cols)
    out_real, out_imag = spectral_transpose(real_part, imag_part, spectral_weight, grid)
    out_real = out_real.reshape(KZ, CHANNELS, rows, cols)
    out_imag = out_imag.reshape(KZ, CHANNELS, rows, cols)
    spatial = (
        einsum_high("kcxy,zk->cxyz", out_real, cosine_deep)
        - einsum_high("kcxy,zk->cxyz", out_imag, sine_deep)
    ) / cells
    point = (
        einsum_high("oc,cxyz->oxyz", mix_weight[:, :CHANNELS], lifted)
        + mix_weight[:, CHANNELS, None, None, None]
    )
    hidden = jax.nn.gelu(spatial + point)
    return scale * (
        einsum_high("o,oxyz->xyz", proj_weight[:CHANNELS], hidden) + proj_weight[CHANNELS]
    )


def local(right_side, permeability, lift_weight, spectral_weight, mix_weight, proj_weight):
    rows, cols, depth = right_side.shape
    n_row = lax.axis_size("row")
    n_col = lax.axis_size("col")
    grid = (rows, cols, n_row, n_col, lax.axis_index("row"), lax.axis_index("col"))
    cells = float(rows * n_row * cols * n_col * depth)
    faces, log_perm = face_arrays(permeability)
    weights = (lift_weight, spectral_weight, mix_weight, proj_weight)

    def precond(residual, squares_total):
        return precondition(residual, squares_total, log_perm, weights, grid, cells)

    solution = jnp.zeros_like(right_side)
    residual = right_side
    kept = []
    update = precond(residual, global_squares(residual))
    kept.append(update)
    direction = update
    for step in range(ITERS):
        image = apply_operator(direction, faces)
        curvature, along = lax.psum(
            (jnp.sum(direction * image), jnp.sum(residual * direction)), ("row", "col")
        )
        alpha = along / curvature
        solution = solution + alpha * direction
        residual = residual - alpha * image
        if step + 1 < ITERS:
            update = precond(residual, global_squares(residual))
            kept.append(update)
            beta = lax.psum(jnp.sum(update * image), ("row", "col")) / curvature
            direction = update - beta * direction
    return (solution, residual, jnp.stack(kept))


LANES = 128
SUBLANES = 8
COL = ("y", "core")
CHIPS = ("row", "y")
BOTH = ("row", "y", "core")
F32 = jnp.float32
BF16 = jnp.bfloat16


def split_table(table):
    high = table.astype(ml_dtypes.bfloat16)
    low = (table - high.astype(np.float64)).astype(ml_dtypes.bfloat16)
    return high, low


def split(value):
    high = value.astype(BF16)
    return high, (value - high.astype(F32)).astype(BF16)


def split_three(value):
    high = value.astype(BF16).astype(F32)
    rest = value - high
    middle = rest.astype(BF16).astype(F32)
    return high, middle, rest - middle


def matmul(left, right):
    return jnp.dot(left, right, preferred_element_type=F32)


def matmul_nt(left, right):
    return lax.dot_general(left, right, (((1,), (1,)), ((), ())), preferred_element_type=F32)


def angles(freqs, places, length):
    turns = np.multiply.outer(freqs, places) % length
    return turns * (2.0 * np.pi / length)


def deep_order(n_row):
    count = KZ // n_row
    order = [
        (part, row * count + place)
        for row in range(n_row)
        for part in range(2)
        for place in range(count)
    ]
    return np.array(order)


def deep_tables(n_row, depth):
    order = deep_order(n_row)
    angle = angles(order[:, 1], np.arange(depth), depth)
    wave = np.where(order[:, :1] == 0, np.cos(angle), -np.sin(angle))
    high, low = split_table(wave)
    return np.concatenate([high, low], 0), np.concatenate([high.T, high.T, high.T, low.T], 1)


def column_tables(n_col, cols):
    freqs = np.arange(KY) - KY // 2
    forward = []
    back = []
    for place in range(n_col):
        angle = angles(freqs, place * cols + np.arange(cols), n_col * cols)
        own = np.arange(KY).reshape(-1, 2, SUBLANES)[:, place % 2].reshape(-1)
        partner = np.arange(KY).reshape(-1, 2, SUBLANES)[:, 1 - place % 2].reshape(-1)
        both = np.concatenate([np.cos(angle), np.sin(angle)], 0)
        high, low = split_table(both)
        forward.append(
            np.concatenate(
                [
                    np.concatenate([high, high], 1),
                    np.concatenate([low, np.zeros_like(low)], 1),
                ],
                0,
            )
        )
        angle = angle[np.concatenate([own, partner])]
        both = np.concatenate([np.cos(angle), np.sin(angle)], 0)
        high, low = split_table(both)
        back.append(
            np.concatenate(
                [
                    np.concatenate([high, low], 1),
                    np.concatenate([high, low], 1),
                    np.concatenate([high, np.zeros_like(low)], 1),
                ],
                0,
            )
        )
    return np.stack(forward), np.stack(back)


GAIN = (math.sqrt(2.0 / math.pi) * 0.044715) ** (1.0 / 3.0)
LINEAR = math.sqrt(2.0 / math.pi) / GAIN


def scaled_gelu(value):
    return value + value * jnp.tanh(value * (value * value + LINEAR))


def call(body, outs, in_specs, out_specs, grid=(), scratch=(), flops=0, moved=0, alias=None, limit=8, near=(), loose=()):
    single = not isinstance(outs, tuple)
    outs = (outs,) if single else outs
    out_specs = (out_specs,) if single else out_specs
    run = pl.pallas_call(
        body,
        out_shape=tuple(
            out if place in loose or out.size <= 2**16 else pltpu.HBM(out.shape, out.dtype)
            for place, out in enumerate(outs)
        ),
        grid=grid,
        in_specs=in_specs,
        out_specs=out_specs,
        scratch_shapes=list(scratch),
        input_output_aliases=alias or {},
        compiler_params=pltpu.CompilerParams(vmem_limit_bytes=limit * 1024 * 1024),
        cost_estimate=pl.CostEstimate(
            flops=int(flops), bytes_accessed=int(moved), transcendentals=0
        ),
    )

    def wrapped(*args):
        held = [
            arg
            if place in near or spec.memory_space == pltpu.SMEM
            else pltpu.with_memory_space_constraint(arg, pltpu.HBM)
            for place, (arg, spec) in enumerate(zip(args, in_specs))
        ]
        found = run(*held)
        return found[0] if single else found

    return wrapped


def whole(memory=pltpu.VMEM):
    return pl.BlockSpec(memory_space=memory)


def shape(*dims):
    return jax.ShapeDtypeStruct(dims, F32)


def lane_sums(value):
    folded = jnp.sum(value.reshape(-1, SUBLANES, value.shape[-1]), axis=0)
    folded = sum(
        folded[:, start : start + LANES] for start in range(0, folded.shape[1], LANES)
    )
    return jnp.sum(folded, axis=0, keepdims=True)


def spread(rows, ref):
    rows = rows + [jnp.zeros_like(rows[0])] * (SUBLANES - len(rows))
    ref[...] = jnp.broadcast_to(jnp.concatenate(rows, 0)[None], ref.shape)


def gathered(ref, row):
    total = jnp.sum(ref[...], axis=0)
    return jnp.sum(total[row : row + 1], axis=1, keepdims=True)


def squares_body(field_ref, perm_ref, _, out_ref, low_ref, high_ref, left_ref, right_ref):
    total = field_ref[0] * field_ref[0]
    for place in range(1, field_ref.shape[0]):
        total = total + field_ref[place] * field_ref[place]
    spread([lane_sums(total)], out_ref)
    rows, cols, _ = perm_ref.shape
    low_ref[...] = perm_ref[0].astype(F32)
    high_ref[...] = perm_ref[rows - 1].astype(F32)
    for place in range(rows):
        plane = perm_ref[place].astype(F32)
        left_ref[place : place + 1, :] = plane[:1]
        right_ref[place : place + 1, :] = plane[cols - 1 :]


def weight_body(weight_ref, *refs):
    *out_refs, hold_ref = refs
    groups, freq, channels, fine, _ = hold_ref.shape
    parts, deep, _, outs, modes = weight_ref.shape
    for channel in range(channels):
        block = weight_ref[:, :, channel].reshape(parts * deep * outs, modes)
        block = block.T.reshape(freq, groups, fine, parts * deep * outs)
        for group in range(groups):
            hold_ref[group, :, channel] = block[:, group]
    place = lax.axis_index(COL)
    for shift, out_ref in enumerate(out_refs):
        out_ref[...] = hold_ref[lax.rem(place + shift, groups)]


def scale_of(total, cells):
    return jnp.sqrt(total / cells + 1e-06)


def lift_channel(weight_ref, channel, scaled, log_perm):
    return scaled_gelu(
        weight_ref[0, channel] * scaled
        + (weight_ref[1, channel] * log_perm + weight_ref[2, channel])
    )


def transform(lift_ref, deep_ref, col_ref, scaled, log_perm, own_ref, partner_ref, lifted_ref, zt_ref):
    half = 2 * KZ
    cols = scaled.shape[1]
    for channel in range(0, CHANNELS, 2):
        pair = [lift_channel(lift_ref, channel + j, scaled, log_perm) for j in range(2)]
        for j in range(2):
            lifted_ref[0, channel + j] = pair[j]
        high, low = split(jnp.concatenate(pair, 1))
        part = matmul(deep_ref[...], high)
        part = part[:half] + part[half:] + matmul(deep_ref[:half], low)
        for j in range(2):
            zt_ref[pl.ds(channel + j, half, stride=CHANNELS), :] = part[:, j * cols : (j + 1) * cols]
    groups = half * CHANNELS // LANES
    part = matmul_nt(col_ref[lax.axis_index(COL)], jnp.concatenate(split(zt_ref[...]), 1))
    part = part[: 2 * KY] + part[2 * KY :]
    lane = lax.broadcasted_iota(jnp.int32, (KY, LANES), 1)
    sign = jnp.where(lane < LANES // 2, 1.0, -1.0).astype(F32)
    n_col = KY // SUBLANES
    core = lax.axis_index("core")
    for row in range(groups):
        lanes = slice(row * LANES, (row + 1) * LANES)
        block = part[:KY, lanes] + pltpu.roll(part[KY:, lanes], LANES // 2, 1) * sign
        for place in range(n_col // 2):
            start = 2 * place * SUBLANES
            even = block[start : start + SUBLANES]
            odd = block[start + SUBLANES : start + 2 * SUBLANES]
            own_ref[row * n_col // 2 + place, 0] = jnp.where(core == 0, even, odd)
            partner_ref[row * n_col // 2 + place, 0] = jnp.where(core == 0, odd, even)


def lift_first_body(cells, lift_ref, sums_ref, res_ref, perm_ref, deep_ref, col_ref, *refs):
    own_ref, partner_ref, lifted_ref, zt_ref = refs[-4:]
    scale = scale_of(gathered(sums_ref, 0), cells)
    scaled = (res_ref[0] / scale).T
    log_perm = jnp.log(perm_ref[0].astype(F32)).T
    transform(lift_ref, deep_ref, col_ref, scaled, log_perm, own_ref, partner_ref, lifted_ref, zt_ref)


def join_body(own_ref, partner_ref, out_ref):
    out_ref[...] = own_ref[...] + partner_ref[...]


def next_scalars(first_ref, sums_ref):
    curvature = gathered(sums_ref, 0)
    alpha = gathered(sums_ref, 1) / curvature
    total = gathered(first_ref, 0) + alpha * (
        alpha * gathered(sums_ref, 2) - 2.0 * gathered(sums_ref, 3)
    )
    return curvature, alpha, jnp.maximum(total, 0.0)


def lift_next_body(cells, lift_ref, first_ref, sums_ref, res_ref, image_ref, perm_ref, deep_ref, col_ref, own_ref, partner_ref, lifted_ref, next_ref, zt_ref):
    _, alpha, total = next_scalars(first_ref, sums_ref)
    scale = scale_of(total, cells)
    residual = res_ref[0] - alpha * image_ref[0]
    next_ref[0] = residual
    scaled = (residual / scale).T
    log_perm = jnp.log(perm_ref[0].astype(F32)).T
    transform(lift_ref, deep_ref, col_ref, scaled, log_perm, own_ref, partner_ref, lifted_ref, zt_ref)


def point_body(mix_ref, lifted_ref, _, __, point_ref):
    size = 4 * SUBLANES
    group = 4

    def step(index, carry):
        lines = pl.ds(pl.multiple_of(index * size, size), size)
        for first in range(0, CHANNELS, group):
            sums = [mix_ref[first + j, CHANNELS] for j in range(group)]
            for channel in range(CHANNELS):
                lifted = lifted_ref[0, channel, lines, :]
                sums = [
                    total + mix_ref[first + j, channel] * lifted for j, total in enumerate(sums)
                ]
            for j, total in enumerate(sums):
                point_ref[0, first + j, lines, :] = total
        return carry

    lax.fori_loop(0, lifted_ref.shape[2] // size, step, 0)


def modes_body(cells, n_row, n_col, n_chip, recv_ref, *refs):
    sources = refs[:n_col]
    _, out_ref, weight_ref, sems, field_ref, turned_ref, spec_ref, odd_ref = refs[n_col:]
    own = lax.axis_index(COL)
    copies = [
        pltpu.make_async_copy(
            source, weight_ref.at[lax.rem(own + n_col - shift, n_col)], sems.at[shift]
        )
        for shift, source in enumerate(sources)
    ]
    for copy in copies:
        copy.start()
    rows = recv_ref.shape[1]
    places = n_row * rows
    tile = (SUBLANES, LANES)
    lane = lax.broadcasted_iota(jnp.int32, tile, 1)
    first = lane < LANES // 2
    sign = jnp.where(first, 1.0, -1.0).astype(F32)
    base = lane - lane % CHANNELS

    def turn(value):
        return pltpu.roll(value, LANES // 2, 1) * sign

    for row in range(n_row):
        for place in range(rows):
            value = recv_ref[row * n_chip, place]
            for chip in range(1, n_chip):
                value = value + recv_ref[row * n_chip + chip, place]
            field_ref[row * rows + place] = value
    angle = 2.0 * np.pi / places
    half = KX // 2

    def weigh(coefs, ref):
        total = None
        for place, coef in enumerate(coefs):
            coef = float(coef)
            if abs(coef) < 1e-12:
                continue
            term = ref[place]
            if coef == -1.0:
                term = -term
            elif coef != 1.0:
                term = coef * term
            total = term if total is None else total + term
        return jnp.zeros(tile, F32) if total is None else total

    middle = places // 2
    for place in range(1, middle):
        value, mirror = field_ref[place], field_ref[places - place]
        field_ref[place] = value + mirror
        turned_ref[place] = turn(value - mirror)
    for freq in range(half + 1):
        turns = freq * np.arange(middle + 1) % places
        even = weigh(np.cos(angle * turns), field_ref)
        odd = weigh(np.concatenate([[0.0], np.sin(angle * turns[1:middle])]), turned_ref)
        if freq < half:
            spec_ref[half + freq] = even + odd
        if freq > 0:
            spec_ref[half - freq] = even - odd

    for copy in copies:
        copy.wait()
    share = KX // n_col
    for freq in range(KX):
        value = spec_ref[freq]
        same = [None, None]
        cross = [None, None]
        for channel in range(CHANNELS):
            wide = jnp.take_along_axis(value, base + channel, axis=1)
            weight = weight_ref[freq // share, freq % share, channel]
            for sums, factor in ((same, weight), (cross, pltpu.roll(weight, LANES // 2, 1))):
                term = factor * wide
                kept = sums[channel % 2]
                sums[channel % 2] = term if kept is None else kept + term
        same = same[0] + same[1]
        cross = cross[0] + cross[1]
        total = jnp.where(
            first,
            same - pltpu.roll(same, LANES // 2, 1),
            cross + pltpu.roll(cross, LANES // 2, 1),
        )
        field_ref[freq] = total
        turned_ref[freq] = -turn(total)
    gain = 0.5 / cells
    evens = [field_ref[half] * gain]
    odds = [None]
    for freq in range(1, half):
        evens.append((field_ref[half + freq] + field_ref[half - freq]) * gain)
        odds.append((turned_ref[half + freq] - turned_ref[half - freq]) * gain)
    evens.append(field_ref[0] * gain)
    odds.append(-turned_ref[0] * gain)
    for freq in range(half + 1):
        spec_ref[freq] = evens[freq]
        if freq > 0:
            odd_ref[freq] = odds[freq]

    def store(place, value):
        for chip in range(n_chip):
            out_ref[(place // rows) * n_chip + chip, place % rows] = value

    for place in range(places // 2 + 1):
        turns = place * np.arange(half + 1) % places
        even = weigh(np.cos(angle * turns), spec_ref)
        odd = weigh(np.sin(angle * turns), odd_ref)
        store(place, even + odd)
        if 0 < place < places // 2:
            store(places - place, even - odd)


def back_transform(recv_ref, other_ref, point_ref, proj_ref, col_ref, deep_ref, wave_ref, scale):
    groups = 2 * KZ * CHANNELS // LANES
    n_col = KY // SUBLANES
    cols = col_ref.shape[2] // 2
    lane = lax.broadcasted_iota(jnp.int32, (KY, LANES), 1)
    sign = jnp.where(lane < LANES // 2, -1.0, 1.0).astype(F32)
    half = 2 * KZ
    pieces = []
    for row in range(groups):
        chips = slice(row * n_col // 2, (row + 1) * n_col // 2)
        value = jnp.concatenate([recv_ref[chips, 0], other_ref[chips, 0]], 0)
        value = value.reshape(KY, LANES)
        turned = pltpu.roll(value, LANES // 2, 1) * sign
        both = jnp.concatenate([value, turned], 0)
        pieces.append(jnp.concatenate(split_three(both), 0).T.astype(BF16))
    part = matmul(jnp.concatenate(pieces, 0), col_ref[lax.axis_index(COL)])
    wave_ref[...] = part[:, :cols] + part[:, cols:]
    total = None
    for out in range(0, CHANNELS, 2):
        waves = jnp.concatenate(
            [wave_ref[pl.ds(out + j, half, stride=CHANNELS), :] for j in range(2)], 1
        )
        high, middle, low = (part.astype(BF16) for part in split_three(waves))
        spatial = matmul(deep_ref[...], jnp.concatenate([high, middle, low, high], 0))
        for j in range(2):
            hidden = scaled_gelu(spatial[:, j * cols : (j + 1) * cols] + point_ref[0, out + j])
            term = proj_ref[out + j] * hidden
            total = term if total is None else total + term
    return (scale * (total + proj_ref[CHANNELS])).T


def put_edges(update, field_ref, low_ref, high_ref, left_ref, right_ref):
    step = pl.program_id(0)
    field_ref[0] = update
    left_ref[pl.ds(step, 1), :] = update[:1]
    right_ref[pl.ds(step, 1), :] = update[update.shape[0] - 1 :]

    @pl.when(step == 0)
    def _():
        low_ref[...] = update

    @pl.when(step == pl.num_programs(0) - 1)
    def _():
        high_ref[...] = update


def back_first_body(cells, proj_ref, sums_ref, recv_ref, other_ref, point_ref, col_ref, deep_ref, *refs):
    kept_ref, *edges, wave_ref = refs[4:]
    scale = scale_of(gathered(sums_ref, 0), cells)
    update = back_transform(
        recv_ref, other_ref, point_ref, proj_ref, col_ref, deep_ref, wave_ref, scale
    )
    kept_ref[0, 0] = update
    put_edges(update, *edges)


def back_next_body(cells, proj_ref, first_ref, sums_ref, recv_ref, other_ref, point_ref, col_ref, deep_ref, _, kept_ref, *refs):
    *edges, wave_ref = refs
    _, _, total = next_scalars(first_ref, sums_ref)
    update = back_transform(
        recv_ref, other_ref, point_ref, proj_ref, col_ref, deep_ref, wave_ref, scale_of(total, cells)
    )
    kept_ref[0, 0] = update
    put_edges(update, *edges)


def stencil(fields, perms):
    own, before, after, left, right = fields
    cols, depth = own.shape
    line = lax.broadcasted_iota(jnp.int32, (cols, depth), 0)
    deep = lax.broadcasted_iota(jnp.int32, (cols, depth), 1)

    def sides(array, before, after, left, right, first, last):
        return (
            before,
            after,
            jnp.where(line == 0, left, pltpu.roll(array, 1, 0)),
            jnp.where(line == cols - 1, right, pltpu.roll(array, cols - 1, 0)),
            jnp.where(deep == 0, first, pltpu.roll(array, 1, 1)),
            jnp.where(deep == depth - 1, last, pltpu.roll(array, depth - 1, 1)),
        )

    perm, *others = perms
    others = [
        jnp.where(other > 0.0, other, edge)
        for other, edge in zip(others, (perm, perm, perm[:1], perm[cols - 1 :]))
    ]
    total = None
    for other, conductance in zip(
        sides(own, before, after, left, right, 0.0, 0.0), sides(perm, *others, perm, perm)
    ):
        term = harmonic(perm, conductance) * (own - other)
        total = term if total is None else total + term
    return total


def add_sums(terms, out_ref, acc_ref):
    step = pl.program_id(0)

    @pl.when(step == 0)
    def _():
        acc_ref[...] = jnp.zeros_like(acc_ref)

    for j, term in enumerate(terms):
        acc_ref[j : j + 1] += lane_sums(term)

    @pl.when(step == pl.num_programs(0) - 1)
    def _():
        spread([acc_ref[j : j + 1] for j in range(len(terms))], out_ref)


def around(ref, index, halo):
    low_ref, high_ref, left_ref, right_ref = halo
    step = pl.program_id(0)
    last = pl.num_programs(0) - 1
    line = pl.ds(step, 1)

    def plane(place):
        return ref[index + (place,)].astype(F32)

    def outside(axis, edge, value):
        return jnp.where(lax.axis_index(axis) == edge, 0.0, value)

    low = outside("row", 0, low_ref[...])
    high = outside("row", lax.axis_size("row") - 1, high_ref[...])
    left = outside(COL, 0, left_ref[line, :])
    right = outside(COL, lax.axis_size(COL) - 1, right_ref[line, :])
    before = jnp.where(step == 0, low, plane(jnp.maximum(step - 1, 0)))
    after = jnp.where(step == last, high, plane(jnp.minimum(step + 1, last)))
    return plane(step), before, after, left, right


def operator_first_body(field_ref, perm_ref, *refs):
    halo, perm_halo = refs[:4], refs[4:8]
    res_ref, image_ref, out_ref, acc_ref = refs[8:]
    fields = around(field_ref, (), halo)
    image = stencil(fields, around(perm_ref, (), perm_halo))
    own = fields[0]
    residual = res_ref[0]
    image_ref[0] = image
    add_sums((own * image, residual * own, image * image, residual * image), out_ref, acc_ref)


def operator_next_body(cells, first_ref, sums_ref, field_ref, old_ref, perm_ref, *refs):
    halo, old, perm_halo = refs[:4], refs[4:8], refs[8:12]
    res_ref, before_ref, way_ref, image_ref, out_ref, acc_ref = refs[12:]
    _, _, total = next_scalars(first_ref, sums_ref)
    factor = scale_of(total, cells) / scale_of(gathered(first_ref, 0), cells)
    old = around(old_ref, (), old)
    fields = [new - factor * other for new, other in zip(around(field_ref, (), halo), old)]
    image = stencil(fields, around(perm_ref, (), perm_halo))
    own = fields[0]
    residual = res_ref[0]
    way_ref[0] = own
    image_ref[0] = image
    add_sums((own * image, own * before_ref[0], residual * own, residual * old[0]), out_ref, acc_ref)


def last_body(sums_ref, later_ref, old_ref, way_ref, res_ref, before_ref, image_ref, sol_ref, out_ref):
    curvature = gathered(sums_ref, 0)
    alpha = gathered(sums_ref, 1) / curvature
    cross = gathered(later_ref, 1)
    delta = cross / curvature
    along = gathered(later_ref, 2) - delta * gathered(later_ref, 3)
    later = along / (gathered(later_ref, 0) - delta * cross)
    sol_ref[0] = alpha * old_ref[0] + later * (way_ref[0] - delta * old_ref[0])
    out_ref[0] = res_ref[0] - later * (image_ref[0] - delta * before_ref[0])


def exchange(blocks, axes):
    return lax.all_to_all(blocks, axes, split_axis=0, concat_axis=0, tiled=True)


def swap(blocks):
    return lax.ppermute(blocks, "core", [(0, 1), (1, 0)])


def add_up(partial):
    return exchange(partial, BOTH)


def neighbours(low, high, left, right):
    found = []
    for axis, first, last in (("row", low, high), (COL, left, right)):
        count = lax.axis_size(axis)
        forward = [(i, (i + 1) % count) for i in range(count)]
        backward = [(target, source) for source, target in forward]
        found.append(lax.ppermute(last, axis, forward))
        found.append(lax.ppermute(first, axis, backward))
    return found


def tiled_local(right_side, permeability, lift_weight, spectral_weight, mix_weight, proj_weight):
    rows, cols, depth = right_side.shape
    n_row = lax.axis_size("row")
    n_col = lax.axis_size(COL)
    count = n_row * n_col
    cells = float(rows * n_row * cols * n_col * depth)
    freq = KX // n_col
    deep_forward, deep_back = (jnp.asarray(t) for t in deep_tables(n_row, depth))
    col_forward, col_back = (jnp.asarray(t) for t in column_tables(n_col, cols))
    lift_weight = GAIN * lift_weight.T
    mix_weight = jnp.where(jnp.arange(CHANNELS + 1) < CHANNELS, 0.5, GAIN) * mix_weight
    proj_weight = jnp.where(jnp.arange(CHANNELS + 1) < CHANNELS, 0.5 / GAIN, 1.0) * proj_weight
    field = shape(rows, cols, depth)
    field_bytes = 4 * rows * cols * depth
    partial = shape(count, SUBLANES, LANES)
    channels = shape(rows, CHANNELS, depth, cols)
    n_chip = n_col // 2
    spectra = shape(n_row * n_chip, rows, SUBLANES, LANES)
    spectra_bytes = 4 * spectra.size
    smem = whole(pltpu.SMEM)
    vmem = whole()
    anywhere = whole(pl.ANY)
    plane = pl.BlockSpec((1, cols, depth), lambda i: (i, 0, 0))
    spectra_block = pl.BlockSpec((n_row * n_chip, 1, SUBLANES, LANES), lambda i: (0, i, 0, 0))
    point_block = pl.BlockSpec((1, CHANNELS, depth, cols), lambda i: (i, 0, 0, 0))
    kept_shape = shape(ITERS, rows, cols, depth)
    lift_flops = 2.0e9
    back_flops = 2.0e9

    weight_shape = (freq, CHANNELS, SUBLANES, LANES)
    kept_weights, *weights = call(
        weight_body,
        (shape(*weight_shape),) * n_col,
        [vmem],
        (vmem,) * n_col,
        scratch=[pltpu.VMEM((n_col,) + weight_shape, F32)],
        moved=8 * spectral_weight.size,
    )(spectral_weight)
    weights = [kept_weights] + [
        lax.ppermute(part, COL, [(i, (i + shift + 1) % n_col) for i in range(n_col)])
        for shift, part in enumerate(weights)
    ]
    edge_shapes = (shape(cols, depth),) * 2 + (shape(rows, depth),) * 2
    squares, *perm_edges = call(
        squares_body,
        (partial,) + edge_shapes,
        [vmem, vmem, anywhere],
        (vmem,) * 5,
        moved=2 * field_bytes,
    )(right_side, permeability, kept_weights)
    squares = add_up(squares)
    perm_halo = neighbours(*perm_edges)
    acc_scratch = pltpu.VMEM((SUBLANES, LANES), F32)
    zt_scratch = pltpu.VMEM((2 * KZ * CHANNELS, cols), F32)

    def points(lifted, part, before, after):
        first = part * rows // 2
        half_block = pl.BlockSpec((1, CHANNELS, depth, cols), lambda i: (first + i, 0, 0, 0))
        return call(
            point_body,
            channels,
            [smem, half_block, anywhere, anywhere],
            half_block,
            grid=(rows // 2,),
            flops=2.5e9,
            moved=16 * field_bytes,
            alias={2: 0} if part else None,
            limit=12,
        )(mix_weight, lifted, before, after)

    def modes(received, before):
        places = rows * n_row
        tiles = lambda size: pltpu.VMEM((size, SUBLANES, LANES), F32)
        return call(
            functools.partial(modes_body, cells, n_row, n_col, n_chip),
            spectra,
            [vmem] + [anywhere] * (n_col + 1),
            vmem,
            scratch=[
                pltpu.VMEM((n_col,) + weight_shape, F32),
                pltpu.SemaphoreType.DMA((n_col,)),
                tiles(places),
                tiles(places),
                tiles(KX),
                tiles(KX),
            ],
            moved=2 * spectra_bytes + 4 * spectral_weight.size,
            near=(0,),
        )(received, *weights, before)

    def mixed_modes(own, partner, lifted):
        blocks = call(join_body, spectra, [vmem, vmem], vmem, near=(0, 1))(own, swap(partner))
        received = exchange(blocks, CHIPS)
        point = points(lifted, 0, blocks, blocks)
        blocks = modes(received, point)
        received = exchange(blocks, CHIPS)
        point = points(lifted, 1, point, blocks)
        return received, swap(received), point

    own, partner, lifted = call(
        functools.partial(lift_first_body, cells),
        (spectra, spectra, channels),
        [smem, vmem, plane, plane, vmem, vmem] + [anywhere] * n_col,
        (spectra_block, spectra_block, point_block),
        limit=16,
        loose=(0, 1),
        near=(6, 7, 8, 9),
        grid=(rows,),
        scratch=[zt_scratch],
        flops=lift_flops,
        moved=2 * field_bytes + spectra_bytes,
    )(lift_weight, squares, right_side, permeability, deep_forward, col_forward, *weights)
    received, other, point = mixed_modes(own, partner, lifted)
    kept, old, *edges = call(
        functools.partial(back_first_body, cells),
        (kept_shape, field) + edge_shapes,
        [smem, vmem, spectra_block, spectra_block, point_block, vmem, vmem]
        + [anywhere] * 4,
        (pl.BlockSpec((1, 1, cols, depth), lambda i: (0, i, 0, 0)), plane) + (vmem,) * 4,
        near=(2, 3, 7, 8, 9, 10),
        loose=(1,),
        grid=(rows,),
        scratch=[zt_scratch],
        limit=12,
        flops=back_flops,
        moved=18 * field_bytes,
    )(proj_weight, squares, received, other, point, col_back, deep_back, *perm_halo)

    old_halo = neighbours(*edges)
    args = (old, permeability, *old_halo, *perm_halo, right_side)
    image, sums = call(
        operator_first_body,
        (field, partial),
        [vmem] * 10 + [plane],
        (plane, vmem),
        grid=(rows,),
        scratch=[acc_scratch],
        moved=9 * field_bytes,
        near=range(11),
        loose=range(3),
    )(*args)
    sums = add_up(sums)

    own, partner, lifted, residual = call(
        functools.partial(lift_next_body, cells),
        (spectra, spectra, channels, field),
        [smem, vmem, vmem, plane, plane, plane, vmem, vmem],
        (spectra_block, spectra_block, point_block, plane),
        limit=16,
        near=(4,),
        loose=(0, 1),
        grid=(rows,),
        scratch=[zt_scratch],
        flops=lift_flops,
        moved=4 * field_bytes + spectra_bytes,
    )(lift_weight, squares, sums, right_side, image, permeability, deep_forward, col_forward)
    received, other, point = mixed_modes(own, partner, lifted)
    kept, update, *edges = call(
        functools.partial(back_next_body, cells),
        (kept_shape, field) + edge_shapes,
        [smem, vmem, vmem, spectra_block, spectra_block, point_block, vmem, vmem, anywhere],
        (pl.BlockSpec((1, 1, cols, depth), lambda i: (1, i, 0, 0)), plane) + (vmem,) * 4,
        near=(3, 4),
        loose=(1,),
        grid=(rows,),
        limit=12,
        scratch=[zt_scratch],
        flops=back_flops,
        moved=19 * field_bytes,
        alias={8: 0},
    )(proj_weight, squares, sums, received, other, point, col_back, deep_back, kept)

    halo = neighbours(*edges)
    args = (squares, sums, update, old, permeability, *halo, *old_halo, *perm_halo, residual, image)
    way, last_image, later = call(
        functools.partial(operator_next_body, cells),
        (field, field, partial),
        [vmem] * 17 + [plane] * 2,
        (plane, plane, vmem),
        grid=(rows,),
        scratch=[acc_scratch],
        near=range(19),
        loose=range(3),
        moved=11 * field_bytes,
    )(*args)
    later = add_up(later)
    answer, residual = call(
        last_body,
        (field, field),
        [vmem, vmem] + [plane] * 5,
        (plane, plane),
        grid=(rows,),
        moved=6 * field_bytes,
        near=range(7),
        loose=range(3),
    )(sums, later, old, way, residual, image, last_image)
    return (answer, residual, kept)


def fits_tiles(mesh, block):
    rows, cols, depth = block
    n_row, n_col = mesh.shape["row"], mesh.shape["col"]
    return (
        ITERS == 2
        and KZ == n_row * (LANES // (2 * CHANNELS))
        and KY == n_col * SUBLANES
        and KX % n_col == 0
        and n_col % 2 == 0
        and cols == LANES
        and depth % LANES == 0
        and rows * n_row >= KX
    )


def solution(mesh):
    placed = (
        P("row", "col", None),
        P("row", "col", None),
        P(),
        P(None, "row", None, None, "col"),
        P(),
        P(),
    )
    outputs = (P("row", "col", None), P("row", "col", None), P(None, "row", "col", None))

    def run(right_side, *others):
        rows, cols, depth = right_side.shape
        n_row, n_col = mesh.shape["row"], mesh.shape["col"]
        if not fits_tiles(mesh, (rows // n_row, cols // n_col, depth)):
            return jax.shard_map(
                local, mesh=mesh, in_specs=placed, out_specs=outputs, check_vma=False
            )(right_side, *others)
        cores = jax.sharding.Mesh(mesh.devices.reshape(n_row, n_col // 2, 2), BOTH)
        placed_cores, outputs_cores = jax.tree.map(
            lambda spec: P(*(COL if axis == "col" else axis for axis in spec)),
            (placed, outputs),
            is_leaf=lambda spec: isinstance(spec, P),
        )
        return jax.shard_map(
            tiled_local,
            mesh=cores,
            in_specs=placed_cores,
            out_specs=outputs_cores,
            check_vma=False,
        )(right_side, *others)

    return run
```

```python
import functools
import math

import jax
import jax.numpy as jnp
import ml_dtypes
import numpy as np
from jax import lax
from jax.experimental import pallas as pl
from jax.experimental.pallas import tpu as pltpu
from jax.sharding import PartitionSpec as P

CHANNELS = 16
KX = 16
KY = 32
KZ = 32
ITERS = 2


HIGHEST = lax.Precision.HIGHEST


def with_halo(block, sides, width):
    for axis, dim in sides:
        count = lax.axis_size(axis)
        forward = [(i, i + 1) for i in range(count - 1)]
        backward = [(target, source) for source, target in forward]
        low = lax.ppermute(
            lax.slice_in_dim(block, block.shape[dim] - width, None, axis=dim), axis, forward
        )
        high = lax.ppermute(lax.slice_in_dim(block, 0, width, axis=dim), axis, backward)
        block = jnp.concatenate([low, block, high], axis=dim)
    return block


def einsum_high(form, left, right):
    return jnp.einsum(form, left, right, precision=HIGHEST)


def harmonic(first, second):
    return 2.0 * first * second / (first + second)


def wave_table(freqs, places, length):
    turns = freqs[None, :] * places[:, None] % length
    angle = turns.astype(jnp.float32) * (2.0 * jnp.pi / length)
    return (jnp.cos(angle), jnp.sin(angle))


def signed_freqs(count):
    return jnp.arange(count, dtype=jnp.int32) - count // 2


def face_arrays(permeability):
    padded = with_halo(permeability, (("row", 0), ("col", 1)), 1).astype(jnp.float32)
    own = permeability.astype(jnp.float32)
    edged = jnp.pad(own, ((1, 1), (1, 1), (0, 0)), mode="edge")
    padded = jnp.where(padded > 0.0, padded, edged)
    first = harmonic(padded[:-1, 1:-1], padded[1:, 1:-1])
    second = harmonic(padded[1:-1, :-1], padded[1:-1, 1:])
    deep = jnp.pad(own, ((0, 0), (0, 0), (1, 1)), mode="edge")
    third = harmonic(deep[:, :, :-1], deep[:, :, 1:])
    return ((first, second, third), jnp.log(own))


def apply_operator(field, faces):
    first, second, third = faces
    padded = with_halo(field, (("row", 0), ("col", 1)), 1)
    padded = jnp.pad(padded, ((0, 0), (0, 0), (1, 1)))
    total = first[:-1] * (field - padded[:-2, 1:-1, 1:-1])
    total = total + first[1:] * (field - padded[2:, 1:-1, 1:-1])
    total = total + second[:, :-1] * (field - padded[1:-1, :-2, 1:-1])
    total = total + second[:, 1:] * (field - padded[1:-1, 2:, 1:-1])
    total = total + third[:, :, :-1] * (field - padded[1:-1, 1:-1, :-2])
    total = total + third[:, :, 1:] * (field - padded[1:-1, 1:-1, 2:])
    return total


def global_squares(field):
    return lax.psum(jnp.sum(field * field), ("row", "col"))


def mix_modes(real_in, imag_in, spectral_weight, deep_count, freq_count):
    block = spectral_weight.reshape(2, deep_count, CHANNELS, CHANNELS, freq_count, KY)
    real_out = einsum_high("kcfg,kcofg->kofg", real_in, block[0]) - einsum_high(
        "kcfg,kcofg->kofg", imag_in, block[1]
    )
    imag_out = einsum_high("kcfg,kcofg->kofg", imag_in, block[0]) + einsum_high(
        "kcfg,kcofg->kofg", real_in, block[1]
    )
    return (real_out, imag_out)


def spectral_transpose(real_part, imag_part, spectral_weight, grid):
    rows, cols, n_row, n_col, row_id, col_id = grid
    full_rows = rows * n_row
    full_cols = cols * n_col
    cosine_rows, sine_rows = wave_table(
        signed_freqs(KX), jnp.arange(full_rows, dtype=jnp.int32), full_rows
    )
    cosine_cols, sine_cols = wave_table(
        signed_freqs(KY), jnp.arange(full_cols, dtype=jnp.int32), full_cols
    )
    real_part, imag_part = (
        lax.all_to_all(real_part, "row", split_axis=0, concat_axis=1, tiled=True),
        lax.all_to_all(imag_part, "row", split_axis=0, concat_axis=1, tiled=True),
    )
    first_real = einsum_high("qxy,xf->qfy", real_part, cosine_rows) + einsum_high(
        "qxy,xf->qfy", imag_part, sine_rows
    )
    first_imag = einsum_high("qxy,xf->qfy", imag_part, cosine_rows) - einsum_high(
        "qxy,xf->qfy", real_part, sine_rows
    )
    first_real, first_imag = (
        lax.all_to_all(first_real, "col", split_axis=1, concat_axis=2, tiled=True),
        lax.all_to_all(first_imag, "col", split_axis=1, concat_axis=2, tiled=True),
    )
    second_real = einsum_high("qfy,yg->qfg", first_real, cosine_cols) + einsum_high(
        "qfy,yg->qfg", first_imag, sine_cols
    )
    second_imag = einsum_high("qfy,yg->qfg", first_imag, cosine_cols) - einsum_high(
        "qfy,yg->qfg", first_real, sine_cols
    )
    deep_count = KZ // n_row
    freq_count = KX // n_col
    shape_in = (deep_count, CHANNELS, freq_count, KY)
    mixed_real, mixed_imag = mix_modes(
        second_real.reshape(shape_in),
        second_imag.reshape(shape_in),
        spectral_weight,
        deep_count,
        freq_count,
    )
    shape_out = (deep_count * CHANNELS, freq_count, KY)
    mixed_real = mixed_real.reshape(shape_out)
    mixed_imag = mixed_imag.reshape(shape_out)
    back_real = einsum_high("qfg,yg->qfy", mixed_real, cosine_cols) - einsum_high(
        "qfg,yg->qfy", mixed_imag, sine_cols
    )
    back_imag = einsum_high("qfg,yg->qfy", mixed_imag, cosine_cols) + einsum_high(
        "qfg,yg->qfy", mixed_real, sine_cols
    )
    back_real, back_imag = (
        lax.all_to_all(back_real, "col", split_axis=2, concat_axis=1, tiled=True),
        lax.all_to_all(back_imag, "col", split_axis=2, concat_axis=1, tiled=True),
    )
    out_real = einsum_high("qfy,xf->qxy", back_real, cosine_rows) - einsum_high(
        "qfy,xf->qxy", back_imag, sine_rows
    )
    out_imag = einsum_high("qfy,xf->qxy", back_imag, cosine_rows) + einsum_high(
        "qfy,xf->qxy", back_real, sine_rows
    )
    out_real, out_imag = (
        lax.all_to_all(out_real, "row", split_axis=1, concat_axis=0, tiled=True),
        lax.all_to_all(out_imag, "row", split_axis=1, concat_axis=0, tiled=True),
    )
    return (out_real, out_imag)


def precondition(residual, squares_total, log_perm, weights, grid, cells):
    lift_weight, spectral_weight, mix_weight, proj_weight = weights
    rows, cols, depth = residual.shape
    scale = jnp.sqrt(squares_total / cells + 1e-06)
    scaled = residual / scale
    lifted = jax.nn.gelu(
        lift_weight[:, 0, None, None, None] * scaled[None]
        + lift_weight[:, 1, None, None, None] * log_perm[None]
        + lift_weight[:, 2, None, None, None]
    )
    cosine_deep, sine_deep = wave_table(
        jnp.arange(KZ, dtype=jnp.int32), jnp.arange(depth, dtype=jnp.int32), depth
    )
    real_part = einsum_high("cxyz,zk->kcxy", lifted, cosine_deep).reshape(KZ * CHANNELS, rows, cols)
    imag_part = -einsum_high("cxyz,zk->kcxy", lifted, sine_deep).reshape(KZ * CHANNELS, rows, cols)
    out_real, out_imag = spectral_transpose(real_part, imag_part, spectral_weight, grid)
    out_real = out_real.reshape(KZ, CHANNELS, rows, cols)
    out_imag = out_imag.reshape(KZ, CHANNELS, rows, cols)
    spatial = (
        einsum_high("kcxy,zk->cxyz", out_real, cosine_deep)
        - einsum_high("kcxy,zk->cxyz", out_imag, sine_deep)
    ) / cells
    point = (
        einsum_high("oc,cxyz->oxyz", mix_weight[:, :CHANNELS], lifted)
        + mix_weight[:, CHANNELS, None, None, None]
    )
    hidden = jax.nn.gelu(spatial + point)
    return scale * (
        einsum_high("o,oxyz->xyz", proj_weight[:CHANNELS], hidden) + proj_weight[CHANNELS]
    )


def local(right_side, permeability, lift_weight, spectral_weight, mix_weight, proj_weight):
    rows, cols, depth = right_side.shape
    n_row = lax.axis_size("row")
    n_col = lax.axis_size("col")
    grid = (rows, cols, n_row, n_col, lax.axis_index("row"), lax.axis_index("col"))
    cells = float(rows * n_row * cols * n_col * depth)
    faces, log_perm = face_arrays(permeability)
    weights = (lift_weight, spectral_weight, mix_weight, proj_weight)

    def precond(residual, squares_total):
        return precondition(residual, squares_total, log_perm, weights, grid, cells)

    solution = jnp.zeros_like(right_side)
    residual = right_side
    kept = []
    update = precond(residual, global_squares(residual))
    kept.append(update)
    direction = update
    for step in range(ITERS):
        image = apply_operator(direction, faces)
        curvature, along = lax.psum(
            (jnp.sum(direction * image), jnp.sum(residual * direction)), ("row", "col")
        )
        alpha = along / curvature
        solution = solution + alpha * direction
        residual = residual - alpha * image
        if step + 1 < ITERS:
            update = precond(residual, global_squares(residual))
            kept.append(update)
            beta = lax.psum(jnp.sum(update * image), ("row", "col")) / curvature
            direction = update - beta * direction
    return (solution, residual, jnp.stack(kept))


LANES = 128
SUBLANES = 8
COL = ("y", "core")
CHIPS = ("row", "y")
BOTH = ("row", "y", "core")
CHUNK = 32
F32 = jnp.float32
BF16 = jnp.bfloat16


def split_table(table):
    high = table.astype(ml_dtypes.bfloat16)
    low = (table - high.astype(np.float64)).astype(ml_dtypes.bfloat16)
    return high, low


def split(value):
    high = value.astype(BF16)
    return high, (value - high.astype(F32)).astype(BF16)


def split_three(value):
    high = value.astype(BF16).astype(F32)
    rest = value - high
    middle = rest.astype(BF16).astype(F32)
    return high, middle, rest - middle


def matmul(left, right):
    return jnp.dot(left, right, preferred_element_type=F32)


def matmul_nt(left, right):
    return lax.dot_general(left, right, (((1,), (1,)), ((), ())), preferred_element_type=F32)


def angles(freqs, places, length):
    turns = np.multiply.outer(freqs, places) % length
    return turns * (2.0 * np.pi / length)


def deep_order(n_row):
    count = KZ // n_row
    order = [
        (part, row * count + place)
        for row in range(n_row)
        for part in range(2)
        for place in range(count)
    ]
    return np.array(order)


def deep_tables(n_row, depth):
    order = deep_order(n_row)
    angle = angles(order[:, 1], np.arange(depth), depth)
    wave = np.where(order[:, :1] == 0, np.cos(angle), -np.sin(angle))
    high, low = split_table(wave)
    return np.concatenate([high, low], 0), np.concatenate([high.T, high.T, high.T, low.T], 1)


def column_tables(n_col, cols):
    freqs = np.arange(KY) - KY // 2
    forward = []
    back = []
    for place in range(n_col):
        angle = angles(freqs, place * cols + np.arange(cols), n_col * cols)
        own = np.arange(KY).reshape(-1, 2, SUBLANES)[:, place % 2].reshape(-1)
        partner = np.arange(KY).reshape(-1, 2, SUBLANES)[:, 1 - place % 2].reshape(-1)
        angle = angle[np.concatenate([own, partner])]
        both = np.concatenate([np.cos(angle), np.sin(angle)], 0)
        high, low = split_table(both)
        forward.append(
            np.concatenate(
                [
                    np.concatenate([high, high], 1),
                    np.concatenate([low, np.zeros_like(low)], 1),
                ],
                0,
            )
        )
        back.append(
            np.concatenate(
                [
                    np.concatenate([high, low], 1),
                    np.concatenate([high, low], 1),
                    np.concatenate([high, np.zeros_like(low)], 1),
                ],
                0,
            )
        )
    return np.stack(forward), np.stack(back)


GAIN = (math.sqrt(2.0 / math.pi) * 0.044715) ** (1.0 / 3.0)
LINEAR = math.sqrt(2.0 / math.pi) / GAIN


def scaled_gelu(value):
    return value + value * jnp.tanh(value * (value * value + LINEAR))


def call(body, outs, in_specs, out_specs, grid=(), scratch=(), flops=0, moved=0, alias=None, limit=8, near=(), loose=()):
    single = not isinstance(outs, tuple)
    outs = (outs,) if single else outs
    out_specs = (out_specs,) if single else out_specs
    run = pl.pallas_call(
        body,
        out_shape=tuple(
            out if place in loose or out.size <= 2**16 else pltpu.HBM(out.shape, out.dtype)
            for place, out in enumerate(outs)
        ),
        grid=grid,
        in_specs=in_specs,
        out_specs=out_specs,
        scratch_shapes=list(scratch),
        input_output_aliases=alias or {},
        compiler_params=pltpu.CompilerParams(vmem_limit_bytes=limit * 1024 * 1024),
        cost_estimate=pl.CostEstimate(
            flops=int(flops), bytes_accessed=int(moved), transcendentals=0
        ),
    )

    def wrapped(*args):
        held = [
            arg
            if place in near or spec.memory_space == pltpu.SMEM
            else pltpu.with_memory_space_constraint(arg, pltpu.HBM)
            for place, (arg, spec) in enumerate(zip(args, in_specs))
        ]
        found = run(*held)
        return found[0] if single else found

    return wrapped


def whole(memory=pltpu.VMEM):
    return pl.BlockSpec(memory_space=memory)


def shape(*dims):
    return jax.ShapeDtypeStruct(dims, F32)


def lane_sums(value):
    folded = jnp.sum(value.reshape(-1, SUBLANES, value.shape[-1]), axis=0)
    folded = sum(
        folded[:, start : start + LANES] for start in range(0, folded.shape[1], LANES)
    )
    return jnp.sum(folded, axis=0, keepdims=True)


def spread(rows, ref):
    rows = rows + [jnp.zeros_like(rows[0])] * (SUBLANES - len(rows))
    ref[...] = jnp.broadcast_to(jnp.concatenate(rows, 0)[None], ref.shape)


def gathered(ref, row):
    total = jnp.sum(ref[...], axis=0)
    return jnp.sum(total[row : row + 1], axis=1, keepdims=True)


def squares_body(field_ref, perm_ref, _, out_ref, low_ref, high_ref, left_ref, right_ref):
    total = field_ref[0] * field_ref[0]
    for place in range(1, field_ref.shape[0]):
        total = total + field_ref[place] * field_ref[place]
    spread([lane_sums(total)], out_ref)
    rows, cols, _ = perm_ref.shape
    low_ref[...] = perm_ref[0].astype(F32)
    high_ref[...] = perm_ref[rows - 1].astype(F32)
    for place in range(rows):
        plane = perm_ref[place].astype(F32)
        left_ref[place : place + 1, :] = plane[:1]
        right_ref[place : place + 1, :] = plane[cols - 1 :]


def weight_body(weight_ref, *refs):
    *out_refs, hold_ref = refs
    groups, freq, channels, fine, _ = hold_ref.shape
    parts, deep, _, outs, modes = weight_ref.shape
    for channel in range(channels):
        block = weight_ref[:, :, channel].reshape(parts * deep * outs, modes)
        block = block.T.reshape(freq, groups, fine, parts * deep * outs)
        for group in range(groups):
            hold_ref[group, :, channel] = block[:, group]
    place = lax.axis_index(COL)
    for shift, out_ref in enumerate(out_refs):
        out_ref[...] = hold_ref[lax.rem(place + shift, groups)]


def scale_of(total, cells):
    return jnp.sqrt(total / cells + 1e-06)


def lift_channel(weight_ref, channel, scaled, log_perm):
    return scaled_gelu(
        weight_ref[0, channel] * scaled
        + (weight_ref[1, channel] * log_perm + weight_ref[2, channel])
    )


def transform(lift_ref, deep_ref, col_ref, scaled, log_perm, own_ref, partner_ref, lifted_ref, zt_ref):
    half = 2 * KZ
    cols = scaled.shape[1]
    for channel in range(0, CHANNELS, 2):
        pair = [lift_channel(lift_ref, channel + j, scaled, log_perm) for j in range(2)]
        for j in range(2):
            lifted_ref[0, channel + j] = pair[j]
        high, low = split(jnp.concatenate(pair, 1))
        part = matmul(deep_ref[...], high)
        part = part[:half] + part[half:] + matmul(deep_ref[:half], low)
        for j in range(2):
            zt_ref[pl.ds(channel + j, half, stride=CHANNELS), :] = part[:, j * cols : (j + 1) * cols]
    groups = half * CHANNELS // LANES
    part = matmul_nt(col_ref[lax.axis_index(COL)], jnp.concatenate(split(zt_ref[...]), 1))
    part = part[: 2 * KY] + part[2 * KY :]
    lane = lax.broadcasted_iota(jnp.int32, (KY, LANES), 1)
    sign = jnp.where(lane < LANES // 2, 1.0, -1.0).astype(F32)
    n_chip = KY // SUBLANES // 2
    for row in range(groups):
        lanes = slice(row * LANES, (row + 1) * LANES)
        block = part[:KY, lanes] + pltpu.roll(part[KY:, lanes], LANES // 2, 1) * sign
        for side, ref in enumerate((own_ref, partner_ref)):
            for place in range(n_chip):
                start = (side * n_chip + place) * SUBLANES
                ref[row * n_chip + place, 0] = block[start : start + SUBLANES]


def lift_first_body(cells, lift_ref, sums_ref, res_ref, perm_ref, deep_ref, col_ref, *refs):
    own_ref, partner_ref, lifted_ref, zt_ref = refs[-4:]
    scale = scale_of(gathered(sums_ref, 0), cells)
    scaled = (res_ref[0] / scale).T
    log_perm = jnp.log(perm_ref[0].astype(F32)).T
    transform(lift_ref, deep_ref, col_ref, scaled, log_perm, own_ref, partner_ref, lifted_ref, zt_ref)


def join_body(own_ref, partner_ref, out_ref):
    out_ref[...] = own_ref[...] + partner_ref[...]


def tie_body(*_):
    pass


def next_scalars(first_ref, sums_ref):
    curvature = gathered(sums_ref, 0)
    alpha = gathered(sums_ref, 1) / curvature
    total = gathered(first_ref, 0) + alpha * (
        alpha * gathered(sums_ref, 2) - 2.0 * gathered(sums_ref, 3)
    )
    return curvature, alpha, jnp.maximum(total, 0.0)


def lift_next_body(cells, lift_ref, first_ref, sums_ref, res_ref, image_ref, perm_ref, deep_ref, col_ref, own_ref, partner_ref, lifted_ref, next_ref, zt_ref):
    _, alpha, total = next_scalars(first_ref, sums_ref)
    scale = scale_of(total, cells)
    residual = res_ref[0] - alpha * image_ref[0]
    next_ref[0] = residual
    scaled = (residual / scale).T
    log_perm = jnp.log(perm_ref[0].astype(F32)).T
    transform(lift_ref, deep_ref, col_ref, scaled, log_perm, own_ref, partner_ref, lifted_ref, zt_ref)


def point_body(mix_ref, lifted_ref, _, __, point_ref):
    size = 4 * SUBLANES
    group = 4

    def step(index, carry):
        lines = pl.ds(pl.multiple_of(index * size, size), size)
        for first in range(0, CHANNELS, group):
            sums = [mix_ref[first + j, CHANNELS] for j in range(group)]
            for channel in range(CHANNELS):
                lifted = lifted_ref[0, channel, lines, :]
                sums = [
                    total + mix_ref[first + j, channel] * lifted for j, total in enumerate(sums)
                ]
            for j, total in enumerate(sums):
                point_ref[0, first + j, lines, :] = total
        return carry

    lax.fori_loop(0, lifted_ref.shape[2] // size, step, 0)


def modes_body(cells, n_row, n_col, n_chip, recv_ref, *refs):
    sources = refs[:n_col]
    _, out_ref, weight_ref, sems, field_ref, turned_ref, spec_ref, odd_ref = refs[n_col:]
    own = lax.axis_index(COL)
    copies = [
        pltpu.make_async_copy(
            source, weight_ref.at[lax.rem(own + n_col - shift, n_col)], sems.at[shift]
        )
        for shift, source in enumerate(sources)
    ]
    for copy in copies:
        copy.start()
    rows = recv_ref.shape[1]
    places = n_row * rows
    tile = (SUBLANES, LANES)
    lane = lax.broadcasted_iota(jnp.int32, tile, 1)
    first = lane < LANES // 2
    sign = jnp.where(first, 1.0, -1.0).astype(F32)
    base = lane - lane % CHANNELS

    def turn(value):
        return pltpu.roll(value, LANES // 2, 1) * sign

    for row in range(n_row):
        for place in range(rows):
            value = recv_ref[row * n_chip, place]
            for chip in range(1, n_chip):
                value = value + recv_ref[row * n_chip + chip, place]
            field_ref[row * rows + place] = value
    angle = 2.0 * np.pi / places
    half = KX // 2

    def weigh(coefs, ref):
        total = None
        for place, coef in enumerate(coefs):
            coef = float(coef)
            if abs(coef) < 1e-12:
                continue
            term = ref[place]
            if coef == -1.0:
                term = -term
            elif coef != 1.0:
                term = coef * term
            total = term if total is None else total + term
        return jnp.zeros(tile, F32) if total is None else total

    middle = places // 2
    for place in range(1, middle):
        value, mirror = field_ref[place], field_ref[places - place]
        field_ref[place] = value + mirror
        turned_ref[place] = turn(value - mirror)
    for freq in range(half + 1):
        turns = freq * np.arange(middle + 1) % places
        even = weigh(np.cos(angle * turns), field_ref)
        odd = weigh(np.concatenate([[0.0], np.sin(angle * turns[1:middle])]), turned_ref)
        if freq < half:
            spec_ref[half + freq] = even + odd
        if freq > 0:
            spec_ref[half - freq] = even - odd

    for copy in copies:
        copy.wait()
    share = KX // n_col
    for freq in range(KX):
        value = spec_ref[freq]
        same = [None, None]
        cross = [None, None]
        for channel in range(CHANNELS):
            wide = jnp.take_along_axis(value, base + channel, axis=1)
            weight = weight_ref[freq // share, freq % share, channel]
            for sums, factor in ((same, weight), (cross, pltpu.roll(weight, LANES // 2, 1))):
                term = factor * wide
                kept = sums[channel % 2]
                sums[channel % 2] = term if kept is None else kept + term
        same = same[0] + same[1]
        cross = cross[0] + cross[1]
        total = jnp.where(
            first,
            same - pltpu.roll(same, LANES // 2, 1),
            cross + pltpu.roll(cross, LANES // 2, 1),
        )
        field_ref[freq] = total
        turned_ref[freq] = -turn(total)
    gain = 0.5 / cells
    evens = [field_ref[half] * gain]
    odds = [None]
    for freq in range(1, half):
        evens.append((field_ref[half + freq] + field_ref[half - freq]) * gain)
        odds.append((turned_ref[half + freq] - turned_ref[half - freq]) * gain)
    evens.append(field_ref[0] * gain)
    odds.append(-turned_ref[0] * gain)
    for freq in range(half + 1):
        spec_ref[freq] = evens[freq]
        if freq > 0:
            odd_ref[freq] = odds[freq]

    def store(place, value):
        for chip in range(n_chip):
            out_ref[(place // rows) * n_chip + chip, place % rows] = value

    for place in range(places // 2 + 1):
        turns = place * np.arange(half + 1) % places
        even = weigh(np.cos(angle * turns), spec_ref)
        odd = weigh(np.sin(angle * turns), odd_ref)
        store(place, even + odd)
        if 0 < place < places // 2:
            store(places - place, even - odd)


def back_transform(recv_ref, other_ref, point_ref, proj_ref, col_ref, deep_ref, wave_ref, total_ref, scale):
    groups = 2 * KZ * CHANNELS // LANES
    n_col = KY // SUBLANES
    cols = col_ref.shape[2] // 2
    lane = lax.broadcasted_iota(jnp.int32, (KY, LANES), 1)
    sign = jnp.where(lane < LANES // 2, -1.0, 1.0).astype(F32)
    half = 2 * KZ
    pieces = []
    for row in range(groups):
        chips = slice(row * n_col // 2, (row + 1) * n_col // 2)
        value = jnp.concatenate([recv_ref[chips, 0], other_ref[chips, 0]], 0)
        value = value.reshape(KY, LANES)
        turned = pltpu.roll(value, LANES // 2, 1) * sign
        both = jnp.concatenate([value, turned], 0)
        pieces.append(jnp.concatenate(split_three(both), 0).T.astype(BF16))
    part = matmul(jnp.concatenate(pieces, 0), col_ref[lax.axis_index(COL)])
    wave_ref[...] = part[:, :cols] + part[:, cols:]

    def waves(out):
        both = [wave_ref[pl.ds(out + j, half, stride=CHANNELS), :] for j in range(2)]
        high, middle, low = (
            part.astype(BF16) for part in split_three(jnp.concatenate(both, 1))
        )
        return jnp.concatenate([high, middle, low, high], 0)

    for out in range(0, CHANNELS, 2):
        spatial = matmul(deep_ref[...], waves(out))
        for start in range(0, spatial.shape[0], CHUNK):
            lines = slice(start, start + CHUNK)
            total = proj_ref[CHANNELS] if out == 0 else total_ref[lines]
            for j in range(2):
                value = spatial[lines, j * cols : (j + 1) * cols] + point_ref[0, out + j, lines]
                total = total + proj_ref[out + j] * scaled_gelu(value)
            total_ref[lines] = total
    return (scale * total_ref[...]).T


def put_lines(update, place, left_ref, right_ref):
    left_ref[pl.ds(place, 1), :] = update[:1]
    right_ref[pl.ds(place, 1), :] = update[update.shape[0] - 1 :]


def back_outer(update, kept_ref, field_ref, low_ref, high_ref, left_ref, right_ref):
    step = pl.program_id(0)
    kept_ref[0, 0] = update
    field_ref[0] = update
    last = left_ref.shape[0] - 1

    @pl.when(step == 0)
    def _():
        low_ref[...] = update
        put_lines(update, 0, left_ref, right_ref)

    @pl.when(step == 1)
    def _():
        high_ref[...] = update
        put_lines(update, last, left_ref, right_ref)


def back_inner(update, left_in, right_in, kept_ref, field_ref, left_ref, right_ref):
    step = pl.program_id(0)
    kept_ref[0, 0] = update
    field_ref[0] = update
    last = left_ref.shape[0] - 1

    @pl.when(step == 0)
    def _():
        for place in (0, last):
            line = slice(place, place + 1)
            left_ref[line] = left_in[line]
            right_ref[line] = right_in[line]

    put_lines(update, step + 1, left_ref, right_ref)


def back_body(scale_from, scalars, waiting, inner, proj_ref, *refs):
    scalar_refs, refs = refs[:scalars], refs[scalars:]
    recv_ref, other_ref, point_ref, col_ref, deep_ref = refs[:5]
    refs = refs[5 + waiting :]
    *outs, wave_ref, total_ref = refs
    update = back_transform(
        recv_ref, other_ref, point_ref, proj_ref, col_ref, deep_ref, wave_ref, total_ref,
        scale_from(*scalar_refs),
    )
    (back_inner if inner else back_outer)(update, *outs)


def stencil(fields, perms):
    own, before, after, left, right = fields
    cols, depth = own.shape
    line = lax.broadcasted_iota(jnp.int32, (cols, depth), 0)
    deep = lax.broadcasted_iota(jnp.int32, (cols, depth), 1)

    def sides(array, before, after, left, right, first, last):
        return (
            before,
            after,
            jnp.where(line == 0, left, pltpu.roll(array, 1, 0)),
            jnp.where(line == cols - 1, right, pltpu.roll(array, cols - 1, 0)),
            jnp.where(deep == 0, first, pltpu.roll(array, 1, 1)),
            jnp.where(deep == depth - 1, last, pltpu.roll(array, depth - 1, 1)),
        )

    perm, *others = perms
    others = [
        jnp.where(other > 0.0, other, edge)
        for other, edge in zip(others, (perm, perm, perm[:1], perm[cols - 1 :]))
    ]
    total = None
    for other, conductance in zip(
        sides(own, before, after, left, right, 0.0, 0.0), sides(perm, *others, perm, perm)
    ):
        term = harmonic(perm, conductance) * (own - other)
        total = term if total is None else total + term
    return total


def add_sums(terms, out_ref, acc_ref):
    step = pl.program_id(0)

    @pl.when(step == 0)
    def _():
        acc_ref[...] = jnp.zeros_like(acc_ref)

    for j, term in enumerate(terms):
        acc_ref[j : j + 1] += lane_sums(term)

    @pl.when(step == pl.num_programs(0) - 1)
    def _():
        spread([acc_ref[j : j + 1] for j in range(len(terms))], out_ref)


def around(ref, index, halo):
    low_ref, high_ref, left_ref, right_ref = halo
    step = pl.program_id(0)
    last = pl.num_programs(0) - 1
    line = pl.ds(step, 1)

    def plane(place):
        return ref[index + (place,)].astype(F32)

    def outside(axis, edge, value):
        return jnp.where(lax.axis_index(axis) == edge, 0.0, value)

    low = outside("row", 0, low_ref[...])
    high = outside("row", lax.axis_size("row") - 1, high_ref[...])
    left = outside(COL, 0, left_ref[line, :])
    right = outside(COL, lax.axis_size(COL) - 1, right_ref[line, :])
    before = jnp.where(step == 0, low, plane(jnp.maximum(step - 1, 0)))
    after = jnp.where(step == last, high, plane(jnp.minimum(step + 1, last)))
    return plane(step), before, after, left, right


def operator_first_body(field_ref, perm_ref, *refs):
    halo, perm_halo = refs[:4], refs[4:8]
    res_ref, image_ref, out_ref, acc_ref = refs[8:]
    fields = around(field_ref, (), halo)
    image = stencil(fields, around(perm_ref, (), perm_halo))
    own = fields[0]
    residual = res_ref[0]
    image_ref[0] = image
    add_sums((own * image, residual * own, image * image, residual * image), out_ref, acc_ref)


def operator_next_body(cells, first_ref, sums_ref, field_ref, old_ref, perm_ref, *refs):
    halo, old, perm_halo = refs[:4], refs[4:8], refs[8:12]
    res_ref, before_ref, way_ref, image_ref, out_ref, acc_ref = refs[12:]
    _, _, total = next_scalars(first_ref, sums_ref)
    factor = scale_of(total, cells) / scale_of(gathered(first_ref, 0), cells)
    old = around(old_ref, (), old)
    fields = [new - factor * other for new, other in zip(around(field_ref, (), halo), old)]
    image = stencil(fields, around(perm_ref, (), perm_halo))
    own = fields[0]
    residual = res_ref[0]
    way_ref[0] = own
    image_ref[0] = image
    add_sums((own * image, own * before_ref[0], residual * own, residual * old[0]), out_ref, acc_ref)


def last_body(sums_ref, later_ref, old_ref, way_ref, res_ref, before_ref, image_ref, sol_ref, out_ref):
    curvature = gathered(sums_ref, 0)
    alpha = gathered(sums_ref, 1) / curvature
    cross = gathered(later_ref, 1)
    delta = cross / curvature
    along = gathered(later_ref, 2) - delta * gathered(later_ref, 3)
    later = along / (gathered(later_ref, 0) - delta * cross)
    sol_ref[0] = alpha * old_ref[0] + later * (way_ref[0] - delta * old_ref[0])
    out_ref[0] = res_ref[0] - later * (image_ref[0] - delta * before_ref[0])


def exchange(blocks, axes):
    return lax.all_to_all(blocks, axes, split_axis=0, concat_axis=0, tiled=True)


def swap(blocks):
    return lax.ppermute(blocks, "core", [(0, 1), (1, 0)])


def add_up(partial):
    return exchange(partial, BOTH)


def shift_planes(axis, first, last):
    count = lax.axis_size(axis)
    forward = [(i, (i + 1) % count) for i in range(count)]
    backward = [(target, source) for source, target in forward]
    return lax.ppermute(last, axis, forward), lax.ppermute(first, axis, backward)


def neighbours(low, high, left, right):
    return shift_planes("row", low, high) + shift_planes(COL, left, right)


def tiled_local(right_side, permeability, lift_weight, spectral_weight, mix_weight, proj_weight):
    rows, cols, depth = right_side.shape
    n_row = lax.axis_size("row")
    n_col = lax.axis_size(COL)
    count = n_row * n_col
    cells = float(rows * n_row * cols * n_col * depth)
    freq = KX // n_col
    deep_forward, deep_back = (jnp.asarray(t) for t in deep_tables(n_row, depth))
    col_forward, col_back = (jnp.asarray(t) for t in column_tables(n_col, cols))
    lift_weight = GAIN * lift_weight.T
    mix_weight = jnp.where(jnp.arange(CHANNELS + 1) < CHANNELS, 0.5, GAIN) * mix_weight
    proj_weight = jnp.where(jnp.arange(CHANNELS + 1) < CHANNELS, 0.5 / GAIN, 1.0) * proj_weight
    field = shape(rows, cols, depth)
    field_bytes = 4 * rows * cols * depth
    partial = shape(count, SUBLANES, LANES)
    channels = shape(rows, CHANNELS, depth, cols)
    n_chip = n_col // 2
    spectra = shape(n_row * n_chip, rows, SUBLANES, LANES)
    spectra_bytes = 4 * spectra.size
    smem = whole(pltpu.SMEM)
    vmem = whole()
    anywhere = whole(pl.ANY)
    plane = pl.BlockSpec((1, cols, depth), lambda i: (i, 0, 0))
    spectra_block = pl.BlockSpec((n_row * n_chip, 1, SUBLANES, LANES), lambda i: (0, i, 0, 0))
    point_block = pl.BlockSpec((1, CHANNELS, depth, cols), lambda i: (i, 0, 0, 0))
    kept_shape = shape(ITERS, rows, cols, depth)
    lift_flops = 2.0e9
    back_flops = 2.0e9

    weight_shape = (freq, CHANNELS, SUBLANES, LANES)
    kept_weights, *weights = call(
        weight_body,
        (shape(*weight_shape),) * n_col,
        [vmem],
        (vmem,) * n_col,
        scratch=[pltpu.VMEM((n_col,) + weight_shape, F32)],
        moved=8 * spectral_weight.size,
    )(spectral_weight)
    weights = [kept_weights] + [
        lax.ppermute(part, COL, [(i, (i + shift + 1) % n_col) for i in range(n_col)])
        for shift, part in enumerate(weights)
    ]
    edge_shapes = (shape(cols, depth),) * 2 + (shape(rows, depth),) * 2
    squares, *perm_edges = call(
        squares_body,
        (partial,) + edge_shapes,
        [vmem, vmem, anywhere],
        (vmem,) * 5,
        moved=2 * field_bytes,
    )(right_side, permeability, kept_weights)
    squares = add_up(squares)
    perm_halo = neighbours(*perm_edges)
    acc_scratch = pltpu.VMEM((SUBLANES, LANES), F32)
    zt_scratch = pltpu.VMEM((2 * KZ * CHANNELS, cols), F32)

    def points(lifted, part, before, after):
        first = part * rows // 2
        half_block = pl.BlockSpec((1, CHANNELS, depth, cols), lambda i: (first + i, 0, 0, 0))
        return call(
            point_body,
            channels,
            [smem, half_block, anywhere, anywhere],
            half_block,
            grid=(rows // 2,),
            flops=2.5e9,
            moved=16 * field_bytes,
            alias={2: 0} if part else None,
            limit=12,
        )(mix_weight, lifted, before, after)

    def modes(received, before):
        places = rows * n_row
        tiles = lambda size: pltpu.VMEM((size, SUBLANES, LANES), F32)
        return call(
            functools.partial(modes_body, cells, n_row, n_col, n_chip),
            spectra,
            [vmem] + [anywhere] * (n_col + 1),
            vmem,
            scratch=[
                pltpu.VMEM((n_col,) + weight_shape, F32),
                pltpu.SemaphoreType.DMA((n_col,)),
                tiles(places),
                tiles(places),
                tiles(KX),
                tiles(KX),
            ],
            moved=2 * spectra_bytes + 4 * spectral_weight.size,
            near=(0,),
        )(received, *weights, before)

    def mixed_modes(own, partner, lifted):
        blocks = call(join_body, spectra, [vmem, vmem], vmem, near=(0, 1))(own, swap(partner))
        received = exchange(blocks, CHIPS)
        point = points(lifted, 0, blocks, blocks)
        blocks = modes(received, point)
        received = exchange(blocks, CHIPS)
        point = points(lifted, 1, point, blocks)
        received = pl.pallas_call(
            tie_body,
            out_shape=spectra,
            in_specs=[anywhere, anywhere],
            out_specs=anywhere,
            input_output_aliases={0: 0},
        )(received, point)
        return received, swap(received), point

    def back(index, scale_from, scalars, fields, waiting):
        def run(place_of, steps, inner, waiting, outs, out_specs, alias, loose):
            count_in = 1 + len(scalars)
            spectra_at = pl.BlockSpec(
                (n_row * n_chip, 1, SUBLANES, LANES), lambda i: (0, place_of(i), 0, 0)
            )
            point_at = pl.BlockSpec(
                (1, CHANNELS, depth, cols), lambda i: (place_of(i), 0, 0, 0)
            )
            kept_at = pl.BlockSpec((1, 1, cols, depth), lambda i: (index, place_of(i), 0, 0))
            plane_at = pl.BlockSpec((1, cols, depth), lambda i: (place_of(i), 0, 0))
            return call(
                functools.partial(
                    back_body,
                    scale_from,
                    len(scalars),
                    2 if inner else len(waiting),
                    inner,
                ),
                outs,
                [smem]
                + [vmem] * len(scalars)
                + [spectra_at, spectra_at, point_at, vmem, vmem]
                + ([anywhere, anywhere, vmem, vmem] if inner else [anywhere] * len(waiting)),
                (kept_at, plane_at) + out_specs,
                grid=(steps,),
                scratch=[zt_scratch, pltpu.VMEM((depth, cols), F32)],
                flops=back_flops / 2,
                moved=9 * field_bytes,
                alias={count_in + 5 + i: o for i, o in alias},
                limit=12,
                near=(count_in, count_in + 1)
                + tuple(
                    count_in + 5 + i
                    for i, array in enumerate(waiting)
                    if array.size != kept_shape.size
                ),
                loose=loose,
            )(proj_weight, *scalars, *fields, col_back, deep_back, *waiting)

        kept, field_out, low, high, left, right = run(
            lambda i: i * (rows - 1),
            2,
            False,
            waiting,
            (kept_shape, field) + edge_shapes,
            (vmem,) * 4,
            [(0, 0)] if index else [],
            (1,),
        )
        halo_rows = shift_planes("row", low, high)
        kept, field_out, left, right = run(
            lambda i: i + 1,
            rows - 2,
            True,
            (kept, field_out, left, right),
            (kept_shape, field) + edge_shapes[2:],
            (vmem,) * 2,
            [(0, 0), (1, 1)],
            (1,),
        )
        return (kept, field_out) + halo_rows + shift_planes(COL, left, right)

    own, partner, lifted = call(
        functools.partial(lift_first_body, cells),
        (spectra, spectra, channels),
        [smem, vmem, plane, plane, vmem, vmem] + [anywhere] * n_col,
        (spectra_block, spectra_block, point_block),
        limit=16,
        loose=(0, 1),
        near=(6, 7, 8, 9),
        grid=(rows,),
        scratch=[zt_scratch],
        flops=lift_flops,
        moved=2 * field_bytes + spectra_bytes,
    )(lift_weight, squares, right_side, permeability, deep_forward, col_forward, *weights)
    received, other, point = mixed_modes(own, partner, lifted)
    kept, old, *edges = back(
        0,
        lambda first_ref: scale_of(gathered(first_ref, 0), cells),
        (squares,),
        (received, other, point),
        perm_halo,
    )

    old_halo = edges
    args = (old, permeability, *old_halo, *perm_halo, right_side)
    image, sums = call(
        operator_first_body,
        (field, partial),
        [vmem] * 10 + [plane],
        (plane, vmem),
        grid=(rows,),
        scratch=[acc_scratch],
        moved=9 * field_bytes,
        near=range(11),
        loose=range(3),
    )(*args)
    sums = add_up(sums)

    own, partner, lifted, residual = call(
        functools.partial(lift_next_body, cells),
        (spectra, spectra, channels, field),
        [smem, vmem, vmem, plane, plane, plane, vmem, vmem],
        (spectra_block, spectra_block, point_block, plane),
        limit=16,
        near=(4,),
        loose=(0, 1),
        grid=(rows,),
        scratch=[zt_scratch],
        flops=lift_flops,
        moved=4 * field_bytes + spectra_bytes,
    )(lift_weight, squares, sums, right_side, image, permeability, deep_forward, col_forward)
    received, other, point = mixed_modes(own, partner, lifted)
    kept, update, *edges = back(
        1,
        lambda first_ref, sums_ref: scale_of(next_scalars(first_ref, sums_ref)[2], cells),
        (squares, sums),
        (received, other, point),
        (kept,),
    )

    halo = edges
    args = (squares, sums, update, old, permeability, *halo, *old_halo, *perm_halo, residual, image)
    way, last_image, later = call(
        functools.partial(operator_next_body, cells),
        (field, field, partial),
        [vmem] * 17 + [plane] * 2,
        (plane, plane, vmem),
        grid=(rows,),
        scratch=[acc_scratch],
        near=range(19),
        loose=range(3),
        moved=11 * field_bytes,
    )(*args)
    later = add_up(later)
    answer, residual = call(
        last_body,
        (field, field),
        [vmem, vmem] + [plane] * 5,
        (plane, plane),
        grid=(rows,),
        moved=6 * field_bytes,
        near=range(7),
        loose=range(3),
    )(sums, later, old, way, residual, image, last_image)
    return (answer, residual, kept)


def fits_tiles(mesh, block):
    rows, cols, depth = block
    n_row, n_col = mesh.shape["row"], mesh.shape["col"]
    return (
        ITERS == 2
        and KZ == n_row * (LANES // (2 * CHANNELS))
        and KY == n_col * SUBLANES
        and KX % n_col == 0
        and n_col % 2 == 0
        and cols == LANES
        and depth % LANES == 0
        and rows * n_row >= KX
        and rows > 2
        and rows % 2 == 0
    )


def solution(mesh):
    placed = (
        P("row", "col", None),
        P("row", "col", None),
        P(),
        P(None, "row", None, None, "col"),
        P(),
        P(),
    )
    outputs = (P("row", "col", None), P("row", "col", None), P(None, "row", "col", None))

    def run(right_side, *others):
        rows, cols, depth = right_side.shape
        n_row, n_col = mesh.shape["row"], mesh.shape["col"]
        if not fits_tiles(mesh, (rows // n_row, cols // n_col, depth)):
            return jax.shard_map(
                local, mesh=mesh, in_specs=placed, out_specs=outputs, check_vma=False
            )(right_side, *others)
        cores = jax.sharding.Mesh(mesh.devices.reshape(n_row, n_col // 2, 2), BOTH)
        placed_cores, outputs_cores = jax.tree.map(
            lambda spec: P(*(COL if axis == "col" else axis for axis in spec)),
            (placed, outputs),
            is_leaf=lambda spec: isinstance(spec, P),
        )
        return jax.shard_map(
            tiled_local,
            mesh=cores,
            in_specs=placed_cores,
            out_specs=outputs_cores,
            check_vma=False,
        )(right_side, *others)

    return run
```

```python
import functools
import math

import jax
import jax.numpy as jnp
import ml_dtypes
import numpy as np
from jax import lax
from jax.experimental import pallas as pl
from jax.experimental.pallas import tpu as pltpu
from jax.sharding import PartitionSpec as P

CHANNELS = 16
KX = 16
KY = 32
KZ = 32
ITERS = 2


HIGHEST = lax.Precision.HIGHEST


def with_halo(block, sides, width):
    for axis, dim in sides:
        count = lax.axis_size(axis)
        forward = [(i, i + 1) for i in range(count - 1)]
        backward = [(target, source) for source, target in forward]
        low = lax.ppermute(
            lax.slice_in_dim(block, block.shape[dim] - width, None, axis=dim), axis, forward
        )
        high = lax.ppermute(lax.slice_in_dim(block, 0, width, axis=dim), axis, backward)
        block = jnp.concatenate([low, block, high], axis=dim)
    return block


def einsum_high(form, left, right):
    return jnp.einsum(form, left, right, precision=HIGHEST)


def harmonic(first, second):
    return 2.0 * first * second / (first + second)


def wave_table(freqs, places, length):
    turns = freqs[None, :] * places[:, None] % length
    angle = turns.astype(jnp.float32) * (2.0 * jnp.pi / length)
    return (jnp.cos(angle), jnp.sin(angle))


def signed_freqs(count):
    return jnp.arange(count, dtype=jnp.int32) - count // 2


def face_arrays(permeability):
    padded = with_halo(permeability, (("row", 0), ("col", 1)), 1).astype(jnp.float32)
    own = permeability.astype(jnp.float32)
    edged = jnp.pad(own, ((1, 1), (1, 1), (0, 0)), mode="edge")
    padded = jnp.where(padded > 0.0, padded, edged)
    first = harmonic(padded[:-1, 1:-1], padded[1:, 1:-1])
    second = harmonic(padded[1:-1, :-1], padded[1:-1, 1:])
    deep = jnp.pad(own, ((0, 0), (0, 0), (1, 1)), mode="edge")
    third = harmonic(deep[:, :, :-1], deep[:, :, 1:])
    return ((first, second, third), jnp.log(own))


def apply_operator(field, faces):
    first, second, third = faces
    padded = with_halo(field, (("row", 0), ("col", 1)), 1)
    padded = jnp.pad(padded, ((0, 0), (0, 0), (1, 1)))
    total = first[:-1] * (field - padded[:-2, 1:-1, 1:-1])
    total = total + first[1:] * (field - padded[2:, 1:-1, 1:-1])
    total = total + second[:, :-1] * (field - padded[1:-1, :-2, 1:-1])
    total = total + second[:, 1:] * (field - padded[1:-1, 2:, 1:-1])
    total = total + third[:, :, :-1] * (field - padded[1:-1, 1:-1, :-2])
    total = total + third[:, :, 1:] * (field - padded[1:-1, 1:-1, 2:])
    return total


def global_squares(field):
    return lax.psum(jnp.sum(field * field), ("row", "col"))


def mix_modes(real_in, imag_in, spectral_weight, deep_count, freq_count):
    block = spectral_weight.reshape(2, deep_count, CHANNELS, CHANNELS, freq_count, KY)
    real_out = einsum_high("kcfg,kcofg->kofg", real_in, block[0]) - einsum_high(
        "kcfg,kcofg->kofg", imag_in, block[1]
    )
    imag_out = einsum_high("kcfg,kcofg->kofg", imag_in, block[0]) + einsum_high(
        "kcfg,kcofg->kofg", real_in, block[1]
    )
    return (real_out, imag_out)


def spectral_transpose(real_part, imag_part, spectral_weight, grid):
    rows, cols, n_row, n_col, row_id, col_id = grid
    full_rows = rows * n_row
    full_cols = cols * n_col
    cosine_rows, sine_rows = wave_table(
        signed_freqs(KX), jnp.arange(full_rows, dtype=jnp.int32), full_rows
    )
    cosine_cols, sine_cols = wave_table(
        signed_freqs(KY), jnp.arange(full_cols, dtype=jnp.int32), full_cols
    )
    real_part, imag_part = (
        lax.all_to_all(real_part, "row", split_axis=0, concat_axis=1, tiled=True),
        lax.all_to_all(imag_part, "row", split_axis=0, concat_axis=1, tiled=True),
    )
    first_real = einsum_high("qxy,xf->qfy", real_part, cosine_rows) + einsum_high(
        "qxy,xf->qfy", imag_part, sine_rows
    )
    first_imag = einsum_high("qxy,xf->qfy", imag_part, cosine_rows) - einsum_high(
        "qxy,xf->qfy", real_part, sine_rows
    )
    first_real, first_imag = (
        lax.all_to_all(first_real, "col", split_axis=1, concat_axis=2, tiled=True),
        lax.all_to_all(first_imag, "col", split_axis=1, concat_axis=2, tiled=True),
    )
    second_real = einsum_high("qfy,yg->qfg", first_real, cosine_cols) + einsum_high(
        "qfy,yg->qfg", first_imag, sine_cols
    )
    second_imag = einsum_high("qfy,yg->qfg", first_imag, cosine_cols) - einsum_high(
        "qfy,yg->qfg", first_real, sine_cols
    )
    deep_count = KZ // n_row
    freq_count = KX // n_col
    shape_in = (deep_count, CHANNELS, freq_count, KY)
    mixed_real, mixed_imag = mix_modes(
        second_real.reshape(shape_in),
        second_imag.reshape(shape_in),
        spectral_weight,
        deep_count,
        freq_count,
    )
    shape_out = (deep_count * CHANNELS, freq_count, KY)
    mixed_real = mixed_real.reshape(shape_out)
    mixed_imag = mixed_imag.reshape(shape_out)
    back_real = einsum_high("qfg,yg->qfy", mixed_real, cosine_cols) - einsum_high(
        "qfg,yg->qfy", mixed_imag, sine_cols
    )
    back_imag = einsum_high("qfg,yg->qfy", mixed_imag, cosine_cols) + einsum_high(
        "qfg,yg->qfy", mixed_real, sine_cols
    )
    back_real, back_imag = (
        lax.all_to_all(back_real, "col", split_axis=2, concat_axis=1, tiled=True),
        lax.all_to_all(back_imag, "col", split_axis=2, concat_axis=1, tiled=True),
    )
    out_real = einsum_high("qfy,xf->qxy", back_real, cosine_rows) - einsum_high(
        "qfy,xf->qxy", back_imag, sine_rows
    )
    out_imag = einsum_high("qfy,xf->qxy", back_imag, cosine_rows) + einsum_high(
        "qfy,xf->qxy", back_real, sine_rows
    )
    out_real, out_imag = (
        lax.all_to_all(out_real, "row", split_axis=1, concat_axis=0, tiled=True),
        lax.all_to_all(out_imag, "row", split_axis=1, concat_axis=0, tiled=True),
    )
    return (out_real, out_imag)


def precondition(residual, squares_total, log_perm, weights, grid, cells):
    lift_weight, spectral_weight, mix_weight, proj_weight = weights
    rows, cols, depth = residual.shape
    scale = jnp.sqrt(squares_total / cells + 1e-06)
    scaled = residual / scale
    lifted = jax.nn.gelu(
        lift_weight[:, 0, None, None, None] * scaled[None]
        + lift_weight[:, 1, None, None, None] * log_perm[None]
        + lift_weight[:, 2, None, None, None]
    )
    cosine_deep, sine_deep = wave_table(
        jnp.arange(KZ, dtype=jnp.int32), jnp.arange(depth, dtype=jnp.int32), depth
    )
    real_part = einsum_high("cxyz,zk->kcxy", lifted, cosine_deep).reshape(KZ * CHANNELS, rows, cols)
    imag_part = -einsum_high("cxyz,zk->kcxy", lifted, sine_deep).reshape(KZ * CHANNELS, rows, cols)
    out_real, out_imag = spectral_transpose(real_part, imag_part, spectral_weight, grid)
    out_real = out_real.reshape(KZ, CHANNELS, rows, cols)
    out_imag = out_imag.reshape(KZ, CHANNELS, rows, cols)
    spatial = (
        einsum_high("kcxy,zk->cxyz", out_real, cosine_deep)
        - einsum_high("kcxy,zk->cxyz", out_imag, sine_deep)
    ) / cells
    point = (
        einsum_high("oc,cxyz->oxyz", mix_weight[:, :CHANNELS], lifted)
        + mix_weight[:, CHANNELS, None, None, None]
    )
    hidden = jax.nn.gelu(spatial + point)
    return scale * (
        einsum_high("o,oxyz->xyz", proj_weight[:CHANNELS], hidden) + proj_weight[CHANNELS]
    )


def local(right_side, permeability, lift_weight, spectral_weight, mix_weight, proj_weight):
    rows, cols, depth = right_side.shape
    n_row = lax.axis_size("row")
    n_col = lax.axis_size("col")
    grid = (rows, cols, n_row, n_col, lax.axis_index("row"), lax.axis_index("col"))
    cells = float(rows * n_row * cols * n_col * depth)
    faces, log_perm = face_arrays(permeability)
    weights = (lift_weight, spectral_weight, mix_weight, proj_weight)

    def precond(residual, squares_total):
        return precondition(residual, squares_total, log_perm, weights, grid, cells)

    solution = jnp.zeros_like(right_side)
    residual = right_side
    kept = []
    update = precond(residual, global_squares(residual))
    kept.append(update)
    direction = update
    for step in range(ITERS):
        image = apply_operator(direction, faces)
        curvature, along = lax.psum(
            (jnp.sum(direction * image), jnp.sum(residual * direction)), ("row", "col")
        )
        alpha = along / curvature
        solution = solution + alpha * direction
        residual = residual - alpha * image
        if step + 1 < ITERS:
            update = precond(residual, global_squares(residual))
            kept.append(update)
            beta = lax.psum(jnp.sum(update * image), ("row", "col")) / curvature
            direction = update - beta * direction
    return (solution, residual, jnp.stack(kept))


LANES = 128
SUBLANES = 8
COL = ("y", "core")
CHIPS = ("row", "y")
BOTH = ("row", "y", "core")
CHUNK = 32
F32 = jnp.float32
BF16 = jnp.bfloat16


def split_table(table):
    high = table.astype(ml_dtypes.bfloat16)
    low = (table - high.astype(np.float64)).astype(ml_dtypes.bfloat16)
    return high, low


def split(value):
    high = value.astype(BF16)
    return high, (value - high.astype(F32)).astype(BF16)


def split_three(value):
    high = value.astype(BF16).astype(F32)
    rest = value - high
    middle = rest.astype(BF16).astype(F32)
    return high, middle, rest - middle


def matmul(left, right):
    return jnp.dot(left, right, preferred_element_type=F32)


def matmul_nt(left, right):
    return lax.dot_general(left, right, (((1,), (1,)), ((), ())), preferred_element_type=F32)


def angles(freqs, places, length):
    turns = np.multiply.outer(freqs, places) % length
    return turns * (2.0 * np.pi / length)


def deep_order(n_row):
    count = KZ // n_row
    order = [
        (part, row * count + place)
        for row in range(n_row)
        for part in range(2)
        for place in range(count)
    ]
    return np.array(order)


def deep_tables(n_row, depth):
    order = deep_order(n_row)
    angle = angles(order[:, 1], np.arange(depth), depth)
    wave = np.where(order[:, :1] == 0, np.cos(angle), -np.sin(angle))
    high, low = split_table(wave)
    return np.concatenate([high, low], 0), np.concatenate([high.T, high.T, high.T, low.T], 1)


def column_tables(n_col, cols):
    freqs = np.arange(KY) - KY // 2
    forward = []
    back = []
    for place in range(n_col):
        angle = angles(freqs, place * cols + np.arange(cols), n_col * cols)
        own = np.arange(KY).reshape(-1, 2, SUBLANES)[:, place % 2].reshape(-1)
        partner = np.arange(KY).reshape(-1, 2, SUBLANES)[:, 1 - place % 2].reshape(-1)
        angle = angle[np.concatenate([own, partner])]
        both = np.concatenate([np.cos(angle), np.sin(angle)], 0)
        high, low = split_table(both)
        forward.append(
            np.concatenate(
                [
                    np.concatenate([high, high], 1),
                    np.concatenate([low, np.zeros_like(low)], 1),
                ],
                0,
            )
        )
        back.append(
            np.concatenate(
                [
                    np.concatenate([high, low], 1),
                    np.concatenate([high, low], 1),
                    np.concatenate([high, np.zeros_like(low)], 1),
                ],
                0,
            )
        )
    return np.stack(forward), np.stack(back)


GAIN = (math.sqrt(2.0 / math.pi) * 0.044715) ** (1.0 / 3.0)
LINEAR = math.sqrt(2.0 / math.pi) / GAIN


def scaled_gelu(value):
    return value + value * jnp.tanh(value * (value * value + LINEAR))


def call(body, outs, in_specs, out_specs, grid=(), scratch=(), flops=0, moved=0, alias=None, limit=8, near=(), loose=()):
    single = not isinstance(outs, tuple)
    outs = (outs,) if single else outs
    out_specs = (out_specs,) if single else out_specs
    run = pl.pallas_call(
        body,
        out_shape=tuple(
            out if place in loose or out.size <= 2**16 else pltpu.HBM(out.shape, out.dtype)
            for place, out in enumerate(outs)
        ),
        grid=grid,
        in_specs=in_specs,
        out_specs=out_specs,
        scratch_shapes=list(scratch),
        input_output_aliases=alias or {},
        compiler_params=pltpu.CompilerParams(vmem_limit_bytes=limit * 1024 * 1024),
        cost_estimate=pl.CostEstimate(
            flops=int(flops), bytes_accessed=int(moved), transcendentals=0
        ),
    )

    def wrapped(*args):
        held = [
            arg
            if place in near or spec.memory_space == pltpu.SMEM
            else pltpu.with_memory_space_constraint(arg, pltpu.HBM)
            for place, (arg, spec) in enumerate(zip(args, in_specs))
        ]
        found = run(*held)
        return found[0] if single else found

    return wrapped


def whole(memory=pltpu.VMEM):
    return pl.BlockSpec(memory_space=memory)


def shape(*dims):
    return jax.ShapeDtypeStruct(dims, F32)


def lane_sums(value):
    folded = jnp.sum(value.reshape(-1, SUBLANES, value.shape[-1]), axis=0)
    folded = sum(
        folded[:, start : start + LANES] for start in range(0, folded.shape[1], LANES)
    )
    return jnp.sum(folded, axis=0, keepdims=True)


def spread(rows, ref):
    rows = rows + [jnp.zeros_like(rows[0])] * (SUBLANES - len(rows))
    ref[...] = jnp.broadcast_to(jnp.concatenate(rows, 0)[None], ref.shape)


def gathered(ref, row):
    total = jnp.sum(ref[...], axis=0)
    return jnp.sum(total[row : row + 1], axis=1, keepdims=True)


def squares_body(field_ref, perm_ref, out_ref, low_ref, high_ref, left_ref, right_ref):
    total = field_ref[0] * field_ref[0]
    for place in range(1, field_ref.shape[0]):
        total = total + field_ref[place] * field_ref[place]
    spread([lane_sums(total)], out_ref)
    rows, cols, _ = perm_ref.shape
    low_ref[...] = perm_ref[0].astype(F32)
    high_ref[...] = perm_ref[rows - 1].astype(F32)
    for place in range(rows):
        plane = perm_ref[place].astype(F32)
        left_ref[place : place + 1, :] = plane[:1]
        right_ref[place : place + 1, :] = plane[cols - 1 :]


def weight_body(weight_ref, *refs):
    *out_refs, hold_ref = refs
    groups, freq, channels, fine, _ = hold_ref.shape
    parts, deep, _, outs, modes = weight_ref.shape
    for channel in range(channels):
        block = weight_ref[:, :, channel].reshape(parts * deep * outs, modes)
        block = block.T.reshape(freq, groups, fine, parts * deep * outs)
        for group in range(groups):
            hold_ref[group, :, channel] = block[:, group]
    place = lax.axis_index(COL)
    for shift, out_ref in enumerate(out_refs):
        out_ref[...] = hold_ref[lax.rem(place + shift, groups)]


def scale_of(total, cells):
    return jnp.sqrt(total / cells + 1e-06)


def lift_channel(weight_ref, channel, scaled, log_perm):
    return scaled_gelu(
        weight_ref[0, channel] * scaled
        + (weight_ref[1, channel] * log_perm + weight_ref[2, channel])
    )


def transform(lift_ref, deep_ref, col_ref, scaled, log_perm, own_ref, partner_ref, lifted_ref, zt_ref):
    half = 2 * KZ
    cols = scaled.shape[1]
    for channel in range(0, CHANNELS, 2):
        pair = [lift_channel(lift_ref, channel + j, scaled, log_perm) for j in range(2)]
        for j in range(2):
            lifted_ref[0, channel + j] = pair[j]
        high, low = split(jnp.concatenate(pair, 1))
        part = matmul(deep_ref[...], high)
        part = part[:half] + part[half:] + matmul(deep_ref[:half], low)
        for j in range(2):
            zt_ref[pl.ds(channel + j, half, stride=CHANNELS), :] = part[:, j * cols : (j + 1) * cols]
    groups = half * CHANNELS // LANES
    part = matmul_nt(col_ref[lax.axis_index(COL)], jnp.concatenate(split(zt_ref[...]), 1))
    part = part[: 2 * KY] + part[2 * KY :]
    lane = lax.broadcasted_iota(jnp.int32, (KY, LANES), 1)
    sign = jnp.where(lane < LANES // 2, 1.0, -1.0).astype(F32)
    n_chip = KY // SUBLANES // 2
    for row in range(groups):
        lanes = slice(row * LANES, (row + 1) * LANES)
        block = part[:KY, lanes] + pltpu.roll(part[KY:, lanes], LANES // 2, 1) * sign
        for side, ref in enumerate((own_ref, partner_ref)):
            for place in range(n_chip):
                start = (side * n_chip + place) * SUBLANES
                ref[row * n_chip + place, 0] = block[start : start + SUBLANES]


def lift_first_body(cells, lift_ref, sums_ref, res_ref, perm_ref, deep_ref, col_ref, *refs):
    own_ref, partner_ref, lifted_ref, zt_ref = refs[-4:]
    scale = scale_of(gathered(sums_ref, 0), cells)
    scaled = (res_ref[0] / scale).T
    log_perm = jnp.log(perm_ref[0].astype(F32)).T
    transform(lift_ref, deep_ref, col_ref, scaled, log_perm, own_ref, partner_ref, lifted_ref, zt_ref)


def join_body(own_ref, partner_ref, out_ref):
    out_ref[...] = own_ref[...] + partner_ref[...]


def tie_body(*_):
    pass


def next_scalars(first_ref, sums_ref):
    curvature = gathered(sums_ref, 0)
    alpha = gathered(sums_ref, 1) / curvature
    total = gathered(first_ref, 0) + alpha * (
        alpha * gathered(sums_ref, 2) - 2.0 * gathered(sums_ref, 3)
    )
    return curvature, alpha, jnp.maximum(total, 0.0)


def lift_next_body(cells, lift_ref, first_ref, sums_ref, res_ref, image_ref, perm_ref, deep_ref, col_ref, own_ref, partner_ref, lifted_ref, next_ref, zt_ref):
    _, alpha, total = next_scalars(first_ref, sums_ref)
    scale = scale_of(total, cells)
    residual = res_ref[0] - alpha * image_ref[0]
    next_ref[0] = residual
    scaled = (residual / scale).T
    log_perm = jnp.log(perm_ref[0].astype(F32)).T
    transform(lift_ref, deep_ref, col_ref, scaled, log_perm, own_ref, partner_ref, lifted_ref, zt_ref)


def point_body(mix_ref, lifted_ref, _, __, point_ref):
    size = 4 * SUBLANES
    group = 4

    def step(index, carry):
        lines = pl.ds(pl.multiple_of(index * size, size), size)
        for first in range(0, CHANNELS, group):
            sums = [mix_ref[first + j, CHANNELS] for j in range(group)]
            for channel in range(CHANNELS):
                lifted = lifted_ref[0, channel, lines, :]
                sums = [
                    total + mix_ref[first + j, channel] * lifted for j, total in enumerate(sums)
                ]
            for j, total in enumerate(sums):
                point_ref[0, first + j, lines, :] = total
        return carry

    lax.fori_loop(0, lifted_ref.shape[2] // size, step, 0)


def modes_body(cells, n_row, n_col, n_chip, recv_ref, *refs):
    sources = refs[:n_col]
    _, out_ref, weight_ref, sems, field_ref, turned_ref, spec_ref, odd_ref = refs[n_col:]
    own = lax.axis_index(COL)
    copies = [
        pltpu.make_async_copy(
            source, weight_ref.at[lax.rem(own + n_col - shift, n_col)], sems.at[shift]
        )
        for shift, source in enumerate(sources)
    ]
    for copy in copies:
        copy.start()
    rows = recv_ref.shape[1]
    places = n_row * rows
    tile = (SUBLANES, LANES)
    lane = lax.broadcasted_iota(jnp.int32, tile, 1)
    first = lane < LANES // 2
    sign = jnp.where(first, 1.0, -1.0).astype(F32)
    base = lane - lane % CHANNELS

    def turn(value):
        return pltpu.roll(value, LANES // 2, 1) * sign

    for row in range(n_row):
        for place in range(rows):
            value = recv_ref[row * n_chip, place]
            for chip in range(1, n_chip):
                value = value + recv_ref[row * n_chip + chip, place]
            field_ref[row * rows + place] = value
    angle = 2.0 * np.pi / places
    half = KX // 2

    def weigh(coefs, ref):
        total = None
        for place, coef in enumerate(coefs):
            coef = float(coef)
            if abs(coef) < 1e-12:
                continue
            term = ref[place]
            if coef == -1.0:
                term = -term
            elif coef != 1.0:
                term = coef * term
            total = term if total is None else total + term
        return jnp.zeros(tile, F32) if total is None else total

    middle = places // 2
    for place in range(1, middle):
        value, mirror = field_ref[place], field_ref[places - place]
        field_ref[place] = value + mirror
        turned_ref[place] = turn(value - mirror)
    for freq in range(half + 1):
        turns = freq * np.arange(middle + 1) % places
        even = weigh(np.cos(angle * turns), field_ref)
        odd = weigh(np.concatenate([[0.0], np.sin(angle * turns[1:middle])]), turned_ref)
        if freq < half:
            spec_ref[half + freq] = even + odd
        if freq > 0:
            spec_ref[half - freq] = even - odd

    for copy in copies:
        copy.wait()
    share = KX // n_col
    for freq in range(KX):
        value = spec_ref[freq]
        same = [None, None]
        cross = [None, None]
        for channel in range(CHANNELS):
            wide = jnp.take_along_axis(value, base + channel, axis=1)
            weight = weight_ref[freq // share, freq % share, channel]
            for sums, factor in ((same, weight), (cross, pltpu.roll(weight, LANES // 2, 1))):
                term = factor * wide
                kept = sums[channel % 2]
                sums[channel % 2] = term if kept is None else kept + term
        same = same[0] + same[1]
        cross = cross[0] + cross[1]
        total = jnp.where(
            first,
            same - pltpu.roll(same, LANES // 2, 1),
            cross + pltpu.roll(cross, LANES // 2, 1),
        )
        field_ref[freq] = total
        turned_ref[freq] = -turn(total)
    gain = 0.5 / cells
    evens = [field_ref[half] * gain]
    odds = [None]
    for freq in range(1, half):
        evens.append((field_ref[half + freq] + field_ref[half - freq]) * gain)
        odds.append((turned_ref[half + freq] - turned_ref[half - freq]) * gain)
    evens.append(field_ref[0] * gain)
    odds.append(-turned_ref[0] * gain)
    for freq in range(half + 1):
        spec_ref[freq] = evens[freq]
        if freq > 0:
            odd_ref[freq] = odds[freq]

    def store(place, value):
        for chip in range(n_chip):
            out_ref[(place // rows) * n_chip + chip, place % rows] = value

    for place in range(places // 2 + 1):
        turns = place * np.arange(half + 1) % places
        even = weigh(np.cos(angle * turns), spec_ref)
        odd = weigh(np.sin(angle * turns), odd_ref)
        store(place, even + odd)
        if 0 < place < places // 2:
            store(places - place, even - odd)


def back_transform(recv_ref, other_ref, point_ref, proj_ref, col_ref, deep_ref, wave_ref, total_ref, scale):
    groups = 2 * KZ * CHANNELS // LANES
    n_col = KY // SUBLANES
    cols = col_ref.shape[2] // 2
    lane = lax.broadcasted_iota(jnp.int32, (KY, LANES), 1)
    sign = jnp.where(lane < LANES // 2, -1.0, 1.0).astype(F32)
    half = 2 * KZ
    pieces = []
    for row in range(groups):
        chips = slice(row * n_col // 2, (row + 1) * n_col // 2)
        value = jnp.concatenate([recv_ref[chips, 0], other_ref[chips, 0]], 0)
        value = value.reshape(KY, LANES)
        turned = pltpu.roll(value, LANES // 2, 1) * sign
        both = jnp.concatenate([value, turned], 0)
        pieces.append(jnp.concatenate(split_three(both), 0).T.astype(BF16))
    part = matmul(jnp.concatenate(pieces, 0), col_ref[lax.axis_index(COL)])
    wave_ref[...] = part[:, :cols] + part[:, cols:]

    def waves(out):
        both = [wave_ref[pl.ds(out + j, half, stride=CHANNELS), :] for j in range(2)]
        high, middle, low = (
            part.astype(BF16) for part in split_three(jnp.concatenate(both, 1))
        )
        return jnp.concatenate([high, middle, low, high], 0)

    for out in range(0, CHANNELS, 2):
        spatial = matmul(deep_ref[...], waves(out))
        for start in range(0, spatial.shape[0], CHUNK):
            lines = slice(start, start + CHUNK)
            total = proj_ref[CHANNELS] if out == 0 else total_ref[lines]
            for j in range(2):
                value = spatial[lines, j * cols : (j + 1) * cols] + point_ref[0, out + j, lines]
                total = total + proj_ref[out + j] * scaled_gelu(value)
            total_ref[lines] = total
    return (scale * total_ref[...]).T


def put_lines(update, place, left_ref, right_ref):
    left_ref[pl.ds(place, 1), :] = update[:1]
    right_ref[pl.ds(place, 1), :] = update[update.shape[0] - 1 :]


def back_outer(update, kept_ref, field_ref, low_ref, high_ref, left_ref, right_ref):
    step = pl.program_id(0)
    kept_ref[0, 0] = update
    field_ref[0] = update
    last = left_ref.shape[0] - 1

    @pl.when(step == 0)
    def _():
        low_ref[...] = update
        put_lines(update, 0, left_ref, right_ref)

    @pl.when(step == 1)
    def _():
        high_ref[...] = update
        put_lines(update, last, left_ref, right_ref)


def back_inner(update, left_in, right_in, kept_ref, field_ref, left_ref, right_ref):
    step = pl.program_id(0)
    kept_ref[0, 0] = update
    field_ref[0] = update
    last = left_ref.shape[0] - 1

    @pl.when(step == 0)
    def _():
        for place in (0, last):
            line = slice(place, place + 1)
            left_ref[line] = left_in[line]
            right_ref[line] = right_in[line]

    put_lines(update, step + 1, left_ref, right_ref)


def back_body(scale_from, scalars, waiting, inner, proj_ref, *refs):
    scalar_refs, refs = refs[:scalars], refs[scalars:]
    recv_ref, other_ref, point_ref, col_ref, deep_ref = refs[:5]
    refs = refs[5 + waiting :]
    *outs, wave_ref, total_ref = refs
    update = back_transform(
        recv_ref, other_ref, point_ref, proj_ref, col_ref, deep_ref, wave_ref, total_ref,
        scale_from(*scalar_refs),
    )
    (back_inner if inner else back_outer)(update, *outs)


def stencil(fields, perms):
    own, before, after, left, right = fields
    cols, depth = own.shape
    line = lax.broadcasted_iota(jnp.int32, (cols, depth), 0)
    deep = lax.broadcasted_iota(jnp.int32, (cols, depth), 1)

    def sides(array, before, after, left, right, first, last):
        return (
            before,
            after,
            jnp.where(line == 0, left, pltpu.roll(array, 1, 0)),
            jnp.where(line == cols - 1, right, pltpu.roll(array, cols - 1, 0)),
            jnp.where(deep == 0, first, pltpu.roll(array, 1, 1)),
            jnp.where(deep == depth - 1, last, pltpu.roll(array, depth - 1, 1)),
        )

    perm, *others = perms
    others = [
        jnp.where(other > 0.0, other, edge)
        for other, edge in zip(others, (perm, perm, perm[:1], perm[cols - 1 :]))
    ]
    total = None
    for other, conductance in zip(
        sides(own, before, after, left, right, 0.0, 0.0), sides(perm, *others, perm, perm)
    ):
        term = harmonic(perm, conductance) * (own - other)
        total = term if total is None else total + term
    return total


def add_sums(terms, out_ref, acc_ref):
    step = pl.program_id(0)

    @pl.when(step == 0)
    def _():
        acc_ref[...] = jnp.zeros_like(acc_ref)

    for j, term in enumerate(terms):
        acc_ref[j : j + 1] += lane_sums(term)

    @pl.when(step == pl.num_programs(0) - 1)
    def _():
        spread([acc_ref[j : j + 1] for j in range(len(terms))], out_ref)


def around(ref, index, halo):
    low_ref, high_ref, left_ref, right_ref = halo
    step = pl.program_id(0)
    last = pl.num_programs(0) - 1
    line = pl.ds(step, 1)

    def plane(place):
        return ref[index + (place,)].astype(F32)

    def outside(axis, edge, value):
        return jnp.where(lax.axis_index(axis) == edge, 0.0, value)

    low = outside("row", 0, low_ref[...])
    high = outside("row", lax.axis_size("row") - 1, high_ref[...])
    left = outside(COL, 0, left_ref[line, :])
    right = outside(COL, lax.axis_size(COL) - 1, right_ref[line, :])
    before = jnp.where(step == 0, low, plane(jnp.maximum(step - 1, 0)))
    after = jnp.where(step == last, high, plane(jnp.minimum(step + 1, last)))
    return plane(step), before, after, left, right


def operator_first_body(field_ref, perm_ref, *refs):
    halo, perm_halo = refs[:4], refs[4:8]
    res_ref, image_ref, out_ref, acc_ref = refs[8:]
    fields = around(field_ref, (), halo)
    image = stencil(fields, around(perm_ref, (), perm_halo))
    own = fields[0]
    residual = res_ref[0]
    image_ref[0] = image
    add_sums((own * image, residual * own, image * image, residual * image), out_ref, acc_ref)


def operator_next_body(cells, first_ref, sums_ref, field_ref, old_ref, perm_ref, *refs):
    halo, old, perm_halo = refs[:4], refs[4:8], refs[8:12]
    res_ref, before_ref, way_ref, image_ref, out_ref, acc_ref = refs[12:]
    _, _, total = next_scalars(first_ref, sums_ref)
    factor = scale_of(total, cells) / scale_of(gathered(first_ref, 0), cells)
    old = around(old_ref, (), old)
    fields = [new - factor * other for new, other in zip(around(field_ref, (), halo), old)]
    image = stencil(fields, around(perm_ref, (), perm_halo))
    own = fields[0]
    residual = res_ref[0]
    way_ref[0] = own
    image_ref[0] = image
    add_sums((own * image, own * before_ref[0], residual * own, residual * old[0]), out_ref, acc_ref)


def last_body(sums_ref, later_ref, old_ref, way_ref, res_ref, before_ref, image_ref, sol_ref, out_ref):
    curvature = gathered(sums_ref, 0)
    alpha = gathered(sums_ref, 1) / curvature
    cross = gathered(later_ref, 1)
    delta = cross / curvature
    along = gathered(later_ref, 2) - delta * gathered(later_ref, 3)
    later = along / (gathered(later_ref, 0) - delta * cross)
    sol_ref[0] = alpha * old_ref[0] + later * (way_ref[0] - delta * old_ref[0])
    out_ref[0] = res_ref[0] - later * (image_ref[0] - delta * before_ref[0])


def exchange(blocks, axes):
    return lax.all_to_all(blocks, axes, split_axis=0, concat_axis=0, tiled=True)


def swap(blocks):
    return lax.ppermute(blocks, "core", [(0, 1), (1, 0)])


def add_up(partial):
    return exchange(partial, BOTH)


def shift_planes(axis, first, last):
    count = lax.axis_size(axis)
    forward = [(i, (i + 1) % count) for i in range(count)]
    backward = [(target, source) for source, target in forward]
    return lax.ppermute(last, axis, forward), lax.ppermute(first, axis, backward)


def neighbours(low, high, left, right):
    return shift_planes("row", low, high) + shift_planes(COL, left, right)


def tiled_local(right_side, permeability, lift_weight, spectral_weight, mix_weight, proj_weight):
    rows, cols, depth = right_side.shape
    n_row = lax.axis_size("row")
    n_col = lax.axis_size(COL)
    count = n_row * n_col
    cells = float(rows * n_row * cols * n_col * depth)
    freq = KX // n_col
    deep_forward, deep_back = (jnp.asarray(t) for t in deep_tables(n_row, depth))
    col_forward, col_back = (jnp.asarray(t) for t in column_tables(n_col, cols))
    lift_weight = GAIN * lift_weight.T
    mix_weight = jnp.where(jnp.arange(CHANNELS + 1) < CHANNELS, 0.5, GAIN) * mix_weight
    proj_weight = jnp.where(jnp.arange(CHANNELS + 1) < CHANNELS, 0.5 / GAIN, 1.0) * proj_weight
    field = shape(rows, cols, depth)
    field_bytes = 4 * rows * cols * depth
    partial = shape(count, SUBLANES, LANES)
    channels = shape(rows, CHANNELS, depth, cols)
    n_chip = n_col // 2
    spectra = shape(n_row * n_chip, rows, SUBLANES, LANES)
    spectra_bytes = 4 * spectra.size
    smem = whole(pltpu.SMEM)
    vmem = whole()
    anywhere = whole(pl.ANY)
    plane = pl.BlockSpec((1, cols, depth), lambda i: (i, 0, 0))
    spectra_block = pl.BlockSpec((n_row * n_chip, 1, SUBLANES, LANES), lambda i: (0, i, 0, 0))
    point_block = pl.BlockSpec((1, CHANNELS, depth, cols), lambda i: (i, 0, 0, 0))
    kept_shape = shape(ITERS, rows, cols, depth)
    lift_flops = 2.0e9
    back_flops = 2.0e9

    weight_shape = (freq, CHANNELS, SUBLANES, LANES)
    kept_weights, *weights = call(
        weight_body,
        (shape(*weight_shape),) * n_col,
        [vmem],
        (vmem,) * n_col,
        scratch=[pltpu.VMEM((n_col,) + weight_shape, F32)],
        moved=8 * spectral_weight.size,
    )(spectral_weight)
    weights = [kept_weights] + [
        lax.ppermute(part, COL, [(i, (i + shift + 1) % n_col) for i in range(n_col)])
        for shift, part in enumerate(weights)
    ]
    edge_shapes = (shape(cols, depth),) * 2 + (shape(rows, depth),) * 2
    squares, *perm_edges = call(
        squares_body,
        (partial,) + edge_shapes,
        [vmem, vmem],
        (vmem,) * 5,
        moved=2 * field_bytes,
    )(right_side, permeability)
    squares = add_up(squares)
    perm_halo = neighbours(*perm_edges)
    acc_scratch = pltpu.VMEM((SUBLANES, LANES), F32)
    zt_scratch = pltpu.VMEM((2 * KZ * CHANNELS, cols), F32)

    def points(lifted, part, before, after):
        first = part * rows // 2
        half_block = pl.BlockSpec((1, CHANNELS, depth, cols), lambda i: (first + i, 0, 0, 0))
        return call(
            point_body,
            channels,
            [smem, half_block, anywhere, anywhere],
            half_block,
            grid=(rows // 2,),
            flops=2.5e9,
            moved=16 * field_bytes,
            alias={2: 0} if part else None,
            limit=12,
        )(mix_weight, lifted, before, after)

    def modes(received, before):
        places = rows * n_row
        tiles = lambda size: pltpu.VMEM((size, SUBLANES, LANES), F32)
        return call(
            functools.partial(modes_body, cells, n_row, n_col, n_chip),
            spectra,
            [vmem] + [anywhere] * (n_col + 1),
            vmem,
            scratch=[
                pltpu.VMEM((n_col,) + weight_shape, F32),
                pltpu.SemaphoreType.DMA((n_col,)),
                tiles(places),
                tiles(places),
                tiles(KX),
                tiles(KX),
            ],
            moved=2 * spectra_bytes + 4 * spectral_weight.size,
            near=(0,),
        )(received, *weights, before)

    def mixed_modes(own, partner, lifted, waiting):
        blocks = call(join_body, spectra, [vmem, vmem], vmem, near=(0, 1))(own, swap(partner))
        received = exchange(blocks, CHIPS)
        point = points(lifted, 0, blocks, blocks)
        blocks = modes(received, point)
        received = exchange(blocks, CHIPS)
        point = points(lifted, 1, point, blocks)
        received = pl.pallas_call(
            tie_body,
            out_shape=spectra,
            in_specs=[anywhere] * (2 + len(waiting)),
            out_specs=anywhere,
            input_output_aliases={0: 0},
        )(received, point, *waiting)
        return received, swap(received), point

    def back(index, scale_from, scalars, fields, waiting):
        def run(place_of, steps, inner, waiting, outs, out_specs, alias, loose):
            count_in = 1 + len(scalars)
            spectra_at = pl.BlockSpec(
                (n_row * n_chip, 1, SUBLANES, LANES), lambda i: (0, place_of(i), 0, 0)
            )
            point_at = pl.BlockSpec(
                (1, CHANNELS, depth, cols), lambda i: (place_of(i), 0, 0, 0)
            )
            kept_at = pl.BlockSpec((1, 1, cols, depth), lambda i: (index, place_of(i), 0, 0))
            plane_at = pl.BlockSpec((1, cols, depth), lambda i: (place_of(i), 0, 0))
            return call(
                functools.partial(
                    back_body,
                    scale_from,
                    len(scalars),
                    2 if inner else len(waiting),
                    inner,
                ),
                outs,
                [smem]
                + [vmem] * len(scalars)
                + [spectra_at, spectra_at, point_at, vmem, vmem]
                + ([anywhere, anywhere, vmem, vmem] if inner else [anywhere] * len(waiting)),
                (kept_at, plane_at) + out_specs,
                grid=(steps,),
                scratch=[zt_scratch, pltpu.VMEM((depth, cols), F32)],
                flops=back_flops / 2,
                moved=9 * field_bytes,
                alias={count_in + 5 + i: o for i, o in alias},
                limit=12,
                near=(count_in + 1,)
                + tuple(
                    count_in + 5 + i
                    for i, array in enumerate(waiting)
                    if array.size != kept_shape.size
                ),
                loose=loose,
            )(proj_weight, *scalars, *fields, col_back, deep_back, *waiting)

        kept, field_out, low, high, left, right = run(
            lambda i: i * (rows - 1),
            2,
            False,
            waiting,
            (kept_shape, field) + edge_shapes,
            (vmem,) * 4,
            [(0, 0)] if index else [],
            (1,),
        )
        halo_rows = shift_planes("row", low, high)
        kept, field_out, left, right = run(
            lambda i: i + 1,
            rows - 2,
            True,
            (kept, field_out, left, right),
            (kept_shape, field) + edge_shapes[2:],
            (vmem,) * 2,
            [(0, 0), (1, 1)],
            (1,),
        )
        return (kept, field_out) + halo_rows + shift_planes(COL, left, right)

    own, partner, lifted = call(
        functools.partial(lift_first_body, cells),
        (spectra, spectra, channels),
        [smem, vmem, plane, plane, vmem, vmem] + [anywhere] * n_col,
        (spectra_block, spectra_block, point_block),
        limit=16,
        loose=(0, 1),
        near=(6, 7, 8, 9),
        grid=(rows,),
        scratch=[zt_scratch],
        flops=lift_flops,
        moved=2 * field_bytes + spectra_bytes,
    )(lift_weight, squares, right_side, permeability, deep_forward, col_forward, *weights)
    received, other, point = mixed_modes(own, partner, lifted, perm_halo)
    kept, old, *edges = back(
        0,
        lambda first_ref: scale_of(gathered(first_ref, 0), cells),
        (squares,),
        (received, other, point),
        (),
    )

    old_halo = edges
    args = (old, permeability, *old_halo, *perm_halo, right_side)
    image, sums = call(
        operator_first_body,
        (field, partial),
        [vmem] * 10 + [plane],
        (plane, vmem),
        grid=(rows,),
        scratch=[acc_scratch],
        moved=9 * field_bytes,
        near=range(11),
        loose=range(3),
    )(*args)
    sums = add_up(sums)

    own, partner, lifted, residual = call(
        functools.partial(lift_next_body, cells),
        (spectra, spectra, channels, field),
        [smem, vmem, vmem, plane, plane, plane, vmem, vmem],
        (spectra_block, spectra_block, point_block, plane),
        limit=16,
        near=(4,),
        loose=(0, 1),
        grid=(rows,),
        scratch=[zt_scratch],
        flops=lift_flops,
        moved=4 * field_bytes + spectra_bytes,
    )(lift_weight, squares, sums, right_side, image, permeability, deep_forward, col_forward)
    received, other, point = mixed_modes(own, partner, lifted, ())
    kept, update, *edges = back(
        1,
        lambda first_ref, sums_ref: scale_of(next_scalars(first_ref, sums_ref)[2], cells),
        (squares, sums),
        (received, other, point),
        (kept,),
    )

    halo = edges
    args = (squares, sums, update, old, permeability, *halo, *old_halo, *perm_halo, residual, image)
    way, last_image, later = call(
        functools.partial(operator_next_body, cells),
        (field, field, partial),
        [vmem] * 17 + [plane] * 2,
        (plane, plane, vmem),
        grid=(rows,),
        scratch=[acc_scratch],
        near=range(19),
        loose=range(3),
        moved=11 * field_bytes,
    )(*args)
    later = add_up(later)
    answer, residual = call(
        last_body,
        (field, field),
        [vmem, vmem] + [plane] * 5,
        (plane, plane),
        grid=(rows,),
        moved=6 * field_bytes,
        near=range(7),
        loose=range(3),
    )(sums, later, old, way, residual, image, last_image)
    return (answer, residual, kept)


def fits_tiles(mesh, block):
    rows, cols, depth = block
    n_row, n_col = mesh.shape["row"], mesh.shape["col"]
    return (
        ITERS == 2
        and KZ == n_row * (LANES // (2 * CHANNELS))
        and KY == n_col * SUBLANES
        and KX % n_col == 0
        and n_col % 2 == 0
        and cols == LANES
        and depth % LANES == 0
        and rows * n_row >= KX
        and rows > 2
        and rows % 2 == 0
    )


def solution(mesh):
    placed = (
        P("row", "col", None),
        P("row", "col", None),
        P(),
        P(None, "row", None, None, "col"),
        P(),
        P(),
    )
    outputs = (P("row", "col", None), P("row", "col", None), P(None, "row", "col", None))

    def run(right_side, *others):
        rows, cols, depth = right_side.shape
        n_row, n_col = mesh.shape["row"], mesh.shape["col"]
        if not fits_tiles(mesh, (rows // n_row, cols // n_col, depth)):
            return jax.shard_map(
                local, mesh=mesh, in_specs=placed, out_specs=outputs, check_vma=False
            )(right_side, *others)
        cores = jax.sharding.Mesh(mesh.devices.reshape(n_row, n_col // 2, 2), BOTH)
        placed_cores, outputs_cores = jax.tree.map(
            lambda spec: P(*(COL if axis == "col" else axis for axis in spec)),
            (placed, outputs),
            is_leaf=lambda spec: isinstance(spec, P),
        )
        return jax.shard_map(
            tiled_local,
            mesh=cores,
            in_specs=placed_cores,
            out_specs=outputs_cores,
            check_vma=False,
        )(right_side, *others)

    return run
```

```python
import functools
import math

import jax
import jax.numpy as jnp
import ml_dtypes
import numpy as np
from jax import lax
from jax.experimental import pallas as pl
from jax.experimental.pallas import tpu as pltpu
from jax.sharding import PartitionSpec as P

CHANNELS = 16
KX = 16
KY = 32
KZ = 32
ITERS = 2


HIGHEST = lax.Precision.HIGHEST


def with_halo(block, sides, width):
    for axis, dim in sides:
        count = lax.axis_size(axis)
        forward = [(i, i + 1) for i in range(count - 1)]
        backward = [(target, source) for source, target in forward]
        low = lax.ppermute(
            lax.slice_in_dim(block, block.shape[dim] - width, None, axis=dim), axis, forward
        )
        high = lax.ppermute(lax.slice_in_dim(block, 0, width, axis=dim), axis, backward)
        block = jnp.concatenate([low, block, high], axis=dim)
    return block


def einsum_high(form, left, right):
    return jnp.einsum(form, left, right, precision=HIGHEST)


def harmonic(first, second):
    return 2.0 * first * second / (first + second)


def wave_table(freqs, places, length):
    turns = freqs[None, :] * places[:, None] % length
    angle = turns.astype(jnp.float32) * (2.0 * jnp.pi / length)
    return (jnp.cos(angle), jnp.sin(angle))


def signed_freqs(count):
    return jnp.arange(count, dtype=jnp.int32) - count // 2


def face_arrays(permeability):
    padded = with_halo(permeability, (("row", 0), ("col", 1)), 1).astype(jnp.float32)
    own = permeability.astype(jnp.float32)
    edged = jnp.pad(own, ((1, 1), (1, 1), (0, 0)), mode="edge")
    padded = jnp.where(padded > 0.0, padded, edged)
    first = harmonic(padded[:-1, 1:-1], padded[1:, 1:-1])
    second = harmonic(padded[1:-1, :-1], padded[1:-1, 1:])
    deep = jnp.pad(own, ((0, 0), (0, 0), (1, 1)), mode="edge")
    third = harmonic(deep[:, :, :-1], deep[:, :, 1:])
    return ((first, second, third), jnp.log(own))


def apply_operator(field, faces):
    first, second, third = faces
    padded = with_halo(field, (("row", 0), ("col", 1)), 1)
    padded = jnp.pad(padded, ((0, 0), (0, 0), (1, 1)))
    total = first[:-1] * (field - padded[:-2, 1:-1, 1:-1])
    total = total + first[1:] * (field - padded[2:, 1:-1, 1:-1])
    total = total + second[:, :-1] * (field - padded[1:-1, :-2, 1:-1])
    total = total + second[:, 1:] * (field - padded[1:-1, 2:, 1:-1])
    total = total + third[:, :, :-1] * (field - padded[1:-1, 1:-1, :-2])
    total = total + third[:, :, 1:] * (field - padded[1:-1, 1:-1, 2:])
    return total


def global_squares(field):
    return lax.psum(jnp.sum(field * field), ("row", "col"))


def mix_modes(real_in, imag_in, spectral_weight, deep_count, freq_count):
    block = spectral_weight.reshape(2, deep_count, CHANNELS, CHANNELS, freq_count, KY)
    real_out = einsum_high("kcfg,kcofg->kofg", real_in, block[0]) - einsum_high(
        "kcfg,kcofg->kofg", imag_in, block[1]
    )
    imag_out = einsum_high("kcfg,kcofg->kofg", imag_in, block[0]) + einsum_high(
        "kcfg,kcofg->kofg", real_in, block[1]
    )
    return (real_out, imag_out)


def spectral_transpose(real_part, imag_part, spectral_weight, grid):
    rows, cols, n_row, n_col, row_id, col_id = grid
    full_rows = rows * n_row
    full_cols = cols * n_col
    cosine_rows, sine_rows = wave_table(
        signed_freqs(KX), jnp.arange(full_rows, dtype=jnp.int32), full_rows
    )
    cosine_cols, sine_cols = wave_table(
        signed_freqs(KY), jnp.arange(full_cols, dtype=jnp.int32), full_cols
    )
    real_part, imag_part = (
        lax.all_to_all(real_part, "row", split_axis=0, concat_axis=1, tiled=True),
        lax.all_to_all(imag_part, "row", split_axis=0, concat_axis=1, tiled=True),
    )
    first_real = einsum_high("qxy,xf->qfy", real_part, cosine_rows) + einsum_high(
        "qxy,xf->qfy", imag_part, sine_rows
    )
    first_imag = einsum_high("qxy,xf->qfy", imag_part, cosine_rows) - einsum_high(
        "qxy,xf->qfy", real_part, sine_rows
    )
    first_real, first_imag = (
        lax.all_to_all(first_real, "col", split_axis=1, concat_axis=2, tiled=True),
        lax.all_to_all(first_imag, "col", split_axis=1, concat_axis=2, tiled=True),
    )
    second_real = einsum_high("qfy,yg->qfg", first_real, cosine_cols) + einsum_high(
        "qfy,yg->qfg", first_imag, sine_cols
    )
    second_imag = einsum_high("qfy,yg->qfg", first_imag, cosine_cols) - einsum_high(
        "qfy,yg->qfg", first_real, sine_cols
    )
    deep_count = KZ // n_row
    freq_count = KX // n_col
    shape_in = (deep_count, CHANNELS, freq_count, KY)
    mixed_real, mixed_imag = mix_modes(
        second_real.reshape(shape_in),
        second_imag.reshape(shape_in),
        spectral_weight,
        deep_count,
        freq_count,
    )
    shape_out = (deep_count * CHANNELS, freq_count, KY)
    mixed_real = mixed_real.reshape(shape_out)
    mixed_imag = mixed_imag.reshape(shape_out)
    back_real = einsum_high("qfg,yg->qfy", mixed_real, cosine_cols) - einsum_high(
        "qfg,yg->qfy", mixed_imag, sine_cols
    )
    back_imag = einsum_high("qfg,yg->qfy", mixed_imag, cosine_cols) + einsum_high(
        "qfg,yg->qfy", mixed_real, sine_cols
    )
    back_real, back_imag = (
        lax.all_to_all(back_real, "col", split_axis=2, concat_axis=1, tiled=True),
        lax.all_to_all(back_imag, "col", split_axis=2, concat_axis=1, tiled=True),
    )
    out_real = einsum_high("qfy,xf->qxy", back_real, cosine_rows) - einsum_high(
        "qfy,xf->qxy", back_imag, sine_rows
    )
    out_imag = einsum_high("qfy,xf->qxy", back_imag, cosine_rows) + einsum_high(
        "qfy,xf->qxy", back_real, sine_rows
    )
    out_real, out_imag = (
        lax.all_to_all(out_real, "row", split_axis=1, concat_axis=0, tiled=True),
        lax.all_to_all(out_imag, "row", split_axis=1, concat_axis=0, tiled=True),
    )
    return (out_real, out_imag)


def precondition(residual, squares_total, log_perm, weights, grid, cells):
    lift_weight, spectral_weight, mix_weight, proj_weight = weights
    rows, cols, depth = residual.shape
    scale = jnp.sqrt(squares_total / cells + 1e-06)
    scaled = residual / scale
    lifted = jax.nn.gelu(
        lift_weight[:, 0, None, None, None] * scaled[None]
        + lift_weight[:, 1, None, None, None] * log_perm[None]
        + lift_weight[:, 2, None, None, None]
    )
    cosine_deep, sine_deep = wave_table(
        jnp.arange(KZ, dtype=jnp.int32), jnp.arange(depth, dtype=jnp.int32), depth
    )
    real_part = einsum_high("cxyz,zk->kcxy", lifted, cosine_deep).reshape(KZ * CHANNELS, rows, cols)
    imag_part = -einsum_high("cxyz,zk->kcxy", lifted, sine_deep).reshape(KZ * CHANNELS, rows, cols)
    out_real, out_imag = spectral_transpose(real_part, imag_part, spectral_weight, grid)
    out_real = out_real.reshape(KZ, CHANNELS, rows, cols)
    out_imag = out_imag.reshape(KZ, CHANNELS, rows, cols)
    spatial = (
        einsum_high("kcxy,zk->cxyz", out_real, cosine_deep)
        - einsum_high("kcxy,zk->cxyz", out_imag, sine_deep)
    ) / cells
    point = (
        einsum_high("oc,cxyz->oxyz", mix_weight[:, :CHANNELS], lifted)
        + mix_weight[:, CHANNELS, None, None, None]
    )
    hidden = jax.nn.gelu(spatial + point)
    return scale * (
        einsum_high("o,oxyz->xyz", proj_weight[:CHANNELS], hidden) + proj_weight[CHANNELS]
    )


def local(right_side, permeability, lift_weight, spectral_weight, mix_weight, proj_weight):
    rows, cols, depth = right_side.shape
    n_row = lax.axis_size("row")
    n_col = lax.axis_size("col")
    grid = (rows, cols, n_row, n_col, lax.axis_index("row"), lax.axis_index("col"))
    cells = float(rows * n_row * cols * n_col * depth)
    faces, log_perm = face_arrays(permeability)
    weights = (lift_weight, spectral_weight, mix_weight, proj_weight)

    def precond(residual, squares_total):
        return precondition(residual, squares_total, log_perm, weights, grid, cells)

    solution = jnp.zeros_like(right_side)
    residual = right_side
    kept = []
    update = precond(residual, global_squares(residual))
    kept.append(update)
    direction = update
    for step in range(ITERS):
        image = apply_operator(direction, faces)
        curvature, along = lax.psum(
            (jnp.sum(direction * image), jnp.sum(residual * direction)), ("row", "col")
        )
        alpha = along / curvature
        solution = solution + alpha * direction
        residual = residual - alpha * image
        if step + 1 < ITERS:
            update = precond(residual, global_squares(residual))
            kept.append(update)
            beta = lax.psum(jnp.sum(update * image), ("row", "col")) / curvature
            direction = update - beta * direction
    return (solution, residual, jnp.stack(kept))


LANES = 128
SUBLANES = 8
COL = ("y", "core")
CHIPS = ("row", "y")
BOTH = ("row", "y", "core")
CHUNK = 32
F32 = jnp.float32
BF16 = jnp.bfloat16


def split_table(table):
    high = table.astype(ml_dtypes.bfloat16)
    low = (table - high.astype(np.float64)).astype(ml_dtypes.bfloat16)
    return high, low


def split(value):
    high = value.astype(BF16)
    return high, (value - high.astype(F32)).astype(BF16)


def split_three(value):
    high = value.astype(BF16).astype(F32)
    rest = value - high
    middle = rest.astype(BF16).astype(F32)
    return high, middle, rest - middle


def matmul(left, right):
    return jnp.dot(left, right, preferred_element_type=F32)


def matmul_nt(left, right):
    return lax.dot_general(left, right, (((1,), (1,)), ((), ())), preferred_element_type=F32)


def angles(freqs, places, length):
    turns = np.multiply.outer(freqs, places) % length
    return turns * (2.0 * np.pi / length)


def deep_order(n_row):
    count = KZ // n_row
    order = [
        (part, row * count + place)
        for row in range(n_row)
        for part in range(2)
        for place in range(count)
    ]
    return np.array(order)


def deep_tables(n_row, depth):
    order = deep_order(n_row)
    angle = angles(order[:, 1], np.arange(depth), depth)
    wave = np.where(order[:, :1] == 0, np.cos(angle), -np.sin(angle))
    high, low = split_table(wave)
    return np.concatenate([high, low], 0), np.concatenate([high.T, high.T, high.T, low.T], 1)


def column_tables(n_col, cols):
    freqs = np.arange(KY) - KY // 2
    forward = []
    back = []
    for place in range(n_col):
        angle = angles(freqs, place * cols + np.arange(cols), n_col * cols)
        own = np.arange(KY).reshape(-1, 2, SUBLANES)[:, place % 2].reshape(-1)
        partner = np.arange(KY).reshape(-1, 2, SUBLANES)[:, 1 - place % 2].reshape(-1)
        angle = angle[np.concatenate([own, partner])]
        both = np.concatenate([np.cos(angle), np.sin(angle)], 0)
        high, low = split_table(both)
        forward.append(
            np.concatenate(
                [
                    np.concatenate([high, high], 1),
                    np.concatenate([low, np.zeros_like(low)], 1),
                ],
                0,
            )
        )
        back.append(
            np.concatenate(
                [
                    np.concatenate([high, low], 1),
                    np.concatenate([high, low], 1),
                    np.concatenate([high, np.zeros_like(low)], 1),
                ],
                0,
            )
        )
    return np.stack(forward), np.stack(back)


GAIN = (math.sqrt(2.0 / math.pi) * 0.044715) ** (1.0 / 3.0)
LINEAR = math.sqrt(2.0 / math.pi) / GAIN


def scaled_gelu(value):
    return value + value * jnp.tanh(value * (value * value + LINEAR))


def call(body, outs, in_specs, out_specs, grid=(), scratch=(), flops=0, moved=0, alias=None, limit=8, near=(), loose=()):
    single = not isinstance(outs, tuple)
    outs = (outs,) if single else outs
    out_specs = (out_specs,) if single else out_specs
    run = pl.pallas_call(
        body,
        out_shape=tuple(
            out if place in loose or out.size <= 2**16 else pltpu.HBM(out.shape, out.dtype)
            for place, out in enumerate(outs)
        ),
        grid=grid,
        in_specs=in_specs,
        out_specs=out_specs,
        scratch_shapes=list(scratch),
        input_output_aliases=alias or {},
        compiler_params=pltpu.CompilerParams(vmem_limit_bytes=limit * 1024 * 1024),
        cost_estimate=pl.CostEstimate(
            flops=int(flops), bytes_accessed=int(moved), transcendentals=0
        ),
    )

    def wrapped(*args):
        held = [
            arg
            if place in near or spec.memory_space == pltpu.SMEM
            else pltpu.with_memory_space_constraint(arg, pltpu.HBM)
            for place, (arg, spec) in enumerate(zip(args, in_specs))
        ]
        found = run(*held)
        return found[0] if single else found

    return wrapped


def whole(memory=pltpu.VMEM):
    return pl.BlockSpec(memory_space=memory)


def shape(*dims):
    return jax.ShapeDtypeStruct(dims, F32)


def lane_sums(value):
    folded = jnp.sum(value.reshape(-1, SUBLANES, value.shape[-1]), axis=0)
    folded = sum(
        folded[:, start : start + LANES] for start in range(0, folded.shape[1], LANES)
    )
    return jnp.sum(folded, axis=0, keepdims=True)


def spread(rows, ref):
    rows = rows + [jnp.zeros_like(rows[0])] * (SUBLANES - len(rows))
    ref[...] = jnp.broadcast_to(jnp.concatenate(rows, 0)[None], ref.shape)


def gathered(ref, row):
    total = jnp.sum(ref[...], axis=0)
    return jnp.sum(total[row : row + 1], axis=1, keepdims=True)


def squares_body(field_ref, perm_ref, out_ref, low_ref, high_ref, left_ref, right_ref):
    total = field_ref[0] * field_ref[0]
    for place in range(1, field_ref.shape[0]):
        total = total + field_ref[place] * field_ref[place]
    spread([lane_sums(total)], out_ref)
    rows, cols, _ = perm_ref.shape
    low_ref[...] = perm_ref[0].astype(F32)
    high_ref[...] = perm_ref[rows - 1].astype(F32)
    for place in range(rows):
        plane = perm_ref[place].astype(F32)
        left_ref[place : place + 1, :] = plane[:1]
        right_ref[place : place + 1, :] = plane[cols - 1 :]


def weight_body(weight_ref, *refs):
    *out_refs, hold_ref = refs
    groups, freq, channels, fine, _ = hold_ref.shape
    parts, deep, _, outs, modes = weight_ref.shape
    for channel in range(channels):
        block = weight_ref[:, :, channel].reshape(parts * deep * outs, modes)
        block = block.T.reshape(freq, groups, fine, parts * deep * outs)
        for group in range(groups):
            hold_ref[group, :, channel] = block[:, group]
    place = lax.axis_index(COL)
    for shift, out_ref in enumerate(out_refs):
        out_ref[...] = hold_ref[lax.rem(place + shift, groups)]


def scale_of(total, cells):
    return jnp.sqrt(total / cells + 1e-06)


def lift_channel(weight_ref, channel, scaled, log_perm):
    return scaled_gelu(
        weight_ref[0, channel] * scaled
        + (weight_ref[1, channel] * log_perm + weight_ref[2, channel])
    )


def transform(lift_ref, deep_ref, col_ref, scaled, log_perm, own_ref, partner_ref, lifted_ref, zt_ref):
    half = 2 * KZ
    cols = scaled.shape[1]
    for channel in range(0, CHANNELS, 2):
        pair = [lift_channel(lift_ref, channel + j, scaled, log_perm) for j in range(2)]
        for j in range(2):
            lifted_ref[0, channel + j] = pair[j]
        high, low = split(jnp.concatenate(pair, 1))
        part = matmul(deep_ref[...], high)
        part = part[:half] + part[half:] + matmul(deep_ref[:half], low)
        for j in range(2):
            zt_ref[pl.ds(channel + j, half, stride=CHANNELS), :] = part[:, j * cols : (j + 1) * cols]
    groups = half * CHANNELS // LANES
    part = matmul_nt(col_ref[lax.axis_index(COL)], jnp.concatenate(split(zt_ref[...]), 1))
    part = part[: 2 * KY] + part[2 * KY :]
    lane = lax.broadcasted_iota(jnp.int32, (KY, LANES), 1)
    sign = jnp.where(lane < LANES // 2, 1.0, -1.0).astype(F32)
    n_chip = KY // SUBLANES // 2
    for row in range(groups):
        lanes = slice(row * LANES, (row + 1) * LANES)
        block = part[:KY, lanes] + pltpu.roll(part[KY:, lanes], LANES // 2, 1) * sign
        for side, ref in enumerate((own_ref, partner_ref)):
            for place in range(n_chip):
                start = (side * n_chip + place) * SUBLANES
                ref[row * n_chip + place, 0] = block[start : start + SUBLANES]


def lift_first_body(cells, lift_ref, sums_ref, res_ref, perm_ref, deep_ref, col_ref, *refs):
    own_ref, partner_ref, lifted_ref, zt_ref = refs[-4:]
    scale = scale_of(gathered(sums_ref, 0), cells)
    scaled = (res_ref[0] / scale).T
    log_perm = jnp.log(perm_ref[0].astype(F32)).T
    transform(lift_ref, deep_ref, col_ref, scaled, log_perm, own_ref, partner_ref, lifted_ref, zt_ref)


def join_body(own_ref, partner_ref, out_ref):
    out_ref[...] = own_ref[...] + partner_ref[...]


def tie_body(*_):
    pass


def next_scalars(first_ref, sums_ref):
    curvature = gathered(sums_ref, 0)
    alpha = gathered(sums_ref, 1) / curvature
    total = gathered(first_ref, 0) + alpha * (
        alpha * gathered(sums_ref, 2) - 2.0 * gathered(sums_ref, 3)
    )
    return curvature, alpha, jnp.maximum(total, 0.0)


def lift_next_body(cells, lift_ref, first_ref, sums_ref, res_ref, image_ref, perm_ref, deep_ref, col_ref, own_ref, partner_ref, lifted_ref, next_ref, zt_ref):
    _, alpha, total = next_scalars(first_ref, sums_ref)
    scale = scale_of(total, cells)
    residual = res_ref[0] - alpha * image_ref[0]
    next_ref[0] = residual
    scaled = (residual / scale).T
    log_perm = jnp.log(perm_ref[0].astype(F32)).T
    transform(lift_ref, deep_ref, col_ref, scaled, log_perm, own_ref, partner_ref, lifted_ref, zt_ref)


def point_body(mix_ref, lifted_ref, _, __, point_ref):
    size = 4 * SUBLANES
    group = 4

    def step(index, carry):
        lines = pl.ds(pl.multiple_of(index * size, size), size)
        for first in range(0, CHANNELS, group):
            sums = [mix_ref[first + j, CHANNELS] for j in range(group)]
            for channel in range(CHANNELS):
                lifted = lifted_ref[0, channel, lines, :]
                sums = [
                    total + mix_ref[first + j, channel] * lifted for j, total in enumerate(sums)
                ]
            for j, total in enumerate(sums):
                point_ref[0, first + j, lines, :] = total
        return carry

    lax.fori_loop(0, lifted_ref.shape[2] // size, step, 0)


def modes_body(cells, n_row, n_col, n_chip, recv_ref, *refs):
    sources = refs[:n_col]
    _, out_ref, weight_ref, sems, field_ref, turned_ref, spec_ref, odd_ref = refs[n_col:]
    own = lax.axis_index(COL)
    copies = [
        pltpu.make_async_copy(
            source, weight_ref.at[lax.rem(own + n_col - shift, n_col)], sems.at[shift]
        )
        for shift, source in enumerate(sources)
    ]
    for copy in copies:
        copy.start()
    rows = recv_ref.shape[1]
    places = n_row * rows
    tile = (SUBLANES, LANES)
    lane = lax.broadcasted_iota(jnp.int32, tile, 1)
    first = lane < LANES // 2
    sign = jnp.where(first, 1.0, -1.0).astype(F32)
    base = lane - lane % CHANNELS

    def turn(value):
        return pltpu.roll(value, LANES // 2, 1) * sign

    for row in range(n_row):
        for place in range(rows):
            value = recv_ref[row * n_chip, place]
            for chip in range(1, n_chip):
                value = value + recv_ref[row * n_chip + chip, place]
            field_ref[row * rows + place] = value
    angle = 2.0 * np.pi / places
    half = KX // 2

    def weigh(coefs, ref):
        total = None
        for place, coef in enumerate(coefs):
            coef = float(coef)
            if abs(coef) < 1e-12:
                continue
            term = ref[place]
            if coef == -1.0:
                term = -term
            elif coef != 1.0:
                term = coef * term
            total = term if total is None else total + term
        return jnp.zeros(tile, F32) if total is None else total

    middle = places // 2
    for place in range(1, middle):
        value, mirror = field_ref[place], field_ref[places - place]
        field_ref[place] = value + mirror
        turned_ref[place] = turn(value - mirror)
    for freq in range(half + 1):
        turns = freq * np.arange(middle + 1) % places
        even = weigh(np.cos(angle * turns), field_ref)
        odd = weigh(np.concatenate([[0.0], np.sin(angle * turns[1:middle])]), turned_ref)
        if freq < half:
            spec_ref[half + freq] = even + odd
        if freq > 0:
            spec_ref[half - freq] = even - odd

    for copy in copies:
        copy.wait()
    share = KX // n_col
    for freq in range(KX):
        value = spec_ref[freq]
        same = [None, None]
        cross = [None, None]
        for channel in range(CHANNELS):
            wide = jnp.take_along_axis(value, base + channel, axis=1)
            weight = weight_ref[freq // share, freq % share, channel]
            for sums, factor in ((same, weight), (cross, pltpu.roll(weight, LANES // 2, 1))):
                term = factor * wide
                kept = sums[channel % 2]
                sums[channel % 2] = term if kept is None else kept + term
        same = same[0] + same[1]
        cross = cross[0] + cross[1]
        total = jnp.where(
            first,
            same - pltpu.roll(same, LANES // 2, 1),
            cross + pltpu.roll(cross, LANES // 2, 1),
        )
        field_ref[freq] = total
        turned_ref[freq] = -turn(total)
    gain = 0.5 / cells
    evens = [field_ref[half] * gain]
    odds = [None]
    for freq in range(1, half):
        evens.append((field_ref[half + freq] + field_ref[half - freq]) * gain)
        odds.append((turned_ref[half + freq] - turned_ref[half - freq]) * gain)
    evens.append(field_ref[0] * gain)
    odds.append(-turned_ref[0] * gain)
    for freq in range(half + 1):
        spec_ref[freq] = evens[freq]
        if freq > 0:
            odd_ref[freq] = odds[freq]

    def store(place, value):
        for chip in range(n_chip):
            out_ref[(place // rows) * n_chip + chip, place % rows] = value

    for place in range(places // 2 + 1):
        turns = place * np.arange(half + 1) % places
        even = weigh(np.cos(angle * turns), spec_ref)
        odd = weigh(np.sin(angle * turns), odd_ref)
        store(place, even + odd)
        if 0 < place < places // 2:
            store(places - place, even - odd)


def back_transform(recv_ref, other_ref, point_ref, proj_ref, col_ref, deep_ref, wave_ref, total_ref, scale):
    groups = 2 * KZ * CHANNELS // LANES
    n_col = KY // SUBLANES
    cols = col_ref.shape[2] // 2
    lane = lax.broadcasted_iota(jnp.int32, (KY, LANES), 1)
    sign = jnp.where(lane < LANES // 2, -1.0, 1.0).astype(F32)
    half = 2 * KZ
    pieces = []
    for row in range(groups):
        chips = slice(row * n_col // 2, (row + 1) * n_col // 2)
        value = jnp.concatenate([recv_ref[chips, 0], other_ref[chips, 0]], 0)
        value = value.reshape(KY, LANES)
        turned = pltpu.roll(value, LANES // 2, 1) * sign
        both = jnp.concatenate([value, turned], 0)
        pieces.append(jnp.concatenate(split_three(both), 0).T.astype(BF16))
    part = matmul(jnp.concatenate(pieces, 0), col_ref[lax.axis_index(COL)])
    wave_ref[...] = part[:, :cols] + part[:, cols:]

    def waves(out):
        both = [wave_ref[pl.ds(out + j, half, stride=CHANNELS), :] for j in range(2)]
        high, middle, low = (
            part.astype(BF16) for part in split_three(jnp.concatenate(both, 1))
        )
        return jnp.concatenate([high, middle, low, high], 0)

    for out in range(0, CHANNELS, 2):
        spatial = matmul(deep_ref[...], waves(out))
        for start in range(0, spatial.shape[0], CHUNK):
            lines = slice(start, start + CHUNK)
            total = proj_ref[CHANNELS] if out == 0 else total_ref[lines]
            for j in range(2):
                value = spatial[lines, j * cols : (j + 1) * cols] + point_ref[0, out + j, lines]
                total = total + proj_ref[out + j] * scaled_gelu(value)
            total_ref[lines] = total
    return (scale * total_ref[...]).T


def put_lines(update, place, left_ref, right_ref):
    left_ref[pl.ds(place, 1), :] = update[:1]
    right_ref[pl.ds(place, 1), :] = update[update.shape[0] - 1 :]


def back_outer(update, kept_ref, field_ref, low_ref, high_ref, left_ref, right_ref):
    step = pl.program_id(0)
    kept_ref[0, 0] = update
    field_ref[0] = update
    last = left_ref.shape[0] - 1

    @pl.when(step == 0)
    def _():
        low_ref[...] = update
        put_lines(update, 0, left_ref, right_ref)

    @pl.when(step == 1)
    def _():
        high_ref[...] = update
        put_lines(update, last, left_ref, right_ref)


def back_inner(update, left_in, right_in, kept_ref, field_ref, left_ref, right_ref):
    step = pl.program_id(0)
    kept_ref[0, 0] = update
    field_ref[0] = update
    last = left_ref.shape[0] - 1

    @pl.when(step == 0)
    def _():
        for place in (0, last):
            line = slice(place, place + 1)
            left_ref[line] = left_in[line]
            right_ref[line] = right_in[line]

    put_lines(update, step + 1, left_ref, right_ref)


def back_body(scale_from, scalars, waiting, inner, proj_ref, *refs):
    scalar_refs, refs = refs[:scalars], refs[scalars:]
    recv_ref, other_ref, point_ref, col_ref, deep_ref = refs[:5]
    refs = refs[5 + waiting :]
    *outs, wave_ref, total_ref = refs
    update = back_transform(
        recv_ref, other_ref, point_ref, proj_ref, col_ref, deep_ref, wave_ref, total_ref,
        scale_from(*scalar_refs),
    )
    (back_inner if inner else back_outer)(update, *outs)


def stencil(fields, perms):
    own, before, after, left, right = fields
    cols, depth = own.shape
    line = lax.broadcasted_iota(jnp.int32, (cols, depth), 0)
    deep = lax.broadcasted_iota(jnp.int32, (cols, depth), 1)

    def sides(array, before, after, left, right, first, last):
        return (
            before,
            after,
            jnp.where(line == 0, left, pltpu.roll(array, 1, 0)),
            jnp.where(line == cols - 1, right, pltpu.roll(array, cols - 1, 0)),
            jnp.where(deep == 0, first, pltpu.roll(array, 1, 1)),
            jnp.where(deep == depth - 1, last, pltpu.roll(array, depth - 1, 1)),
        )

    perm, *others = perms
    others = [
        jnp.where(other > 0.0, other, edge)
        for other, edge in zip(others, (perm, perm, perm[:1], perm[cols - 1 :]))
    ]
    total = None
    for other, conductance in zip(
        sides(own, before, after, left, right, 0.0, 0.0), sides(perm, *others, perm, perm)
    ):
        term = harmonic(perm, conductance) * (own - other)
        total = term if total is None else total + term
    return total


def add_sums(terms, out_ref, acc_ref):
    step = pl.program_id(0)

    @pl.when(step == 0)
    def _():
        acc_ref[...] = jnp.zeros_like(acc_ref)

    for j, term in enumerate(terms):
        acc_ref[j : j + 1] += lane_sums(term)

    @pl.when(step == pl.num_programs(0) - 1)
    def _():
        spread([acc_ref[j : j + 1] for j in range(len(terms))], out_ref)


def around(ref, index, halo):
    low_ref, high_ref, left_ref, right_ref = halo
    step = pl.program_id(0)
    last = pl.num_programs(0) - 1
    line = pl.ds(step, 1)

    def plane(place):
        return ref[index + (place,)].astype(F32)

    def outside(axis, edge, value):
        return jnp.where(lax.axis_index(axis) == edge, 0.0, value)

    low = outside("row", 0, low_ref[...])
    high = outside("row", lax.axis_size("row") - 1, high_ref[...])
    left = outside(COL, 0, left_ref[line, :])
    right = outside(COL, lax.axis_size(COL) - 1, right_ref[line, :])
    before = jnp.where(step == 0, low, plane(jnp.maximum(step - 1, 0)))
    after = jnp.where(step == last, high, plane(jnp.minimum(step + 1, last)))
    return plane(step), before, after, left, right


def operator_first_body(field_ref, perm_ref, *refs):
    halo, perm_halo = refs[:4], refs[4:8]
    res_ref, image_ref, out_ref, acc_ref = refs[8:]
    fields = around(field_ref, (), halo)
    image = stencil(fields, around(perm_ref, (), perm_halo))
    own = fields[0]
    residual = res_ref[0]
    image_ref[0] = image
    add_sums((own * image, residual * own, image * image, residual * image), out_ref, acc_ref)


def operator_next_body(cells, first_ref, sums_ref, field_ref, old_ref, perm_ref, *refs):
    halo, old, perm_halo = refs[:4], refs[4:8], refs[8:12]
    res_ref, before_ref, way_ref, image_ref, out_ref, acc_ref = refs[12:]
    _, _, total = next_scalars(first_ref, sums_ref)
    factor = scale_of(total, cells) / scale_of(gathered(first_ref, 0), cells)
    old = around(old_ref, (), old)
    fields = [new - factor * other for new, other in zip(around(field_ref, (), halo), old)]
    image = stencil(fields, around(perm_ref, (), perm_halo))
    own = fields[0]
    residual = res_ref[0]
    way_ref[0] = own
    image_ref[0] = image
    add_sums((own * image, own * before_ref[0], residual * own, residual * old[0]), out_ref, acc_ref)


def last_body(sums_ref, later_ref, old_ref, way_ref, res_ref, before_ref, image_ref, sol_ref, out_ref):
    curvature = gathered(sums_ref, 0)
    alpha = gathered(sums_ref, 1) / curvature
    cross = gathered(later_ref, 1)
    delta = cross / curvature
    along = gathered(later_ref, 2) - delta * gathered(later_ref, 3)
    later = along / (gathered(later_ref, 0) - delta * cross)
    sol_ref[0] = alpha * old_ref[0] + later * (way_ref[0] - delta * old_ref[0])
    out_ref[0] = res_ref[0] - later * (image_ref[0] - delta * before_ref[0])


def exchange(blocks, axes):
    return lax.all_to_all(blocks, axes, split_axis=0, concat_axis=0, tiled=True)


def swap(blocks):
    return lax.ppermute(blocks, "core", [(0, 1), (1, 0)])


def add_up(partial):
    return exchange(partial, BOTH)


def shift_planes(axis, first, last):
    count = lax.axis_size(axis)
    forward = [(i, (i + 1) % count) for i in range(count)]
    backward = [(target, source) for source, target in forward]
    return lax.ppermute(last, axis, forward), lax.ppermute(first, axis, backward)


def neighbours(low, high, left, right):
    return shift_planes("row", low, high) + shift_planes(COL, left, right)


def tiled_local(right_side, permeability, lift_weight, spectral_weight, mix_weight, proj_weight):
    rows, cols, depth = right_side.shape
    n_row = lax.axis_size("row")
    n_col = lax.axis_size(COL)
    count = n_row * n_col
    cells = float(rows * n_row * cols * n_col * depth)
    freq = KX // n_col
    deep_forward, deep_back = (jnp.asarray(t) for t in deep_tables(n_row, depth))
    col_forward, col_back = (jnp.asarray(t) for t in column_tables(n_col, cols))
    lift_weight = GAIN * lift_weight.T
    mix_weight = jnp.where(jnp.arange(CHANNELS + 1) < CHANNELS, 0.5, GAIN) * mix_weight
    proj_weight = jnp.where(jnp.arange(CHANNELS + 1) < CHANNELS, 0.5 / GAIN, 1.0) * proj_weight
    field = shape(rows, cols, depth)
    field_bytes = 4 * rows * cols * depth
    partial = shape(count, SUBLANES, LANES)
    channels = shape(rows, CHANNELS, depth, cols)
    n_chip = n_col // 2
    spectra = shape(n_row * n_chip, rows, SUBLANES, LANES)
    spectra_bytes = 4 * spectra.size
    smem = whole(pltpu.SMEM)
    vmem = whole()
    anywhere = whole(pl.ANY)
    plane = pl.BlockSpec((1, cols, depth), lambda i: (i, 0, 0))
    spectra_block = pl.BlockSpec((n_row * n_chip, 1, SUBLANES, LANES), lambda i: (0, i, 0, 0))
    point_block = pl.BlockSpec((1, CHANNELS, depth, cols), lambda i: (i, 0, 0, 0))
    kept_shape = shape(ITERS, rows, cols, depth)
    lift_flops = 2.0e9
    back_flops = 2.0e9

    weight_shape = (freq, CHANNELS, SUBLANES, LANES)
    kept_weights, *weights = call(
        weight_body,
        (shape(*weight_shape),) * n_col,
        [vmem],
        (vmem,) * n_col,
        scratch=[pltpu.VMEM((n_col,) + weight_shape, F32)],
        moved=8 * spectral_weight.size,
    )(spectral_weight)
    weights = [kept_weights] + [
        lax.ppermute(part, COL, [(i, (i + shift + 1) % n_col) for i in range(n_col)])
        for shift, part in enumerate(weights)
    ]
    edge_shapes = (shape(cols, depth),) * 2 + (shape(rows, depth),) * 2
    squares, *perm_edges = call(
        squares_body,
        (partial,) + edge_shapes,
        [vmem, vmem],
        (vmem,) * 5,
        moved=2 * field_bytes,
    )(right_side, permeability)
    squares = add_up(squares)
    perm_halo = neighbours(*perm_edges)
    acc_scratch = pltpu.VMEM((SUBLANES, LANES), F32)
    zt_scratch = pltpu.VMEM((2 * KZ * CHANNELS, cols), F32)

    def points(lifted, part, before, after):
        first = part * rows // 2
        quarter = pl.BlockSpec(
            (1, CHANNELS, depth // 4, cols), lambda i, j: (first + i, 0, j, 0)
        )
        return call(
            point_body,
            channels,
            [smem, quarter, anywhere, anywhere],
            quarter,
            grid=(rows // 2, 4),
            flops=2.5e9,
            moved=16 * field_bytes,
            alias={2: 0} if part else None,
            limit=12,
        )(mix_weight, lifted, before, after)

    def modes(received, before):
        places = rows * n_row
        tiles = lambda size: pltpu.VMEM((size, SUBLANES, LANES), F32)
        return call(
            functools.partial(modes_body, cells, n_row, n_col, n_chip),
            spectra,
            [vmem] + [anywhere] * (n_col + 1),
            vmem,
            scratch=[
                pltpu.VMEM((n_col,) + weight_shape, F32),
                pltpu.SemaphoreType.DMA((n_col,)),
                tiles(places),
                tiles(places),
                tiles(KX),
                tiles(KX),
            ],
            moved=2 * spectra_bytes + 4 * spectral_weight.size,
            near=(0,),
        )(received, *weights, before)

    def mixed_modes(own, partner, lifted, waiting):
        blocks = call(join_body, spectra, [vmem, vmem], vmem, near=(0, 1))(own, swap(partner))
        received = exchange(blocks, CHIPS)
        point = points(lifted, 0, blocks, blocks)
        blocks = modes(received, point)
        received = exchange(blocks, CHIPS)
        point = points(lifted, 1, point, blocks)
        received = pl.pallas_call(
            tie_body,
            out_shape=spectra,
            in_specs=[anywhere] * (2 + len(waiting)),
            out_specs=anywhere,
            input_output_aliases={0: 0},
        )(received, point, *waiting)
        return received, swap(received), point

    def back(index, scale_from, scalars, fields, waiting):
        def run(place_of, steps, inner, waiting, outs, out_specs, alias, loose):
            count_in = 1 + len(scalars)
            spectra_at = pl.BlockSpec(
                (n_row * n_chip, 1, SUBLANES, LANES), lambda i: (0, place_of(i), 0, 0)
            )
            point_at = pl.BlockSpec(
                (1, CHANNELS, depth, cols), lambda i: (place_of(i), 0, 0, 0)
            )
            kept_at = pl.BlockSpec((1, 1, cols, depth), lambda i: (index, place_of(i), 0, 0))
            plane_at = pl.BlockSpec((1, cols, depth), lambda i: (place_of(i), 0, 0))
            return call(
                functools.partial(
                    back_body,
                    scale_from,
                    len(scalars),
                    2 if inner else len(waiting),
                    inner,
                ),
                outs,
                [smem]
                + [vmem] * len(scalars)
                + [spectra_at, spectra_at, point_at, vmem, vmem]
                + ([anywhere, anywhere, vmem, vmem] if inner else [anywhere] * len(waiting)),
                (kept_at, plane_at) + out_specs,
                grid=(steps,),
                scratch=[zt_scratch, pltpu.VMEM((depth, cols), F32)],
                flops=back_flops / 2,
                moved=9 * field_bytes,
                alias={count_in + 5 + i: o for i, o in alias},
                limit=12,
                near=(count_in + 1,)
                + tuple(
                    count_in + 5 + i
                    for i, array in enumerate(waiting)
                    if array.size != kept_shape.size
                ),
                loose=loose,
            )(proj_weight, *scalars, *fields, col_back, deep_back, *waiting)

        kept, field_out, low, high, left, right = run(
            lambda i: i * (rows - 1),
            2,
            False,
            waiting,
            (kept_shape, field) + edge_shapes,
            (vmem,) * 4,
            [(0, 0)] if index else [],
            (1,),
        )
        halo_rows = shift_planes("row", low, high)
        kept, field_out, left, right = run(
            lambda i: i + 1,
            rows - 2,
            True,
            (kept, field_out, left, right),
            (kept_shape, field) + edge_shapes[2:],
            (vmem,) * 2,
            [(0, 0), (1, 1)],
            (1,),
        )
        return (kept, field_out) + halo_rows + shift_planes(COL, left, right)

    own, partner, lifted = call(
        functools.partial(lift_first_body, cells),
        (spectra, spectra, channels),
        [smem, vmem, plane, plane, vmem, vmem] + [anywhere] * n_col,
        (spectra_block, spectra_block, point_block),
        limit=16,
        loose=(0, 1),
        near=(6, 7, 8, 9),
        grid=(rows,),
        scratch=[zt_scratch],
        flops=lift_flops,
        moved=2 * field_bytes + spectra_bytes,
    )(lift_weight, squares, right_side, permeability, deep_forward, col_forward, *weights)
    received, other, point = mixed_modes(own, partner, lifted, perm_halo)
    kept, old, *edges = back(
        0,
        lambda first_ref: scale_of(gathered(first_ref, 0), cells),
        (squares,),
        (received, other, point),
        (),
    )

    old_halo = edges
    args = (old, permeability, *old_halo, *perm_halo, right_side)
    image, sums = call(
        operator_first_body,
        (field, partial),
        [vmem] * 10 + [plane],
        (plane, vmem),
        grid=(rows,),
        scratch=[acc_scratch],
        moved=9 * field_bytes,
        near=range(11),
        loose=range(3),
    )(*args)
    sums = add_up(sums)

    own, partner, lifted, residual = call(
        functools.partial(lift_next_body, cells),
        (spectra, spectra, channels, field),
        [smem, vmem, vmem, plane, plane, plane, vmem, vmem],
        (spectra_block, spectra_block, point_block, plane),
        limit=16,
        near=(4,),
        loose=(0, 1),
        grid=(rows,),
        scratch=[zt_scratch],
        flops=lift_flops,
        moved=4 * field_bytes + spectra_bytes,
    )(lift_weight, squares, sums, right_side, image, permeability, deep_forward, col_forward)
    received, other, point = mixed_modes(own, partner, lifted, ())
    kept, update, *edges = back(
        1,
        lambda first_ref, sums_ref: scale_of(next_scalars(first_ref, sums_ref)[2], cells),
        (squares, sums),
        (received, other, point),
        (kept,),
    )

    halo = edges
    args = (squares, sums, update, old, permeability, *halo, *old_halo, *perm_halo, residual, image)
    way, last_image, later = call(
        functools.partial(operator_next_body, cells),
        (field, field, partial),
        [vmem] * 17 + [plane] * 2,
        (plane, plane, vmem),
        grid=(rows,),
        scratch=[acc_scratch],
        near=range(19),
        loose=range(3),
        moved=11 * field_bytes,
    )(*args)
    later = add_up(later)
    answer, residual = call(
        last_body,
        (field, field),
        [vmem, vmem] + [plane] * 5,
        (plane, plane),
        grid=(rows,),
        moved=6 * field_bytes,
        near=range(7),
        loose=range(3),
    )(sums, later, old, way, residual, image, last_image)
    return (answer, residual, kept)


def fits_tiles(mesh, block):
    rows, cols, depth = block
    n_row, n_col = mesh.shape["row"], mesh.shape["col"]
    return (
        ITERS == 2
        and KZ == n_row * (LANES // (2 * CHANNELS))
        and KY == n_col * SUBLANES
        and KX % n_col == 0
        and n_col % 2 == 0
        and cols == LANES
        and depth % LANES == 0
        and rows * n_row >= KX
        and rows > 2
        and rows % 2 == 0
    )


def solution(mesh):
    placed = (
        P("row", "col", None),
        P("row", "col", None),
        P(),
        P(None, "row", None, None, "col"),
        P(),
        P(),
    )
    outputs = (P("row", "col", None), P("row", "col", None), P(None, "row", "col", None))

    def run(right_side, *others):
        rows, cols, depth = right_side.shape
        n_row, n_col = mesh.shape["row"], mesh.shape["col"]
        if not fits_tiles(mesh, (rows // n_row, cols // n_col, depth)):
            return jax.shard_map(
                local, mesh=mesh, in_specs=placed, out_specs=outputs, check_vma=False
            )(right_side, *others)
        cores = jax.sharding.Mesh(mesh.devices.reshape(n_row, n_col // 2, 2), BOTH)
        placed_cores, outputs_cores = jax.tree.map(
            lambda spec: P(*(COL if axis == "col" else axis for axis in spec)),
            (placed, outputs),
            is_leaf=lambda spec: isinstance(spec, P),
        )
        return jax.shard_map(
            tiled_local,
            mesh=cores,
            in_specs=placed_cores,
            out_specs=outputs_cores,
            check_vma=False,
        )(right_side, *others)

    return run
```

```python
import functools
import math

import jax
import jax.numpy as jnp
import ml_dtypes
import numpy as np
from jax import lax
from jax.experimental import pallas as pl
from jax.experimental.pallas import tpu as pltpu
from jax.sharding import PartitionSpec as P

CHANNELS = 16
KX = 16
KY = 32
KZ = 32
ITERS = 2


HIGHEST = lax.Precision.HIGHEST


def with_halo(block, sides, width):
    for axis, dim in sides:
        count = lax.axis_size(axis)
        forward = [(i, i + 1) for i in range(count - 1)]
        backward = [(target, source) for source, target in forward]
        low = lax.ppermute(
            lax.slice_in_dim(block, block.shape[dim] - width, None, axis=dim), axis, forward
        )
        high = lax.ppermute(lax.slice_in_dim(block, 0, width, axis=dim), axis, backward)
        block = jnp.concatenate([low, block, high], axis=dim)
    return block


def einsum_high(form, left, right):
    return jnp.einsum(form, left, right, precision=HIGHEST)


def harmonic(first, second):
    return 2.0 * first * second / (first + second)


def wave_table(freqs, places, length):
    turns = freqs[None, :] * places[:, None] % length
    angle = turns.astype(jnp.float32) * (2.0 * jnp.pi / length)
    return (jnp.cos(angle), jnp.sin(angle))


def signed_freqs(count):
    return jnp.arange(count, dtype=jnp.int32) - count // 2


def face_arrays(permeability):
    padded = with_halo(permeability, (("row", 0), ("col", 1)), 1).astype(jnp.float32)
    own = permeability.astype(jnp.float32)
    edged = jnp.pad(own, ((1, 1), (1, 1), (0, 0)), mode="edge")
    padded = jnp.where(padded > 0.0, padded, edged)
    first = harmonic(padded[:-1, 1:-1], padded[1:, 1:-1])
    second = harmonic(padded[1:-1, :-1], padded[1:-1, 1:])
    deep = jnp.pad(own, ((0, 0), (0, 0), (1, 1)), mode="edge")
    third = harmonic(deep[:, :, :-1], deep[:, :, 1:])
    return ((first, second, third), jnp.log(own))


def apply_operator(field, faces):
    first, second, third = faces
    padded = with_halo(field, (("row", 0), ("col", 1)), 1)
    padded = jnp.pad(padded, ((0, 0), (0, 0), (1, 1)))
    total = first[:-1] * (field - padded[:-2, 1:-1, 1:-1])
    total = total + first[1:] * (field - padded[2:, 1:-1, 1:-1])
    total = total + second[:, :-1] * (field - padded[1:-1, :-2, 1:-1])
    total = total + second[:, 1:] * (field - padded[1:-1, 2:, 1:-1])
    total = total + third[:, :, :-1] * (field - padded[1:-1, 1:-1, :-2])
    total = total + third[:, :, 1:] * (field - padded[1:-1, 1:-1, 2:])
    return total


def global_squares(field):
    return lax.psum(jnp.sum(field * field), ("row", "col"))


def mix_modes(real_in, imag_in, spectral_weight, deep_count, freq_count):
    block = spectral_weight.reshape(2, deep_count, CHANNELS, CHANNELS, freq_count, KY)
    real_out = einsum_high("kcfg,kcofg->kofg", real_in, block[0]) - einsum_high(
        "kcfg,kcofg->kofg", imag_in, block[1]
    )
    imag_out = einsum_high("kcfg,kcofg->kofg", imag_in, block[0]) + einsum_high(
        "kcfg,kcofg->kofg", real_in, block[1]
    )
    return (real_out, imag_out)


def spectral_transpose(real_part, imag_part, spectral_weight, grid):
    rows, cols, n_row, n_col, row_id, col_id = grid
    full_rows = rows * n_row
    full_cols = cols * n_col
    cosine_rows, sine_rows = wave_table(
        signed_freqs(KX), jnp.arange(full_rows, dtype=jnp.int32), full_rows
    )
    cosine_cols, sine_cols = wave_table(
        signed_freqs(KY), jnp.arange(full_cols, dtype=jnp.int32), full_cols
    )
    real_part, imag_part = (
        lax.all_to_all(real_part, "row", split_axis=0, concat_axis=1, tiled=True),
        lax.all_to_all(imag_part, "row", split_axis=0, concat_axis=1, tiled=True),
    )
    first_real = einsum_high("qxy,xf->qfy", real_part, cosine_rows) + einsum_high(
        "qxy,xf->qfy", imag_part, sine_rows
    )
    first_imag = einsum_high("qxy,xf->qfy", imag_part, cosine_rows) - einsum_high(
        "qxy,xf->qfy", real_part, sine_rows
    )
    first_real, first_imag = (
        lax.all_to_all(first_real, "col", split_axis=1, concat_axis=2, tiled=True),
        lax.all_to_all(first_imag, "col", split_axis=1, concat_axis=2, tiled=True),
    )
    second_real = einsum_high("qfy,yg->qfg", first_real, cosine_cols) + einsum_high(
        "qfy,yg->qfg", first_imag, sine_cols
    )
    second_imag = einsum_high("qfy,yg->qfg", first_imag, cosine_cols) - einsum_high(
        "qfy,yg->qfg", first_real, sine_cols
    )
    deep_count = KZ // n_row
    freq_count = KX // n_col
    shape_in = (deep_count, CHANNELS, freq_count, KY)
    mixed_real, mixed_imag = mix_modes(
        second_real.reshape(shape_in),
        second_imag.reshape(shape_in),
        spectral_weight,
        deep_count,
        freq_count,
    )
    shape_out = (deep_count * CHANNELS, freq_count, KY)
    mixed_real = mixed_real.reshape(shape_out)
    mixed_imag = mixed_imag.reshape(shape_out)
    back_real = einsum_high("qfg,yg->qfy", mixed_real, cosine_cols) - einsum_high(
        "qfg,yg->qfy", mixed_imag, sine_cols
    )
    back_imag = einsum_high("qfg,yg->qfy", mixed_imag, cosine_cols) + einsum_high(
        "qfg,yg->qfy", mixed_real, sine_cols
    )
    back_real, back_imag = (
        lax.all_to_all(back_real, "col", split_axis=2, concat_axis=1, tiled=True),
        lax.all_to_all(back_imag, "col", split_axis=2, concat_axis=1, tiled=True),
    )
    out_real = einsum_high("qfy,xf->qxy", back_real, cosine_rows) - einsum_high(
        "qfy,xf->qxy", back_imag, sine_rows
    )
    out_imag = einsum_high("qfy,xf->qxy", back_imag, cosine_rows) + einsum_high(
        "qfy,xf->qxy", back_real, sine_rows
    )
    out_real, out_imag = (
        lax.all_to_all(out_real, "row", split_axis=1, concat_axis=0, tiled=True),
        lax.all_to_all(out_imag, "row", split_axis=1, concat_axis=0, tiled=True),
    )
    return (out_real, out_imag)


def precondition(residual, squares_total, log_perm, weights, grid, cells):
    lift_weight, spectral_weight, mix_weight, proj_weight = weights
    rows, cols, depth = residual.shape
    scale = jnp.sqrt(squares_total / cells + 1e-06)
    scaled = residual / scale
    lifted = jax.nn.gelu(
        lift_weight[:, 0, None, None, None] * scaled[None]
        + lift_weight[:, 1, None, None, None] * log_perm[None]
        + lift_weight[:, 2, None, None, None]
    )
    cosine_deep, sine_deep = wave_table(
        jnp.arange(KZ, dtype=jnp.int32), jnp.arange(depth, dtype=jnp.int32), depth
    )
    real_part = einsum_high("cxyz,zk->kcxy", lifted, cosine_deep).reshape(KZ * CHANNELS, rows, cols)
    imag_part = -einsum_high("cxyz,zk->kcxy", lifted, sine_deep).reshape(KZ * CHANNELS, rows, cols)
    out_real, out_imag = spectral_transpose(real_part, imag_part, spectral_weight, grid)
    out_real = out_real.reshape(KZ, CHANNELS, rows, cols)
    out_imag = out_imag.reshape(KZ, CHANNELS, rows, cols)
    spatial = (
        einsum_high("kcxy,zk->cxyz", out_real, cosine_deep)
        - einsum_high("kcxy,zk->cxyz", out_imag, sine_deep)
    ) / cells
    point = (
        einsum_high("oc,cxyz->oxyz", mix_weight[:, :CHANNELS], lifted)
        + mix_weight[:, CHANNELS, None, None, None]
    )
    hidden = jax.nn.gelu(spatial + point)
    return scale * (
        einsum_high("o,oxyz->xyz", proj_weight[:CHANNELS], hidden) + proj_weight[CHANNELS]
    )


def local(right_side, permeability, lift_weight, spectral_weight, mix_weight, proj_weight):
    rows, cols, depth = right_side.shape
    n_row = lax.axis_size("row")
    n_col = lax.axis_size("col")
    grid = (rows, cols, n_row, n_col, lax.axis_index("row"), lax.axis_index("col"))
    cells = float(rows * n_row * cols * n_col * depth)
    faces, log_perm = face_arrays(permeability)
    weights = (lift_weight, spectral_weight, mix_weight, proj_weight)

    def precond(residual, squares_total):
        return precondition(residual, squares_total, log_perm, weights, grid, cells)

    solution = jnp.zeros_like(right_side)
    residual = right_side
    kept = []
    update = precond(residual, global_squares(residual))
    kept.append(update)
    direction = update
    for step in range(ITERS):
        image = apply_operator(direction, faces)
        curvature, along = lax.psum(
            (jnp.sum(direction * image), jnp.sum(residual * direction)), ("row", "col")
        )
        alpha = along / curvature
        solution = solution + alpha * direction
        residual = residual - alpha * image
        if step + 1 < ITERS:
            update = precond(residual, global_squares(residual))
            kept.append(update)
            beta = lax.psum(jnp.sum(update * image), ("row", "col")) / curvature
            direction = update - beta * direction
    return (solution, residual, jnp.stack(kept))


LANES = 128
SUBLANES = 8
COL = ("y", "core")
CHIPS = ("row", "y")
BOTH = ("row", "y", "core")
CHUNK = 32
F32 = jnp.float32
BF16 = jnp.bfloat16


def split_table(table):
    high = table.astype(ml_dtypes.bfloat16)
    low = (table - high.astype(np.float64)).astype(ml_dtypes.bfloat16)
    return high, low


def split(value):
    high = value.astype(BF16)
    return high, (value - high.astype(F32)).astype(BF16)


def split_three(value):
    high = value.astype(BF16).astype(F32)
    rest = value - high
    middle = rest.astype(BF16).astype(F32)
    return high, middle, rest - middle


def matmul(left, right):
    return jnp.dot(left, right, preferred_element_type=F32)


def matmul_nt(left, right):
    return lax.dot_general(left, right, (((1,), (1,)), ((), ())), preferred_element_type=F32)


def angles(freqs, places, length):
    turns = np.multiply.outer(freqs, places) % length
    return turns * (2.0 * np.pi / length)


def deep_order(n_row):
    count = KZ // n_row
    order = [
        (part, row * count + place)
        for row in range(n_row)
        for part in range(2)
        for place in range(count)
    ]
    return np.array(order)


def deep_tables(n_row, depth):
    order = deep_order(n_row)
    angle = angles(order[:, 1], np.arange(depth), depth)
    wave = np.where(order[:, :1] == 0, np.cos(angle), -np.sin(angle))
    high, low = split_table(wave)
    return np.concatenate([high, low], 0), np.concatenate([high.T, high.T, high.T, low.T], 1)


def column_tables(n_col, cols):
    freqs = np.arange(KY) - KY // 2
    forward = []
    back = []
    for place in range(n_col):
        angle = angles(freqs, place * cols + np.arange(cols), n_col * cols)
        own = np.arange(KY).reshape(-1, 2, SUBLANES)[:, place % 2].reshape(-1)
        partner = np.arange(KY).reshape(-1, 2, SUBLANES)[:, 1 - place % 2].reshape(-1)
        angle = angle[np.concatenate([own, partner])]
        both = np.concatenate([np.cos(angle), np.sin(angle)], 0)
        high, low = split_table(both)
        forward.append(
            np.concatenate(
                [
                    np.concatenate([high, high], 1),
                    np.concatenate([low, np.zeros_like(low)], 1),
                ],
                0,
            )
        )
        back.append(
            np.concatenate(
                [
                    np.concatenate([high, low], 1),
                    np.concatenate([high, low], 1),
                    np.concatenate([high, np.zeros_like(low)], 1),
                ],
                0,
            )
        )
    return np.stack(forward), np.stack(back)


GAIN = (math.sqrt(2.0 / math.pi) * 0.044715) ** (1.0 / 3.0)
LINEAR = math.sqrt(2.0 / math.pi) / GAIN


def scaled_gelu(value):
    return value + value * jnp.tanh(value * (value * value + LINEAR))


def call(body, outs, in_specs, out_specs, grid=(), scratch=(), flops=0, moved=0, alias=None, limit=8, near=(), loose=()):
    single = not isinstance(outs, tuple)
    outs = (outs,) if single else outs
    out_specs = (out_specs,) if single else out_specs
    run = pl.pallas_call(
        body,
        out_shape=tuple(
            out if place in loose or out.size <= 2**16 else pltpu.HBM(out.shape, out.dtype)
            for place, out in enumerate(outs)
        ),
        grid=grid,
        in_specs=in_specs,
        out_specs=out_specs,
        scratch_shapes=list(scratch),
        input_output_aliases=alias or {},
        compiler_params=pltpu.CompilerParams(vmem_limit_bytes=limit * 1024 * 1024),
        cost_estimate=pl.CostEstimate(
            flops=int(flops), bytes_accessed=int(moved), transcendentals=0
        ),
    )

    def wrapped(*args):
        held = [
            arg
            if place in near or spec.memory_space == pltpu.SMEM
            else pltpu.with_memory_space_constraint(arg, pltpu.HBM)
            for place, (arg, spec) in enumerate(zip(args, in_specs))
        ]
        found = run(*held)
        return found[0] if single else found

    return wrapped


def whole(memory=pltpu.VMEM):
    return pl.BlockSpec(memory_space=memory)


def shape(*dims):
    return jax.ShapeDtypeStruct(dims, F32)


def lane_sums(value):
    folded = jnp.sum(value.reshape(-1, SUBLANES, value.shape[-1]), axis=0)
    folded = sum(
        folded[:, start : start + LANES] for start in range(0, folded.shape[1], LANES)
    )
    return jnp.sum(folded, axis=0, keepdims=True)


def spread(rows, ref):
    rows = rows + [jnp.zeros_like(rows[0])] * (SUBLANES - len(rows))
    ref[...] = jnp.broadcast_to(jnp.concatenate(rows, 0)[None], ref.shape)


def gathered(ref, row):
    total = jnp.sum(ref[...], axis=0)
    return jnp.sum(total[row : row + 1], axis=1, keepdims=True)


def squares_body(field_ref, perm_ref, out_ref, low_ref, high_ref, left_ref, right_ref):
    total = field_ref[0] * field_ref[0]
    for place in range(1, field_ref.shape[0]):
        total = total + field_ref[place] * field_ref[place]
    spread([lane_sums(total)], out_ref)
    rows, cols, _ = perm_ref.shape
    low_ref[...] = perm_ref[0].astype(F32)
    high_ref[...] = perm_ref[rows - 1].astype(F32)
    for place in range(rows):
        plane = perm_ref[place].astype(F32)
        left_ref[place : place + 1, :] = plane[:1]
        right_ref[place : place + 1, :] = plane[cols - 1 :]


def weight_body(weight_ref, *refs):
    *out_refs, hold_ref = refs
    groups, freq, channels, fine, _ = hold_ref.shape
    parts, deep, _, outs, modes = weight_ref.shape
    for channel in range(channels):
        block = weight_ref[:, :, channel].reshape(parts * deep * outs, modes)
        block = block.T.reshape(freq, groups, fine, parts * deep * outs)
        for group in range(groups):
            hold_ref[group, :, channel] = block[:, group]
    place = lax.axis_index(COL)
    for shift, out_ref in enumerate(out_refs):
        out_ref[...] = hold_ref[lax.rem(place + shift, groups)]


def scale_of(total, cells):
    return jnp.sqrt(total / cells + 1e-06)


def lift_channel(weight_ref, channel, scaled, log_perm):
    return scaled_gelu(
        weight_ref[0, channel] * scaled
        + (weight_ref[1, channel] * log_perm + weight_ref[2, channel])
    )


def transform(lift_ref, deep_ref, col_ref, scaled, log_perm, own_ref, partner_ref, lifted_ref, zt_ref):
    half = 2 * KZ
    cols = scaled.shape[1]
    for channel in range(0, CHANNELS, 2):
        pair = [lift_channel(lift_ref, channel + j, scaled, log_perm) for j in range(2)]
        for j in range(2):
            lifted_ref[0, channel + j] = pair[j]
        high, low = split(jnp.concatenate(pair, 1))
        part = matmul(deep_ref[...], high)
        part = part[:half] + part[half:] + matmul(deep_ref[:half], low)
        for j in range(2):
            zt_ref[pl.ds(channel + j, half, stride=CHANNELS), :] = part[:, j * cols : (j + 1) * cols]
    groups = half * CHANNELS // LANES
    part = matmul_nt(col_ref[lax.axis_index(COL)], jnp.concatenate(split(zt_ref[...]), 1))
    part = part[: 2 * KY] + part[2 * KY :]
    lane = lax.broadcasted_iota(jnp.int32, (KY, LANES), 1)
    sign = jnp.where(lane < LANES // 2, 1.0, -1.0).astype(F32)
    n_chip = KY // SUBLANES // 2
    for row in range(groups):
        lanes = slice(row * LANES, (row + 1) * LANES)
        block = part[:KY, lanes] + pltpu.roll(part[KY:, lanes], LANES // 2, 1) * sign
        for side, ref in enumerate((own_ref, partner_ref)):
            for place in range(n_chip):
                start = (side * n_chip + place) * SUBLANES
                ref[row * n_chip + place, 0] = block[start : start + SUBLANES]


def lift_first_body(cells, lift_ref, sums_ref, res_ref, perm_ref, deep_ref, col_ref, *refs):
    own_ref, partner_ref, lifted_ref, zt_ref = refs[-4:]
    scale = scale_of(gathered(sums_ref, 0), cells)
    scaled = (res_ref[0] / scale).T
    log_perm = jnp.log(perm_ref[0].astype(F32)).T
    transform(lift_ref, deep_ref, col_ref, scaled, log_perm, own_ref, partner_ref, lifted_ref, zt_ref)


def join_body(own_ref, partner_ref, out_ref):
    out_ref[...] = own_ref[...] + partner_ref[...]


def tie_body(*_):
    pass


def next_scalars(first_ref, sums_ref):
    curvature = gathered(sums_ref, 0)
    alpha = gathered(sums_ref, 1) / curvature
    total = gathered(first_ref, 0) + alpha * (
        alpha * gathered(sums_ref, 2) - 2.0 * gathered(sums_ref, 3)
    )
    return curvature, alpha, jnp.maximum(total, 0.0)


def lift_next_body(cells, lift_ref, first_ref, sums_ref, res_ref, image_ref, perm_ref, deep_ref, col_ref, own_ref, partner_ref, lifted_ref, next_ref, zt_ref):
    _, alpha, total = next_scalars(first_ref, sums_ref)
    scale = scale_of(total, cells)
    residual = res_ref[0] - alpha * image_ref[0]
    next_ref[0] = residual
    scaled = (residual / scale).T
    log_perm = jnp.log(perm_ref[0].astype(F32)).T
    transform(lift_ref, deep_ref, col_ref, scaled, log_perm, own_ref, partner_ref, lifted_ref, zt_ref)


def point_body(mix_ref, lifted_ref, _, __, point_ref):
    size = 8 * SUBLANES
    group = 4

    def step(index, carry):
        lines = pl.ds(pl.multiple_of(index * size, size), size)
        for first in range(0, CHANNELS, group):
            sums = [mix_ref[first + j, CHANNELS] for j in range(group)]
            for channel in range(CHANNELS):
                lifted = lifted_ref[0, channel, lines, :]
                sums = [
                    total + mix_ref[first + j, channel] * lifted for j, total in enumerate(sums)
                ]
            for j, total in enumerate(sums):
                point_ref[0, first + j, lines, :] = total
        return carry

    lax.fori_loop(0, lifted_ref.shape[2] // size, step, 0)


def modes_body(cells, n_row, n_col, n_chip, recv_ref, *refs):
    sources = refs[:n_col]
    _, out_ref, weight_ref, sems, field_ref, turned_ref, spec_ref, odd_ref = refs[n_col:]
    own = lax.axis_index(COL)
    copies = [
        pltpu.make_async_copy(
            source, weight_ref.at[lax.rem(own + n_col - shift, n_col)], sems.at[shift]
        )
        for shift, source in enumerate(sources)
    ]
    for copy in copies:
        copy.start()
    rows = recv_ref.shape[1]
    places = n_row * rows
    tile = (SUBLANES, LANES)
    lane = lax.broadcasted_iota(jnp.int32, tile, 1)
    first = lane < LANES // 2
    sign = jnp.where(first, 1.0, -1.0).astype(F32)
    base = lane - lane % CHANNELS

    def turn(value):
        return pltpu.roll(value, LANES // 2, 1) * sign

    for row in range(n_row):
        for place in range(rows):
            value = recv_ref[row * n_chip, place]
            for chip in range(1, n_chip):
                value = value + recv_ref[row * n_chip + chip, place]
            field_ref[row * rows + place] = value
    angle = 2.0 * np.pi / places
    half = KX // 2

    def weigh(coefs, ref):
        total = None
        for place, coef in enumerate(coefs):
            coef = float(coef)
            if abs(coef) < 1e-12:
                continue
            term = ref[place]
            if coef == -1.0:
                term = -term
            elif coef != 1.0:
                term = coef * term
            total = term if total is None else total + term
        return jnp.zeros(tile, F32) if total is None else total

    middle = places // 2
    for place in range(1, middle):
        value, mirror = field_ref[place], field_ref[places - place]
        field_ref[place] = value + mirror
        turned_ref[place] = turn(value - mirror)
    for freq in range(half + 1):
        turns = freq * np.arange(middle + 1) % places
        even = weigh(np.cos(angle * turns), field_ref)
        odd = weigh(np.concatenate([[0.0], np.sin(angle * turns[1:middle])]), turned_ref)
        if freq < half:
            spec_ref[half + freq] = even + odd
        if freq > 0:
            spec_ref[half - freq] = even - odd

    for copy in copies:
        copy.wait()
    share = KX // n_col
    for freq in range(KX):
        value = spec_ref[freq]
        same = [None, None]
        cross = [None, None]
        for channel in range(CHANNELS):
            wide = jnp.take_along_axis(value, base + channel, axis=1)
            weight = weight_ref[freq // share, freq % share, channel]
            for sums, factor in ((same, weight), (cross, pltpu.roll(weight, LANES // 2, 1))):
                term = factor * wide
                kept = sums[channel % 2]
                sums[channel % 2] = term if kept is None else kept + term
        same = same[0] + same[1]
        cross = cross[0] + cross[1]
        total = jnp.where(
            first,
            same - pltpu.roll(same, LANES // 2, 1),
            cross + pltpu.roll(cross, LANES // 2, 1),
        )
        field_ref[freq] = total
        turned_ref[freq] = -turn(total)
    gain = 0.5 / cells
    evens = [field_ref[half] * gain]
    odds = [None]
    for freq in range(1, half):
        evens.append((field_ref[half + freq] + field_ref[half - freq]) * gain)
        odds.append((turned_ref[half + freq] - turned_ref[half - freq]) * gain)
    evens.append(field_ref[0] * gain)
    odds.append(-turned_ref[0] * gain)
    for freq in range(half + 1):
        spec_ref[freq] = evens[freq]
        if freq > 0:
            odd_ref[freq] = odds[freq]

    def store(place, value):
        for chip in range(n_chip):
            out_ref[(place // rows) * n_chip + chip, place % rows] = value

    for place in range(places // 2 + 1):
        turns = place * np.arange(half + 1) % places
        even = weigh(np.cos(angle * turns), spec_ref)
        odd = weigh(np.sin(angle * turns), odd_ref)
        store(place, even + odd)
        if 0 < place < places // 2:
            store(places - place, even - odd)


def back_transform(recv_ref, other_ref, point_ref, proj_ref, col_ref, deep_ref, wave_ref, total_ref, scale):
    groups = 2 * KZ * CHANNELS // LANES
    n_col = KY // SUBLANES
    cols = col_ref.shape[2] // 2
    lane = lax.broadcasted_iota(jnp.int32, (KY, LANES), 1)
    sign = jnp.where(lane < LANES // 2, -1.0, 1.0).astype(F32)
    half = 2 * KZ
    pieces = []
    for row in range(groups):
        chips = slice(row * n_col // 2, (row + 1) * n_col // 2)
        value = jnp.concatenate([recv_ref[chips, 0], other_ref[chips, 0]], 0)
        value = value.reshape(KY, LANES)
        turned = pltpu.roll(value, LANES // 2, 1) * sign
        both = jnp.concatenate([value, turned], 0)
        pieces.append(jnp.concatenate(split_three(both), 0).T.astype(BF16))
    part = matmul(jnp.concatenate(pieces, 0), col_ref[lax.axis_index(COL)])
    wave_ref[...] = part[:, :cols] + part[:, cols:]

    def waves(out):
        both = [wave_ref[pl.ds(out + j, half, stride=CHANNELS), :] for j in range(2)]
        high, middle, low = (
            part.astype(BF16) for part in split_three(jnp.concatenate(both, 1))
        )
        return jnp.concatenate([high, middle, low, high], 0)

    for out in range(0, CHANNELS, 2):
        spatial = matmul(deep_ref[...], waves(out))
        for start in range(0, spatial.shape[0], CHUNK):
            lines = slice(start, start + CHUNK)
            total = proj_ref[CHANNELS] if out == 0 else total_ref[lines]
            for j in range(2):
                value = spatial[lines, j * cols : (j + 1) * cols] + point_ref[0, out + j, lines]
                total = total + proj_ref[out + j] * scaled_gelu(value)
            total_ref[lines] = total
    return (scale * total_ref[...]).T


def put_lines(update, place, left_ref, right_ref):
    left_ref[pl.ds(place, 1), :] = update[:1]
    right_ref[pl.ds(place, 1), :] = update[update.shape[0] - 1 :]


def back_outer(update, kept_ref, field_ref, low_ref, high_ref, left_ref, right_ref):
    step = pl.program_id(0)
    kept_ref[0, 0] = update
    field_ref[0] = update
    last = left_ref.shape[0] - 1

    @pl.when(step == 0)
    def _():
        low_ref[...] = update
        put_lines(update, 0, left_ref, right_ref)

    @pl.when(step == 1)
    def _():
        high_ref[...] = update
        put_lines(update, last, left_ref, right_ref)


def back_inner(update, left_in, right_in, kept_ref, field_ref, left_ref, right_ref):
    step = pl.program_id(0)
    kept_ref[0, 0] = update
    field_ref[0] = update
    last = left_ref.shape[0] - 1

    @pl.when(step == 0)
    def _():
        for place in (0, last):
            line = slice(place, place + 1)
            left_ref[line] = left_in[line]
            right_ref[line] = right_in[line]

    put_lines(update, step + 1, left_ref, right_ref)


def back_body(scale_from, scalars, waiting, inner, proj_ref, *refs):
    scalar_refs, refs = refs[:scalars], refs[scalars:]
    recv_ref, other_ref, point_ref, col_ref, deep_ref = refs[:5]
    refs = refs[5 + waiting :]
    *outs, wave_ref, total_ref = refs
    update = back_transform(
        recv_ref, other_ref, point_ref, proj_ref, col_ref, deep_ref, wave_ref, total_ref,
        scale_from(*scalar_refs),
    )
    (back_inner if inner else back_outer)(update, *outs)


def stencil(fields, perms):
    own, before, after, left, right = fields
    cols, depth = own.shape
    line = lax.broadcasted_iota(jnp.int32, (cols, depth), 0)
    deep = lax.broadcasted_iota(jnp.int32, (cols, depth), 1)

    def sides(array, before, after, left, right, first, last):
        return (
            before,
            after,
            jnp.where(line == 0, left, pltpu.roll(array, 1, 0)),
            jnp.where(line == cols - 1, right, pltpu.roll(array, cols - 1, 0)),
            jnp.where(deep == 0, first, pltpu.roll(array, 1, 1)),
            jnp.where(deep == depth - 1, last, pltpu.roll(array, depth - 1, 1)),
        )

    perm, *others = perms
    others = [
        jnp.where(other > 0.0, other, edge)
        for other, edge in zip(others, (perm, perm, perm[:1], perm[cols - 1 :]))
    ]
    total = None
    for other, conductance in zip(
        sides(own, before, after, left, right, 0.0, 0.0), sides(perm, *others, perm, perm)
    ):
        term = harmonic(perm, conductance) * (own - other)
        total = term if total is None else total + term
    return total


def add_sums(terms, out_ref, acc_ref):
    step = pl.program_id(0)

    @pl.when(step == 0)
    def _():
        acc_ref[...] = jnp.zeros_like(acc_ref)

    for j, term in enumerate(terms):
        acc_ref[j : j + 1] += lane_sums(term)

    @pl.when(step == pl.num_programs(0) - 1)
    def _():
        spread([acc_ref[j : j + 1] for j in range(len(terms))], out_ref)


def around(ref, index, halo):
    low_ref, high_ref, left_ref, right_ref = halo
    step = pl.program_id(0)
    last = pl.num_programs(0) - 1
    line = pl.ds(step, 1)

    def plane(place):
        return ref[index + (place,)].astype(F32)

    def outside(axis, edge, value):
        return jnp.where(lax.axis_index(axis) == edge, 0.0, value)

    low = outside("row", 0, low_ref[...])
    high = outside("row", lax.axis_size("row") - 1, high_ref[...])
    left = outside(COL, 0, left_ref[line, :])
    right = outside(COL, lax.axis_size(COL) - 1, right_ref[line, :])
    before = jnp.where(step == 0, low, plane(jnp.maximum(step - 1, 0)))
    after = jnp.where(step == last, high, plane(jnp.minimum(step + 1, last)))
    return plane(step), before, after, left, right


def operator_first_body(field_ref, perm_ref, *refs):
    halo, perm_halo = refs[:4], refs[4:8]
    res_ref, image_ref, out_ref, acc_ref = refs[8:]
    fields = around(field_ref, (), halo)
    image = stencil(fields, around(perm_ref, (), perm_halo))
    own = fields[0]
    residual = res_ref[0]
    image_ref[0] = image
    add_sums((own * image, residual * own, image * image, residual * image), out_ref, acc_ref)


def operator_next_body(cells, first_ref, sums_ref, field_ref, old_ref, perm_ref, *refs):
    halo, old, perm_halo = refs[:4], refs[4:8], refs[8:12]
    res_ref, before_ref, way_ref, image_ref, out_ref, acc_ref = refs[12:]
    _, _, total = next_scalars(first_ref, sums_ref)
    factor = scale_of(total, cells) / scale_of(gathered(first_ref, 0), cells)
    old = around(old_ref, (), old)
    fields = [new - factor * other for new, other in zip(around(field_ref, (), halo), old)]
    image = stencil(fields, around(perm_ref, (), perm_halo))
    own = fields[0]
    residual = res_ref[0]
    way_ref[0] = own
    image_ref[0] = image
    add_sums((own * image, own * before_ref[0], residual * own, residual * old[0]), out_ref, acc_ref)


def last_body(sums_ref, later_ref, old_ref, way_ref, res_ref, before_ref, image_ref, sol_ref, out_ref):
    curvature = gathered(sums_ref, 0)
    alpha = gathered(sums_ref, 1) / curvature
    cross = gathered(later_ref, 1)
    delta = cross / curvature
    along = gathered(later_ref, 2) - delta * gathered(later_ref, 3)
    later = along / (gathered(later_ref, 0) - delta * cross)
    sol_ref[0] = alpha * old_ref[0] + later * (way_ref[0] - delta * old_ref[0])
    out_ref[0] = res_ref[0] - later * (image_ref[0] - delta * before_ref[0])


def exchange(blocks, axes):
    return lax.all_to_all(blocks, axes, split_axis=0, concat_axis=0, tiled=True)


def swap(blocks):
    return lax.ppermute(blocks, "core", [(0, 1), (1, 0)])


def add_up(partial):
    return exchange(partial, BOTH)


def shift_planes(axis, first, last):
    count = lax.axis_size(axis)
    forward = [(i, (i + 1) % count) for i in range(count)]
    backward = [(target, source) for source, target in forward]
    return lax.ppermute(last, axis, forward), lax.ppermute(first, axis, backward)


def neighbours(low, high, left, right):
    return shift_planes("row", low, high) + shift_planes(COL, left, right)


def tiled_local(right_side, permeability, lift_weight, spectral_weight, mix_weight, proj_weight):
    rows, cols, depth = right_side.shape
    n_row = lax.axis_size("row")
    n_col = lax.axis_size(COL)
    count = n_row * n_col
    cells = float(rows * n_row * cols * n_col * depth)
    freq = KX // n_col
    deep_forward, deep_back = (jnp.asarray(t) for t in deep_tables(n_row, depth))
    col_forward, col_back = (jnp.asarray(t) for t in column_tables(n_col, cols))
    lift_weight = GAIN * lift_weight.T
    mix_weight = jnp.where(jnp.arange(CHANNELS + 1) < CHANNELS, 0.5, GAIN) * mix_weight
    proj_weight = jnp.where(jnp.arange(CHANNELS + 1) < CHANNELS, 0.5 / GAIN, 1.0) * proj_weight
    field = shape(rows, cols, depth)
    field_bytes = 4 * rows * cols * depth
    partial = shape(count, SUBLANES, LANES)
    channels = shape(rows, CHANNELS, depth, cols)
    n_chip = n_col // 2
    spectra = shape(n_row * n_chip, rows, SUBLANES, LANES)
    spectra_bytes = 4 * spectra.size
    smem = whole(pltpu.SMEM)
    vmem = whole()
    anywhere = whole(pl.ANY)
    plane = pl.BlockSpec((1, cols, depth), lambda i: (i, 0, 0))
    spectra_block = pl.BlockSpec((n_row * n_chip, 1, SUBLANES, LANES), lambda i: (0, i, 0, 0))
    point_block = pl.BlockSpec((1, CHANNELS, depth, cols), lambda i: (i, 0, 0, 0))
    kept_shape = shape(ITERS, rows, cols, depth)
    lift_flops = 2.0e9
    back_flops = 2.0e9

    weight_shape = (freq, CHANNELS, SUBLANES, LANES)
    kept_weights, *weights = call(
        weight_body,
        (shape(*weight_shape),) * n_col,
        [vmem],
        (vmem,) * n_col,
        scratch=[pltpu.VMEM((n_col,) + weight_shape, F32)],
        moved=8 * spectral_weight.size,
    )(spectral_weight)
    weights = [kept_weights] + [
        lax.ppermute(part, COL, [(i, (i + shift + 1) % n_col) for i in range(n_col)])
        for shift, part in enumerate(weights)
    ]
    edge_shapes = (shape(cols, depth),) * 2 + (shape(rows, depth),) * 2
    squares, *perm_edges = call(
        squares_body,
        (partial,) + edge_shapes,
        [vmem, vmem],
        (vmem,) * 5,
        moved=2 * field_bytes,
    )(right_side, permeability)
    squares = add_up(squares)
    perm_halo = neighbours(*perm_edges)
    acc_scratch = pltpu.VMEM((SUBLANES, LANES), F32)
    zt_scratch = pltpu.VMEM((2 * KZ * CHANNELS, cols), F32)

    def points(lifted, part, before, after):
        first = part * rows // 2
        half_block = pl.BlockSpec((1, CHANNELS, depth, cols), lambda i: (first + i, 0, 0, 0))
        return call(
            point_body,
            channels,
            [smem, half_block, anywhere, anywhere],
            half_block,
            grid=(rows // 2,),
            flops=2.5e9,
            moved=16 * field_bytes,
            alias={2: 0} if part else None,
            limit=12,
        )(mix_weight, lifted, before, after)

    def modes(received, before):
        places = rows * n_row
        tiles = lambda size: pltpu.VMEM((size, SUBLANES, LANES), F32)
        return call(
            functools.partial(modes_body, cells, n_row, n_col, n_chip),
            spectra,
            [vmem] + [anywhere] * (n_col + 1),
            vmem,
            scratch=[
                pltpu.VMEM((n_col,) + weight_shape, F32),
                pltpu.SemaphoreType.DMA((n_col,)),
                tiles(places),
                tiles(places),
                tiles(KX),
                tiles(KX),
            ],
            moved=2 * spectra_bytes + 4 * spectral_weight.size,
            near=(0,),
        )(received, *weights, before)

    def mixed_modes(own, partner, lifted, waiting):
        blocks = call(join_body, spectra, [vmem, vmem], vmem, near=(0, 1))(own, swap(partner))
        received = exchange(blocks, CHIPS)
        point = points(lifted, 0, blocks, blocks)
        blocks = modes(received, point)
        received = exchange(blocks, CHIPS)
        point = points(lifted, 1, point, blocks)
        received = pl.pallas_call(
            tie_body,
            out_shape=spectra,
            in_specs=[anywhere] * (2 + len(waiting)),
            out_specs=anywhere,
            input_output_aliases={0: 0},
        )(received, point, *waiting)
        return received, swap(received), point

    def back(index, scale_from, scalars, fields, waiting):
        def run(place_of, steps, inner, waiting, outs, out_specs, alias, loose):
            count_in = 1 + len(scalars)
            spectra_at = pl.BlockSpec(
                (n_row * n_chip, 1, SUBLANES, LANES), lambda i: (0, place_of(i), 0, 0)
            )
            point_at = pl.BlockSpec(
                (1, CHANNELS, depth, cols), lambda i: (place_of(i), 0, 0, 0)
            )
            kept_at = pl.BlockSpec((1, 1, cols, depth), lambda i: (index, place_of(i), 0, 0))
            plane_at = pl.BlockSpec((1, cols, depth), lambda i: (place_of(i), 0, 0))
            return call(
                functools.partial(
                    back_body,
                    scale_from,
                    len(scalars),
                    2 if inner else len(waiting),
                    inner,
                ),
                outs,
                [smem]
                + [vmem] * len(scalars)
                + [spectra_at, spectra_at, point_at, vmem, vmem]
                + ([anywhere, anywhere, vmem, vmem] if inner else [anywhere] * len(waiting)),
                (kept_at, plane_at) + out_specs,
                grid=(steps,),
                scratch=[zt_scratch, pltpu.VMEM((depth, cols), F32)],
                flops=back_flops / 2,
                moved=9 * field_bytes,
                alias={count_in + 5 + i: o for i, o in alias},
                limit=12,
                near=(count_in + 1,)
                + tuple(
                    count_in + 5 + i
                    for i, array in enumerate(waiting)
                    if array.size != kept_shape.size
                ),
                loose=loose,
            )(proj_weight, *scalars, *fields, col_back, deep_back, *waiting)

        kept, field_out, low, high, left, right = run(
            lambda i: i * (rows - 1),
            2,
            False,
            waiting,
            (kept_shape, field) + edge_shapes,
            (vmem,) * 4,
            [(0, 0)] if index else [],
            (1,),
        )
        halo_rows = shift_planes("row", low, high)
        kept, field_out, left, right = run(
            lambda i: i + 1,
            rows - 2,
            True,
            (kept, field_out, left, right),
            (kept_shape, field) + edge_shapes[2:],
            (vmem,) * 2,
            [(0, 0), (1, 1)],
            (1,),
        )
        return (kept, field_out) + halo_rows + shift_planes(COL, left, right)

    own, partner, lifted = call(
        functools.partial(lift_first_body, cells),
        (spectra, spectra, channels),
        [smem, vmem, plane, plane, vmem, vmem] + [anywhere] * n_col,
        (spectra_block, spectra_block, point_block),
        limit=16,
        loose=(0, 1),
        near=(6, 7, 8, 9),
        grid=(rows,),
        scratch=[zt_scratch],
        flops=lift_flops,
        moved=2 * field_bytes + spectra_bytes,
    )(lift_weight, squares, right_side, permeability, deep_forward, col_forward, *weights)
    received, other, point = mixed_modes(own, partner, lifted, perm_halo)
    kept, old, *edges = back(
        0,
        lambda first_ref: scale_of(gathered(first_ref, 0), cells),
        (squares,),
        (received, other, point),
        (),
    )

    old_halo = edges
    args = (old, permeability, *old_halo, *perm_halo, right_side)
    image, sums = call(
        operator_first_body,
        (field, partial),
        [vmem] * 10 + [plane],
        (plane, vmem),
        grid=(rows,),
        scratch=[acc_scratch],
        moved=9 * field_bytes,
        near=range(11),
        loose=range(3),
    )(*args)
    sums = add_up(sums)

    own, partner, lifted, residual = call(
        functools.partial(lift_next_body, cells),
        (spectra, spectra, channels, field),
        [smem, vmem, vmem, plane, plane, plane, vmem, vmem],
        (spectra_block, spectra_block, point_block, plane),
        limit=16,
        near=(4,),
        loose=(0, 1),
        grid=(rows,),
        scratch=[zt_scratch],
        flops=lift_flops,
        moved=4 * field_bytes + spectra_bytes,
    )(lift_weight, squares, sums, right_side, image, permeability, deep_forward, col_forward)
    received, other, point = mixed_modes(own, partner, lifted, ())
    kept, update, *edges = back(
        1,
        lambda first_ref, sums_ref: scale_of(next_scalars(first_ref, sums_ref)[2], cells),
        (squares, sums),
        (received, other, point),
        (kept,),
    )

    halo = edges
    args = (squares, sums, update, old, permeability, *halo, *old_halo, *perm_halo, residual, image)
    way, last_image, later = call(
        functools.partial(operator_next_body, cells),
        (field, field, partial),
        [vmem] * 17 + [plane] * 2,
        (plane, plane, vmem),
        grid=(rows,),
        scratch=[acc_scratch],
        near=range(19),
        loose=range(3),
        moved=11 * field_bytes,
    )(*args)
    later = add_up(later)
    answer, residual = call(
        last_body,
        (field, field),
        [vmem, vmem] + [plane] * 5,
        (plane, plane),
        grid=(rows,),
        moved=6 * field_bytes,
        near=range(7),
        loose=range(3),
    )(sums, later, old, way, residual, image, last_image)
    return (answer, residual, kept)


def fits_tiles(mesh, block):
    rows, cols, depth = block
    n_row, n_col = mesh.shape["row"], mesh.shape["col"]
    return (
        ITERS == 2
        and KZ == n_row * (LANES // (2 * CHANNELS))
        and KY == n_col * SUBLANES
        and KX % n_col == 0
        and n_col % 2 == 0
        and cols == LANES
        and depth % LANES == 0
        and rows * n_row >= KX
        and rows > 2
        and rows % 2 == 0
    )


def solution(mesh):
    placed = (
        P("row", "col", None),
        P("row", "col", None),
        P(),
        P(None, "row", None, None, "col"),
        P(),
        P(),
    )
    outputs = (P("row", "col", None), P("row", "col", None), P(None, "row", "col", None))

    def run(right_side, *others):
        rows, cols, depth = right_side.shape
        n_row, n_col = mesh.shape["row"], mesh.shape["col"]
        if not fits_tiles(mesh, (rows // n_row, cols // n_col, depth)):
            return jax.shard_map(
                local, mesh=mesh, in_specs=placed, out_specs=outputs, check_vma=False
            )(right_side, *others)
        cores = jax.sharding.Mesh(mesh.devices.reshape(n_row, n_col // 2, 2), BOTH)
        placed_cores, outputs_cores = jax.tree.map(
            lambda spec: P(*(COL if axis == "col" else axis for axis in spec)),
            (placed, outputs),
            is_leaf=lambda spec: isinstance(spec, P),
        )
        return jax.shard_map(
            tiled_local,
            mesh=cores,
            in_specs=placed_cores,
            out_specs=outputs_cores,
            check_vma=False,
        )(right_side, *others)

    return run
```

```python
import functools
import math

import jax
import jax.numpy as jnp
import ml_dtypes
import numpy as np
from jax import lax
from jax.experimental import pallas as pl
from jax.experimental.pallas import tpu as pltpu
from jax.sharding import PartitionSpec as P

CHANNELS = 16
KX = 16
KY = 32
KZ = 32
ITERS = 2


HIGHEST = lax.Precision.HIGHEST


def with_halo(block, sides, width):
    for axis, dim in sides:
        count = lax.axis_size(axis)
        forward = [(i, i + 1) for i in range(count - 1)]
        backward = [(target, source) for source, target in forward]
        low = lax.ppermute(
            lax.slice_in_dim(block, block.shape[dim] - width, None, axis=dim), axis, forward
        )
        high = lax.ppermute(lax.slice_in_dim(block, 0, width, axis=dim), axis, backward)
        block = jnp.concatenate([low, block, high], axis=dim)
    return block


def einsum_high(form, left, right):
    return jnp.einsum(form, left, right, precision=HIGHEST)


def harmonic(first, second):
    return 2.0 * first * second / (first + second)


def wave_table(freqs, places, length):
    turns = freqs[None, :] * places[:, None] % length
    angle = turns.astype(jnp.float32) * (2.0 * jnp.pi / length)
    return (jnp.cos(angle), jnp.sin(angle))


def signed_freqs(count):
    return jnp.arange(count, dtype=jnp.int32) - count // 2


def face_arrays(permeability):
    padded = with_halo(permeability, (("row", 0), ("col", 1)), 1).astype(jnp.float32)
    own = permeability.astype(jnp.float32)
    edged = jnp.pad(own, ((1, 1), (1, 1), (0, 0)), mode="edge")
    padded = jnp.where(padded > 0.0, padded, edged)
    first = harmonic(padded[:-1, 1:-1], padded[1:, 1:-1])
    second = harmonic(padded[1:-1, :-1], padded[1:-1, 1:])
    deep = jnp.pad(own, ((0, 0), (0, 0), (1, 1)), mode="edge")
    third = harmonic(deep[:, :, :-1], deep[:, :, 1:])
    return ((first, second, third), jnp.log(own))


def apply_operator(field, faces):
    first, second, third = faces
    padded = with_halo(field, (("row", 0), ("col", 1)), 1)
    padded = jnp.pad(padded, ((0, 0), (0, 0), (1, 1)))
    total = first[:-1] * (field - padded[:-2, 1:-1, 1:-1])
    total = total + first[1:] * (field - padded[2:, 1:-1, 1:-1])
    total = total + second[:, :-1] * (field - padded[1:-1, :-2, 1:-1])
    total = total + second[:, 1:] * (field - padded[1:-1, 2:, 1:-1])
    total = total + third[:, :, :-1] * (field - padded[1:-1, 1:-1, :-2])
    total = total + third[:, :, 1:] * (field - padded[1:-1, 1:-1, 2:])
    return total


def global_squares(field):
    return lax.psum(jnp.sum(field * field), ("row", "col"))


def mix_modes(real_in, imag_in, spectral_weight, deep_count, freq_count):
    block = spectral_weight.reshape(2, deep_count, CHANNELS, CHANNELS, freq_count, KY)
    real_out = einsum_high("kcfg,kcofg->kofg", real_in, block[0]) - einsum_high(
        "kcfg,kcofg->kofg", imag_in, block[1]
    )
    imag_out = einsum_high("kcfg,kcofg->kofg", imag_in, block[0]) + einsum_high(
        "kcfg,kcofg->kofg", real_in, block[1]
    )
    return (real_out, imag_out)


def spectral_transpose(real_part, imag_part, spectral_weight, grid):
    rows, cols, n_row, n_col, row_id, col_id = grid
    full_rows = rows * n_row
    full_cols = cols * n_col
    cosine_rows, sine_rows = wave_table(
        signed_freqs(KX), jnp.arange(full_rows, dtype=jnp.int32), full_rows
    )
    cosine_cols, sine_cols = wave_table(
        signed_freqs(KY), jnp.arange(full_cols, dtype=jnp.int32), full_cols
    )
    real_part, imag_part = (
        lax.all_to_all(real_part, "row", split_axis=0, concat_axis=1, tiled=True),
        lax.all_to_all(imag_part, "row", split_axis=0, concat_axis=1, tiled=True),
    )
    first_real = einsum_high("qxy,xf->qfy", real_part, cosine_rows) + einsum_high(
        "qxy,xf->qfy", imag_part, sine_rows
    )
    first_imag = einsum_high("qxy,xf->qfy", imag_part, cosine_rows) - einsum_high(
        "qxy,xf->qfy", real_part, sine_rows
    )
    first_real, first_imag = (
        lax.all_to_all(first_real, "col", split_axis=1, concat_axis=2, tiled=True),
        lax.all_to_all(first_imag, "col", split_axis=1, concat_axis=2, tiled=True),
    )
    second_real = einsum_high("qfy,yg->qfg", first_real, cosine_cols) + einsum_high(
        "qfy,yg->qfg", first_imag, sine_cols
    )
    second_imag = einsum_high("qfy,yg->qfg", first_imag, cosine_cols) - einsum_high(
        "qfy,yg->qfg", first_real, sine_cols
    )
    deep_count = KZ // n_row
    freq_count = KX // n_col
    shape_in = (deep_count, CHANNELS, freq_count, KY)
    mixed_real, mixed_imag = mix_modes(
        second_real.reshape(shape_in),
        second_imag.reshape(shape_in),
        spectral_weight,
        deep_count,
        freq_count,
    )
    shape_out = (deep_count * CHANNELS, freq_count, KY)
    mixed_real = mixed_real.reshape(shape_out)
    mixed_imag = mixed_imag.reshape(shape_out)
    back_real = einsum_high("qfg,yg->qfy", mixed_real, cosine_cols) - einsum_high(
        "qfg,yg->qfy", mixed_imag, sine_cols
    )
    back_imag = einsum_high("qfg,yg->qfy", mixed_imag, cosine_cols) + einsum_high(
        "qfg,yg->qfy", mixed_real, sine_cols
    )
    back_real, back_imag = (
        lax.all_to_all(back_real, "col", split_axis=2, concat_axis=1, tiled=True),
        lax.all_to_all(back_imag, "col", split_axis=2, concat_axis=1, tiled=True),
    )
    out_real = einsum_high("qfy,xf->qxy", back_real, cosine_rows) - einsum_high(
        "qfy,xf->qxy", back_imag, sine_rows
    )
    out_imag = einsum_high("qfy,xf->qxy", back_imag, cosine_rows) + einsum_high(
        "qfy,xf->qxy", back_real, sine_rows
    )
    out_real, out_imag = (
        lax.all_to_all(out_real, "row", split_axis=1, concat_axis=0, tiled=True),
        lax.all_to_all(out_imag, "row", split_axis=1, concat_axis=0, tiled=True),
    )
    return (out_real, out_imag)


def precondition(residual, squares_total, log_perm, weights, grid, cells):
    lift_weight, spectral_weight, mix_weight, proj_weight = weights
    rows, cols, depth = residual.shape
    scale = jnp.sqrt(squares_total / cells + 1e-06)
    scaled = residual / scale
    lifted = jax.nn.gelu(
        lift_weight[:, 0, None, None, None] * scaled[None]
        + lift_weight[:, 1, None, None, None] * log_perm[None]
        + lift_weight[:, 2, None, None, None]
    )
    cosine_deep, sine_deep = wave_table(
        jnp.arange(KZ, dtype=jnp.int32), jnp.arange(depth, dtype=jnp.int32), depth
    )
    real_part = einsum_high("cxyz,zk->kcxy", lifted, cosine_deep).reshape(KZ * CHANNELS, rows, cols)
    imag_part = -einsum_high("cxyz,zk->kcxy", lifted, sine_deep).reshape(KZ * CHANNELS, rows, cols)
    out_real, out_imag = spectral_transpose(real_part, imag_part, spectral_weight, grid)
    out_real = out_real.reshape(KZ, CHANNELS, rows, cols)
    out_imag = out_imag.reshape(KZ, CHANNELS, rows, cols)
    spatial = (
        einsum_high("kcxy,zk->cxyz", out_real, cosine_deep)
        - einsum_high("kcxy,zk->cxyz", out_imag, sine_deep)
    ) / cells
    point = (
        einsum_high("oc,cxyz->oxyz", mix_weight[:, :CHANNELS], lifted)
        + mix_weight[:, CHANNELS, None, None, None]
    )
    hidden = jax.nn.gelu(spatial + point)
    return scale * (
        einsum_high("o,oxyz->xyz", proj_weight[:CHANNELS], hidden) + proj_weight[CHANNELS]
    )


def local(right_side, permeability, lift_weight, spectral_weight, mix_weight, proj_weight):
    rows, cols, depth = right_side.shape
    n_row = lax.axis_size("row")
    n_col = lax.axis_size("col")
    grid = (rows, cols, n_row, n_col, lax.axis_index("row"), lax.axis_index("col"))
    cells = float(rows * n_row * cols * n_col * depth)
    faces, log_perm = face_arrays(permeability)
    weights = (lift_weight, spectral_weight, mix_weight, proj_weight)

    def precond(residual, squares_total):
        return precondition(residual, squares_total, log_perm, weights, grid, cells)

    solution = jnp.zeros_like(right_side)
    residual = right_side
    kept = []
    update = precond(residual, global_squares(residual))
    kept.append(update)
    direction = update
    for step in range(ITERS):
        image = apply_operator(direction, faces)
        curvature, along = lax.psum(
            (jnp.sum(direction * image), jnp.sum(residual * direction)), ("row", "col")
        )
        alpha = along / curvature
        solution = solution + alpha * direction
        residual = residual - alpha * image
        if step + 1 < ITERS:
            update = precond(residual, global_squares(residual))
            kept.append(update)
            beta = lax.psum(jnp.sum(update * image), ("row", "col")) / curvature
            direction = update - beta * direction
    return (solution, residual, jnp.stack(kept))


LANES = 128
SUBLANES = 8
COL = ("y", "core")
CHIPS = ("row", "y")
BOTH = ("row", "y", "core")
CHUNK = 32
F32 = jnp.float32
BF16 = jnp.bfloat16


def split_table(table):
    high = table.astype(ml_dtypes.bfloat16)
    low = (table - high.astype(np.float64)).astype(ml_dtypes.bfloat16)
    return high, low


def split(value):
    high = value.astype(BF16)
    return high, (value - high.astype(F32)).astype(BF16)


def split_three(value):
    high = value.astype(BF16).astype(F32)
    rest = value - high
    middle = rest.astype(BF16).astype(F32)
    return high, middle, rest - middle


def matmul(left, right):
    return jnp.dot(left, right, preferred_element_type=F32)


def matmul_nt(left, right):
    return lax.dot_general(left, right, (((1,), (1,)), ((), ())), preferred_element_type=F32)


def angles(freqs, places, length):
    turns = np.multiply.outer(freqs, places) % length
    return turns * (2.0 * np.pi / length)


def deep_order(n_row):
    count = KZ // n_row
    order = [
        (part, row * count + place)
        for row in range(n_row)
        for part in range(2)
        for place in range(count)
    ]
    return np.array(order)


def deep_tables(n_row, depth):
    order = deep_order(n_row)
    angle = angles(order[:, 1], np.arange(depth), depth)
    wave = np.where(order[:, :1] == 0, np.cos(angle), -np.sin(angle))
    high, low = split_table(wave)
    return np.concatenate([high, low], 0), np.concatenate([high.T, high.T, high.T, low.T], 1)


def column_tables(n_col, cols):
    freqs = np.arange(KY) - KY // 2
    forward = []
    back = []
    for place in range(n_col):
        angle = angles(freqs, place * cols + np.arange(cols), n_col * cols)
        own = np.arange(KY).reshape(-1, 2, SUBLANES)[:, place % 2].reshape(-1)
        partner = np.arange(KY).reshape(-1, 2, SUBLANES)[:, 1 - place % 2].reshape(-1)
        angle = angle[np.concatenate([own, partner])]
        both = np.concatenate([np.cos(angle), np.sin(angle)], 0)
        high, low = split_table(both)
        forward.append(
            np.concatenate(
                [
                    np.concatenate([high, high], 1),
                    np.concatenate([low, np.zeros_like(low)], 1),
                ],
                0,
            )
        )
        back.append(
            np.concatenate(
                [
                    np.concatenate([high, low], 1),
                    np.concatenate([high, low], 1),
                    np.concatenate([high, np.zeros_like(low)], 1),
                ],
                0,
            )
        )
    return np.stack(forward), np.stack(back)


GAIN = (math.sqrt(2.0 / math.pi) * 0.044715) ** (1.0 / 3.0)
LINEAR = math.sqrt(2.0 / math.pi) / GAIN


def scaled_gelu(value):
    return value + value * jnp.tanh(value * (value * value + LINEAR))


def call(body, outs, in_specs, out_specs, grid=(), scratch=(), flops=0, moved=0, alias=None, limit=8, near=(), loose=()):
    single = not isinstance(outs, tuple)
    outs = (outs,) if single else outs
    out_specs = (out_specs,) if single else out_specs
    run = pl.pallas_call(
        body,
        out_shape=tuple(
            out if place in loose or out.size <= 2**16 else pltpu.HBM(out.shape, out.dtype)
            for place, out in enumerate(outs)
        ),
        grid=grid,
        in_specs=in_specs,
        out_specs=out_specs,
        scratch_shapes=list(scratch),
        input_output_aliases=alias or {},
        compiler_params=pltpu.CompilerParams(vmem_limit_bytes=limit * 1024 * 1024),
        cost_estimate=pl.CostEstimate(
            flops=int(flops), bytes_accessed=int(moved), transcendentals=0
        ),
    )

    def wrapped(*args):
        held = [
            arg
            if place in near or spec.memory_space == pltpu.SMEM
            else pltpu.with_memory_space_constraint(arg, pltpu.HBM)
            for place, (arg, spec) in enumerate(zip(args, in_specs))
        ]
        found = run(*held)
        return found[0] if single else found

    return wrapped


def whole(memory=pltpu.VMEM):
    return pl.BlockSpec(memory_space=memory)


def shape(*dims):
    return jax.ShapeDtypeStruct(dims, F32)


def lane_sums(value):
    folded = jnp.sum(value.reshape(-1, SUBLANES, value.shape[-1]), axis=0)
    folded = sum(
        folded[:, start : start + LANES] for start in range(0, folded.shape[1], LANES)
    )
    return jnp.sum(folded, axis=0, keepdims=True)


def spread(rows, ref):
    rows = rows + [jnp.zeros_like(rows[0])] * (SUBLANES - len(rows))
    ref[...] = jnp.broadcast_to(jnp.concatenate(rows, 0)[None], ref.shape)


def gathered(ref, row):
    total = jnp.sum(ref[...], axis=0)
    return jnp.sum(total[row : row + 1], axis=1, keepdims=True)


def squares_body(field_ref, perm_ref, out_ref, low_ref, high_ref, left_ref, right_ref):
    total = field_ref[0] * field_ref[0]
    for place in range(1, field_ref.shape[0]):
        total = total + field_ref[place] * field_ref[place]
    spread([lane_sums(total)], out_ref)
    rows, cols, _ = perm_ref.shape
    low_ref[...] = perm_ref[0].astype(F32)
    high_ref[...] = perm_ref[rows - 1].astype(F32)
    for place in range(rows):
        plane = perm_ref[place].astype(F32)
        left_ref[place : place + 1, :] = plane[:1]
        right_ref[place : place + 1, :] = plane[cols - 1 :]


def weight_body(weight_ref, *refs):
    *out_refs, hold_ref = refs
    groups, freq, channels, fine, _ = hold_ref.shape
    parts, deep, _, outs, modes = weight_ref.shape
    for channel in range(channels):
        block = weight_ref[:, :, channel].reshape(parts * deep * outs, modes)
        block = block.T.reshape(freq, groups, fine, parts * deep * outs)
        for group in range(groups):
            hold_ref[group, :, channel] = block[:, group]
    place = lax.axis_index(COL)
    for shift, out_ref in enumerate(out_refs):
        out_ref[...] = hold_ref[lax.rem(place + shift, groups)]


def scale_of(total, cells):
    return jnp.sqrt(total / cells + 1e-06)


def lift_channel(weight_ref, channel, scaled, log_perm):
    return scaled_gelu(
        weight_ref[0, channel] * scaled
        + (weight_ref[1, channel] * log_perm + weight_ref[2, channel])
    )


def transform(lift_ref, deep_ref, col_ref, scaled, log_perm, own_ref, partner_ref, lifted_ref, zt_ref):
    half = 2 * KZ
    cols = scaled.shape[1]
    for channel in range(0, CHANNELS, 2):
        pair = [lift_channel(lift_ref, channel + j, scaled, log_perm) for j in range(2)]
        for j in range(2):
            lifted_ref[0, channel + j] = pair[j]
        high, low = split(jnp.concatenate(pair, 1))
        part = matmul(deep_ref[...], high)
        part = part[:half] + part[half:] + matmul(deep_ref[:half], low)
        for j in range(2):
            zt_ref[pl.ds(channel + j, half, stride=CHANNELS), :] = part[:, j * cols : (j + 1) * cols]
    groups = half * CHANNELS // LANES
    part = matmul_nt(col_ref[lax.axis_index(COL)], jnp.concatenate(split(zt_ref[...]), 1))
    part = part[: 2 * KY] + part[2 * KY :]
    lane = lax.broadcasted_iota(jnp.int32, (KY, LANES), 1)
    sign = jnp.where(lane < LANES // 2, 1.0, -1.0).astype(F32)
    n_chip = KY // SUBLANES // 2
    for row in range(groups):
        lanes = slice(row * LANES, (row + 1) * LANES)
        block = part[:KY, lanes] + pltpu.roll(part[KY:, lanes], LANES // 2, 1) * sign
        for side, ref in enumerate((own_ref, partner_ref)):
            for place in range(n_chip):
                start = (side * n_chip + place) * SUBLANES
                ref[row * n_chip + place, 0] = block[start : start + SUBLANES]


def lift_first_body(cells, lift_ref, sums_ref, res_ref, perm_ref, deep_ref, col_ref, *refs):
    own_ref, partner_ref, lifted_ref, zt_ref = refs[-4:]
    scale = scale_of(gathered(sums_ref, 0), cells)
    scaled = (res_ref[0] / scale).T
    log_perm = jnp.log(perm_ref[0].astype(F32)).T
    transform(lift_ref, deep_ref, col_ref, scaled, log_perm, own_ref, partner_ref, lifted_ref, zt_ref)


def join_body(own_ref, partner_ref, out_ref):
    out_ref[...] = own_ref[...] + partner_ref[...]


def tie_body(*_):
    pass


def next_scalars(first_ref, sums_ref):
    curvature = gathered(sums_ref, 0)
    alpha = gathered(sums_ref, 1) / curvature
    total = gathered(first_ref, 0) + alpha * (
        alpha * gathered(sums_ref, 2) - 2.0 * gathered(sums_ref, 3)
    )
    return curvature, alpha, jnp.maximum(total, 0.0)


def lift_next_body(cells, lift_ref, first_ref, sums_ref, res_ref, image_ref, perm_ref, deep_ref, col_ref, own_ref, partner_ref, lifted_ref, next_ref, zt_ref):
    _, alpha, total = next_scalars(first_ref, sums_ref)
    scale = scale_of(total, cells)
    residual = res_ref[0] - alpha * image_ref[0]
    next_ref[0] = residual
    scaled = (residual / scale).T
    log_perm = jnp.log(perm_ref[0].astype(F32)).T
    transform(lift_ref, deep_ref, col_ref, scaled, log_perm, own_ref, partner_ref, lifted_ref, zt_ref)


def point_body(mix_ref, lifted_ref, _, __, point_ref):
    size = 16 * SUBLANES
    group = 2

    def step(index, carry):
        lines = pl.ds(pl.multiple_of(index * size, size), size)
        for first in range(0, CHANNELS, group):
            sums = [mix_ref[first + j, CHANNELS] for j in range(group)]
            for channel in range(CHANNELS):
                lifted = lifted_ref[0, channel, lines, :]
                sums = [
                    total + mix_ref[first + j, channel] * lifted for j, total in enumerate(sums)
                ]
            for j, total in enumerate(sums):
                point_ref[0, first + j, lines, :] = total
        return carry

    lax.fori_loop(0, lifted_ref.shape[2] // size, step, 0)


def modes_body(cells, n_row, n_col, n_chip, recv_ref, *refs):
    sources = refs[:n_col]
    _, out_ref, weight_ref, sems, field_ref, turned_ref, spec_ref, odd_ref = refs[n_col:]
    own = lax.axis_index(COL)
    copies = [
        pltpu.make_async_copy(
            source, weight_ref.at[lax.rem(own + n_col - shift, n_col)], sems.at[shift]
        )
        for shift, source in enumerate(sources)
    ]
    for copy in copies:
        copy.start()
    rows = recv_ref.shape[1]
    places = n_row * rows
    tile = (SUBLANES, LANES)
    lane = lax.broadcasted_iota(jnp.int32, tile, 1)
    first = lane < LANES // 2
    sign = jnp.where(first, 1.0, -1.0).astype(F32)
    base = lane - lane % CHANNELS

    def turn(value):
        return pltpu.roll(value, LANES // 2, 1) * sign

    for row in range(n_row):
        for place in range(rows):
            value = recv_ref[row * n_chip, place]
            for chip in range(1, n_chip):
                value = value + recv_ref[row * n_chip + chip, place]
            field_ref[row * rows + place] = value
    angle = 2.0 * np.pi / places
    half = KX // 2

    def weigh(coefs, ref):
        total = None
        for place, coef in enumerate(coefs):
            coef = float(coef)
            if abs(coef) < 1e-12:
                continue
            term = ref[place]
            if coef == -1.0:
                term = -term
            elif coef != 1.0:
                term = coef * term
            total = term if total is None else total + term
        return jnp.zeros(tile, F32) if total is None else total

    middle = places // 2
    for place in range(1, middle):
        value, mirror = field_ref[place], field_ref[places - place]
        field_ref[place] = value + mirror
        turned_ref[place] = turn(value - mirror)
    for freq in range(half + 1):
        turns = freq * np.arange(middle + 1) % places
        even = weigh(np.cos(angle * turns), field_ref)
        odd = weigh(np.concatenate([[0.0], np.sin(angle * turns[1:middle])]), turned_ref)
        if freq < half:
            spec_ref[half + freq] = even + odd
        if freq > 0:
            spec_ref[half - freq] = even - odd

    for copy in copies:
        copy.wait()
    share = KX // n_col
    for freq in range(KX):
        value = spec_ref[freq]
        same = [None, None]
        cross = [None, None]
        for channel in range(CHANNELS):
            wide = jnp.take_along_axis(value, base + channel, axis=1)
            weight = weight_ref[freq // share, freq % share, channel]
            for sums, factor in ((same, weight), (cross, pltpu.roll(weight, LANES // 2, 1))):
                term = factor * wide
                kept = sums[channel % 2]
                sums[channel % 2] = term if kept is None else kept + term
        same = same[0] + same[1]
        cross = cross[0] + cross[1]
        total = jnp.where(
            first,
            same - pltpu.roll(same, LANES // 2, 1),
            cross + pltpu.roll(cross, LANES // 2, 1),
        )
        field_ref[freq] = total
        turned_ref[freq] = -turn(total)
    gain = 0.5 / cells
    evens = [field_ref[half] * gain]
    odds = [None]
    for freq in range(1, half):
        evens.append((field_ref[half + freq] + field_ref[half - freq]) * gain)
        odds.append((turned_ref[half + freq] - turned_ref[half - freq]) * gain)
    evens.append(field_ref[0] * gain)
    odds.append(-turned_ref[0] * gain)
    for freq in range(half + 1):
        spec_ref[freq] = evens[freq]
        if freq > 0:
            odd_ref[freq] = odds[freq]

    def store(place, value):
        for chip in range(n_chip):
            out_ref[(place // rows) * n_chip + chip, place % rows] = value

    for place in range(places // 2 + 1):
        turns = place * np.arange(half + 1) % places
        even = weigh(np.cos(angle * turns), spec_ref)
        odd = weigh(np.sin(angle * turns), odd_ref)
        store(place, even + odd)
        if 0 < place < places // 2:
            store(places - place, even - odd)


def back_transform(recv_ref, other_ref, point_ref, proj_ref, col_ref, deep_ref, wave_ref, total_ref, scale):
    groups = 2 * KZ * CHANNELS // LANES
    n_col = KY // SUBLANES
    cols = col_ref.shape[2] // 2
    lane = lax.broadcasted_iota(jnp.int32, (KY, LANES), 1)
    sign = jnp.where(lane < LANES // 2, -1.0, 1.0).astype(F32)
    half = 2 * KZ
    pieces = []
    for row in range(groups):
        chips = slice(row * n_col // 2, (row + 1) * n_col // 2)
        value = jnp.concatenate([recv_ref[chips, 0], other_ref[chips, 0]], 0)
        value = value.reshape(KY, LANES)
        turned = pltpu.roll(value, LANES // 2, 1) * sign
        both = jnp.concatenate([value, turned], 0)
        pieces.append(jnp.concatenate(split_three(both), 0).T.astype(BF16))
    part = matmul(jnp.concatenate(pieces, 0), col_ref[lax.axis_index(COL)])
    wave_ref[...] = part[:, :cols] + part[:, cols:]

    def waves(out):
        both = [wave_ref[pl.ds(out + j, half, stride=CHANNELS), :] for j in range(2)]
        high, middle, low = (
            part.astype(BF16) for part in split_three(jnp.concatenate(both, 1))
        )
        return jnp.concatenate([high, middle, low, high], 0)

    for out in range(0, CHANNELS, 2):
        spatial = matmul(deep_ref[...], waves(out))
        for start in range(0, spatial.shape[0], CHUNK):
            lines = slice(start, start + CHUNK)
            total = proj_ref[CHANNELS] if out == 0 else total_ref[lines]
            for j in range(2):
                value = spatial[lines, j * cols : (j + 1) * cols] + point_ref[0, out + j, lines]
                total = total + proj_ref[out + j] * scaled_gelu(value)
            total_ref[lines] = total
    return (scale * total_ref[...]).T


def put_lines(update, place, left_ref, right_ref):
    left_ref[pl.ds(place, 1), :] = update[:1]
    right_ref[pl.ds(place, 1), :] = update[update.shape[0] - 1 :]


def back_outer(update, kept_ref, field_ref, low_ref, high_ref, left_ref, right_ref):
    step = pl.program_id(0)
    kept_ref[0, 0] = update
    field_ref[0] = update
    last = left_ref.shape[0] - 1

    @pl.when(step == 0)
    def _():
        low_ref[...] = update
        put_lines(update, 0, left_ref, right_ref)

    @pl.when(step == 1)
    def _():
        high_ref[...] = update
        put_lines(update, last, left_ref, right_ref)


def back_inner(update, left_in, right_in, kept_ref, field_ref, left_ref, right_ref):
    step = pl.program_id(0)
    kept_ref[0, 0] = update
    field_ref[0] = update
    last = left_ref.shape[0] - 1

    @pl.when(step == 0)
    def _():
        for place in (0, last):
            line = slice(place, place + 1)
            left_ref[line] = left_in[line]
            right_ref[line] = right_in[line]

    put_lines(update, step + 1, left_ref, right_ref)


def back_body(scale_from, scalars, waiting, inner, proj_ref, *refs):
    scalar_refs, refs = refs[:scalars], refs[scalars:]
    recv_ref, other_ref, point_ref, col_ref, deep_ref = refs[:5]
    refs = refs[5 + waiting :]
    *outs, wave_ref, total_ref = refs
    update = back_transform(
        recv_ref, other_ref, point_ref, proj_ref, col_ref, deep_ref, wave_ref, total_ref,
        scale_from(*scalar_refs),
    )
    (back_inner if inner else back_outer)(update, *outs)


def stencil(fields, perms):
    own, before, after, left, right = fields
    cols, depth = own.shape
    line = lax.broadcasted_iota(jnp.int32, (cols, depth), 0)
    deep = lax.broadcasted_iota(jnp.int32, (cols, depth), 1)

    def sides(array, before, after, left, right, first, last):
        return (
            before,
            after,
            jnp.where(line == 0, left, pltpu.roll(array, 1, 0)),
            jnp.where(line == cols - 1, right, pltpu.roll(array, cols - 1, 0)),
            jnp.where(deep == 0, first, pltpu.roll(array, 1, 1)),
            jnp.where(deep == depth - 1, last, pltpu.roll(array, depth - 1, 1)),
        )

    perm, *others = perms
    others = [
        jnp.where(other > 0.0, other, edge)
        for other, edge in zip(others, (perm, perm, perm[:1], perm[cols - 1 :]))
    ]
    total = None
    for other, conductance in zip(
        sides(own, before, after, left, right, 0.0, 0.0), sides(perm, *others, perm, perm)
    ):
        term = harmonic(perm, conductance) * (own - other)
        total = term if total is None else total + term
    return total


def add_sums(terms, out_ref, acc_ref):
    step = pl.program_id(0)

    @pl.when(step == 0)
    def _():
        acc_ref[...] = jnp.zeros_like(acc_ref)

    for j, term in enumerate(terms):
        acc_ref[j : j + 1] += lane_sums(term)

    @pl.when(step == pl.num_programs(0) - 1)
    def _():
        spread([acc_ref[j : j + 1] for j in range(len(terms))], out_ref)


def around(ref, index, halo):
    low_ref, high_ref, left_ref, right_ref = halo
    step = pl.program_id(0)
    last = pl.num_programs(0) - 1
    line = pl.ds(step, 1)

    def plane(place):
        return ref[index + (place,)].astype(F32)

    def outside(axis, edge, value):
        return jnp.where(lax.axis_index(axis) == edge, 0.0, value)

    low = outside("row", 0, low_ref[...])
    high = outside("row", lax.axis_size("row") - 1, high_ref[...])
    left = outside(COL, 0, left_ref[line, :])
    right = outside(COL, lax.axis_size(COL) - 1, right_ref[line, :])
    before = jnp.where(step == 0, low, plane(jnp.maximum(step - 1, 0)))
    after = jnp.where(step == last, high, plane(jnp.minimum(step + 1, last)))
    return plane(step), before, after, left, right


def operator_first_body(field_ref, perm_ref, *refs):
    halo, perm_halo = refs[:4], refs[4:8]
    res_ref, image_ref, out_ref, acc_ref = refs[8:]
    fields = around(field_ref, (), halo)
    image = stencil(fields, around(perm_ref, (), perm_halo))
    own = fields[0]
    residual = res_ref[0]
    image_ref[0] = image
    add_sums((own * image, residual * own, image * image, residual * image), out_ref, acc_ref)


def operator_next_body(cells, first_ref, sums_ref, field_ref, old_ref, perm_ref, *refs):
    halo, old, perm_halo = refs[:4], refs[4:8], refs[8:12]
    res_ref, before_ref, way_ref, image_ref, out_ref, acc_ref = refs[12:]
    _, _, total = next_scalars(first_ref, sums_ref)
    factor = scale_of(total, cells) / scale_of(gathered(first_ref, 0), cells)
    old = around(old_ref, (), old)
    fields = [new - factor * other for new, other in zip(around(field_ref, (), halo), old)]
    image = stencil(fields, around(perm_ref, (), perm_halo))
    own = fields[0]
    residual = res_ref[0]
    way_ref[0] = own
    image_ref[0] = image
    add_sums((own * image, own * before_ref[0], residual * own, residual * old[0]), out_ref, acc_ref)


def last_body(sums_ref, later_ref, old_ref, way_ref, res_ref, before_ref, image_ref, sol_ref, out_ref):
    curvature = gathered(sums_ref, 0)
    alpha = gathered(sums_ref, 1) / curvature
    cross = gathered(later_ref, 1)
    delta = cross / curvature
    along = gathered(later_ref, 2) - delta * gathered(later_ref, 3)
    later = along / (gathered(later_ref, 0) - delta * cross)
    sol_ref[0] = alpha * old_ref[0] + later * (way_ref[0] - delta * old_ref[0])
    out_ref[0] = res_ref[0] - later * (image_ref[0] - delta * before_ref[0])


def exchange(blocks, axes):
    return lax.all_to_all(blocks, axes, split_axis=0, concat_axis=0, tiled=True)


def swap(blocks):
    return lax.ppermute(blocks, "core", [(0, 1), (1, 0)])


def add_up(partial):
    return exchange(partial, BOTH)


def shift_planes(axis, first, last):
    count = lax.axis_size(axis)
    forward = [(i, (i + 1) % count) for i in range(count)]
    backward = [(target, source) for source, target in forward]
    return lax.ppermute(last, axis, forward), lax.ppermute(first, axis, backward)


def neighbours(low, high, left, right):
    return shift_planes("row", low, high) + shift_planes(COL, left, right)


def tiled_local(right_side, permeability, lift_weight, spectral_weight, mix_weight, proj_weight):
    rows, cols, depth = right_side.shape
    n_row = lax.axis_size("row")
    n_col = lax.axis_size(COL)
    count = n_row * n_col
    cells = float(rows * n_row * cols * n_col * depth)
    freq = KX // n_col
    deep_forward, deep_back = (jnp.asarray(t) for t in deep_tables(n_row, depth))
    col_forward, col_back = (jnp.asarray(t) for t in column_tables(n_col, cols))
    lift_weight = GAIN * lift_weight.T
    mix_weight = jnp.where(jnp.arange(CHANNELS + 1) < CHANNELS, 0.5, GAIN) * mix_weight
    proj_weight = jnp.where(jnp.arange(CHANNELS + 1) < CHANNELS, 0.5 / GAIN, 1.0) * proj_weight
    field = shape(rows, cols, depth)
    field_bytes = 4 * rows * cols * depth
    partial = shape(count, SUBLANES, LANES)
    channels = shape(rows, CHANNELS, depth, cols)
    n_chip = n_col // 2
    spectra = shape(n_row * n_chip, rows, SUBLANES, LANES)
    spectra_bytes = 4 * spectra.size
    smem = whole(pltpu.SMEM)
    vmem = whole()
    anywhere = whole(pl.ANY)
    plane = pl.BlockSpec((1, cols, depth), lambda i: (i, 0, 0))
    spectra_block = pl.BlockSpec((n_row * n_chip, 1, SUBLANES, LANES), lambda i: (0, i, 0, 0))
    point_block = pl.BlockSpec((1, CHANNELS, depth, cols), lambda i: (i, 0, 0, 0))
    kept_shape = shape(ITERS, rows, cols, depth)
    lift_flops = 2.0e9
    back_flops = 2.0e9

    weight_shape = (freq, CHANNELS, SUBLANES, LANES)
    kept_weights, *weights = call(
        weight_body,
        (shape(*weight_shape),) * n_col,
        [vmem],
        (vmem,) * n_col,
        scratch=[pltpu.VMEM((n_col,) + weight_shape, F32)],
        moved=8 * spectral_weight.size,
    )(spectral_weight)
    weights = [kept_weights] + [
        lax.ppermute(part, COL, [(i, (i + shift + 1) % n_col) for i in range(n_col)])
        for shift, part in enumerate(weights)
    ]
    edge_shapes = (shape(cols, depth),) * 2 + (shape(rows, depth),) * 2
    squares, *perm_edges = call(
        squares_body,
        (partial,) + edge_shapes,
        [vmem, vmem],
        (vmem,) * 5,
        moved=2 * field_bytes,
    )(right_side, permeability)
    squares = add_up(squares)
    perm_halo = neighbours(*perm_edges)
    acc_scratch = pltpu.VMEM((SUBLANES, LANES), F32)
    zt_scratch = pltpu.VMEM((2 * KZ * CHANNELS, cols), F32)

    def points(lifted, part, before, after):
        first = part * rows // 2
        half_block = pl.BlockSpec((1, CHANNELS, depth, cols), lambda i: (first + i, 0, 0, 0))
        return call(
            point_body,
            channels,
            [smem, half_block, anywhere, anywhere],
            half_block,
            grid=(rows // 2,),
            flops=2.5e9,
            moved=16 * field_bytes,
            alias={2: 0} if part else None,
            limit=12,
        )(mix_weight, lifted, before, after)

    def modes(received, before):
        places = rows * n_row
        tiles = lambda size: pltpu.VMEM((size, SUBLANES, LANES), F32)
        return call(
            functools.partial(modes_body, cells, n_row, n_col, n_chip),
            spectra,
            [vmem] + [anywhere] * (n_col + 1),
            vmem,
            scratch=[
                pltpu.VMEM((n_col,) + weight_shape, F32),
                pltpu.SemaphoreType.DMA((n_col,)),
                tiles(places),
                tiles(places),
                tiles(KX),
                tiles(KX),
            ],
            moved=2 * spectra_bytes + 4 * spectral_weight.size,
            near=(0,),
        )(received, *weights, before)

    def mixed_modes(own, partner, lifted, waiting):
        blocks = call(join_body, spectra, [vmem, vmem], vmem, near=(0, 1))(own, swap(partner))
        received = exchange(blocks, CHIPS)
        point = points(lifted, 0, blocks, blocks)
        blocks = modes(received, point)
        received = exchange(blocks, CHIPS)
        point = points(lifted, 1, point, blocks)
        received = pl.pallas_call(
            tie_body,
            out_shape=spectra,
            in_specs=[anywhere] * (2 + len(waiting)),
            out_specs=anywhere,
            input_output_aliases={0: 0},
        )(received, point, *waiting)
        return received, swap(received), point

    def back(index, scale_from, scalars, fields, waiting):
        def run(place_of, steps, inner, waiting, outs, out_specs, alias, loose):
            count_in = 1 + len(scalars)
            spectra_at = pl.BlockSpec(
                (n_row * n_chip, 1, SUBLANES, LANES), lambda i: (0, place_of(i), 0, 0)
            )
            point_at = pl.BlockSpec(
                (1, CHANNELS, depth, cols), lambda i: (place_of(i), 0, 0, 0)
            )
            kept_at = pl.BlockSpec((1, 1, cols, depth), lambda i: (index, place_of(i), 0, 0))
            plane_at = pl.BlockSpec((1, cols, depth), lambda i: (place_of(i), 0, 0))
            return call(
                functools.partial(
                    back_body,
                    scale_from,
                    len(scalars),
                    2 if inner else len(waiting),
                    inner,
                ),
                outs,
                [smem]
                + [vmem] * len(scalars)
                + [spectra_at, spectra_at, point_at, vmem, vmem]
                + ([anywhere, anywhere, vmem, vmem] if inner else [anywhere] * len(waiting)),
                (kept_at, plane_at) + out_specs,
                grid=(steps,),
                scratch=[zt_scratch, pltpu.VMEM((depth, cols), F32)],
                flops=back_flops / 2,
                moved=9 * field_bytes,
                alias={count_in + 5 + i: o for i, o in alias},
                limit=12,
                near=(count_in + 1,)
                + tuple(
                    count_in + 5 + i
                    for i, array in enumerate(waiting)
                    if array.size != kept_shape.size
                ),
                loose=loose,
            )(proj_weight, *scalars, *fields, col_back, deep_back, *waiting)

        kept, field_out, low, high, left, right = run(
            lambda i: i * (rows - 1),
            2,
            False,
            waiting,
            (kept_shape, field) + edge_shapes,
            (vmem,) * 4,
            [(0, 0)] if index else [],
            (1,),
        )
        halo_rows = shift_planes("row", low, high)
        kept, field_out, left, right = run(
            lambda i: i + 1,
            rows - 2,
            True,
            (kept, field_out, left, right),
            (kept_shape, field) + edge_shapes[2:],
            (vmem,) * 2,
            [(0, 0), (1, 1)],
            (1,),
        )
        return (kept, field_out) + halo_rows + shift_planes(COL, left, right)

    own, partner, lifted = call(
        functools.partial(lift_first_body, cells),
        (spectra, spectra, channels),
        [smem, vmem, plane, plane, vmem, vmem] + [anywhere] * n_col,
        (spectra_block, spectra_block, point_block),
        limit=16,
        loose=(0, 1),
        near=(6, 7, 8, 9),
        grid=(rows,),
        scratch=[zt_scratch],
        flops=lift_flops,
        moved=2 * field_bytes + spectra_bytes,
    )(lift_weight, squares, right_side, permeability, deep_forward, col_forward, *weights)
    received, other, point = mixed_modes(own, partner, lifted, perm_halo)
    kept, old, *edges = back(
        0,
        lambda first_ref: scale_of(gathered(first_ref, 0), cells),
        (squares,),
        (received, other, point),
        (),
    )

    old_halo = edges
    args = (old, permeability, *old_halo, *perm_halo, right_side)
    image, sums = call(
        operator_first_body,
        (field, partial),
        [vmem] * 10 + [plane],
        (plane, vmem),
        grid=(rows,),
        scratch=[acc_scratch],
        moved=9 * field_bytes,
        near=range(11),
        loose=range(3),
    )(*args)
    sums = add_up(sums)

    own, partner, lifted, residual = call(
        functools.partial(lift_next_body, cells),
        (spectra, spectra, channels, field),
        [smem, vmem, vmem, plane, plane, plane, vmem, vmem],
        (spectra_block, spectra_block, point_block, plane),
        limit=16,
        near=(4,),
        loose=(0, 1),
        grid=(rows,),
        scratch=[zt_scratch],
        flops=lift_flops,
        moved=4 * field_bytes + spectra_bytes,
    )(lift_weight, squares, sums, right_side, image, permeability, deep_forward, col_forward)
    received, other, point = mixed_modes(own, partner, lifted, ())
    kept, update, *edges = back(
        1,
        lambda first_ref, sums_ref: scale_of(next_scalars(first_ref, sums_ref)[2], cells),
        (squares, sums),
        (received, other, point),
        (kept,),
    )

    halo = edges
    args = (squares, sums, update, old, permeability, *halo, *old_halo, *perm_halo, residual, image)
    way, last_image, later = call(
        functools.partial(operator_next_body, cells),
        (field, field, partial),
        [vmem] * 17 + [plane] * 2,
        (plane, plane, vmem),
        grid=(rows,),
        scratch=[acc_scratch],
        near=range(19),
        loose=range(3),
        moved=11 * field_bytes,
    )(*args)
    later = add_up(later)
    answer, residual = call(
        last_body,
        (field, field),
        [vmem, vmem] + [plane] * 5,
        (plane, plane),
        grid=(rows,),
        moved=6 * field_bytes,
        near=range(7),
        loose=range(3),
    )(sums, later, old, way, residual, image, last_image)
    return (answer, residual, kept)


def fits_tiles(mesh, block):
    rows, cols, depth = block
    n_row, n_col = mesh.shape["row"], mesh.shape["col"]
    return (
        ITERS == 2
        and KZ == n_row * (LANES // (2 * CHANNELS))
        and KY == n_col * SUBLANES
        and KX % n_col == 0
        and n_col % 2 == 0
        and cols == LANES
        and depth % LANES == 0
        and rows * n_row >= KX
        and rows > 2
        and rows % 2 == 0
    )


def solution(mesh):
    placed = (
        P("row", "col", None),
        P("row", "col", None),
        P(),
        P(None, "row", None, None, "col"),
        P(),
        P(),
    )
    outputs = (P("row", "col", None), P("row", "col", None), P(None, "row", "col", None))

    def run(right_side, *others):
        rows, cols, depth = right_side.shape
        n_row, n_col = mesh.shape["row"], mesh.shape["col"]
        if not fits_tiles(mesh, (rows // n_row, cols // n_col, depth)):
            return jax.shard_map(
                local, mesh=mesh, in_specs=placed, out_specs=outputs, check_vma=False
            )(right_side, *others)
        cores = jax.sharding.Mesh(mesh.devices.reshape(n_row, n_col // 2, 2), BOTH)
        placed_cores, outputs_cores = jax.tree.map(
            lambda spec: P(*(COL if axis == "col" else axis for axis in spec)),
            (placed, outputs),
            is_leaf=lambda spec: isinstance(spec, P),
        )
        return jax.shard_map(
            tiled_local,
            mesh=cores,
            in_specs=placed_cores,
            out_specs=outputs_cores,
            check_vma=False,
        )(right_side, *others)

    return run
```
